32 devices in a mesh: groups: 2 (over y), tm: 4 (over z), space: 4 (over x, core).
Axes of the slice: x: 2, y: 2, z: 4, core: 2. Of those that a mesh axis runs over, the one named last changes fastest.
Arguments:
- forcing: bfloat16 [128, 512, 128], P('tm', ('groups', 'space')), parts along dimension 1, may hold values from -6 to 6
- initial_state: float32 [512, 128], P(('groups', 'space')), parts along dimension 0, may hold values from -6 to 6
- connectivity: int32 [256, 6], P('space'), may hold values from -16 to 271, as said below
- pattern: int32 [256, 6], P('space'), may hold values 0 or 1
- diag_block: float32 [128, 128], replicated, may hold values from -0.3125 to 0.3125
- face_blocks: float32 [6, 128, 128], replicated, may hold values from -0.15625 to 0.15625
- coarse_block: float32 [128, 128], replicated, may hold values from -1 to 1
Outputs:
- solution: float32 [128, 512, 128], P('tm', ('groups', 'space')), parts along dimension 1
The draws below stay inside these ranges and needn't reach their ends.
There are 2 independent parts, one for each index of `groups`. The reference program is written for one: setup_inputs(seed, part) draws one part's arguments, and reference() takes and returns one part's arrays. A program takes and returns all parts, laid end to end along the dimension named above; an argument that names none is the same for every part. Nothing has to cross between parts.
Inputs may be any that keep to these rules, and one draw needn't show every extreme that they name: `connectivity`: faces 0 and 3 of element e connect to e - 1 and e + 1, faces 2 and 5 to e - 16 and e + 16, face 1 to an element 2 to 15 below e and face 4 to one 2 to 15 above e; values outside 0 to 255 stand for no element.
All inputs are finite; a program needn't handle non-finite values. No bound on the sum of `pattern` on one device may be relied on, other than what follows from the above.
Results may differ from the reference program's by a relative error of at most 0.0003.
Values may be sent and summed in bfloat16 or wider, within the bound.
No kernel may reach another device: no remote copies, remote signals or barrier semaphores. Data moves between devices by JAX's collectives and lax.ppermute only.
A program may use at most 64 MiB of HBM per device.

```python
import math
import jax
import jax.numpy as jnp
from jax import lax

BLOCK = 128
FACES = 6
COARSEN = 4
ITERS = 2
REACH = 16
NSTEPS = 128
ELEMENTS = 256


def draw_connectivity(key, part):
    key = jax.random.fold_in(key, 11)
    first_key, second_key = jax.random.split(key)
    rows = jnp.arange(ELEMENTS, dtype=jnp.int32)[:, None]
    lower = jax.random.randint(first_key, (ELEMENTS, 1), 2, REACH, dtype=jnp.int32)
    upper = jax.random.randint(second_key, (ELEMENTS, 1), 2, REACH, dtype=jnp.int32)
    unit = jnp.ones((ELEMENTS, 1), jnp.int32)
    offsets = jnp.concatenate([-unit, -lower, -REACH * unit, unit, upper, REACH * unit], axis=1)
    return (rows + offsets).astype(jnp.int32)


def draw_coarse_block(key, part):
    key = jax.random.fold_in(key, 23)
    noise = jnp.clip(jax.random.normal(key, (BLOCK, BLOCK), jnp.float32), -4.0, 4.0)
    return 0.93 * jnp.eye(BLOCK, dtype=jnp.float32) + 0.06 / math.sqrt(BLOCK) * noise


def with_ends(entries, own_key, least, top_value):
    longest = entries.shape.index(max(entries.shape))
    spots = []
    for shift in (0, 1):
        where = [jax.random.randint(jax.random.fold_in(own_key, axis), (), 0, length) for axis, length in enumerate(entries.shape)]
        where[longest] = (where[longest] + shift) % entries.shape[longest]
        spots.append(tuple(where))
    return entries.at[spots[0]].set(least).at[spots[1]].set(top_value)


def block_levels(rng, extent, shards, least, largest):
    level = 1.0
    for axis_at, blocks in shards:
        draws = jax.random.uniform(jax.random.fold_in(jax.random.fold_in(rng, 6), axis_at), (blocks,), jnp.float32, least / len(shards), largest / len(shards))
        level = level * jnp.repeat(jnp.exp(draws), extent[axis_at] // blocks).reshape((-1,) + (1,) * (len(extent) - 1 - axis_at))
    return level


def normal_values(rng, shape, spread, reach, pieces=(), kind=jnp.bfloat16):
    drawn = spread * jax.random.normal(rng, shape, jnp.float32)
    if pieces:
        drawn = drawn * block_levels(rng, shape, pieces, -0.22, 0.18)
    return jnp.clip(drawn, -reach, reach).astype(kind)


def setup_inputs(seed: int = 0, part: int = 0) -> dict:
    key_list = jax.random.split(jax.random.key(seed), 8)
    own_keys = jax.random.split(jax.random.fold_in(key_list[7], part), 8)
    forcing = normal_values(own_keys[0], (NSTEPS, ELEMENTS, BLOCK), 1.0, 6.0, ((0, 4), (1, 4)))
    initial_state = normal_values(own_keys[1], (ELEMENTS, BLOCK), 1.0, 6.0, ((0, 4),), jnp.float32)
    connectivity = draw_connectivity(jax.random.fold_in(key_list[7], 71), part)
    pattern = with_ends((jax.random.randint(key_list[3], (ELEMENTS, FACES), 0, 4) < 3).astype(jnp.int32), jax.random.fold_in(key_list[3], 1), 0, 1)
    diag_block = normal_values(key_list[4], (BLOCK, BLOCK), (3 * BLOCK) ** -0.5, 0.3125, (), jnp.float32)
    face_blocks = normal_values(key_list[5], (FACES, BLOCK, BLOCK), (11 * BLOCK) ** -0.5, 0.15625, (), jnp.float32)
    coarse_block = draw_coarse_block(jax.random.fold_in(key_list[7], 71), part)
    return {"forcing": forcing, "initial_state": initial_state, "connectivity": connectivity, "pattern": pattern, "diag_block": diag_block, "face_blocks": face_blocks, "coarse_block": coarse_block}


def stack_blocks(diag_block, face_blocks):
    allb = jnp.concatenate([diag_block[None], face_blocks], axis=0)
    return jnp.transpose(allb, (0, 2, 1)).reshape(-1, allb.shape[1])


def advance(state, connectivity, pattern, stacked):
    width = state.shape[2]
    padded = jnp.pad(state, ((0, 0), (REACH, REACH), (0, 0)))
    neighbours = jnp.take(padded, connectivity + REACH, axis=1)
    neighbours = neighbours * pattern.astype(jnp.float32)[None, :, :, None]
    joined = jnp.concatenate([state[:, :, None, :], neighbours], axis=2)
    flat = joined.reshape(-1, (FACES + 1) * width)
    out = jnp.dot(flat, stacked, precision=lax.Precision.HIGHEST, preferred_element_type=jnp.float32)
    return out.reshape(state.shape)


def relax(starts, force, connectivity, pattern, stacked):
    current = starts
    points = []
    for inner in range(COARSEN - 1):
        current = advance(current, connectivity, pattern, stacked) + force[:, inner]
        points.append(current)
    ends = advance(current, connectivity, pattern, stacked) + force[:, COARSEN - 1]
    return points, ends


def reference(forcing, initial_state, connectivity, pattern, diag_block, face_blocks, coarse_block):
    stacked = stack_blocks(diag_block, face_blocks)
    ncoarse = NSTEPS // COARSEN
    force = forcing.astype(jnp.float32).reshape(ncoarse, COARSEN, ELEMENTS, BLOCK)
    cvalues = jnp.zeros((ncoarse, ELEMENTS, BLOCK), jnp.float32)
    psi_t = coarse_block.T

    def coarse_step(carry, resid_row):
        nxt = jnp.dot(carry, psi_t, precision=lax.Precision.HIGHEST, preferred_element_type=jnp.float32) + resid_row
        return nxt, nxt

    for sweep in range(ITERS):
        starts = jnp.concatenate([initial_state[None], cvalues[:-1]], axis=0)
        points, ends = relax(starts, force, connectivity, pattern, stacked)
        resid = ends - cvalues
        _, corr = lax.scan(coarse_step, jnp.zeros((ELEMENTS, BLOCK), jnp.float32), resid)
        cvalues = cvalues + corr
    starts = jnp.concatenate([initial_state[None], cvalues[:-1]], axis=0)
    points, ends = relax(starts, force, connectivity, pattern, stacked)
    solution = jnp.stack(points + [cvalues], axis=1)
    return solution.reshape(NSTEPS, ELEMENTS, BLOCK)
```

```python
import functools

import jax
import jax.numpy as jnp
from jax import lax
from jax.experimental import pallas as pl
from jax.experimental.pallas import tpu as pltpu
from jax.sharding import PartitionSpec as P

COARSEN = 4
REACH = 16
F32 = jnp.float32
BF16 = jnp.bfloat16
CHUNK = 32
SCAN = 64


def shifted(value, steps):
    count = lax.axis_size("space")
    pairs = [(i, i + steps) for i in range(count) if 0 <= i + steps < count]
    return lax.ppermute(value, "space", pairs)


def split(u):
    lead = u.astype(BF16).astype(F32)
    return jnp.concatenate([u, u - lead], axis=1).astype(BF16)


def product(x, weights):
    m = x.shape[0] // 16
    r = jnp.dot(x, weights, preferred_element_type=F32).reshape(m, 16, 256)
    return r[:, :8, :128] + (r[:, 8:, :128] + r[:, :8, 128:])


def product_rows(u, weights):
    return product(split(u).reshape(-1, 128), weights)


def put_halves(ref, w):
    lead = w.astype(BF16)
    ref[:, 0:128] = lead
    ref[:, 128:256] = (w - lead.astype(F32)).astype(BF16)


def scan_tiles(y, pw):
    row = lax.broadcasted_iota(jnp.int32, y.shape, 1)
    for level in range(3):
        d = 1 << level
        z = product_rows(y, pw[pl.ds(level * 128, 128), :])
        y = y + jnp.where(row >= d, pltpu.roll(z, d, axis=1), 0.0)
    return y


def apply_phi(src, idx, w, low, high, emit):
    def body(c, carry):
        base = low + c * CHUNK
        cols = [src[pl.ds(base, CHUNK)].reshape(CHUNK * 16, 128)]
        for f in range(6):
            cols.append(jnp.concatenate([src[idx[f, base + e]] for e in range(CHUNK)], axis=0))
        emit(base, product(jnp.concatenate(cols, axis=1), w[...]))
        return carry

    lax.fori_loop(0, (high - low) // CHUNK, body, 0)


def entering(ag, we, out, n):
    t, x, count = lax.axis_index("tm"), lax.axis_index("space"), lax.axis_size("space")
    left_on = (x > 0).astype(F32)
    right_on = (x < count - 1).astype(F32)
    at = [jnp.maximum(x - 1, 0) * n, x * n, jnp.minimum(x + 1, count - 1) * n]
    out[...] = jnp.zeros_like(out)

    def body(s, carry):
        parts = [ag[s, pl.ds(pl.multiple_of(a, n), n), :] for a in at]
        value = jnp.concatenate([parts[0] * left_on, parts[1], parts[2] * right_on], axis=0)
        m = value.shape[0]
        lead = value.astype(BF16)
        rest = (value - lead.astype(F32)).astype(BF16)
        r = jnp.dot(jnp.concatenate([lead, rest], axis=0), we[s], preferred_element_type=F32)
        out[...] += r[:m, :128] + (r[m:, :128] + r[:m, 128:])
        return carry

    lax.fori_loop(0, t, body, 0)


def pack_kernel(forcing, init, conn, pattern, fe, tab, pay_left, pay_right, rows, square):
    n = init.shape[0]
    stride = COARSEN * n
    step = 256
    for at in range(0, rows.shape[0], step):
        rows[pl.ds(at, step), :] = forcing[pl.ds(at, step), :].astype(F32)

    def body(pair, carry):
        e = pair * 2
        for k in range(COARSEN):
            two = [rows[pl.ds(k * n + e + j, 8, stride=stride), :] for j in range(2)]
            fe[k, pl.ds(pl.multiple_of(e * 8, 16), 16), :] = jnp.concatenate(two, axis=0).astype(BF16)
        return carry

    lax.fori_loop(0, n // 2, body, 0, unroll=4)
    place = lax.broadcasted_iota(jnp.int32, (n, 6), 0) + lax.axis_index("space") * n
    offs = ((conn[...] - place) * pattern[...]).astype(F32)
    square[...] = jnp.zeros_like(square)
    square[0:n, 0:6] = offs
    square[n : 2 * n, 0:6] = offs
    tab[...] = square[...].T[0:16, :].astype(BF16)
    lead = init[...].astype(BF16)
    rest = (init[...] - lead.astype(F32)).astype(BF16)
    at = 0
    for k in range(COARSEN - 1):
        width = (COARSEN - 1 - k) * REACH * 8
        pay_left[pl.ds(at, width), :] = fe[k, pl.ds(0, width), :]
        pay_right[pl.ds(at, width), :] = fe[k, pl.ds(n * 8 - width, width), :]
        at += width
    for pay in (pay_left, pay_right):
        pay[pl.ds(at, n), :] = lead
        pay[pl.ds(at + n, n), :] = rest
        pay[pl.ds(at + 2 * n, 16), :] = tab[...]


def weight_kernel(diag, faces, coarse, w, pw, we):
    put_halves(w.at[pl.ds(0, 128)], diag[...].T)
    for f in range(6):
        put_halves(w.at[pl.ds(128 * (f + 1), 128)], faces[f].T)

    def thirds(a):
        one = a.astype(BF16)
        rest = a - one.astype(F32)
        two = rest.astype(BF16)
        return one, two, (rest - two.astype(F32)).astype(BF16)

    def mul(a, b):
        (a1, a2, a3), (b1, b2, b3) = thirds(a), thirds(b)
        total = jnp.zeros((128, 128), F32)
        for x, y in ((a3, b1), (a1, b3), (a2, b2), (a2, b1), (a1, b2), (a1, b1)):
            total += jnp.dot(x, y, preferred_element_type=F32)
        return total

    power = coarse[...].T
    for level in range(3):
        put_halves(pw.at[pl.ds(128 * level, 128)], power)
        power = mul(power, power)
    t = lax.axis_index("tm")
    we[...] = jnp.zeros_like(we)
    one = (lax.broadcasted_iota(jnp.int32, (128, 128), 0) == lax.broadcasted_iota(jnp.int32, (128, 128), 1)).astype(F32)

    def body(k, current):
        put_halves(we.at[t - 1 - k], current)
        return mul(current, power)

    lax.fori_loop(0, t, body, one)


def window(dst, left, own, right, k, low, n):
    at = sum((COARSEN - 1 - j) * REACH * 8 for j in range(k))
    have = (COARSEN - 1 - k) * REACH * 8
    side = (n - low) * 8
    if side:
        dst[pl.ds(0, side), :] = left[pl.ds(at + have - side, side), :]
        dst[pl.ds(side + n * 8, side), :] = right[pl.ds(at, side), :]
    dst[pl.ds(side, n * 8), :] = own[k]


def first_kernel(fe, tab, init, left, right, w, pw, w1, end, idx_out, iw, s0, s1, fx, y, idx_v, idx, sem):
    n = init.shape[0]
    full = 3 * n
    tail = left.shape[0] - 16
    lane = lax.broadcasted_iota(jnp.int32, (8, 128), 1)

    def table(ref, at):
        return ref[pl.ds(at, 16), :].astype(F32)[0:8]

    low = jnp.where(lane < n, table(left, tail), table(tab, 0))
    high = jnp.where(lane < n, table(right, tail), 0.0)
    for at, offs in ((0, low), (128, high)):
        value = jnp.where(offs != 0.0, lane + at + offs.astype(jnp.int32), full)
        idx_v[:, pl.ds(at, 128)] = value
        idx_out[:, pl.ds(at, 128)] = value
    copy = pltpu.make_async_copy(idx_v, idx, sem)
    copy.start()

    first = (lax.axis_index("tm") == 0).astype(F32)

    def joined(ref):
        return ref[pl.ds(tail - 2 * n, n), :].astype(F32) + ref[pl.ds(tail - n, n), :].astype(F32)

    iw[pl.ds(0, n), :] = joined(left) * first
    iw[pl.ds(n, n), :] = init[...] * first
    iw[pl.ds(2 * n, n), :] = joined(right) * first
    y[...] = jnp.zeros_like(y)
    y[pl.ds(0, full, stride=8), :] = iw[...]

    def fill(c, carry):
        at = c * CHUNK
        s0[pl.ds(at, CHUNK)] = split(y[pl.ds(pl.multiple_of(at * 8, CHUNK * 8), CHUNK * 8), :].reshape(CHUNK, 8, 128))
        return carry

    lax.fori_loop(0, full // CHUNK, fill, 0)
    s0[full] = jnp.zeros((16, 128), BF16)
    s1[full] = jnp.zeros((16, 128), BF16)
    copy.wait()
    bufs = [s0, s1]
    for k in range(COARSEN):
        lo = (k + 1) * REACH
        window(fx, left, fe, right, k, lo, n)
        src, dst = bufs[k % 2], bufs[(k + 1) % 2]

        def emit(base, value, lo=lo, dst=dst, last=k == COARSEN - 1):
            at = pl.multiple_of((base - lo) * 8, CHUNK * 8)
            value = value + fx[pl.ds(at, CHUNK * 8), :].astype(F32).reshape(CHUNK, 8, 128)
            if last:
                w1[pl.ds(base - lo, CHUNK)] = value
            else:
                dst[pl.ds(base, CHUNK)] = split(value)

        apply_phi(src, idx, w, lo, full - lo, emit)
    y[pl.ds(0, n * 8), :] = scan_tiles(w1[...], pw).reshape(n * 8, 128)
    end[...] = y[pl.ds(7, n, stride=8), :]


def second_kernel(idx, own, left, right, ag, w, pw, we, res, res_left, res_right, end, total, start, s0, s1, y, ent):
    n = own.shape[0]
    full = 3 * n
    entering(ag, we, ent, n)
    for j, ref in enumerate((left, own, right)):
        y[pl.ds(j * n * 8, n * 8), :] = pltpu.roll(ref[...], 1, axis=1).reshape(n * 8, 128)
    y[pl.ds(0, full, stride=8), :] = ent[...]

    def scan(c, carry):
        rows = pl.ds(pl.multiple_of(c * SCAN * 8, SCAN * 8), SCAN * 8)
        value = scan_tiles(y[rows, :].reshape(SCAN, 8, 128), pw)
        y[rows, :] = value.reshape(SCAN * 8, 128)
        s0[pl.ds(c * SCAN, SCAN)] = split(value)
        return carry

    lax.fori_loop(0, full // SCAN, scan, 0)
    start[...] = y[pl.ds(REACH * 8, (full - 2 * REACH) * 8), :]
    s0[full] = jnp.zeros((16, 128), BF16)
    s1[full] = jnp.zeros((16, 128), BF16)
    bufs = [s0, s1]
    for k in range(COARSEN):
        lo = (k + 1) * REACH
        src, dst = bufs[k % 2], bufs[(k + 1) % 2]

        def emit(base, value, lo=lo, dst=dst, last=k == COARSEN - 1):
            if last:
                at = base - lo
                total[pl.ds(at, CHUNK)] = value + own[pl.ds(at, CHUNK)]
                before = y[pl.ds(pl.multiple_of(base * 8, CHUNK * 8), CHUNK * 8), :].reshape(CHUNK, 8, 128)
                res[pl.ds(at, CHUNK)] = value - product_rows(before, pw[pl.ds(0, 128), :])
            else:
                dst[pl.ds(base, CHUNK)] = split(value)

        apply_phi(src, idx, w, lo, full - lo, emit)
    side = (COARSEN - 1) * REACH
    res_left[...] = res[pl.ds(0, side)]
    res_right[...] = res[pl.ds(n - side, side)]
    y[pl.ds(0, n * 8), :] = scan_tiles(res[...], pw).reshape(n * 8, 128)
    end[...] = y[pl.ds(7, n, stride=8), :]


def third_kernel(
    idx, own, left, right, ag, total, start, iw, fe, pay_left, pay_right, w, pw, we, out, s0, s1, fx, y, u, ent
):
    n = own.shape[0]
    full = 3 * n
    side = (COARSEN - 1) * REACH
    entering(ag, we, ent, n)
    y[pl.ds((n - side) * 8, side * 8), :] = pltpu.roll(left[...], 1, axis=1).reshape(side * 8, 128)
    y[pl.ds(n * 8, n * 8), :] = pltpu.roll(own[...], 1, axis=1).reshape(n * 8, 128)
    y[pl.ds(2 * n * 8, side * 8), :] = pltpu.roll(right[...], 1, axis=1).reshape(side * 8, 128)
    count = full - 2 * REACH
    y[pl.ds(REACH * 8, count, stride=8), :] = ent[pl.ds(REACH, count), :]
    stride = COARSEN * n

    def scan(c, carry):
        rows = pl.ds(pl.multiple_of((REACH + c * CHUNK) * 8, REACH * 8), CHUNK * 8)
        y[rows, :] = scan_tiles(y[rows, :].reshape(CHUNK, 8, 128), pw).reshape(CHUNK * 8, 128)
        return carry

    lax.fori_loop(0, count // CHUNK, scan, 0)
    corr = y[pl.ds(n * 8, n * 8), :].reshape(n, 8, 128)
    u[...] = product_rows(corr, pw[pl.ds(0, 128), :]) + total[...]

    def put(k):
        def body(e, carry):
            out[pl.ds(k * n + e, 8, stride=stride), :] = u[e]
            return carry

        lax.fori_loop(0, n, body, 0, unroll=8)

    put(COARSEN - 1)
    y[pl.ds(REACH * 8, count * 8), :] = y[pl.ds(REACH * 8, count * 8), :] + start[...]
    y[pl.ds(REACH * 8, count, stride=8), :] = y[pl.ds(REACH * 8, count, stride=8), :] + iw[pl.ds(REACH, count), :]

    def fill(c, carry):
        at = REACH + c * CHUNK
        rows = pl.ds(pl.multiple_of(at * 8, REACH * 8), CHUNK * 8)
        s0[pl.ds(at, CHUNK)] = split(y[rows, :].reshape(CHUNK, 8, 128))
        return carry

    lax.fori_loop(0, count // CHUNK, fill, 0)
    s0[full] = jnp.zeros((16, 128), BF16)
    s1[full] = jnp.zeros((16, 128), BF16)
    bufs = [s0, s1]
    for k in range(COARSEN - 1):
        lo = (k + 2) * REACH
        window(fx, pay_left, fe, pay_right, k, lo, n)
        src, dst = bufs[k % 2], bufs[(k + 1) % 2]

        def emit(base, value, lo=lo, dst=dst, last=k == COARSEN - 2):
            at = pl.multiple_of((base - lo) * 8, CHUNK * 8)
            value = value + fx[pl.ds(at, CHUNK * 8), :].astype(F32).reshape(CHUNK, 8, 128)
            y[pl.ds(pl.multiple_of(base * 8, REACH * 8), CHUNK * 8), :] = value.reshape(CHUNK * 8, 128)
            if not last:
                dst[pl.ds(base, CHUNK)] = split(value)

        apply_phi(src, idx, w, lo, full - lo, emit)
        u[...] = y[pl.ds(n * 8, n * 8), :].reshape(n, 8, 128)
        put(k)


def call(kernel, inputs, outs, scratch, smem=0, flops=0):
    specs = [pl.BlockSpec(memory_space=pltpu.SMEM)] * smem
    specs += [pl.BlockSpec(memory_space=pltpu.VMEM)] * (len(inputs) - smem)
    moved = sum(a.size * a.dtype.itemsize for a in list(inputs) + list(outs))
    return pl.pallas_call(
        kernel,
        out_shape=outs,
        name=kernel.__name__,
        in_specs=specs,
        out_specs=[pl.BlockSpec(memory_space=pltpu.VMEM)] * len(outs),
        scratch_shapes=scratch,
        compiler_params=pltpu.CompilerParams(vmem_limit_bytes=40 * 1024 * 1024),
        cost_estimate=pl.CostEstimate(flops=flops, bytes_accessed=moved, transcendentals=0),
    )(*inputs)


def local(forcing, initial_state, connectivity, pattern, diag_block, face_blocks, coarse_block):
    n, width = initial_state.shape
    steps = forcing.shape[0]
    full = 3 * n
    tm = lax.axis_size("tm")
    space = lax.axis_size("space")
    shape = jax.ShapeDtypeStruct
    tile = shape((n, 8, width), F32)
    ends = shape((n, width), F32)
    step_flops = 2 * 16 * 7 * width * 2 * width
    pay_rows = sum((COARSEN - 1 - k) * REACH * 8 for k in range(COARSEN)) + 2 * n + 16
    pay = shape((pay_rows, width), BF16)
    fe, tab, pay_left, pay_right = call(
        pack_kernel,
        (forcing.reshape(steps * n, width), initial_state, connectivity, pattern),
        (shape((COARSEN, n * 8, width), BF16), shape((16, 128), BF16), pay, pay),
        [pltpu.VMEM((steps * n, width), F32), pltpu.VMEM((128, 128), F32)],
        flops=10**6,
    )
    from_left, from_right = shifted(pay_right, 1), shifted(pay_left, -1)
    w, pw, we = call(
        weight_kernel,
        (diag_block, face_blocks, coarse_block),
        (shape((7 * width, 2 * width), BF16), shape((3 * width, 2 * width), BF16), shape((tm, width, 2 * width), BF16)),
        [],
        flops=10**9,
    )
    state = pltpu.VMEM((full + 1, 16, width), BF16)
    rows = pltpu.VMEM((full * 8, width), F32)
    force = pltpu.VMEM(((full - 2 * REACH) * 8, width), BF16)
    w1, end, idx, iw = call(
        first_kernel,
        (fe, tab, initial_state, from_left, from_right, w, pw),
        (tile, ends, shape((8, 256), jnp.int32), shape((full, width), F32)),
        [state, state, force, rows, pltpu.VMEM((8, 256), jnp.int32), pltpu.SMEM((8, 256), jnp.int32), pltpu.SemaphoreType.DMA],
        flops=step_flops * 7 * n,
    )

    def gathered(value):
        return lax.all_gather(value, ("tm", "space"), axis=0, tiled=True).reshape(tm, space * n, width)

    ag = gathered(end)
    left, right = shifted(w1, 1), shifted(w1, -1)
    side = shape(((COARSEN - 1) * REACH, 8, width), F32)
    entry = pltpu.VMEM((full, width), F32)
    res, res_left, res_right, end, total, start = call(
        second_kernel,
        (idx, w1, left, right, ag, w, pw, we),
        (tile, side, side, ends, tile, shape(((full - 2 * REACH) * 8, width), F32)),
        [state, state, rows, entry],
        smem=1,
        flops=step_flops * 7 * n,
    )
    ag = gathered(end)
    left, right = shifted(res_right, 1), shifted(res_left, -1)
    (out,) = call(
        third_kernel,
        (idx, res, left, right, ag, total, start, iw, fe, from_left, from_right, w, pw, we),
        (shape((steps * n, width), F32),),
        [state, state, force, rows, pltpu.VMEM((n, 8, width), F32), entry],
        smem=1,
        flops=step_flops * 5 * n,
    )
    return out.reshape(steps, n, width)


def solution(mesh):
    return jax.shard_map(
        local,
        mesh=mesh,
        in_specs=(
            P("tm", ("groups", "space"), None),
            P(("groups", "space"), None),
            P("space", None),
            P("space", None),
            P(),
            P(),
            P(),
        ),
        out_specs=P("tm", ("groups", "space"), None),
        check_vma=False,
    )
```

```python
import functools

import jax
import jax.numpy as jnp
from jax import lax
from jax.experimental import pallas as pl
from jax.experimental.pallas import tpu as pltpu
from jax.sharding import PartitionSpec as P

COARSEN = 4
REACH = 16
F32 = jnp.float32
BF16 = jnp.bfloat16
CHUNK = 32


def swapped(value, first):
    count = lax.axis_size("space")
    pairs = []
    for i in range(first, count - 1, 2):
        pairs += [(i, i + 1), (i + 1, i)]
    return lax.ppermute(value, "space", pairs)


def earlier(value):
    count = lax.axis_size("tm")
    if count <= 8:
        return [lax.ppermute(value, "tm", [(i, i + s) for i in range(count - s)]) for s in range(1, count)]
    every = lax.all_gather(value, "tm")
    at = lax.axis_index("tm") - jnp.arange(1, count)
    picked = jnp.where((at >= 0)[:, None, None], jnp.take(every, jnp.maximum(at, 0), axis=0), 0.0)
    return [picked[s] for s in range(count - 1)]


def split(u):
    lead = u.astype(BF16).astype(F32)
    return jnp.concatenate([u, u - lead], axis=1).astype(BF16)


def split_rows(u):
    lead = u.astype(BF16)
    return jnp.concatenate([lead, (u - lead.astype(F32)).astype(BF16)], axis=0)


def product(x, weights):
    m = x.shape[0] // 16
    r = jnp.dot(x, weights, preferred_element_type=F32).reshape(m, 16, 256)
    return r[:, :8, :128] + (r[:, 8:, :128] + r[:, :8, 128:])


def product_rows(x, weights):
    m = x.shape[0] // 2
    r = jnp.dot(x, weights, preferred_element_type=F32)
    return r[:m, :128] + (r[m:, :128] + r[:m, 128:])


def put_halves(ref, w):
    lead = w.astype(BF16)
    ref[:, 0:128] = lead
    ref[:, 128:256] = (w - lead.astype(F32)).astype(BF16)


def power(pk, k):
    return pk[pl.ds(128 * (7 - k), 128), :]


def scan_starts(values, pk):
    y = values
    row = lax.broadcasted_iota(jnp.int32, y.shape, 1)
    for d in (1, 2, 4):
        z = product(split(y).reshape(-1, 128), power(pk, d))
        y = y + jnp.where(row >= d, pltpu.roll(z, d, axis=1), 0.0)
    return jnp.where(row >= 1, pltpu.roll(y, 1, axis=1), 0.0)


def block_end(y, pk, n):
    parts = [y[pl.ds(i, n, stride=8), :] for i in range(8)]
    return product_rows(split_rows(jnp.concatenate(parts, axis=1)), pk[...])


def enter(arrivals, we, pk, y, n):
    value = jnp.concatenate([a[...] for a in arrivals], axis=1)
    entry = product_rows(split_rows(value), we[...])
    y[pl.ds(0, n, stride=8), :] = entry
    rows = split_rows(entry)
    for i in range(1, 8):
        y[pl.ds(i, n, stride=8), :] = product_rows(rows, power(pk, i))
    return y[...].reshape(n, 8, 128)


def apply_phi(src, idx, w, low, high, emit):
    size = (high - low) // 2 if high - low > 64 else high - low

    def body(c, carry):
        base = low + c * size
        cols = [src[pl.ds(base, size)].reshape(size * 16, 128)]
        for f in range(6):
            cols.append(jnp.concatenate([src[idx[f, base + e]] for e in range(size)], axis=0))
        emit(base, size, product(jnp.concatenate(cols, axis=1), w[...]))
        return carry

    lax.fori_loop(0, (high - low) // size, body, 0)


def even_place():
    return lax.rem(lax.axis_index("space"), 2) == 0


def pack_kernel(forcing, init, conn, pattern, fe, tab, pay_even, pay_odd, rows, offs):
    n = init.shape[0]
    stride = COARSEN * n
    step = 256
    for at in range(0, rows.shape[0], step):
        rows[pl.ds(at, step), :] = forcing[pl.ds(at, step), :].astype(F32)

    def body(pair, carry):
        e = pair * 2
        for k in range(COARSEN):
            two = [rows[pl.ds(k * n + e + j, 8, stride=stride), :] for j in range(2)]
            fe[k, pl.ds(pl.multiple_of(e * 8, 16), 16), :] = jnp.concatenate(two, axis=0).astype(BF16)
        return carry

    lax.fori_loop(0, n // 2, body, 0, unroll=4)
    place = lax.broadcasted_iota(jnp.int32, (6, n), 1) + lax.axis_index("space") * n
    value = ((conn[...] - place) * pattern[...]).astype(F32)
    offs[...] = jnp.zeros_like(offs)
    offs[0:6, 0:n] = value
    offs[0:6, n : 2 * n] = value
    tab[...] = offs[...].astype(BF16)
    lead = init[...].astype(BF16)
    rest = (init[...] - lead.astype(F32)).astype(BF16)
    even = even_place()
    at = 0
    for k in range(COARSEN - 1):
        width = (COARSEN - 1 - k) * REACH * 8
        for pay, right in ((pay_even, even), (pay_odd, jnp.logical_not(even))):
            begin = pl.multiple_of(jnp.where(right, n * 8 - width, 0), 128)
            pay[pl.ds(at, width), :] = fe[k, pl.ds(begin, width), :]
        at += width
    for pay in (pay_even, pay_odd):
        pay[pl.ds(at, n), :] = lead
        pay[pl.ds(at + n, n), :] = rest
        pay[pl.ds(at + 2 * n, 16), :] = tab[...]


def weight_kernel(diag, faces, coarse, w, pk, we):
    put_halves(w.at[pl.ds(0, 128)], diag[...].T)
    for f in range(6):
        put_halves(w.at[pl.ds(128 * (f + 1), 128)], faces[f].T)

    def thirds(a):
        one = a.astype(BF16)
        rest = a - one.astype(F32)
        two = rest.astype(BF16)
        return one, two, (rest - two.astype(F32)).astype(BF16)

    def mul(a, b):
        (a1, a2, a3), (b1, b2, b3) = thirds(a), thirds(b)
        total = jnp.zeros((128, 128), F32)
        for x, y in ((a3, b1), (a1, b3), (a2, b2), (a2, b1), (a1, b2), (a1, b1)):
            total += jnp.dot(x, y, preferred_element_type=F32)
        return total

    rows = lax.broadcasted_iota(jnp.int32, (128, 128), 0)
    one = (rows == lax.broadcasted_iota(jnp.int32, (128, 128), 1)).astype(F32)
    powers = [one, coarse[...].T]
    for k in range(2, 9):
        powers.append(mul(powers[k // 2], powers[k - k // 2]))
    for k in range(8):
        put_halves(pk.at[pl.ds(128 * (7 - k), 128)], powers[k])

    def body(k, current):
        put_halves(we.at[pl.ds(pl.multiple_of(k * 128, 128), 128)], current)
        return mul(current, powers[8])

    lax.fori_loop(0, we.shape[0] // 128, body, one)


def window(dst, even_ref, odd_ref, own, k, low, n):
    at = sum((COARSEN - 1 - j) * REACH * 8 for j in range(k))
    have = (COARSEN - 1 - k) * REACH * 8
    side = (n - low) * 8
    even = even_place()
    if side:
        for ref, right in ((even_ref, even), (odd_ref, jnp.logical_not(even))):
            begin = pl.multiple_of(jnp.where(right, at, at + have - side), 128)
            to = pl.multiple_of(jnp.where(right, side + n * 8, 0), 128)
            dst[pl.ds(to, side), :] = ref[pl.ds(begin, side), :]
    dst[pl.ds(side, n * 8), :] = own[k]


def first_kernel(
    fe, tab, init, got_even, got_odd, w, pk, w1, end, idx_out, s0, s1, fx, y, i16, square, idx_v, idx, sem
):
    n = init.shape[0]
    full = 3 * n
    tail = got_even.shape[0] - 16
    even = even_place()
    lane = lax.broadcasted_iota(jnp.int32, (8, 128), 1)

    def table(ref, at):
        return ref[pl.ds(at, 16), :].astype(F32)[0:8]

    from_even, from_odd = table(got_even, tail), table(got_odd, tail)
    low = jnp.where(lane < n, jnp.where(even, from_odd, from_even), table(tab, 0))
    high = jnp.where(lane < n, jnp.where(even, from_even, from_odd), 0.0)
    columns = []
    for at, offs in ((0, low), (128, high)):
        value = jnp.where(offs != 0.0, lane + at + offs.astype(jnp.int32), full)
        idx_v[:, pl.ds(at, 128)] = value
        idx_out[:, pl.ds(at, 128)] = value
        square[...] = jnp.zeros_like(square)
        square[0:8, :] = value.astype(F32)
        columns.append(square[...].T)
    copy = pltpu.make_async_copy(idx_v, idx, sem)
    copy.start()

    i16[pl.ds(full, i16.shape[0] - full), :] = jnp.zeros((i16.shape[0] - full, 256), BF16)
    lead = init[...].astype(BF16)
    i16[pl.ds(n, n), 0:128] = lead
    i16[pl.ds(n, n), 128:256] = (init[...] - lead.astype(F32)).astype(BF16)
    for ref, right in ((got_even, even), (got_odd, jnp.logical_not(even))):
        to = pl.multiple_of(jnp.where(right, 2 * n, 0), n)
        i16[pl.ds(to, n), 0:128] = ref[pl.ds(tail - 2 * n, n), :]
        i16[pl.ds(to, n), 128:256] = ref[pl.ds(tail - n, n), :]
    count = full - 2 * REACH
    place = jnp.concatenate([columns[0][REACH:128], columns[1][0 : full - REACH - 128]], axis=0)
    spot = lax.broadcasted_iota(jnp.int32, (count, 256), 1).astype(F32)
    cols = [i16[pl.ds(REACH, count), :]]
    for f in range(6):
        hot = (spot == place[:, f : f + 1]).astype(F32).astype(BF16)
        cols.append(jnp.dot(hot, i16[...], preferred_element_type=F32).astype(BF16))
    leads = jnp.concatenate([c[:, 0:128] for c in cols], axis=1)
    rests = jnp.concatenate([c[:, 128:256] for c in cols], axis=1)
    pushed = product_rows(jnp.concatenate([leads, rests], axis=0), w[...])
    window(fx, got_even, got_odd, fe, 0, REACH, n)
    y[pl.ds(0, count * 8), :] = fx[pl.ds(0, count * 8), :].astype(F32)
    first = (lax.axis_index("tm") == 0).astype(F32)
    y[pl.ds(0, count, stride=8), :] = y[pl.ds(0, count, stride=8), :] + pushed * first

    def fill(c, carry):
        rows = pl.ds(pl.multiple_of(c * CHUNK * 8, CHUNK * 8), CHUNK * 8)
        s1[pl.ds(REACH + c * CHUNK, CHUNK)] = split(y[rows, :].reshape(CHUNK, 8, 128))
        return carry

    lax.fori_loop(0, count // CHUNK, fill, 0)
    s0[full] = jnp.zeros((16, 128), BF16)
    s1[full] = jnp.zeros((16, 128), BF16)
    copy.wait()
    bufs = [s0, s1]
    for k in range(1, COARSEN):
        lo = (k + 1) * REACH
        window(fx, got_even, got_odd, fe, k, lo, n)
        src, dst = bufs[k % 2], bufs[(k + 1) % 2]

        def emit(base, size, value, lo=lo, dst=dst, last=k == COARSEN - 1):
            at = pl.multiple_of((base - lo) * 8, 128)
            value = value + fx[pl.ds(at, size * 8), :].astype(F32).reshape(size, 8, 128)
            if last:
                w1[pl.ds(base - lo, size)] = value
                y[pl.ds(at, size * 8), :] = value.reshape(size * 8, 128)
            else:
                dst[pl.ds(base, size)] = split(value)

        apply_phi(src, idx, w, lo, full - lo, emit)
    end[...] = block_end(y, pk, n)


def scan_kernel(values, pk, starts):
    starts[...] = scan_starts(values[...], pk)


def enter_first_kernel(*refs):
    *arrivals, starts, we, pk, state, y = refs
    n = starts.shape[0]
    state[...] = split(enter(arrivals, we, pk, y, n) + starts[...])


def enter_second_kernel(*refs):
    *arrivals, starts, before, init, we, pk, state, pay_even, pay_odd, corr, y = refs
    n = starts.shape[0]
    value = enter(arrivals, we, pk, y, n) + starts[...]
    corr[...] = value
    old = before[...].astype(F32)
    y[...] = (value + (old[:, 0:8] + old[:, 8:16])).reshape(n * 8, 128)
    first = (lax.axis_index("tm") == 0).astype(F32)
    y[pl.ds(0, n, stride=8), :] = y[pl.ds(0, n, stride=8), :] + init[...] * first
    state[...] = split(y[...].reshape(n, 8, 128))
    side = (COARSEN - 1) * REACH
    even = even_place()
    pay_even[...] = state[pl.ds(jnp.where(even, n - side, 0), side)]
    pay_odd[...] = state[pl.ds(jnp.where(even, 0, n - side), side)]


def point_kernel(corr, total, pk, points):
    points[...] = product(split(corr[...]).reshape(-1, 128), power(pk, 1)) + total[...]


def gather_blocks(dst, own, got_even, got_odd, n):
    side = got_even.shape[0]
    even = even_place()
    dst[pl.ds(n, n)] = own[...]
    for ref, right in ((got_even, even), (got_odd, jnp.logical_not(even))):
        dst[pl.ds(jnp.where(right, 2 * n, n - side), side)] = ref[...]
    dst[3 * n] = jnp.zeros((16, 128), BF16)


def second_kernel(idx, own, got_even, got_odd, w1, w, pk, res, end, total, s0, s1, y):
    n = own.shape[0]
    full = 3 * n
    gather_blocks(s0, own, got_even, got_odd, n)
    s1[full] = jnp.zeros((16, 128), BF16)
    bufs = [s0, s1]
    for k in range(COARSEN):
        lo = (k + 1) * REACH
        src, dst = bufs[k % 2], bufs[(k + 1) % 2]

        def emit(base, size, value, lo=lo, dst=dst, last=k == COARSEN - 1):
            if last:
                at = base - lo
                total[pl.ds(at, size)] = value + w1[pl.ds(at, size)]
                value = value - product(own[pl.ds(at, size)].reshape(size * 16, 128), power(pk, 1))
                res[pl.ds(at, size)] = value
                y[pl.ds(pl.multiple_of(at * 8, 128), size * 8), :] = value.reshape(size * 8, 128)
            else:
                dst[pl.ds(base, size)] = split(value)

        apply_phi(src, idx, w, lo, full - lo, emit)
    end[...] = block_end(y, pk, n)


def third_kernel(idx, own, got_even, got_odd, points, fe, pay_even, pay_odd, w, out, s0, s1, fx, u):
    n = own.shape[0]
    full = 3 * n
    stride = COARSEN * n
    gather_blocks(s0, own, got_even, got_odd, n)
    s1[full] = jnp.zeros((16, 128), BF16)

    def put(k, ref, at):
        def body(e, carry):
            out[pl.ds(k * n + e, 8, stride=stride), :] = ref[at + e]
            return carry

        lax.fori_loop(0, n, body, 0, unroll=8)

    put(COARSEN - 1, points, 0)
    bufs = [s0, s1]
    for k in range(COARSEN - 1):
        lo = (k + 2) * REACH
        window(fx, pay_even, pay_odd, fe, k, lo, n)
        src, dst = bufs[k % 2], bufs[(k + 1) % 2]

        def emit(base, size, value, lo=lo, dst=dst, last=k == COARSEN - 2):
            at = pl.multiple_of((base - lo) * 8, 128)
            value = value + fx[pl.ds(at, size * 8), :].astype(F32).reshape(size, 8, 128)
            u[pl.ds(base, size)] = value
            if not last:
                dst[pl.ds(base, size)] = split(value)

        apply_phi(src, idx, w, lo, full - lo, emit)
        put(k, u, n)


def call(kernel, inputs, outs, scratch, smem=0, flops=10**7):
    specs = [pl.BlockSpec(memory_space=pltpu.SMEM)] * smem
    specs += [pl.BlockSpec(memory_space=pltpu.VMEM)] * (len(inputs) - smem)
    moved = sum(a.size * a.dtype.itemsize for a in list(inputs) + list(outs))
    return pl.pallas_call(
        kernel,
        out_shape=outs,
        name=kernel.__name__,
        in_specs=specs,
        out_specs=[pl.BlockSpec(memory_space=pltpu.VMEM)] * len(outs),
        scratch_shapes=scratch,
        compiler_params=pltpu.CompilerParams(vmem_limit_bytes=32 * 1024 * 1024),
        cost_estimate=pl.CostEstimate(flops=flops, bytes_accessed=moved, transcendentals=0),
    )(*inputs)


def local(forcing, initial_state, connectivity, pattern, diag_block, face_blocks, coarse_block):
    n, width = initial_state.shape
    steps = forcing.shape[0]
    full = 3 * n
    tm = lax.axis_size("tm")
    shape = jax.ShapeDtypeStruct
    tiles = shape((n, 8, width), F32)
    state = shape((n, 16, width), BF16)
    ends = shape((n, width), F32)
    step_flops = 2 * 16 * 7 * width * 2 * width
    pay_rows = sum((COARSEN - 1 - k) * REACH * 8 for k in range(COARSEN)) + 2 * n + 16
    pay = shape((pay_rows, width), BF16)
    fe, tab, pay_even, pay_odd = call(
        pack_kernel,
        (forcing.reshape(steps * n, width), initial_state, connectivity.T, pattern.T),
        (shape((COARSEN, n * 8, width), BF16), shape((16, 128), BF16), pay, pay),
        [pltpu.VMEM((steps * n, width), F32), pltpu.VMEM((16, 128), F32)],
    )
    pay_odd, pay_even = swapped(pay_odd, 1), swapped(pay_even, 0)
    w, pk, we = call(
        weight_kernel,
        (diag_block, face_blocks, coarse_block),
        (
            shape((7 * width, 2 * width), BF16),
            shape((8 * width, 2 * width), BF16),
            shape(((tm - 1) * width, 2 * width), BF16),
        ),
        [],
        flops=10**9,
    )
    spaces = pltpu.VMEM((full + 1, 16, width), BF16)
    force = pltpu.VMEM(((full - 2 * REACH) * 8, width), BF16)
    rows = pltpu.VMEM((n * 8, width), F32)
    w1, end, idx = call(
        first_kernel,
        (fe, tab, initial_state, pay_even, pay_odd, w, pk),
        (tiles, ends, shape((8, 256), jnp.int32)),
        [
            spaces,
            spaces,
            force,
            pltpu.VMEM(((full - 2 * REACH) * 8, width), F32),
            pltpu.VMEM((256, 256), BF16),
            pltpu.VMEM((128, 128), F32),
            pltpu.VMEM((8, 256), jnp.int32),
            pltpu.SMEM((8, 256), jnp.int32),
            pltpu.SemaphoreType.DMA,
        ],
        flops=step_flops * 5 * n,
    )
    arrivals = earlier(end)
    (starts,) = call(scan_kernel, (w1, pk), (tiles,), [])
    (coarse,) = call(enter_first_kernel, (*arrivals, starts, we, pk), (state,), [rows])
    got_odd, got_even = swapped(coarse, 1), swapped(coarse, 0)
    res, end, total = call(
        second_kernel,
        (idx, coarse, got_even, got_odd, w1, w, pk),
        (tiles, ends, tiles),
        [spaces, spaces, rows],
        smem=1,
        flops=step_flops * 7 * n,
    )
    arrivals = earlier(end)
    (starts,) = call(scan_kernel, (res, pk), (tiles,), [])
    side = shape(((COARSEN - 1) * REACH, 16, width), BF16)
    coarse, end_even, end_odd, corr = call(
        enter_second_kernel,
        (*arrivals, starts, coarse, initial_state, we, pk),
        (state, side, side, tiles),
        [rows],
    )
    got_odd, got_even = swapped(end_odd, 1), swapped(end_even, 0)
    (points,) = call(point_kernel, (corr, total, pk), (tiles,), [])
    (out,) = call(
        third_kernel,
        (idx, coarse, got_even, got_odd, points, fe, pay_even, pay_odd, w),
        (shape((steps * n, width), F32),),
        [spaces, spaces, force, pltpu.VMEM((full, 8, width), F32)],
        smem=1,
        flops=step_flops * 5 * n,
    )
    return out.reshape(steps, n, width)


def solution(mesh):
    return jax.shard_map(
        local,
        mesh=mesh,
        in_specs=(
            P("tm", ("groups", "space"), None),
            P(("groups", "space"), None),
            P("space", None),
            P("space", None),
            P(),
            P(),
            P(),
        ),
        out_specs=P("tm", ("groups", "space"), None),
        check_vma=False,
    )
```

```python
import functools

import jax
import jax.numpy as jnp
from jax import lax
from jax.experimental import pallas as pl
from jax.experimental.pallas import tpu as pltpu
from jax.sharding import PartitionSpec as P

COARSEN = 4
REACH = 16
F32 = jnp.float32
BF16 = jnp.bfloat16
CHUNK = 32


def swapped(value, first):
    count = lax.axis_size("space")
    pairs = []
    for i in range(first, count - 1, 2):
        pairs += [(i, i + 1), (i + 1, i)]
    return lax.ppermute(value, "space", pairs)


def earlier(value):
    count = lax.axis_size("tm")
    if count <= 8:
        return [lax.ppermute(value, "tm", [(i, i + s) for i in range(count - s)]) for s in range(1, count)]
    every = lax.all_gather(value, "tm")
    at = lax.axis_index("tm") - jnp.arange(1, count)
    picked = jnp.where((at >= 0)[:, None, None], jnp.take(every, jnp.maximum(at, 0), axis=0), 0.0)
    return [picked[s] for s in range(count - 1)]


def split(u):
    lead = u.astype(BF16).astype(F32)
    return jnp.concatenate([u, u - lead], axis=1).astype(BF16)


def split_rows(u):
    lead = u.astype(BF16)
    return jnp.concatenate([lead, (u - lead.astype(F32)).astype(BF16)], axis=0)


def product(x, weights):
    m = x.shape[0] // 16
    r = jnp.dot(x, weights, preferred_element_type=F32).reshape(m, 16, 256)
    return r[:, :8, :128] + (r[:, 8:, :128] + r[:, :8, 128:])


def product_rows(x, weights):
    m = x.shape[0] // 2
    r = jnp.dot(x, weights, preferred_element_type=F32)
    return r[:m, :128] + (r[m:, :128] + r[:m, 128:])


def put_halves(ref, w):
    lead = w.astype(BF16)
    ref[:, 0:128] = lead
    ref[:, 128:256] = (w - lead.astype(F32)).astype(BF16)


def power(pk, k):
    return pk[pl.ds(128 * (7 - k), 128), :]


def scan_starts(values, pk):
    y = values
    row = lax.broadcasted_iota(jnp.int32, y.shape, 1)
    for d in (1, 2, 4):
        z = product(split(y).reshape(-1, 128), power(pk, d))
        y = y + jnp.where(row >= d, pltpu.roll(z, d, axis=1), 0.0)
    return jnp.where(row >= 1, pltpu.roll(y, 1, axis=1), 0.0)


def block_end(y, pk, n):
    parts = [y[pl.ds(i, n, stride=8), :] for i in range(8)]
    return product_rows(split_rows(jnp.concatenate(parts, axis=1)), pk[...])


def enter(arrivals, we, pk, y, n):
    value = jnp.concatenate([a[...] for a in arrivals], axis=1)
    entry = product_rows(split_rows(value), we[...])
    y[pl.ds(0, n, stride=8), :] = entry
    rows = split_rows(entry)
    for i in range(1, 8):
        y[pl.ds(i, n, stride=8), :] = product_rows(rows, power(pk, i))
    return y[...].reshape(n, 8, 128)


def apply_phi(src, idx, w, base, size):
    cols = [src[pl.ds(base, size)].reshape(size * 16, 128)]
    for f in range(6):
        cols.append(jnp.concatenate([src[idx[f, base + e]] for e in range(size)], axis=0))
    return product(jnp.concatenate(cols, axis=1), w[...])


def even_place():
    return lax.rem(lax.axis_index("space"), 2) == 0


def mirrored(low, size, full):
    return jnp.where(even_place(), full - low - size, low)


def pack_kernel(
    forcing, init, conn, pattern, fe, tab, pay_even, pay_odd, landed, rows, init_v, conn_v, pattern_v, offs, sems
):
    n = init_v.shape[0]
    copies = [pltpu.make_async_copy(forcing.at[:, k], landed.at[k], sems.at[k]) for k in range(COARSEN)]
    small = ((conn, conn_v), (pattern, pattern_v), (init, init_v))
    copies += [pltpu.make_async_copy(src, dst, sems.at[COARSEN + i]) for i, (src, dst) in enumerate(small)]
    for copy in copies:
        copy.start()
    for copy in copies[COARSEN:]:
        copy.wait()
    place = lax.broadcasted_iota(jnp.int32, (6, n), 1) + lax.axis_index("space") * n
    value = ((conn_v[...] - place) * pattern_v[...]).astype(F32)
    offs[...] = jnp.zeros_like(offs)
    offs[0:6, 0:n] = value
    offs[0:6, n : 2 * n] = value
    tab[...] = offs[...].astype(BF16)
    lead = init_v[...].astype(BF16)
    rest = (init_v[...] - lead.astype(F32)).astype(BF16)
    even = even_place()
    at = sum((COARSEN - 1 - k) * REACH * 8 for k in range(COARSEN))
    for pay in (pay_even, pay_odd):
        pay[pl.ds(at, n), :] = lead
        pay[pl.ds(at + n, n), :] = rest
        pay[pl.ds(at + 2 * n, 16), :] = tab[...]
    at = 0
    for k in range(COARSEN):
        copies[k].wait()
        for i in range(8):
            rows[pl.ds(i * n, n), :] = landed[k, i].astype(F32)

        def body(pair, carry, k=k):
            e = pair * 2
            two = [rows[pl.ds(e + j, 8, stride=n), :] for j in range(2)]
            fe[k, pl.ds(pl.multiple_of(e * 8, 16), 16), :] = jnp.concatenate(two, axis=0).astype(BF16)
            return carry

        lax.fori_loop(0, n // 2, body, 0, unroll=8)
        width = (COARSEN - 1 - k) * REACH * 8
        if width:
            for pay, right in ((pay_even, even), (pay_odd, jnp.logical_not(even))):
                begin = pl.multiple_of(jnp.where(right, n * 8 - width, 0), 128)
                pay[pl.ds(at, width), :] = fe[k, pl.ds(begin, width), :]
        at += width


def weight_kernel(diag, faces, coarse, w, pk, we):
    put_halves(w.at[pl.ds(0, 128)], diag[...].T)
    for f in range(6):
        put_halves(w.at[pl.ds(128 * (f + 1), 128)], faces[f].T)

    def thirds(a):
        one = a.astype(BF16)
        rest = a - one.astype(F32)
        two = rest.astype(BF16)
        return one, two, (rest - two.astype(F32)).astype(BF16)

    def mul(a, b):
        (a1, a2, a3), (b1, b2, b3) = thirds(a), thirds(b)
        total = jnp.zeros((128, 128), F32)
        for x, y in ((a3, b1), (a1, b3), (a2, b2), (a2, b1), (a1, b2), (a1, b1)):
            total += jnp.dot(x, y, preferred_element_type=F32)
        return total

    rows = lax.broadcasted_iota(jnp.int32, (128, 128), 0)
    one = (rows == lax.broadcasted_iota(jnp.int32, (128, 128), 1)).astype(F32)
    powers = [one, coarse[...].T]
    for k in range(2, 9):
        powers.append(mul(powers[k // 2], powers[k - k // 2]))
    for k in range(8):
        put_halves(pk.at[pl.ds(128 * (7 - k), 128)], powers[k])

    def body(k, current):
        put_halves(we.at[pl.ds(pl.multiple_of(k * 128, 128), 128)], current)
        return mul(current, powers[8])

    lax.fori_loop(0, we.shape[0] // 128, body, one)


def put_force(dst, own, got, right, k, n):
    at = sum((COARSEN - 1 - j) * REACH * 8 for j in range(k))
    width = (COARSEN - 1 - k) * REACH * 8
    dst[pl.ds(n * 8, n * 8), :] = own[k]
    if width:
        to = pl.multiple_of(jnp.where(right, 2 * n * 8, n * 8 - width), 128)
        dst[pl.ds(to, width), :] = got[pl.ds(at, width), :]


def force_at(src, base, size):
    at = pl.multiple_of(base * 8, 128)
    return src[pl.ds(at, size * 8), :].astype(F32).reshape(size, 8, 128)


def put_tables(tab, got_even, got_odd, idx_v, columns, square, full, n):
    even = even_place()
    lane = lax.broadcasted_iota(jnp.int32, (8, 128), 1)

    def table(ref):
        return 0.0 if ref is None else ref[pl.ds(ref.shape[0] - 16, 16), :].astype(F32)[0:8]

    from_even, from_odd = table(got_even), table(got_odd)
    low = jnp.where(lane < n, jnp.where(even, from_odd, from_even), table(tab))
    high = jnp.where(lane < n, jnp.where(even, from_even, from_odd), 0.0)
    for at, offs in ((0, low), (128, high)):
        value = jnp.where(offs != 0.0, lane + at + offs.astype(jnp.int32), full)
        idx_v[:, pl.ds(at, 128)] = value
        square[...] = jnp.zeros_like(square)
        square[0:8, :] = value.astype(F32)
        columns[pl.ds(at, 128), :] = square[...].T


def push_init(init, got_even, got_odd, w, columns, i16, base, count, n):
    even = even_place()
    i16[...] = jnp.zeros_like(i16)
    lead = init[...].astype(BF16)
    i16[pl.ds(n, n), 0:128] = lead
    i16[pl.ds(n, n), 128:256] = (init[...] - lead.astype(F32)).astype(BF16)
    for ref, right in ((got_even, even), (got_odd, jnp.logical_not(even))):
        if ref is not None:
            at = ref.shape[0] - 16
            to = pl.multiple_of(jnp.where(right, 2 * n, 0), n)
            i16[pl.ds(to, n), 0:128] = ref[pl.ds(at - 2 * n, n), :]
            i16[pl.ds(to, n), 128:256] = ref[pl.ds(at - n, n), :]
    rows = pl.ds(pl.multiple_of(base, REACH), count)
    place = columns[rows, :]
    spot = lax.broadcasted_iota(jnp.int32, (count, 256), 1).astype(F32)
    cols = [i16[rows, :]]
    for f in range(6):
        hot = (spot == place[:, f : f + 1]).astype(F32).astype(BF16)
        cols.append(jnp.dot(hot, i16[...], preferred_element_type=F32).astype(BF16))
    leads = jnp.concatenate([c[:, 0:128] for c in cols], axis=1)
    rests = jnp.concatenate([c[:, 128:256] for c in cols], axis=1)
    pushed = product_rows(jnp.concatenate([leads, rests], axis=0), w[...])
    return pushed * (lax.axis_index("tm") == 0).astype(F32)


STRIPS = (5 * REACH, 4 * REACH, 3 * REACH)
STRIP = 2 * REACH


def put_strips(strips, states, full):
    for strip, state, low in zip(strips, states, STRIPS):
        strip[...] = state[pl.ds(mirrored(low, STRIP, full), STRIP)]


def get_strips(strips, states, full):
    for strip, state, low in zip(strips, states, STRIPS):
        state[pl.ds(mirrored(low, STRIP, full), STRIP)] = strip[...]
        state[full] = jnp.zeros((16, 128), BF16)


def first_early_kernel(
    fe, tab, init, got, w, strip1, strip2, strip3, s1, s2, s3, force, y, i16, columns, square, idx_v, idx, sem
):
    n = init.shape[0]
    full = 3 * n
    even = even_place()
    put_tables(tab, got, None, idx_v, columns, square, full, n)
    copy = pltpu.make_async_copy(idx_v, idx, sem)
    copy.start()
    count = 6 * REACH
    base = mirrored(REACH, count, full)
    pushed = push_init(init, got, None, w, columns, i16, base, count, n)
    put_force(force, fe, got, even, 0, n)
    y[pl.ds(0, count * 8), :] = force[pl.ds(pl.multiple_of(base * 8, 128), count * 8), :].astype(F32)
    y[pl.ds(0, count, stride=8), :] = y[pl.ds(0, count, stride=8), :] + pushed
    s1[pl.ds(base, count)] = split(y[pl.ds(0, count * 8), :].reshape(count, 8, 128))
    for state in (s1, s2, s3):
        state[full] = jnp.zeros((16, 128), BF16)
    copy.wait()
    for k, src, dst in ((1, s1, s2), (2, s2, s3)):
        put_force(force, fe, got, even, k, n)
        size = (6 - 2 * k) * REACH
        base = mirrored((k + 1) * REACH, size, full)
        dst[pl.ds(base, size)] = split(apply_phi(src, idx, w, base, size) + force_at(force, base, size))
    put_strips((strip1, strip2, strip3), (s1, s2, s3), full)


def first_late_kernel(
    fe, tab, init, got_even, got_odd, strip1, strip2, strip3, w, pk, w1, end, idx_out,
    s1, s2, s3, force, y, i16, columns, square, idx, sem
):
    n = init.shape[0]
    full = 3 * n
    odd = jnp.logical_not(even_place())
    put_tables(tab, got_even, got_odd, idx_out, columns, square, full, n)
    copy = pltpu.make_async_copy(idx_out, idx, sem)
    copy.start()
    count = 4 * REACH
    base = mirrored(7 * REACH, count, full)
    pushed = push_init(init, got_even, got_odd, w, columns, i16, base, count, n)
    put_force(force, fe, got_odd, odd, 0, n)
    y[...] = force[pl.ds(pl.multiple_of(base * 8, 128), count * 8), :].astype(F32)
    y[pl.ds(0, count, stride=8), :] = y[pl.ds(0, count, stride=8), :] + pushed
    s1[pl.ds(base, count)] = split(y[...].reshape(count, 8, 128))
    get_strips((strip1, strip2, strip3), (s1, s2, s3), full)
    copy.wait()
    for k, src, dst in ((1, s1, s2), (2, s2, s3), (3, s3, None)):
        put_force(force, fe, got_odd, odd, k, n)
        base = mirrored((7 - k) * REACH, count, full)
        value = apply_phi(src, idx, w, base, count) + force_at(force, base, count)
        if dst is None:
            w1[...] = value
            y[...] = value.reshape(n * 8, 128)
        else:
            dst[pl.ds(base, count)] = split(value)
    end[...] = block_end(y, pk, n)


def scan_kernel(values, pk, starts):
    starts[...] = scan_starts(values[...], pk)


def enter_first_kernel(*refs):
    *arrivals, starts, we, pk, state, y = refs
    n = starts.shape[0]
    state[...] = split(enter(arrivals, we, pk, y, n) + starts[...])


def enter_second_kernel(*refs):
    *arrivals, starts, before, init, we, pk, state, pay_even, pay_odd, corr, y = refs
    n = starts.shape[0]
    value = enter(arrivals, we, pk, y, n) + starts[...]
    corr[...] = value
    old = before[...].astype(F32)
    y[...] = (value + (old[:, 0:8] + old[:, 8:16])).reshape(n * 8, 128)
    first = (lax.axis_index("tm") == 0).astype(F32)
    y[pl.ds(0, n, stride=8), :] = y[pl.ds(0, n, stride=8), :] + init[...] * first
    state[...] = split(y[...].reshape(n, 8, 128))
    side = (COARSEN - 1) * REACH
    even = even_place()
    pay_even[...] = state[pl.ds(jnp.where(even, n - side, 0), side)]
    pay_odd[...] = state[pl.ds(jnp.where(even, 0, n - side), side)]


def put_block(dst, own, got, right, n):
    side = got.shape[0]
    dst[pl.ds(n, n)] = own[...]
    dst[pl.ds(jnp.where(right, 2 * n, n - side), side)] = got[...]
    dst[3 * n] = jnp.zeros((16, 128), BF16)


def second_early_kernel(idx, own, got, w, strip1, strip2, strip3, s0, s1, s2, s3):
    n = own.shape[0]
    full = 3 * n
    put_block(s0, own, got, even_place(), n)
    for state in (s1, s2, s3):
        state[full] = jnp.zeros((16, 128), BF16)
    for k, src, dst in ((1, s0, s1), (2, s1, s2), (3, s2, s3)):
        size = (8 - 2 * k) * REACH
        base = mirrored(k * REACH, size, full)
        dst[pl.ds(base, size)] = split(apply_phi(src, idx, w, base, size))
    put_strips((strip1, strip2, strip3), (s1, s2, s3), full)


def second_late_kernel(idx, own, got, strip1, strip2, strip3, w1, w, pk, res, end, total, s0, s1, s2, s3, y):
    n = own.shape[0]
    full = 3 * n
    put_block(s0, own, got, jnp.logical_not(even_place()), n)
    get_strips((strip1, strip2, strip3), (s1, s2, s3), full)
    count = 4 * REACH
    for k, src, dst in ((1, s0, s1), (2, s1, s2), (3, s2, s3)):
        base = mirrored((8 - k) * REACH, count, full)
        dst[pl.ds(base, count)] = split(apply_phi(src, idx, w, base, count))
    value = apply_phi(s3, idx, w, n, n)
    total[...] = value + w1[...]
    value = value - product(own[...].reshape(n * 16, 128), power(pk, 1))
    res[...] = value
    y[...] = value.reshape(n * 8, 128)
    end[...] = block_end(y, pk, n)


def write_out(out, k, value, begin, flip, sems):
    size = value.shape[0]
    for e in range(size):
        flip[pl.ds(e, 8, stride=size), :] = value[e]
    rows = pl.ds(pl.multiple_of(begin, REACH), size)
    copies = [
        pltpu.make_async_copy(flip.at[pl.ds(i * size, size)], out.at[i * COARSEN + k, rows], sems.at[k, i])
        for i in range(8)
    ]
    for copy in copies:
        copy.start()
    return copies


def third_early_kernel(
    idx, own, got, corr, total, fe, pay, w, pk, out, strip1, strip2, s0, s1, s2, force, flip0, flip1, flip2, flip3, sems
):
    n = own.shape[0]
    full = 3 * n
    even = even_place()
    points = product(split(corr[...]).reshape(-1, 128), power(pk, 1)) + total[...]
    copies = write_out(out, COARSEN - 1, points, 0, flip3, sems)
    put_block(s0, own, got, even, n)
    for state in (s1, s2):
        state[full] = jnp.zeros((16, 128), BF16)
    for k, src, dst, flip in ((0, s0, s1, flip0), (1, s1, s2, flip1), (2, s2, None, flip2)):
        put_force(force, fe, pay, even, k, n)
        size = (5 - 2 * k) * REACH
        base = mirrored((2 + k) * REACH, size, full)
        value = apply_phi(src, idx, w, base, size) + force_at(force, base, size)
        if dst is not None:
            dst[pl.ds(base, size)] = split(value)
        mine = (3 - k) * REACH
        skip = size - mine
        kept = jnp.where(even, value[:mine], value[skip:])
        copies += write_out(out, k, kept, jnp.where(even, n - mine, 0), flip, sems)
    put_strips((strip1, strip2), (s1, s2), full)
    for copy in copies:
        copy.wait()


def third_late_kernel(
    idx, own, got, strip1, strip2, fe, pay, w, partial, out, s0, s1, s2, force, flip0, flip1, flip2, sems
):
    n = own.shape[0]
    full = 3 * n
    even = even_place()
    odd = jnp.logical_not(even)
    put_block(s0, own, got, odd, n)
    get_strips((strip1, strip2), (s1, s2), full)
    copies = []
    size = 3 * REACH
    for k, src, dst, flip in ((0, s0, s1, flip0), (1, s1, s2, flip1), (2, s2, None, flip2)):
        put_force(force, fe, pay, odd, k, n)
        base = mirrored((7 - k) * REACH, size, full)
        value = apply_phi(src, idx, w, base, size) + force_at(force, base, size)
        if dst is not None:
            dst[pl.ds(base, size)] = split(value)
        mine = (k + 1) * REACH
        kept = jnp.where(even, value[size - mine :], value[:mine])
        copies += write_out(out, k, kept, jnp.where(even, 0, n - mine), flip, sems)
    for copy in copies:
        copy.wait()


def call(kernel, inputs, outs, scratch, spaces="", out_spaces="", aliases=None, flops=10**7, room=32):
    kinds = {"s": pltpu.SMEM, "h": pltpu.HBM, "v": pltpu.VMEM}

    def specs(arrays, letters):
        letters = letters.ljust(len(arrays), "v")
        return [pl.BlockSpec(memory_space=kinds[letter]) for letter in letters]

    moved = sum(a.size * a.dtype.itemsize for a in list(inputs) + list(outs))
    return pl.pallas_call(
        kernel,
        out_shape=outs,
        name=kernel.__name__,
        in_specs=specs(inputs, spaces),
        out_specs=specs(outs, out_spaces),
        scratch_shapes=scratch,
        input_output_aliases=aliases or {},
        compiler_params=pltpu.CompilerParams(vmem_limit_bytes=room * 1024 * 1024),
        cost_estimate=pl.CostEstimate(flops=flops, bytes_accessed=moved, transcendentals=0),
    )(*inputs)


def local(forcing, initial_state, connectivity, pattern, diag_block, face_blocks, coarse_block):
    n, width = initial_state.shape
    steps = forcing.shape[0]
    full = 3 * n
    tm = lax.axis_size("tm")
    shape = jax.ShapeDtypeStruct
    vmem = pltpu.VMEM
    dma = pltpu.SemaphoreType.DMA
    tiles = shape((n, 8, width), F32)
    state = shape((n, 16, width), BF16)
    ends = shape((n, width), F32)
    step_flops = 2 * 16 * 7 * width * 2 * width
    pay_rows = sum((COARSEN - 1 - k) * REACH * 8 for k in range(COARSEN)) + 2 * n + 16
    pay = shape((pay_rows, width), BF16)
    fe, tab, pay_even, pay_odd = call(
        pack_kernel,
        (forcing.reshape(steps // COARSEN, COARSEN, n, width), initial_state, connectivity.T, pattern.T),
        (shape((COARSEN, n * 8, width), BF16), shape((16, 128), BF16), pay, pay),
        [
            vmem((COARSEN, 8, n, width), BF16),
            vmem((8 * n, width), F32),
            vmem((n, width), F32),
            vmem((6, n), jnp.int32),
            vmem((6, n), jnp.int32),
            vmem((16, 128), F32),
            dma((COARSEN + 3,)),
        ],
        spaces="hhhh",
        room=62,
    )
    pay_odd, pay_even = swapped(pay_odd, 1), swapped(pay_even, 0)
    w, pk, we = call(
        weight_kernel,
        (diag_block, face_blocks, coarse_block),
        (
            shape((7 * width, 2 * width), BF16),
            shape((8 * width, 2 * width), BF16),
            shape(((tm - 1) * width, 2 * width), BF16),
        ),
        [],
        flops=10**9,
    )
    spaces = vmem((full + 1, 16, width), BF16)
    force = vmem((full * 8, width), BF16)
    rows = vmem((n * 8, width), F32)
    strip = shape((STRIP, 16, width), BF16)
    tables = [vmem((256, 256), BF16), vmem((256, 128), F32), vmem((128, 128), F32)]
    smem = pltpu.SMEM((8, 256), jnp.int32)
    strips = call(
        first_early_kernel,
        (fe, tab, initial_state, pay_even, w),
        (strip, strip, strip),
        [spaces] * 3 + [force, vmem((6 * REACH * 8, width), F32)] + tables + [vmem((8, 256), jnp.int32), smem, dma],
        flops=step_flops * 6 * REACH,
    )
    w1, end, idx = call(
        first_late_kernel,
        (fe, tab, initial_state, pay_even, pay_odd, *strips, w, pk),
        (tiles, ends, shape((8, 256), jnp.int32)),
        [spaces] * 3 + [force, rows] + tables + [smem, dma],
        flops=step_flops * 12 * REACH,
    )
    arrivals = earlier(end)
    (starts,) = call(scan_kernel, (w1, pk), (tiles,), [])
    (coarse,) = call(enter_first_kernel, (*arrivals, starts, we, pk), (state,), [rows])
    got_odd, got_even = swapped(coarse, 1), swapped(coarse, 0)
    strips = call(
        second_early_kernel,
        (idx, coarse, got_even, w),
        (strip, strip, strip),
        [spaces] * 4,
        spaces="s",
        flops=step_flops * 12 * REACH,
    )
    res, end, total = call(
        second_late_kernel,
        (idx, coarse, got_odd, *strips, w1, w, pk),
        (tiles, ends, tiles),
        [spaces] * 4 + [rows],
        spaces="s",
        flops=step_flops * 16 * REACH,
    )
    arrivals = earlier(end)
    (starts,) = call(scan_kernel, (res, pk), (tiles,), [])
    side = shape(((COARSEN - 1) * REACH, 16, width), BF16)
    coarse, end_even, end_odd, corr = call(
        enter_second_kernel,
        (*arrivals, starts, coarse, initial_state, we, pk),
        (state, side, side, tiles),
        [rows],
    )
    got_odd, got_even = swapped(end_odd, 1), swapped(end_even, 0)
    result = shape((steps, n, width), F32)
    flips = [vmem((8 * m * REACH, width), F32) for m in (3, 2, 1)]
    out, *strips = call(
        third_early_kernel,
        (idx, coarse, got_even, corr, total, fe, pay_even, w, pk),
        (result, strip, strip),
        [spaces] * 3 + [force] + flips + [rows, dma((COARSEN, 8))],
        spaces="s",
        out_spaces="h",
        flops=step_flops * 9 * REACH,
    )
    (out,) = call(
        third_late_kernel,
        (idx, coarse, got_odd, *strips, fe, pay_odd, w, out),
        (result,),
        [spaces] * 3 + [force] + flips[::-1] + [dma((COARSEN - 1, 8))],
        spaces="svvvvvvvh",
        out_spaces="h",
        aliases={8: 0},
        flops=step_flops * 9 * REACH,
    )
    return out


def solution(mesh):
    return jax.shard_map(
        local,
        mesh=mesh,
        in_specs=(
            P("tm", ("groups", "space"), None),
            P(("groups", "space"), None),
            P("space", None),
            P("space", None),
            P(),
            P(),
            P(),
        ),
        out_specs=P("tm", ("groups", "space"), None),
        check_vma=False,
    )
```

```python
import functools

import jax
import jax.numpy as jnp
from jax import lax
from jax.experimental import pallas as pl
from jax.experimental.pallas import tpu as pltpu
from jax.sharding import PartitionSpec as P

COARSEN = 4
REACH = 16
F32 = jnp.float32
BF16 = jnp.bfloat16
CHUNK = 32


def swapped(value, first):
    count = lax.axis_size("space")
    pairs = []
    for i in range(first, count - 1, 2):
        pairs += [(i, i + 1), (i + 1, i)]
    return lax.ppermute(value, "space", pairs)


def exchanged(ends):
    return lax.all_to_all(ends, "tm", 0, 0)


def split(u):
    lead = u.astype(BF16).astype(F32)
    return jnp.concatenate([u, u - lead], axis=1).astype(BF16)


def split_rows(u):
    lead = u.astype(BF16)
    return jnp.concatenate([lead, (u - lead.astype(F32)).astype(BF16)], axis=0)


def product(x, weights):
    m = x.shape[0] // 16
    r = jnp.dot(x, weights, preferred_element_type=F32).reshape(m, 16, 256)
    return r[:, :8, :128] + (r[:, 8:, :128] + r[:, :8, 128:])


def product_rows(x, weights):
    m = x.shape[0] // 2
    r = jnp.dot(x, weights, preferred_element_type=F32)
    return r[:m, :128] + (r[m:, :128] + r[:m, 128:])


def put_halves(ref, w):
    lead = w.astype(BF16)
    ref[:, 0:128] = lead
    ref[:, 128:256] = (w - lead.astype(F32)).astype(BF16)


def power(pk, k):
    return pk[pl.ds(128 * (7 - k), 128), :]


def scan_starts(values, pk):
    y = values
    row = lax.broadcasted_iota(jnp.int32, y.shape, 1)
    for d in (1, 2, 4):
        z = product(split(y).reshape(-1, 128), power(pk, d))
        y = y + jnp.where(row >= d, pltpu.roll(z, d, axis=1), 0.0)
    return jnp.where(row >= 1, pltpu.roll(y, 1, axis=1), 0.0)


def block_end(ends, y, pk, n):
    parts = [y[pl.ds(i, n, stride=8), :] for i in range(8)]
    end = product_rows(split_rows(jnp.concatenate(parts, axis=1)), pk[...])
    for i in range(ends.shape[0]):
        ends[i] = end


def enter(ends, we, pk, y, n):
    value = jnp.concatenate([ends[i] for i in range(ends.shape[0])], axis=1)
    entry = product_rows(split_rows(value), we[...])
    y[pl.ds(0, n, stride=8), :] = entry
    rows = split_rows(entry)
    for i in range(1, 8):
        y[pl.ds(i, n, stride=8), :] = product_rows(rows, power(pk, i))
    return y[...].reshape(n, 8, 128)


def gathered(src, idx, base, size, f):
    if f == 0:
        return src[pl.ds(base, size)].reshape(size * 16, 128)
    return jnp.concatenate([src[idx[f - 1, base + e]] for e in range(size)], axis=0)


def phi_halves(src, idx, w, base, size):
    size = size // 2
    parts = []
    for at in (base, base + size):
        x = jnp.concatenate([gathered(src, idx, at, size, f) for f in range(7)], axis=1)
        parts.append(product(x, w[...]))
    return jnp.concatenate(parts, axis=0)


def phi_pairs(src, idx, w, base, size):
    total = None
    for f in (0, 2, 4, 6):
        x = jnp.concatenate([gathered(src, idx, base, size, f + j) for j in range(min(2, 7 - f))], axis=1)
        r = jnp.dot(x, w[pl.ds(f * 128, x.shape[1]), :], preferred_element_type=F32)
        total = r if total is None else total + r
    r = total.reshape(size, 16, 256)
    return r[:, :8, :128] + (r[:, 8:, :128] + r[:, :8, 128:])


def phi_through(src, idx, w, base, size, lhs):
    for f in range(7):
        lhs[pl.ds(0, size * 16), f * 128 : (f + 1) * 128] = gathered(src, idx, base, size, f)
    return product(lhs[pl.ds(0, size * 16), :], w[...])


def even_place():
    return lax.rem(lax.axis_index("space"), 2) == 0


def mirrored(low, size, full):
    return jnp.where(even_place(), full - low - size, low)


def pack_kernel(
    forcing, init, conn, pattern, fe, tab, pay_even, pay_odd, landed, rows, init_v, conn_v, pattern_v, offs, sems
):
    n = init_v.shape[0]
    copies = [pltpu.make_async_copy(forcing.at[:, k], landed.at[k], sems.at[k]) for k in range(COARSEN)]
    small = ((conn, conn_v), (pattern, pattern_v), (init, init_v))
    copies += [pltpu.make_async_copy(src, dst, sems.at[COARSEN + i]) for i, (src, dst) in enumerate(small)]
    for copy in copies:
        copy.start()
    for copy in copies[COARSEN:]:
        copy.wait()
    place = lax.broadcasted_iota(jnp.int32, (6, n), 1) + lax.axis_index("space") * n
    value = ((conn_v[...] - place) * pattern_v[...]).astype(F32)
    offs[...] = jnp.zeros_like(offs)
    offs[0:6, 0:n] = value
    offs[0:6, n : 2 * n] = value
    tab[...] = offs[...].astype(BF16)
    lead = init_v[...].astype(BF16)
    rest = (init_v[...] - lead.astype(F32)).astype(BF16)
    even = even_place()
    at = sum((COARSEN - 1 - k) * REACH * 8 for k in range(COARSEN))
    for pay in (pay_even, pay_odd):
        pay[pl.ds(at, n), :] = lead
        pay[pl.ds(at + n, n), :] = rest
        pay[pl.ds(at + 2 * n, 16), :] = tab[...]
    at = 0
    for k in range(COARSEN):
        copies[k].wait()
        for i in range(8):
            rows[pl.ds(i * n, n), :] = landed[k, i].astype(F32)

        def body(pair, carry, k=k):
            e = pair * 2
            two = [rows[pl.ds(e + j, 8, stride=n), :] for j in range(2)]
            fe[k, pl.ds(pl.multiple_of(e * 8, 16), 16), :] = jnp.concatenate(two, axis=0).astype(BF16)
            return carry

        lax.fori_loop(0, n // 2, body, 0, unroll=8)
        width = (COARSEN - 1 - k) * REACH * 8
        if width:
            for pay, right in ((pay_even, even), (pay_odd, jnp.logical_not(even))):
                begin = pl.multiple_of(jnp.where(right, n * 8 - width, 0), 128)
                pay[pl.ds(at, width), :] = fe[k, pl.ds(begin, width), :]
        at += width


def weight_kernel(diag, faces, coarse, w, pk, we):
    put_halves(w.at[pl.ds(0, 128)], diag[...].T)
    for f in range(6):
        put_halves(w.at[pl.ds(128 * (f + 1), 128)], faces[f].T)

    def thirds(a):
        one = a.astype(BF16)
        rest = a - one.astype(F32)
        two = rest.astype(BF16)
        return one, two, (rest - two.astype(F32)).astype(BF16)

    def mul(a, b):
        (a1, a2, a3), (b1, b2, b3) = thirds(a), thirds(b)
        total = jnp.zeros((128, 128), F32)
        for x, y in ((a3, b1), (a1, b3), (a2, b2), (a2, b1), (a1, b2), (a1, b1)):
            total += jnp.dot(x, y, preferred_element_type=F32)
        return total

    rows = lax.broadcasted_iota(jnp.int32, (128, 128), 0)
    one = (rows == lax.broadcasted_iota(jnp.int32, (128, 128), 1)).astype(F32)
    powers = [one, coarse[...].T]
    for k in range(2, 9):
        powers.append(mul(powers[k // 2], powers[k - k // 2]))
    for k in range(8):
        put_halves(pk.at[pl.ds(128 * (7 - k), 128)], powers[k])

    t = lax.axis_index("tm")
    we[...] = jnp.zeros_like(we)

    def body(k, current):
        put_halves(we.at[pl.ds(pl.multiple_of((t - 1 - k) * 128, 128), 128)], current)
        return mul(current, powers[8])

    lax.fori_loop(0, t, body, one)


def put_force(dst, own, got, right, k, n):
    at = sum((COARSEN - 1 - j) * REACH * 8 for j in range(k))
    width = (COARSEN - 1 - k) * REACH * 8
    dst[pl.ds(n * 8, n * 8), :] = own[k]
    if width:
        to = pl.multiple_of(jnp.where(right, 2 * n * 8, n * 8 - width), 128)
        dst[pl.ds(to, width), :] = got[pl.ds(at, width), :]


def force_at(src, base, size):
    at = pl.multiple_of(base * 8, 128)
    return src[pl.ds(at, size * 8), :].astype(F32).reshape(size, 8, 128)


def put_tables(tab, got_even, got_odd, idx_v, columns, square, full, n):
    even = even_place()
    lane = lax.broadcasted_iota(jnp.int32, (8, 128), 1)

    def table(ref):
        return 0.0 if ref is None else ref[pl.ds(ref.shape[0] - 16, 16), :].astype(F32)[0:8]

    from_even, from_odd = table(got_even), table(got_odd)
    low = jnp.where(lane < n, jnp.where(even, from_odd, from_even), table(tab))
    high = jnp.where(lane < n, jnp.where(even, from_even, from_odd), 0.0)
    for at, offs in ((0, low), (128, high)):
        value = jnp.where(offs != 0.0, lane + at + offs.astype(jnp.int32), full)
        idx_v[:, pl.ds(at, 128)] = value
        square[...] = jnp.zeros_like(square)
        square[0:8, :] = value.astype(F32)
        columns[pl.ds(at, 128), :] = square[...].T


def push_init(init, got_even, got_odd, w, columns, i16, base, count, n):
    even = even_place()
    i16[...] = jnp.zeros_like(i16)
    lead = init[...].astype(BF16)
    i16[pl.ds(n, n), 0:128] = lead
    i16[pl.ds(n, n), 128:256] = (init[...] - lead.astype(F32)).astype(BF16)
    for ref, right in ((got_even, even), (got_odd, jnp.logical_not(even))):
        if ref is not None:
            at = ref.shape[0] - 16
            to = pl.multiple_of(jnp.where(right, 2 * n, 0), n)
            i16[pl.ds(to, n), 0:128] = ref[pl.ds(at - 2 * n, n), :]
            i16[pl.ds(to, n), 128:256] = ref[pl.ds(at - n, n), :]
    rows = pl.ds(pl.multiple_of(base, REACH), count)
    place = columns[rows, :]
    spot = lax.broadcasted_iota(jnp.int32, (count, 256), 1).astype(F32)
    cols = [i16[rows, :]]
    for f in range(6):
        hot = (spot == place[:, f : f + 1]).astype(F32).astype(BF16)
        cols.append(jnp.dot(hot, i16[...], preferred_element_type=F32).astype(BF16))
    leads = jnp.concatenate([c[:, 0:128] for c in cols], axis=1)
    rests = jnp.concatenate([c[:, 128:256] for c in cols], axis=1)
    pushed = product_rows(jnp.concatenate([leads, rests], axis=0), w[...])
    return pushed * (lax.axis_index("tm") == 0).astype(F32)


STRIPS = (5 * REACH, 4 * REACH, 3 * REACH)
STRIP = 2 * REACH


def put_strips(strips, states, full):
    for strip, state, low in zip(strips, states, STRIPS):
        strip[...] = state[pl.ds(mirrored(low, STRIP, full), STRIP)]


def get_strips(strips, states, full):
    for strip, state, low in zip(strips, states, STRIPS):
        state[pl.ds(mirrored(low, STRIP, full), STRIP)] = strip[...]
        state[full] = jnp.zeros((16, 128), BF16)


def first_early_kernel(
    fe, tab, init, got, w, strip1, strip2, strip3, s1, s2, s3, force, y, i16, columns, square, idx_v, idx, sem
):
    n = init.shape[0]
    full = 3 * n
    even = even_place()
    put_tables(tab, got, None, idx_v, columns, square, full, n)
    copy = pltpu.make_async_copy(idx_v, idx, sem)
    copy.start()
    count = 6 * REACH
    base = mirrored(REACH, count, full)
    pushed = push_init(init, got, None, w, columns, i16, base, count, n)
    put_force(force, fe, got, even, 0, n)
    y[pl.ds(0, count * 8), :] = force[pl.ds(pl.multiple_of(base * 8, 128), count * 8), :].astype(F32)
    y[pl.ds(0, count, stride=8), :] = y[pl.ds(0, count, stride=8), :] + pushed
    s1[pl.ds(base, count)] = split(y[pl.ds(0, count * 8), :].reshape(count, 8, 128))
    for state in (s1, s2, s3):
        state[full] = jnp.zeros((16, 128), BF16)
    copy.wait()
    for k, src, dst in ((1, s1, s2), (2, s2, s3)):
        put_force(force, fe, got, even, k, n)
        size = (6 - 2 * k) * REACH
        base = mirrored((k + 1) * REACH, size, full)
        dst[pl.ds(base, size)] = split(phi_halves(src, idx, w, base, size) + force_at(force, base, size))
    put_strips((strip1, strip2, strip3), (s1, s2, s3), full)


def first_late_kernel(
    fe, tab, init, got_even, got_odd, strip1, strip2, strip3, w, pk, w1, ends, idx_out,
    s1, s2, s3, force, y, i16, columns, square, idx, sem
):
    n = init.shape[0]
    full = 3 * n
    odd = jnp.logical_not(even_place())
    put_tables(tab, got_even, got_odd, idx_out, columns, square, full, n)
    copy = pltpu.make_async_copy(idx_out, idx, sem)
    copy.start()
    count = 4 * REACH
    base = mirrored(7 * REACH, count, full)
    pushed = push_init(init, got_even, got_odd, w, columns, i16, base, count, n)
    put_force(force, fe, got_odd, odd, 0, n)
    y[...] = force[pl.ds(pl.multiple_of(base * 8, 128), count * 8), :].astype(F32)
    y[pl.ds(0, count, stride=8), :] = y[pl.ds(0, count, stride=8), :] + pushed
    s1[pl.ds(base, count)] = split(y[...].reshape(count, 8, 128))
    get_strips((strip1, strip2, strip3), (s1, s2, s3), full)
    copy.wait()
    for k, src, dst in ((1, s1, s2), (2, s2, s3), (3, s3, None)):
        put_force(force, fe, got_odd, odd, k, n)
        base = mirrored((7 - k) * REACH, count, full)
        value = phi_halves(src, idx, w, base, count) + force_at(force, base, count)
        if dst is None:
            w1[...] = value
            y[...] = value.reshape(n * 8, 128)
        else:
            dst[pl.ds(base, count)] = split(value)
    block_end(ends, y, pk, n)


def scan_kernel(values, pk, starts):
    starts[...] = scan_starts(values[...], pk)


def enter_first_kernel(ends, starts, we, pk, state, y):
    n = starts.shape[0]
    state[...] = split(enter(ends, we, pk, y, n) + starts[...])


def enter_second_kernel(ends, starts, before, init, we, pk, state, pay_even, pay_odd, corr, y):
    n = starts.shape[0]
    value = enter(ends, we, pk, y, n) + starts[...]
    corr[...] = value
    old = before[...].astype(F32)
    y[...] = (value + (old[:, 0:8] + old[:, 8:16])).reshape(n * 8, 128)
    first = (lax.axis_index("tm") == 0).astype(F32)
    y[pl.ds(0, n, stride=8), :] = y[pl.ds(0, n, stride=8), :] + init[...] * first
    state[...] = split(y[...].reshape(n, 8, 128))
    side = (COARSEN - 1) * REACH
    even = even_place()
    pay_even[...] = state[pl.ds(jnp.where(even, n - side, 0), side)]
    pay_odd[...] = state[pl.ds(jnp.where(even, 0, n - side), side)]


def put_block(dst, own, got, right, n):
    side = got.shape[0]
    dst[pl.ds(n, n)] = own[...]
    dst[pl.ds(jnp.where(right, 2 * n, n - side), side)] = got[...]
    dst[3 * n] = jnp.zeros((16, 128), BF16)


def second_early_kernel(idx, own, got, w, strip1, strip2, strip3, s0, s1, s2, s3):
    n = own.shape[0]
    full = 3 * n
    put_block(s0, own, got, even_place(), n)
    for state in (s1, s2, s3):
        state[full] = jnp.zeros((16, 128), BF16)
    for k, src, dst in ((1, s0, s1), (2, s1, s2), (3, s2, s3)):
        size = (8 - 2 * k) * REACH
        base = mirrored(k * REACH, size, full)
        dst[pl.ds(base, size)] = split(phi_pairs(src, idx, w, base, size))
    put_strips((strip1, strip2, strip3), (s1, s2, s3), full)


def second_late_kernel(idx, own, got, strip1, strip2, strip3, w1, w, pk, res, ends, total, s0, s1, s2, s3, y):
    n = own.shape[0]
    full = 3 * n
    put_block(s0, own, got, jnp.logical_not(even_place()), n)
    get_strips((strip1, strip2, strip3), (s1, s2, s3), full)
    count = 4 * REACH
    for k, src, dst in ((1, s0, s1), (2, s1, s2), (3, s2, s3)):
        base = mirrored((8 - k) * REACH, count, full)
        dst[pl.ds(base, count)] = split(phi_pairs(src, idx, w, base, count))
    value = phi_pairs(s3, idx, w, n, n)
    total[...] = value + w1[...]
    value = value - product(own[...].reshape(n * 16, 128), power(pk, 1))
    res[...] = value
    y[...] = value.reshape(n * 8, 128)
    block_end(ends, y, pk, n)


def write_out(out, k, value, begin, flip, sems):
    size = value.shape[0]
    for e in range(size):
        flip[pl.ds(e, 8, stride=size), :] = value[e]
    rows = pl.ds(pl.multiple_of(begin, REACH), size)
    copies = [
        pltpu.make_async_copy(flip.at[pl.ds(i * size, size)], out.at[i * COARSEN + k, rows], sems.at[k, i])
        for i in range(8)
    ]
    for copy in copies:
        copy.start()
    return copies


def third_early_kernel(
    idx, own, got, corr, total, fe, pay, w, pk, out, strip1, strip2,
    s0, s1, s2, force, lhs, flip0, flip1, flip2, flip3, sems
):
    n = own.shape[0]
    full = 3 * n
    even = even_place()
    points = product(split(corr[...]).reshape(-1, 128), power(pk, 1)) + total[...]
    copies = write_out(out, COARSEN - 1, points, 0, flip3, sems)
    put_block(s0, own, got, even, n)
    for state in (s1, s2):
        state[full] = jnp.zeros((16, 128), BF16)
    for k, src, dst, flip in ((0, s0, s1, flip0), (1, s1, s2, flip1), (2, s2, None, flip2)):
        put_force(force, fe, pay, even, k, n)
        size = (5 - 2 * k) * REACH
        base = mirrored((2 + k) * REACH, size, full)
        value = phi_through(src, idx, w, base, size, lhs) + force_at(force, base, size)
        if dst is not None:
            dst[pl.ds(base, size)] = split(value)
        mine = (3 - k) * REACH
        skip = size - mine
        kept = jnp.where(even, value[:mine], value[skip:])
        copies += write_out(out, k, kept, jnp.where(even, n - mine, 0), flip, sems)
    put_strips((strip1, strip2), (s1, s2), full)
    for copy in copies:
        copy.wait()


def third_late_kernel(
    idx, own, got, strip1, strip2, fe, pay, w, partial, out, s0, s1, s2, force, lhs, flip0, flip1, flip2, sems
):
    n = own.shape[0]
    full = 3 * n
    even = even_place()
    odd = jnp.logical_not(even)
    put_block(s0, own, got, odd, n)
    get_strips((strip1, strip2), (s1, s2), full)
    copies = []
    size = 3 * REACH
    for k, src, dst, flip in ((0, s0, s1, flip0), (1, s1, s2, flip1), (2, s2, None, flip2)):
        put_force(force, fe, pay, odd, k, n)
        base = mirrored((7 - k) * REACH, size, full)
        value = phi_through(src, idx, w, base, size, lhs) + force_at(force, base, size)
        if dst is not None:
            dst[pl.ds(base, size)] = split(value)
        mine = (k + 1) * REACH
        kept = jnp.where(even, value[size - mine :], value[:mine])
        copies += write_out(out, k, kept, jnp.where(even, 0, n - mine), flip, sems)
    for copy in copies:
        copy.wait()


def call(kernel, inputs, outs, scratch, spaces="", out_spaces="", aliases=None, flops=10**7, room=32):
    kinds = {"s": pltpu.SMEM, "h": pltpu.HBM, "v": pltpu.VMEM}

    def specs(arrays, letters):
        letters = letters.ljust(len(arrays), "v")
        return [pl.BlockSpec(memory_space=kinds[letter]) for letter in letters]

    moved = sum(a.size * a.dtype.itemsize for a in list(inputs) + list(outs))
    return pl.pallas_call(
        kernel,
        out_shape=outs,
        name=kernel.__name__,
        in_specs=specs(inputs, spaces),
        out_specs=specs(outs, out_spaces),
        scratch_shapes=scratch,
        input_output_aliases=aliases or {},
        compiler_params=pltpu.CompilerParams(vmem_limit_bytes=room * 1024 * 1024),
        cost_estimate=pl.CostEstimate(flops=flops, bytes_accessed=moved, transcendentals=0),
    )(*inputs)


def local(forcing, initial_state, connectivity, pattern, diag_block, face_blocks, coarse_block):
    n, width = initial_state.shape
    steps = forcing.shape[0]
    full = 3 * n
    tm = lax.axis_size("tm")
    shape = jax.ShapeDtypeStruct
    vmem = pltpu.VMEM
    dma = pltpu.SemaphoreType.DMA
    tiles = shape((n, 8, width), F32)
    state = shape((n, 16, width), BF16)
    all_ends = shape((tm, n, width), F32)
    step_flops = 2 * 16 * 7 * width * 2 * width
    pay_rows = sum((COARSEN - 1 - k) * REACH * 8 for k in range(COARSEN)) + 2 * n + 16
    pay = shape((pay_rows, width), BF16)
    fe, tab, pay_even, pay_odd = call(
        pack_kernel,
        (forcing.reshape(steps // COARSEN, COARSEN, n, width), initial_state, connectivity.T, pattern.T),
        (shape((COARSEN, n * 8, width), BF16), shape((16, 128), BF16), pay, pay),
        [
            vmem((COARSEN, 8, n, width), BF16),
            vmem((8 * n, width), F32),
            vmem((n, width), F32),
            vmem((6, n), jnp.int32),
            vmem((6, n), jnp.int32),
            vmem((16, 128), F32),
            dma((COARSEN + 3,)),
        ],
        spaces="hhhh",
        room=62,
    )
    pay_odd, pay_even = swapped(pay_odd, 1), swapped(pay_even, 0)
    w, pk, we = call(
        weight_kernel,
        (diag_block, face_blocks, coarse_block),
        (
            shape((7 * width, 2 * width), BF16),
            shape((8 * width, 2 * width), BF16),
            shape((tm * width, 2 * width), BF16),
        ),
        [],
        flops=10**9,
    )
    spaces = vmem((full + 1, 16, width), BF16)
    force = vmem((full * 8, width), BF16)
    rows = vmem((n * 8, width), F32)
    strip = shape((STRIP, 16, width), BF16)
    tables = [vmem((256, 256), BF16), vmem((256, 128), F32), vmem((128, 128), F32)]
    smem = pltpu.SMEM((8, 256), jnp.int32)
    strips = call(
        first_early_kernel,
        (fe, tab, initial_state, pay_even, w),
        (strip, strip, strip),
        [spaces] * 3 + [force, vmem((6 * REACH * 8, width), F32)] + tables + [vmem((8, 256), jnp.int32), smem, dma],
        flops=step_flops * 6 * REACH,
    )
    w1, ends, idx = call(
        first_late_kernel,
        (fe, tab, initial_state, pay_even, pay_odd, *strips, w, pk),
        (tiles, all_ends, shape((8, 256), jnp.int32)),
        [spaces] * 3 + [force, rows] + tables + [smem, dma],
        flops=step_flops * 12 * REACH,
    )
    ends = exchanged(ends)
    (starts,) = call(scan_kernel, (w1, pk), (tiles,), [])
    (coarse,) = call(enter_first_kernel, (ends, starts, we, pk), (state,), [rows])
    got_odd, got_even = swapped(coarse, 1), swapped(coarse, 0)
    strips = call(
        second_early_kernel,
        (idx, coarse, got_even, w),
        (strip, strip, strip),
        [spaces] * 4,
        spaces="s",
        flops=step_flops * 12 * REACH,
    )
    res, ends, total = call(
        second_late_kernel,
        (idx, coarse, got_odd, *strips, w1, w, pk),
        (tiles, all_ends, tiles),
        [spaces] * 4 + [rows],
        spaces="s",
        flops=step_flops * 16 * REACH,
    )
    ends = exchanged(ends)
    (starts,) = call(scan_kernel, (res, pk), (tiles,), [])
    side = shape(((COARSEN - 1) * REACH, 16, width), BF16)
    coarse, end_even, end_odd, corr = call(
        enter_second_kernel,
        (ends, starts, coarse, initial_state, we, pk),
        (state, side, side, tiles),
        [rows],
    )
    got_odd, got_even = swapped(end_odd, 1), swapped(end_even, 0)
    result = shape((steps, n, width), F32)
    lhs = vmem((5 * REACH * 16, 7 * width), BF16)
    flips = [vmem((8 * m * REACH, width), F32) for m in (3, 2, 1)]
    out, *strips = call(
        third_early_kernel,
        (idx, coarse, got_even, corr, total, fe, pay_even, w, pk),
        (result, strip, strip),
        [spaces] * 3 + [force, lhs] + flips + [rows, dma((COARSEN, 8))],
        spaces="s",
        out_spaces="h",
        flops=step_flops * 9 * REACH,
    )
    (out,) = call(
        third_late_kernel,
        (idx, coarse, got_odd, *strips, fe, pay_odd, w, out),
        (result,),
        [spaces] * 3 + [force, lhs] + flips[::-1] + [dma((COARSEN - 1, 8))],
        spaces="svvvvvvvh",
        out_spaces="h",
        aliases={8: 0},
        flops=step_flops * 9 * REACH,
    )
    return out


def solution(mesh):
    return jax.shard_map(
        local,
        mesh=mesh,
        in_specs=(
            P("tm", ("groups", "space"), None),
            P(("groups", "space"), None),
            P("space", None),
            P("space", None),
            P(),
            P(),
            P(),
        ),
        out_specs=P("tm", ("groups", "space"), None),
        check_vma=False,
    )
```

```python
import functools

import jax
import jax.numpy as jnp
from jax import lax
from jax.experimental import pallas as pl
from jax.experimental.pallas import tpu as pltpu
from jax.sharding import PartitionSpec as P

COARSEN = 4
REACH = 16
F32 = jnp.float32
BF16 = jnp.bfloat16
CHUNK = 32


def swapped(value, first):
    count = lax.axis_size("space")
    pairs = []
    for i in range(first, count - 1, 2):
        pairs += [(i, i + 1), (i + 1, i)]
    return lax.ppermute(value, "space", pairs)


def earlier(value):
    count = lax.axis_size("tm")
    if count <= 8:
        return [lax.ppermute(value, "tm", [(i, i + s) for i in range(count - s)]) for s in range(1, count)]
    every = lax.all_gather(value, "tm")
    at = lax.axis_index("tm") - jnp.arange(1, count)
    picked = jnp.where((at >= 0)[:, None, None], jnp.take(every, jnp.maximum(at, 0), axis=0), 0.0)
    return [picked[s] for s in range(count - 1)]


def split(u):
    lead = u.astype(BF16).astype(F32)
    return jnp.concatenate([u, u - lead], axis=1).astype(BF16)


def split_rows(u):
    lead = u.astype(BF16)
    return jnp.concatenate([lead, (u - lead.astype(F32)).astype(BF16)], axis=0)


def product(x, weights):
    m = x.shape[0] // 16
    r = jnp.dot(x, weights, preferred_element_type=F32).reshape(m, 16, 256)
    return r[:, :8, :128] + (r[:, 8:, :128] + r[:, :8, 128:])


def product_rows(x, weights):
    m = x.shape[0] // 2
    r = jnp.dot(x, weights, preferred_element_type=F32)
    return r[:m, :128] + (r[m:, :128] + r[:m, 128:])


def put_halves(ref, w):
    lead = w.astype(BF16)
    ref[:, 0:128] = lead
    ref[:, 128:256] = (w - lead.astype(F32)).astype(BF16)


def power(pk, k):
    return pk[pl.ds(128 * (7 - k), 128), :]


def scan_starts(values, pk):
    y = values
    row = lax.broadcasted_iota(jnp.int32, y.shape, 1)
    for d in (1, 2, 4):
        z = product(split(y).reshape(-1, 128), power(pk, d))
        y = y + jnp.where(row >= d, pltpu.roll(z, d, axis=1), 0.0)
    return jnp.where(row >= 1, pltpu.roll(y, 1, axis=1), 0.0)


def block_end(y, pk, n):
    parts = [y[pl.ds(i, n, stride=8), :] for i in range(8)]
    return product_rows(split_rows(jnp.concatenate(parts, axis=1)), pk[...])


def enter(arrivals, we, pk, y, n):
    value = jnp.concatenate([a[...] for a in arrivals], axis=1)
    entry = product_rows(split_rows(value), we[...])
    y[pl.ds(0, n, stride=8), :] = entry
    rows = split_rows(entry)
    for i in range(1, 8):
        y[pl.ds(i, n, stride=8), :] = product_rows(rows, power(pk, i))
    return y[...].reshape(n, 8, 128)


def apply_phi(src, idx, w, base, size):
    cols = [src[pl.ds(base, size)].reshape(size * 16, 128)]
    for f in range(6):
        cols.append(jnp.concatenate([src[idx[f, base + e]] for e in range(size)], axis=0))
    return product(jnp.concatenate(cols, axis=1), w[...])


def even_place():
    return lax.rem(lax.axis_index("space"), 2) == 0


def by_parity(body):
    even = even_place()
    pl.when(even)(lambda: body(True))
    pl.when(jnp.logical_not(even))(lambda: body(False))


def mirrored(low, size, full, even):
    return full - low - size if even else low


def pack_kernel(
    forcing, init, conn, pattern, fe, tab, pay_even, pay_odd, landed, rows, init_v, conn_v, pattern_v, offs, sems
):
    n = init_v.shape[0]
    copies = [pltpu.make_async_copy(forcing.at[:, k], landed.at[k], sems.at[k]) for k in range(COARSEN)]
    small = ((conn, conn_v), (pattern, pattern_v), (init, init_v))
    copies += [pltpu.make_async_copy(src, dst, sems.at[COARSEN + i]) for i, (src, dst) in enumerate(small)]
    for copy in copies:
        copy.start()
    for copy in copies[COARSEN:]:
        copy.wait()
    place = lax.broadcasted_iota(jnp.int32, (6, n), 1) + lax.axis_index("space") * n
    value = ((conn_v[...] - place) * pattern_v[...]).astype(F32)
    offs[...] = jnp.zeros_like(offs)
    offs[0:6, 0:n] = value
    offs[0:6, n : 2 * n] = value
    tab[...] = offs[...].astype(BF16)
    lead = init_v[...].astype(BF16)
    rest = (init_v[...] - lead.astype(F32)).astype(BF16)
    even = even_place()
    at = sum((COARSEN - 1 - k) * REACH * 8 for k in range(COARSEN))
    for pay in (pay_even, pay_odd):
        pay[pl.ds(at, n), :] = lead
        pay[pl.ds(at + n, n), :] = rest
        pay[pl.ds(at + 2 * n, 16), :] = tab[...]
    at = 0
    for k in range(COARSEN):
        copies[k].wait()
        for i in range(8):
            rows[pl.ds(i * n, n), :] = landed[k, i].astype(F32)

        def body(pair, carry, k=k):
            e = pair * 2
            two = [rows[pl.ds(e + j, 8, stride=n), :] for j in range(2)]
            fe[k, pl.ds(pl.multiple_of(e * 8, 16), 16), :] = jnp.concatenate(two, axis=0).astype(BF16)
            return carry

        lax.fori_loop(0, n // 2, body, 0, unroll=8)
        width = (COARSEN - 1 - k) * REACH * 8
        if width:
            for pay, right in ((pay_even, even), (pay_odd, jnp.logical_not(even))):
                begin = pl.multiple_of(jnp.where(right, n * 8 - width, 0), 128)
                pay[pl.ds(at, width), :] = fe[k, pl.ds(begin, width), :]
        at += width


def weight_kernel(diag, faces, coarse, w, pk, we):
    put_halves(w.at[pl.ds(0, 128)], diag[...].T)
    for f in range(6):
        put_halves(w.at[pl.ds(128 * (f + 1), 128)], faces[f].T)

    def thirds(a):
        one = a.astype(BF16)
        rest = a - one.astype(F32)
        two = rest.astype(BF16)
        return one, two, (rest - two.astype(F32)).astype(BF16)

    def mul(a, b):
        (a1, a2, a3), (b1, b2, b3) = thirds(a), thirds(b)
        total = jnp.zeros((128, 128), F32)
        for x, y in ((a3, b1), (a1, b3), (a2, b2), (a2, b1), (a1, b2), (a1, b1)):
            total += jnp.dot(x, y, preferred_element_type=F32)
        return total

    rows = lax.broadcasted_iota(jnp.int32, (128, 128), 0)
    one = (rows == lax.broadcasted_iota(jnp.int32, (128, 128), 1)).astype(F32)
    powers = [one, coarse[...].T]
    for k in range(2, 9):
        powers.append(mul(powers[k // 2], powers[k - k // 2]))
    for k in range(8):
        put_halves(pk.at[pl.ds(128 * (7 - k), 128)], powers[k])

    def body(k, current):
        put_halves(we.at[pl.ds(pl.multiple_of(k * 128, 128), 128)], current)
        return mul(current, powers[8])

    lax.fori_loop(0, we.shape[0] // 128, body, one)


def put_force(dst, own, got, right, k, n):
    at = sum((COARSEN - 1 - j) * REACH * 8 for j in range(k))
    width = (COARSEN - 1 - k) * REACH * 8
    dst[pl.ds(n * 8, n * 8), :] = own[k]
    if width:
        to = 2 * n * 8 if right else n * 8 - width
        dst[pl.ds(to, width), :] = got[pl.ds(at, width), :]


def force_at(src, base, size):
    return src[pl.ds(base * 8, size * 8), :].astype(F32).reshape(size, 8, 128)


def put_tables(tab, got_even, got_odd, idx_v, columns, square, full, n, even):
    lane = lax.broadcasted_iota(jnp.int32, (8, 128), 1)

    def table(ref):
        return 0.0 if ref is None else ref[pl.ds(ref.shape[0] - 16, 16), :].astype(F32)[0:8]

    from_even, from_odd = table(got_even), table(got_odd)
    low = jnp.where(lane < n, from_odd if even else from_even, table(tab))
    high = jnp.where(lane < n, from_even if even else from_odd, 0.0)
    for at, offs in ((0, low), (128, high)):
        value = jnp.where(offs != 0.0, lane + at + offs.astype(jnp.int32), full)
        idx_v[:, pl.ds(at, 128)] = value
        square[...] = jnp.zeros_like(square)
        square[0:8, :] = value.astype(F32)
        columns[pl.ds(at, 128), :] = square[...].T


def push_init(init, got_even, got_odd, w, columns, i16, base, count, n, even):
    i16[...] = jnp.zeros_like(i16)
    lead = init[...].astype(BF16)
    i16[pl.ds(n, n), 0:128] = lead
    i16[pl.ds(n, n), 128:256] = (init[...] - lead.astype(F32)).astype(BF16)
    for ref, right in ((got_even, even), (got_odd, not even)):
        if ref is not None:
            at = ref.shape[0] - 16
            to = 2 * n if right else 0
            i16[pl.ds(to, n), 0:128] = ref[pl.ds(at - 2 * n, n), :]
            i16[pl.ds(to, n), 128:256] = ref[pl.ds(at - n, n), :]
    rows = pl.ds(base, count)
    place = columns[rows, :]
    spot = lax.broadcasted_iota(jnp.int32, (count, 256), 1).astype(F32)
    cols = [i16[rows, :]]
    for f in range(6):
        hot = (spot == place[:, f : f + 1]).astype(F32).astype(BF16)
        cols.append(jnp.dot(hot, i16[...], preferred_element_type=F32).astype(BF16))
    leads = jnp.concatenate([c[:, 0:128] for c in cols], axis=1)
    rests = jnp.concatenate([c[:, 128:256] for c in cols], axis=1)
    pushed = product_rows(jnp.concatenate([leads, rests], axis=0), w[...])
    return pushed * (lax.axis_index("tm") == 0).astype(F32)


STRIPS = (5 * REACH, 4 * REACH, 3 * REACH)
STRIP = 2 * REACH


def put_strips(strips, states, full, even):
    for strip, state, low in zip(strips, states, STRIPS):
        strip[...] = state[pl.ds(mirrored(low, STRIP, full, even), STRIP)]


def get_strips(strips, states, full, even):
    for strip, state, low in zip(strips, states, STRIPS):
        state[pl.ds(mirrored(low, STRIP, full, even), STRIP)] = strip[...]
        state[full] = jnp.zeros((16, 128), BF16)


def first_early_kernel(
    fe, tab, init, got, w, strip1, strip2, strip3, s1, s2, s3, force, y, i16, columns, square, idx_v, idx, sem
):
    def body(even):
        n = init.shape[0]
        full = 3 * n
        put_tables(tab, got, None, idx_v, columns, square, full, n, even)
        copy = pltpu.make_async_copy(idx_v, idx, sem)
        copy.start()
        count = 6 * REACH
        base = mirrored(REACH, count, full, even)
        pushed = push_init(init, got, None, w, columns, i16, base, count, n, even)
        put_force(force, fe, got, even, 0, n)
        y[pl.ds(0, count * 8), :] = force[pl.ds(base * 8, count * 8), :].astype(F32)
        y[pl.ds(0, count, stride=8), :] = y[pl.ds(0, count, stride=8), :] + pushed
        s1[pl.ds(base, count)] = split(y[pl.ds(0, count * 8), :].reshape(count, 8, 128))
        for state in (s1, s2, s3):
            state[full] = jnp.zeros((16, 128), BF16)
        copy.wait()
        for k, src, dst in ((1, s1, s2), (2, s2, s3)):
            put_force(force, fe, got, even, k, n)
            size = (6 - 2 * k) * REACH
            base = mirrored((k + 1) * REACH, size, full, even)
            dst[pl.ds(base, size)] = split(apply_phi(src, idx, w, base, size) + force_at(force, base, size))
        put_strips((strip1, strip2, strip3), (s1, s2, s3), full, even)

    by_parity(body)


def first_late_kernel(
    fe, tab, init, got_even, got_odd, strip1, strip2, strip3, w, pk, w1, end, idx_out,
    s1, s2, s3, force, y, i16, columns, square, idx, sem
):
    def body(even):
        n = init.shape[0]
        full = 3 * n
        put_tables(tab, got_even, got_odd, idx_out, columns, square, full, n, even)
        copy = pltpu.make_async_copy(idx_out, idx, sem)
        copy.start()
        count = 4 * REACH
        base = mirrored(7 * REACH, count, full, even)
        pushed = push_init(init, got_even, got_odd, w, columns, i16, base, count, n, even)
        put_force(force, fe, got_odd, not even, 0, n)
        y[...] = force[pl.ds(base * 8, count * 8), :].astype(F32)
        y[pl.ds(0, count, stride=8), :] = y[pl.ds(0, count, stride=8), :] + pushed
        s1[pl.ds(base, count)] = split(y[...].reshape(count, 8, 128))
        get_strips((strip1, strip2, strip3), (s1, s2, s3), full, even)
        copy.wait()
        for k, src, dst in ((1, s1, s2), (2, s2, s3), (3, s3, None)):
            put_force(force, fe, got_odd, not even, k, n)
            base = mirrored((7 - k) * REACH, count, full, even)
            value = apply_phi(src, idx, w, base, count) + force_at(force, base, count)
            if dst is None:
                w1[...] = value
                y[...] = value.reshape(n * 8, 128)
            else:
                dst[pl.ds(base, count)] = split(value)
        end[...] = block_end(y, pk, n)

    by_parity(body)


def scan_kernel(values, pk, starts):
    starts[...] = scan_starts(values[...], pk)


def scan_sum_kernel(values, w1, coarse, pk, starts, total):
    starts[...] = scan_starts(values[...], pk)
    total[...] = values[...] + (w1[...] + coarse[...])


def enter_first_kernel(*refs):
    *arrivals, starts, we, pk, state, y = refs
    n = starts.shape[0]
    state[...] = split(enter(arrivals, we, pk, y, n) + starts[...])


def enter_second_kernel(*refs):
    *arrivals, starts, before, init, we, pk, state, pay_even, pay_odd, corr, y = refs
    n = starts.shape[0]
    value = enter(arrivals, we, pk, y, n) + starts[...]
    corr[...] = value
    old = before[...].astype(F32)
    y[...] = (value + (old[:, 0:8] + old[:, 8:16])).reshape(n * 8, 128)
    first = (lax.axis_index("tm") == 0).astype(F32)
    y[pl.ds(0, n, stride=8), :] = y[pl.ds(0, n, stride=8), :] + init[...] * first
    state[...] = split(y[...].reshape(n, 8, 128))
    side = (COARSEN - 1) * REACH
    even = even_place()
    pay_even[...] = state[pl.ds(jnp.where(even, n - side, 0), side)]
    pay_odd[...] = state[pl.ds(jnp.where(even, 0, n - side), side)]


def put_block(dst, own, got, right, n):
    side = got.shape[0]
    dst[pl.ds(n, n)] = own[...]
    dst[pl.ds(2 * n if right else n - side, side)] = got[...]
    dst[3 * n] = jnp.zeros((16, 128), BF16)


def second_early_kernel(idx, own, got, w, pk, strip1, strip2, strip3, coarse, s0, s1, s2, s3):
    def body(even):
        n = own.shape[0]
        full = 3 * n
        coarse[...] = product(own[...].reshape(n * 16, 128), power(pk, 1))
        put_block(s0, own, got, even, n)
        for state in (s1, s2, s3):
            state[full] = jnp.zeros((16, 128), BF16)
        for k, src, dst in ((1, s0, s1), (2, s1, s2), (3, s2, s3)):
            size = (8 - 2 * k) * REACH
            base = mirrored(k * REACH, size, full, even)
            dst[pl.ds(base, size)] = split(apply_phi(src, idx, w, base, size))
        put_strips((strip1, strip2, strip3), (s1, s2, s3), full, even)

    by_parity(body)


def second_late_kernel(idx, own, got, strip1, strip2, strip3, coarse, w, pk, res, end, s0, s1, s2, s3, y):
    def body(even):
        n = own.shape[0]
        full = 3 * n
        put_block(s0, own, got, not even, n)
        get_strips((strip1, strip2, strip3), (s1, s2, s3), full, even)
        count = 4 * REACH
        for k, src, dst in ((1, s0, s1), (2, s1, s2), (3, s2, s3)):
            base = mirrored((8 - k) * REACH, count, full, even)
            dst[pl.ds(base, count)] = split(apply_phi(src, idx, w, base, count))
        value = apply_phi(s3, idx, w, n, n)
        value = value - coarse[...]
        res[...] = value
        y[...] = value.reshape(n * 8, 128)
        end[...] = block_end(y, pk, n)

    by_parity(body)


def write_out(out, k, value, begin, flip, sems):
    size = value.shape[0]
    for e in range(size):
        flip[pl.ds(e, 8, stride=size), :] = value[e]
    rows = pl.ds(begin, size)
    copies = [
        pltpu.make_async_copy(flip.at[pl.ds(i * size, size)], out.at[i * COARSEN + k, rows], sems.at[k, i])
        for i in range(8)
    ]
    for copy in copies:
        copy.start()
    return copies


def third_early_kernel(
    idx, own, got, corr, total, fe, pay, w, pk, out, strip1, strip2, s0, s1, s2, force, flip0, flip1, flip2, flip3, sems
):
    def body(even):
        n = own.shape[0]
        full = 3 * n
        points = product(split(corr[...]).reshape(-1, 128), power(pk, 1)) + total[...]
        copies = write_out(out, COARSEN - 1, points, 0, flip3, sems)
        put_block(s0, own, got, even, n)
        for state in (s1, s2):
            state[full] = jnp.zeros((16, 128), BF16)
        for k, src, dst, flip in ((0, s0, s1, flip0), (1, s1, s2, flip1), (2, s2, None, flip2)):
            put_force(force, fe, pay, even, k, n)
            size = (5 - 2 * k) * REACH
            base = mirrored((2 + k) * REACH, size, full, even)
            value = apply_phi(src, idx, w, base, size) + force_at(force, base, size)
            if dst is not None:
                dst[pl.ds(base, size)] = split(value)
            mine = (3 - k) * REACH
            skip = size - mine
            kept = value[:mine] if even else value[skip:]
            copies += write_out(out, k, kept, n - mine if even else 0, flip, sems)
        put_strips((strip1, strip2), (s1, s2), full, even)
        for copy in copies:
            copy.wait()

    by_parity(body)


def third_late_kernel(
    idx, own, got, strip1, strip2, fe, pay, w, partial, out, s0, s1, s2, force, flip0, flip1, flip2, sems
):
    def body(even):
        n = own.shape[0]
        full = 3 * n
        put_block(s0, own, got, not even, n)
        get_strips((strip1, strip2), (s1, s2), full, even)
        copies = []
        size = 3 * REACH
        for k, src, dst, flip in ((0, s0, s1, flip0), (1, s1, s2, flip1), (2, s2, None, flip2)):
            put_force(force, fe, pay, not even, k, n)
            base = mirrored((7 - k) * REACH, size, full, even)
            value = apply_phi(src, idx, w, base, size) + force_at(force, base, size)
            if dst is not None:
                dst[pl.ds(base, size)] = split(value)
            mine = (k + 1) * REACH
            kept = value[size - mine :] if even else value[:mine]
            copies += write_out(out, k, kept, 0 if even else n - mine, flip, sems)
        for copy in copies:
            copy.wait()

    by_parity(body)


def call(kernel, inputs, outs, scratch, spaces="", out_spaces="", aliases=None, flops=10**7, room=32):
    kinds = {"s": pltpu.SMEM, "h": pltpu.HBM, "v": pltpu.VMEM}

    def specs(arrays, letters):
        letters = letters.ljust(len(arrays), "v")
        return [pl.BlockSpec(memory_space=kinds[letter]) for letter in letters]

    moved = sum(a.size * a.dtype.itemsize for a in list(inputs) + list(outs))
    return pl.pallas_call(
        kernel,
        out_shape=outs,
        name=kernel.__name__,
        in_specs=specs(inputs, spaces),
        out_specs=specs(outs, out_spaces),
        scratch_shapes=scratch,
        input_output_aliases=aliases or {},
        compiler_params=pltpu.CompilerParams(vmem_limit_bytes=room * 1024 * 1024),
        cost_estimate=pl.CostEstimate(flops=flops, bytes_accessed=moved, transcendentals=0),
    )(*inputs)


def local(forcing, initial_state, connectivity, pattern, diag_block, face_blocks, coarse_block):
    n, width = initial_state.shape
    steps = forcing.shape[0]
    full = 3 * n
    tm = lax.axis_size("tm")
    shape = jax.ShapeDtypeStruct
    vmem = pltpu.VMEM
    dma = pltpu.SemaphoreType.DMA
    tiles = shape((n, 8, width), F32)
    state = shape((n, 16, width), BF16)
    ends = shape((n, width), F32)
    step_flops = 2 * 16 * 7 * width * 2 * width
    pay_rows = sum((COARSEN - 1 - k) * REACH * 8 for k in range(COARSEN)) + 2 * n + 16
    pay = shape((pay_rows, width), BF16)
    fe, tab, pay_even, pay_odd = call(
        pack_kernel,
        (forcing.reshape(steps // COARSEN, COARSEN, n, width), initial_state, connectivity.T, pattern.T),
        (shape((COARSEN, n * 8, width), BF16), shape((16, 128), BF16), pay, pay),
        [
            vmem((COARSEN, 8, n, width), BF16),
            vmem((8 * n, width), F32),
            vmem((n, width), F32),
            vmem((6, n), jnp.int32),
            vmem((6, n), jnp.int32),
            vmem((16, 128), F32),
            dma((COARSEN + 3,)),
        ],
        spaces="hhhh",
        room=62,
    )
    pay_odd, pay_even = swapped(pay_odd, 1), swapped(pay_even, 0)
    w, pk, we = call(
        weight_kernel,
        (diag_block, face_blocks, coarse_block),
        (
            shape((7 * width, 2 * width), BF16),
            shape((8 * width, 2 * width), BF16),
            shape(((tm - 1) * width, 2 * width), BF16),
        ),
        [],
        flops=10**9,
    )
    spaces = vmem((full + 1, 16, width), BF16)
    force = vmem((full * 8, width), BF16)
    rows = vmem((n * 8, width), F32)
    strip = shape((STRIP, 16, width), BF16)
    tables = [vmem((256, 256), BF16), vmem((256, 128), F32), vmem((128, 128), F32)]
    smem = pltpu.SMEM((8, 256), jnp.int32)
    strips = call(
        first_early_kernel,
        (fe, tab, initial_state, pay_even, w),
        (strip, strip, strip),
        [spaces] * 3 + [force, vmem((6 * REACH * 8, width), F32)] + tables + [vmem((8, 256), jnp.int32), smem, dma],
        flops=step_flops * 6 * REACH,
    )
    w1, end, idx = call(
        first_late_kernel,
        (fe, tab, initial_state, pay_even, pay_odd, *strips, w, pk),
        (tiles, ends, shape((8, 256), jnp.int32)),
        [spaces] * 3 + [force, rows] + tables + [smem, dma],
        flops=step_flops * 12 * REACH,
    )
    arrivals = earlier(end)
    (starts,) = call(scan_kernel, (w1, pk), (tiles,), [])
    (coarse,) = call(enter_first_kernel, (*arrivals, starts, we, pk), (state,), [rows])
    got_odd, got_even = swapped(coarse, 1), swapped(coarse, 0)
    *strips, moved = call(
        second_early_kernel,
        (idx, coarse, got_even, w, pk),
        (strip, strip, strip, tiles),
        [spaces] * 4,
        spaces="s",
        flops=step_flops * 12 * REACH,
    )
    res, end = call(
        second_late_kernel,
        (idx, coarse, got_odd, *strips, moved, w, pk),
        (tiles, ends),
        [spaces] * 4 + [rows],
        spaces="s",
        flops=step_flops * 16 * REACH,
    )
    arrivals = earlier(end)
    starts, total = call(scan_sum_kernel, (res, w1, moved, pk), (tiles, tiles), [])
    side = shape(((COARSEN - 1) * REACH, 16, width), BF16)
    coarse, end_even, end_odd, corr = call(
        enter_second_kernel,
        (*arrivals, starts, coarse, initial_state, we, pk),
        (state, side, side, tiles),
        [rows],
    )
    got_odd, got_even = swapped(end_odd, 1), swapped(end_even, 0)
    result = shape((steps, n, width), F32)
    flips = [vmem((8 * m * REACH, width), F32) for m in (3, 2, 1)]
    out, *strips = call(
        third_early_kernel,
        (idx, coarse, got_even, corr, total, fe, pay_even, w, pk),
        (result, strip, strip),
        [spaces] * 3 + [force] + flips + [rows, dma((COARSEN, 8))],
        spaces="s",
        out_spaces="h",
        flops=step_flops * 9 * REACH,
    )
    (out,) = call(
        third_late_kernel,
        (idx, coarse, got_odd, *strips, fe, pay_odd, w, out),
        (result,),
        [spaces] * 3 + [force] + flips[::-1] + [dma((COARSEN - 1, 8))],
        spaces="svvvvvvvh",
        out_spaces="h",
        aliases={8: 0},
        flops=step_flops * 9 * REACH,
    )
    return out


def solution(mesh):
    return jax.shard_map(
        local,
        mesh=mesh,
        in_specs=(
            P("tm", ("groups", "space"), None),
            P(("groups", "space"), None),
            P("space", None),
            P("space", None),
            P(),
            P(),
            P(),
        ),
        out_specs=P("tm", ("groups", "space"), None),
        check_vma=False,
    )
```

```python
import functools

import jax
import jax.numpy as jnp
from jax import lax
from jax.experimental import pallas as pl
from jax.experimental.pallas import tpu as pltpu
from jax.sharding import PartitionSpec as P

COARSEN = 4
REACH = 16
F32 = jnp.float32
BF16 = jnp.bfloat16
CHUNK = 32


def swapped(value, first):
    count = lax.axis_size("space")
    pairs = []
    for i in range(first, count - 1, 2):
        pairs += [(i, i + 1), (i + 1, i)]
    return lax.ppermute(value, "space", pairs)


def earlier(value):
    count = lax.axis_size("tm")
    if count <= 8:
        return [lax.ppermute(value, "tm", [(i, i + s) for i in range(count - s)]) for s in range(1, count)]
    every = lax.all_gather(value, "tm")
    at = lax.axis_index("tm") - jnp.arange(1, count)
    picked = jnp.where((at >= 0)[:, None, None], jnp.take(every, jnp.maximum(at, 0), axis=0), 0.0)
    return [picked[s] for s in range(count - 1)]


def split(u):
    lead = u.astype(BF16).astype(F32)
    return jnp.concatenate([u, u - lead], axis=1).astype(BF16)


def split_rows(u):
    lead = u.astype(BF16)
    return jnp.concatenate([lead, (u - lead.astype(F32)).astype(BF16)], axis=0)


def product(x, weights):
    m = x.shape[0] // 16
    r = jnp.dot(x, weights, preferred_element_type=F32).reshape(m, 16, 256)
    return r[:, :8, :128] + (r[:, 8:, :128] + r[:, :8, 128:])


def product_rows(x, weights):
    m = x.shape[0] // 2
    r = jnp.dot(x, weights, preferred_element_type=F32)
    return r[:m, :128] + (r[m:, :128] + r[:m, 128:])


def put_halves(ref, w):
    lead = w.astype(BF16)
    ref[:, 0:128] = lead
    ref[:, 128:256] = (w - lead.astype(F32)).astype(BF16)


def power(pk, k):
    return pk[pl.ds(128 * (7 - k), 128), :]


def scan_starts(values, pk):
    y = values
    row = lax.broadcasted_iota(jnp.int32, y.shape, 1)
    for d in (1, 2, 4):
        z = product(split(y).reshape(-1, 128), power(pk, d))
        y = y + jnp.where(row >= d, pltpu.roll(z, d, axis=1), 0.0)
    return jnp.where(row >= 1, pltpu.roll(y, 1, axis=1), 0.0)


def block_end(y, pk, n):
    parts = [y[pl.ds(i, n, stride=8), :] for i in range(8)]
    return product_rows(split_rows(jnp.concatenate(parts, axis=1)), pk[...])


def enter(arrivals, we, pk, y, n):
    value = jnp.concatenate([a[...] for a in arrivals], axis=1)
    entry = product_rows(split_rows(value), we[...])
    y[pl.ds(0, n, stride=8), :] = entry
    rows = split_rows(entry)
    for i in range(1, 8):
        y[pl.ds(i, n, stride=8), :] = product_rows(rows, power(pk, i))
    return y[...].reshape(n, 8, 128)


FIXED = {0: -1, 2: -REACH, 3: 1, 5: REACH}


def apply_phi(src, idx, masks, w, base, size):
    cols = [src[pl.ds(base, size)].reshape(size * 16, 128)]
    for f in range(6):
        if masks is not None and f in FIXED:
            near = src[pl.ds(base + FIXED[f], size)] * masks[list(FIXED).index(f), pl.ds(base, size)]
            cols.append(near.reshape(size * 16, 128))
        else:
            cols.append(jnp.concatenate([src[idx[f, base + e]] for e in range(size)], axis=0))
    return product(jnp.concatenate(cols, axis=1), w[...])


def even_place():
    return lax.rem(lax.axis_index("space"), 2) == 0


def by_parity(body):
    even = even_place()
    pl.when(even)(lambda: body(True))
    pl.when(jnp.logical_not(even))(lambda: body(False))


def mirrored(low, size, full, even):
    return full - low - size if even else low


def pack_kernel(
    forcing, init, conn, pattern, fe_out, even_out, odd_out,
    landed, rows, init_v, conn_v, pattern_v, offs, fe, pay_even, pay_odd, sems, out_sems
):
    n = init_v.shape[0]
    pitch = n + 8
    copies = [pltpu.make_async_copy(forcing.at[:, k], landed.at[k], sems.at[k]) for k in range(COARSEN)]
    small = ((conn, conn_v), (pattern, pattern_v), (init, init_v))
    copies += [pltpu.make_async_copy(src, dst, sems.at[COARSEN + i]) for i, (src, dst) in enumerate(small)]
    for copy in copies:
        copy.start()
    for copy in copies[COARSEN:]:
        copy.wait()
    place = lax.broadcasted_iota(jnp.int32, (6, n), 1) + lax.axis_index("space") * n
    value = ((conn_v[...] - place) * pattern_v[...]).astype(F32)
    offs[...] = jnp.zeros_like(offs)
    offs[0:6, 0:n] = value
    offs[0:6, n : 2 * n] = value
    tab = offs[...].astype(BF16)
    fe[pl.ds(COARSEN * n * 8, 16), :] = tab
    lead = init_v[...].astype(BF16)
    rest = (init_v[...] - lead.astype(F32)).astype(BF16)
    even = even_place()
    at = sum((COARSEN - 1 - k) * REACH * 8 for k in range(COARSEN))
    for pay in (pay_even, pay_odd):
        pay[pl.ds(at, n), :] = lead
        pay[pl.ds(at + n, n), :] = rest
        pay[pl.ds(at + 2 * n, 16), :] = tab
    at = 0
    results = []
    for k in range(COARSEN):
        copies[k].wait()
        for i in range(8):
            rows[pl.ds(i * pitch, n), :] = landed[k, i].astype(F32)

        def body(pair, carry, k=k):
            e = pair * 2
            two = [rows[pl.ds(e + j, 8, stride=pitch), :] for j in range(2)]
            fe[pl.ds(pl.multiple_of((k * n + e) * 8, 16), 16), :] = jnp.concatenate(two, axis=0).astype(BF16)
            return carry

        lax.fori_loop(0, n // 2, body, 0, unroll=8)
        width = (COARSEN - 1 - k) * REACH * 8
        if width:
            for pay, right in ((pay_even, even), (pay_odd, jnp.logical_not(even))):
                begin = pl.multiple_of(k * n * 8 + jnp.where(right, n * 8 - width, 0), 128)
                pay[pl.ds(at, width), :] = fe[pl.ds(begin, width), :]
        at += width
        if k == COARSEN - 2:
            results.append(pltpu.make_async_copy(pay_odd, odd_out, out_sems.at[0]))
            results.append(pltpu.make_async_copy(pay_even, even_out, out_sems.at[1]))
            results[0].start()
            results[1].start()
    results.append(pltpu.make_async_copy(fe, fe_out, out_sems.at[2]))
    results[2].start()
    for result in results:
        result.wait()


def weight_kernel(diag, faces, coarse, w, pk, we):
    put_halves(w.at[pl.ds(0, 128)], diag[...].T)
    for f in range(6):
        put_halves(w.at[pl.ds(128 * (f + 1), 128)], faces[f].T)

    def thirds(a):
        one = a.astype(BF16)
        rest = a - one.astype(F32)
        two = rest.astype(BF16)
        return one, two, (rest - two.astype(F32)).astype(BF16)

    def mul(a, b):
        (a1, a2, a3), (b1, b2, b3) = thirds(a), thirds(b)
        total = jnp.zeros((128, 128), F32)
        for x, y in ((a3, b1), (a1, b3), (a2, b2), (a2, b1), (a1, b2), (a1, b1)):
            total += jnp.dot(x, y, preferred_element_type=F32)
        return total

    rows = lax.broadcasted_iota(jnp.int32, (128, 128), 0)
    one = (rows == lax.broadcasted_iota(jnp.int32, (128, 128), 1)).astype(F32)
    powers = [one, coarse[...].T]
    for k in range(2, 9):
        powers.append(mul(powers[k // 2], powers[k - k // 2]))
    for k in range(8):
        put_halves(pk.at[pl.ds(128 * (7 - k), 128)], powers[k])

    def body(k, current):
        put_halves(we.at[pl.ds(pl.multiple_of(k * 128, 128), 128)], current)
        return mul(current, powers[8])

    lax.fori_loop(0, we.shape[0] // 128, body, one)


def put_force(dst, own, got, right, k, n):
    at = sum((COARSEN - 1 - j) * REACH * 8 for j in range(k))
    width = (COARSEN - 1 - k) * REACH * 8
    dst[pl.ds(n * 8, n * 8), :] = own[pl.ds(k * n * 8, n * 8), :]
    if width:
        to = 2 * n * 8 if right else n * 8 - width
        dst[pl.ds(to, width), :] = got[pl.ds(at, width), :]


def force_at(src, base, size):
    return src[pl.ds(base * 8, size * 8), :].astype(F32).reshape(size, 8, 128)


def put_tables(fe, got_even, got_odd, idx_v, columns, square, full, n, even):
    lane = lax.broadcasted_iota(jnp.int32, (8, 128), 1)

    def table(ref):
        return 0.0 if ref is None else ref[pl.ds(ref.shape[0] - 16, 16), :].astype(F32)[0:8]

    from_even, from_odd = table(got_even), table(got_odd)
    low = jnp.where(lane < n, from_odd if even else from_even, table(fe))
    high = jnp.where(lane < n, from_even if even else from_odd, 0.0)
    for at, offs in ((0, low), (128, high)):
        value = jnp.where(offs != 0.0, lane + at + offs.astype(jnp.int32), full)
        idx_v[:, pl.ds(at, 128)] = value
        square[...] = jnp.zeros_like(square)
        square[0:8, :] = value.astype(F32)
        columns[pl.ds(at, 128), :] = square[...].T


def push_init(init, got_even, got_odd, w, columns, i16, base, count, n, even):
    i16[...] = jnp.zeros_like(i16)
    lead = init[...].astype(BF16)
    i16[pl.ds(n, n), 0:128] = lead
    i16[pl.ds(n, n), 128:256] = (init[...] - lead.astype(F32)).astype(BF16)
    for ref, right in ((got_even, even), (got_odd, not even)):
        if ref is not None:
            at = ref.shape[0] - 16
            to = 2 * n if right else 0
            i16[pl.ds(to, n), 0:128] = ref[pl.ds(at - 2 * n, n), :]
            i16[pl.ds(to, n), 128:256] = ref[pl.ds(at - n, n), :]
    rows = pl.ds(base, count)
    place = columns[rows, :]
    spot = lax.broadcasted_iota(jnp.int32, (count, 256), 1).astype(F32)
    cols = [i16[rows, :]]
    for f in range(6):
        hot = (spot == place[:, f : f + 1]).astype(F32).astype(BF16)
        cols.append(jnp.dot(hot, i16[...], preferred_element_type=F32).astype(BF16))
    leads = jnp.concatenate([c[:, 0:128] for c in cols], axis=1)
    rests = jnp.concatenate([c[:, 128:256] for c in cols], axis=1)
    pushed = product_rows(jnp.concatenate([leads, rests], axis=0), w[...])
    return pushed * (lax.axis_index("tm") == 0).astype(F32)


STRIPS = (5 * REACH, 4 * REACH, 3 * REACH)
STRIP = 2 * REACH


def put_strips(strips, states, full, even):
    for strip, state, low in zip(strips, states, STRIPS):
        strip[...] = state[pl.ds(mirrored(low, STRIP, full, even), STRIP)]


def get_strips(strips, states, full, even):
    for strip, state, low in zip(strips, states, STRIPS):
        state[pl.ds(mirrored(low, STRIP, full, even), STRIP)] = strip[...]
        state[full] = jnp.zeros((16, 128), BF16)


def first_early_kernel(
    fe, init, got, w, strip1, strip2, strip3, s1, s2, s3, force, y, i16, columns, square, idx_v, idx, sem
):
    def body(even):
        n = init.shape[0]
        full = 3 * n
        put_tables(fe, got, None, idx_v, columns, square, full, n, even)
        copy = pltpu.make_async_copy(idx_v, idx, sem)
        copy.start()
        count = 6 * REACH
        base = mirrored(REACH, count, full, even)
        pushed = push_init(init, got, None, w, columns, i16, base, count, n, even)
        put_force(force, fe, got, even, 0, n)
        y[pl.ds(0, count * 8), :] = force[pl.ds(base * 8, count * 8), :].astype(F32)
        y[pl.ds(0, count, stride=8), :] = y[pl.ds(0, count, stride=8), :] + pushed
        s1[pl.ds(base, count)] = split(y[pl.ds(0, count * 8), :].reshape(count, 8, 128))
        for state in (s1, s2, s3):
            state[full] = jnp.zeros((16, 128), BF16)
        copy.wait()
        for k, src, dst in ((1, s1, s2), (2, s2, s3)):
            put_force(force, fe, got, even, k, n)
            size = (6 - 2 * k) * REACH
            base = mirrored((k + 1) * REACH, size, full, even)
            dst[pl.ds(base, size)] = split(apply_phi(src, idx, None, w, base, size) + force_at(force, base, size))
        put_strips((strip1, strip2, strip3), (s1, s2, s3), full, even)

    by_parity(body)


def first_late_kernel(
    fe, init, got_even, got_odd, strip1, strip2, strip3, w, pk, w1, end, idx_out,
    s1, s2, s3, force, y, i16, columns, square, idx, sem
):
    def body(even):
        n = init.shape[0]
        full = 3 * n
        put_tables(fe, got_even, got_odd, idx_out, columns, square, full, n, even)
        copy = pltpu.make_async_copy(idx_out, idx, sem)
        copy.start()
        count = 4 * REACH
        base = mirrored(7 * REACH, count, full, even)
        pushed = push_init(init, got_even, got_odd, w, columns, i16, base, count, n, even)
        put_force(force, fe, got_odd, not even, 0, n)
        y[...] = force[pl.ds(base * 8, count * 8), :].astype(F32)
        y[pl.ds(0, count, stride=8), :] = y[pl.ds(0, count, stride=8), :] + pushed
        s1[pl.ds(base, count)] = split(y[...].reshape(count, 8, 128))
        get_strips((strip1, strip2, strip3), (s1, s2, s3), full, even)
        copy.wait()
        for k, src, dst in ((1, s1, s2), (2, s2, s3), (3, s3, None)):
            put_force(force, fe, got_odd, not even, k, n)
            base = mirrored((7 - k) * REACH, count, full, even)
            value = apply_phi(src, idx, None, w, base, count) + force_at(force, base, count)
            if dst is None:
                w1[...] = value
                y[...] = value.reshape(n * 8, 128)
            else:
                dst[pl.ds(base, count)] = split(value)
        end[...] = block_end(y, pk, n)

    by_parity(body)


def scan_kernel(values, pk, idx, starts, masks, square, there):
    starts[...] = scan_starts(values[...], pk)
    full = masks.shape[1]
    for at in range(0, full, 128):
        square[...] = jnp.zeros_like(square)
        square[0:8, :] = (idx[:, pl.ds(at, 128)] != full).astype(F32)
        count = min(128, full - at)
        turned = square[...].T
        for m, f in enumerate(FIXED):
            there[m, pl.ds(at, count), :] = jnp.broadcast_to(turned[:count, f : f + 1], (count, 128))

    def body(e, carry):
        for m in range(len(FIXED)):
            masks[m, e] = jnp.broadcast_to(there[m, pl.ds(e, 1), :], (16, 128)).astype(BF16)
        return carry

    lax.fori_loop(REACH, full - REACH, body, 0, unroll=8)


def scan_sum_kernel(values, w1, coarse, pk, starts, total):
    starts[...] = scan_starts(values[...], pk)
    total[...] = values[...] + (w1[...] + coarse[...])


def enter_first_kernel(*refs):
    *arrivals, starts, we, pk, state, y = refs
    n = starts.shape[0]
    state[...] = split(enter(arrivals, we, pk, y, n) + starts[...])


def enter_second_kernel(*refs):
    *arrivals, starts, before, init, we, pk, state, pay_even, pay_odd, corr, y = refs
    n = starts.shape[0]
    value = enter(arrivals, we, pk, y, n) + starts[...]
    corr[...] = value
    old = before[...].astype(F32)
    y[...] = (value + (old[:, 0:8] + old[:, 8:16])).reshape(n * 8, 128)
    first = (lax.axis_index("tm") == 0).astype(F32)
    y[pl.ds(0, n, stride=8), :] = y[pl.ds(0, n, stride=8), :] + init[...] * first
    state[...] = split(y[...].reshape(n, 8, 128))
    side = (COARSEN - 1) * REACH
    even = even_place()
    pay_even[...] = state[pl.ds(jnp.where(even, n - side, 0), side)]
    pay_odd[...] = state[pl.ds(jnp.where(even, 0, n - side), side)]


def put_block(dst, own, got, right, n):
    side = got.shape[0]
    dst[pl.ds(n, n)] = own[...]
    dst[pl.ds(2 * n if right else n - side, side)] = got[...]
    dst[3 * n] = jnp.zeros((16, 128), BF16)


def second_early_kernel(idx, own, got, masks, w, pk, strip1, strip2, strip3, coarse, s0, s1, s2, s3):
    def body(even):
        n = own.shape[0]
        full = 3 * n
        coarse[...] = product(own[...].reshape(n * 16, 128), power(pk, 1))
        put_block(s0, own, got, even, n)
        for state in (s1, s2, s3):
            state[full] = jnp.zeros((16, 128), BF16)
        for k, src, dst in ((1, s0, s1), (2, s1, s2), (3, s2, s3)):
            size = (8 - 2 * k) * REACH
            base = mirrored(k * REACH, size, full, even)
            dst[pl.ds(base, size)] = split(apply_phi(src, idx, masks, w, base, size))
        put_strips((strip1, strip2, strip3), (s1, s2, s3), full, even)

    by_parity(body)


def second_late_kernel(idx, own, got, strip1, strip2, strip3, coarse, masks, w, pk, res, end, s0, s1, s2, s3, y):
    def body(even):
        n = own.shape[0]
        full = 3 * n
        put_block(s0, own, got, not even, n)
        get_strips((strip1, strip2, strip3), (s1, s2, s3), full, even)
        count = 4 * REACH
        for k, src, dst in ((1, s0, s1), (2, s1, s2), (3, s2, s3)):
            base = mirrored((8 - k) * REACH, count, full, even)
            dst[pl.ds(base, count)] = split(apply_phi(src, idx, masks, w, base, count))
        value = apply_phi(s3, idx, masks, w, n, n)
        value = value - coarse[...]
        res[...] = value
        y[...] = value.reshape(n * 8, 128)
        end[...] = block_end(y, pk, n)

    by_parity(body)


def write_out(out, k, value, begin, flip, sems):
    size = value.shape[0]
    pitch = size + 8
    for e in range(size):
        flip[pl.ds(e, 8, stride=pitch), :] = value[e]
    rows = pl.ds(begin, size)
    copies = [
        pltpu.make_async_copy(flip.at[pl.ds(i * pitch, size)], out.at[i * COARSEN + k, rows], sems.at[k, i])
        for i in range(8)
    ]
    for copy in copies:
        copy.start()
    return copies


def third_early_kernel(
    idx, own, got, corr, total, fe, pay, masks, w, pk, out, strip1, strip2, s0, s1, s2, force, flip0, flip1, flip2, flip3, sems
):
    def body(even):
        n = own.shape[0]
        full = 3 * n
        points = product(split(corr[...]).reshape(-1, 128), power(pk, 1)) + total[...]
        copies = write_out(out, COARSEN - 1, points, 0, flip3, sems)
        put_block(s0, own, got, even, n)
        for state in (s1, s2):
            state[full] = jnp.zeros((16, 128), BF16)
        for k, src, dst, flip in ((0, s0, s1, flip0), (1, s1, s2, flip1), (2, s2, None, flip2)):
            put_force(force, fe, pay, even, k, n)
            size = (5 - 2 * k) * REACH
            base = mirrored((2 + k) * REACH, size, full, even)
            value = apply_phi(src, idx, masks, w, base, size) + force_at(force, base, size)
            if dst is not None:
                dst[pl.ds(base, size)] = split(value)
            mine = (3 - k) * REACH
            skip = size - mine
            kept = value[:mine] if even else value[skip:]
            copies += write_out(out, k, kept, n - mine if even else 0, flip, sems)
        put_strips((strip1, strip2), (s1, s2), full, even)
        for copy in copies:
            copy.wait()

    by_parity(body)


def third_late_kernel(
    idx, own, got, strip1, strip2, fe, pay, masks, w, partial, out, s0, s1, s2, force, flip0, flip1, flip2, sems
):
    def body(even):
        n = own.shape[0]
        full = 3 * n
        put_block(s0, own, got, not even, n)
        get_strips((strip1, strip2), (s1, s2), full, even)
        copies = []
        size = 3 * REACH
        for k, src, dst, flip in ((0, s0, s1, flip0), (1, s1, s2, flip1), (2, s2, None, flip2)):
            put_force(force, fe, pay, not even, k, n)
            base = mirrored((7 - k) * REACH, size, full, even)
            value = apply_phi(src, idx, masks, w, base, size) + force_at(force, base, size)
            if dst is not None:
                dst[pl.ds(base, size)] = split(value)
            mine = (k + 1) * REACH
            kept = value[size - mine :] if even else value[:mine]
            copies += write_out(out, k, kept, 0 if even else n - mine, flip, sems)
        for copy in copies:
            copy.wait()

    by_parity(body)


def call(kernel, inputs, outs, scratch, spaces="", out_spaces="", aliases=None, flops=10**7, room=32):
    kinds = {"s": pltpu.SMEM, "h": pltpu.HBM, "v": pltpu.VMEM}

    def specs(arrays, letters):
        letters = letters.ljust(len(arrays), "v")
        return [pl.BlockSpec(memory_space=kinds[letter]) for letter in letters]

    moved = sum(a.size * a.dtype.itemsize for a in list(inputs) + list(outs))
    return pl.pallas_call(
        kernel,
        out_shape=outs,
        name=kernel.__name__,
        in_specs=specs(inputs, spaces),
        out_specs=specs(outs, out_spaces),
        scratch_shapes=scratch,
        input_output_aliases=aliases or {},
        compiler_params=pltpu.CompilerParams(vmem_limit_bytes=room * 1024 * 1024),
        cost_estimate=pl.CostEstimate(flops=flops, bytes_accessed=moved, transcendentals=0),
    )(*inputs)


def local(forcing, initial_state, connectivity, pattern, diag_block, face_blocks, coarse_block):
    n, width = initial_state.shape
    steps = forcing.shape[0]
    full = 3 * n
    tm = lax.axis_size("tm")
    shape = jax.ShapeDtypeStruct
    vmem = pltpu.VMEM
    dma = pltpu.SemaphoreType.DMA
    tiles = shape((n, 8, width), F32)
    state = shape((n, 16, width), BF16)
    ends = shape((n, width), F32)
    step_flops = 2 * 16 * 7 * width * 2 * width
    pay_rows = sum((COARSEN - 1 - k) * REACH * 8 for k in range(COARSEN)) + 2 * n + 16
    pay = shape((pay_rows, width), BF16)
    all_force = ((COARSEN * n * 8 + 16), width)
    fe, pay_even, pay_odd = call(
        pack_kernel,
        (forcing.reshape(steps // COARSEN, COARSEN, n, width), initial_state, connectivity.T, pattern.T),
        (shape(all_force, BF16), pay, pay),
        [
            vmem((COARSEN, 8, n, width), BF16),
            vmem((8 * (n + 8), width), F32),
            vmem((n, width), F32),
            vmem((6, n), jnp.int32),
            vmem((6, n), jnp.int32),
            vmem((16, 128), F32),
            vmem(all_force, BF16),
            vmem((pay_rows, width), BF16),
            vmem((pay_rows, width), BF16),
            dma((COARSEN + 3,)),
            dma((3,)),
        ],
        spaces="hhhh",
        out_spaces="hhh",
        room=62,
    )
    pay_odd, pay_even = swapped(pay_odd, 1), swapped(pay_even, 0)
    w, pk, we = call(
        weight_kernel,
        (diag_block, face_blocks, coarse_block),
        (
            shape((7 * width, 2 * width), BF16),
            shape((8 * width, 2 * width), BF16),
            shape(((tm - 1) * width, 2 * width), BF16),
        ),
        [],
        flops=10**9,
    )
    spaces = vmem((full + 1, 16, width), BF16)
    force = vmem((full * 8, width), BF16)
    rows = vmem((n * 8, width), F32)
    strip = shape((STRIP, 16, width), BF16)
    tables = [vmem((256, 256), BF16), vmem((256, 128), F32), vmem((128, 128), F32)]
    smem = pltpu.SMEM((8, 256), jnp.int32)
    strips = call(
        first_early_kernel,
        (fe, initial_state, pay_even, w),
        (strip, strip, strip),
        [spaces] * 3 + [force, vmem((6 * REACH * 8, width), F32)] + tables + [vmem((8, 256), jnp.int32), smem, dma],
        flops=step_flops * 6 * REACH,
    )
    w1, end, idx = call(
        first_late_kernel,
        (fe, initial_state, pay_even, pay_odd, *strips, w, pk),
        (tiles, ends, shape((8, 256), jnp.int32)),
        [spaces] * 3 + [force, rows] + tables + [smem, dma],
        flops=step_flops * 12 * REACH,
    )
    arrivals = earlier(end)
    starts, masks = call(
        scan_kernel,
        (w1, pk, idx),
        (tiles, shape((len(FIXED), full, 16, width), BF16)),
        [vmem((128, 128), F32), vmem((len(FIXED), full, width), F32)],
    )
    (coarse,) = call(enter_first_kernel, (*arrivals, starts, we, pk), (state,), [rows])
    got_odd, got_even = swapped(coarse, 1), swapped(coarse, 0)
    *strips, moved = call(
        second_early_kernel,
        (idx, coarse, got_even, masks, w, pk),
        (strip, strip, strip, tiles),
        [spaces] * 4,
        spaces="s",
        flops=step_flops * 12 * REACH,
    )
    res, end = call(
        second_late_kernel,
        (idx, coarse, got_odd, *strips, moved, masks, w, pk),
        (tiles, ends),
        [spaces] * 4 + [rows],
        spaces="s",
        flops=step_flops * 16 * REACH,
    )
    arrivals = earlier(end)
    starts, total = call(scan_sum_kernel, (res, w1, moved, pk), (tiles, tiles), [])
    side = shape(((COARSEN - 1) * REACH, 16, width), BF16)
    coarse, end_even, end_odd, corr = call(
        enter_second_kernel,
        (*arrivals, starts, coarse, initial_state, we, pk),
        (state, side, side, tiles),
        [rows],
    )
    got_odd, got_even = swapped(end_odd, 1), swapped(end_even, 0)
    result = shape((steps, n, width), F32)
    flips = [vmem((8 * (m * REACH + 8), width), F32) for m in (3, 2, 1)]
    out, *strips = call(
        third_early_kernel,
        (idx, coarse, got_even, corr, total, fe, pay_even, masks, w, pk),
        (result, strip, strip),
        [spaces] * 3 + [force] + flips + [vmem((8 * (n + 8), width), F32), dma((COARSEN, 8))],
        spaces="s",
        out_spaces="h",
        flops=step_flops * 9 * REACH,
    )
    (out,) = call(
        third_late_kernel,
        (idx, coarse, got_odd, *strips, fe, pay_odd, masks, w, out),
        (result,),
        [spaces] * 3 + [force] + flips[::-1] + [dma((COARSEN - 1, 8))],
        spaces="svvvvvvvvh",
        out_spaces="h",
        aliases={9: 0},
        flops=step_flops * 9 * REACH,
    )
    return out


def solution(mesh):
    return jax.shard_map(
        local,
        mesh=mesh,
        in_specs=(
            P("tm", ("groups", "space"), None),
            P(("groups", "space"), None),
            P("space", None),
            P("space", None),
            P(),
            P(),
            P(),
        ),
        out_specs=P("tm", ("groups", "space"), None),
        check_vma=False,
    )
```

```python
import functools

import jax
import jax.numpy as jnp
from jax import lax
from jax.experimental import pallas as pl
from jax.experimental.pallas import tpu as pltpu
from jax.sharding import PartitionSpec as P

COARSEN = 4
REACH = 16
F32 = jnp.float32
BF16 = jnp.bfloat16
CHUNK = 32


def swapped(value, first):
    count = lax.axis_size("space")
    pairs = []
    for i in range(first, count - 1, 2):
        pairs += [(i, i + 1), (i + 1, i)]
    return lax.ppermute(value, "space", pairs)


def shift_order(count):
    return (2, 3, 1) if count == 4 else tuple(range(1, count))


def earlier(value):
    count = lax.axis_size("tm")
    shifts = shift_order(count)
    if count <= 8:
        return [lax.ppermute(value, "tm", [(i, i + s) for i in range(count - s)]) for s in shifts]
    every = lax.all_gather(value, "tm")
    at = lax.axis_index("tm") - jnp.array(shifts)
    picked = jnp.where((at >= 0)[:, None, None], jnp.take(every, jnp.maximum(at, 0), axis=0), 0.0)
    return [picked[s] for s in range(count - 1)]


def split(u):
    lead = u.astype(BF16).astype(F32)
    return jnp.concatenate([u, u - lead], axis=1).astype(BF16)


def split_rows(u):
    lead = u.astype(BF16)
    return jnp.concatenate([lead, (u - lead.astype(F32)).astype(BF16)], axis=0)


def product(x, weights):
    m = x.shape[0] // 16
    r = jnp.dot(x, weights, preferred_element_type=F32).reshape(m, 16, 256)
    return r[:, :8, :128] + (r[:, 8:, :128] + r[:, :8, 128:])


def product_rows(x, weights):
    m = x.shape[0] // 2
    r = jnp.dot(x, weights, preferred_element_type=F32)
    return r[:m, :128] + (r[m:, :128] + r[:m, 128:])


def put_halves(ref, w):
    lead = w.astype(BF16)
    ref[:, 0:128] = lead
    ref[:, 128:256] = (w - lead.astype(F32)).astype(BF16)


def power(pk, k):
    return pk[pl.ds(128 * (7 - k), 128), :]


def scan_starts(values, pk):
    y = values
    row = lax.broadcasted_iota(jnp.int32, y.shape, 1)
    for d in (1, 2, 4):
        z = product(split(y).reshape(-1, 128), power(pk, d))
        y = y + jnp.where(row >= d, pltpu.roll(z, d, axis=1), 0.0)
    return jnp.where(row >= 1, pltpu.roll(y, 1, axis=1), 0.0)


def block_end(y, pk, n):
    parts = [y[pl.ds(i, n, stride=8), :] for i in range(8)]
    return product_rows(split_rows(jnp.concatenate(parts, axis=1)), pk[...])


def enter(arrivals, we, pk, y, n):
    by_shift = dict(zip(shift_order(len(arrivals) + 1), arrivals))
    value = jnp.concatenate([by_shift[shift][...] for shift in sorted(by_shift)], axis=1)
    entry = product_rows(split_rows(value), we[...])
    y[pl.ds(0, n, stride=8), :] = entry
    rows = split_rows(entry)
    for i in range(1, 8):
        y[pl.ds(i, n, stride=8), :] = product_rows(rows, power(pk, i))
    return y[...].reshape(n, 8, 128)


def apply_phi(src, idx, w, base, size):
    cols = [src[pl.ds(base, size)].reshape(size * 16, 128)]
    for f in range(6):
        cols.append(jnp.concatenate([src[idx[f, base + e]] for e in range(size)], axis=0))
    return product(jnp.concatenate(cols, axis=1), w[...])


def even_place():
    return lax.rem(lax.axis_index("space"), 2) == 0


def by_parity(body):
    even = even_place()
    pl.when(even)(lambda: body(True))
    pl.when(jnp.logical_not(even))(lambda: body(False))


def mirrored(low, size, full, even):
    return full - low - size if even else low


def pack_kernel(
    forcing, init, conn, pattern, fe_out, even_out, odd_out,
    landed, rows, init_v, conn_v, pattern_v, offs, fe, pay_even, pay_odd, sems, out_sems
):
    n = init_v.shape[0]
    pitch = n + 8
    copies = [pltpu.make_async_copy(forcing.at[:, k], landed.at[k], sems.at[k]) for k in range(COARSEN)]
    small = ((conn, conn_v), (pattern, pattern_v), (init, init_v))
    copies += [pltpu.make_async_copy(src, dst, sems.at[COARSEN + i]) for i, (src, dst) in enumerate(small)]
    for copy in copies:
        copy.start()
    for copy in copies[COARSEN:]:
        copy.wait()
    place = lax.broadcasted_iota(jnp.int32, (6, n), 1) + lax.axis_index("space") * n
    value = ((conn_v[...] - place) * pattern_v[...]).astype(F32)
    offs[...] = jnp.zeros_like(offs)
    offs[0:6, 0:n] = value
    offs[0:6, n : 2 * n] = value
    tab = offs[...].astype(BF16)
    fe[pl.ds(COARSEN * n * 8, 16), :] = tab
    lead = init_v[...].astype(BF16)
    rest = (init_v[...] - lead.astype(F32)).astype(BF16)
    even = even_place()
    at = sum((COARSEN - 1 - k) * REACH * 8 for k in range(COARSEN))
    for pay in (pay_even, pay_odd):
        pay[pl.ds(at, n), :] = lead
        pay[pl.ds(at + n, n), :] = rest
        pay[pl.ds(at + 2 * n, 16), :] = tab
    at = 0
    results = []
    for k in range(COARSEN):
        copies[k].wait()
        for i in range(8):
            rows[pl.ds(i * pitch, n), :] = landed[k, i].astype(F32)

        def body(pair, carry, k=k):
            e = pair * 2
            two = [rows[pl.ds(e + j, 8, stride=pitch), :] for j in range(2)]
            fe[pl.ds(pl.multiple_of((k * n + e) * 8, 16), 16), :] = jnp.concatenate(two, axis=0).astype(BF16)
            return carry

        lax.fori_loop(0, n // 2, body, 0, unroll=8)
        width = (COARSEN - 1 - k) * REACH * 8
        if width:
            for pay, right in ((pay_even, even), (pay_odd, jnp.logical_not(even))):
                begin = pl.multiple_of(k * n * 8 + jnp.where(right, n * 8 - width, 0), 128)
                pay[pl.ds(at, width), :] = fe[pl.ds(begin, width), :]
        at += width
        if k == COARSEN - 2:
            results.append(pltpu.make_async_copy(pay_odd, odd_out, out_sems.at[0]))
            results.append(pltpu.make_async_copy(pay_even, even_out, out_sems.at[1]))
            results[0].start()
            results[1].start()
    results.append(pltpu.make_async_copy(fe, fe_out, out_sems.at[2]))
    results[2].start()
    for result in results:
        result.wait()


def weight_kernel(diag, faces, coarse, w, pk, we):
    put_halves(w.at[pl.ds(0, 128)], diag[...].T)
    for f in range(6):
        put_halves(w.at[pl.ds(128 * (f + 1), 128)], faces[f].T)

    def thirds(a):
        one = a.astype(BF16)
        rest = a - one.astype(F32)
        two = rest.astype(BF16)
        return one, two, (rest - two.astype(F32)).astype(BF16)

    def mul(a, b):
        (a1, a2, a3), (b1, b2, b3) = thirds(a), thirds(b)
        total = jnp.zeros((128, 128), F32)
        for x, y in ((a3, b1), (a1, b3), (a2, b2), (a2, b1), (a1, b2), (a1, b1)):
            total += jnp.dot(x, y, preferred_element_type=F32)
        return total

    rows = lax.broadcasted_iota(jnp.int32, (128, 128), 0)
    one = (rows == lax.broadcasted_iota(jnp.int32, (128, 128), 1)).astype(F32)
    powers = [one, coarse[...].T]
    for k in range(2, 9):
        powers.append(mul(powers[k // 2], powers[k - k // 2]))
    for k in range(8):
        put_halves(pk.at[pl.ds(128 * (7 - k), 128)], powers[k])

    def body(k, current):
        put_halves(we.at[pl.ds(pl.multiple_of(k * 128, 128), 128)], current)
        return mul(current, powers[8])

    lax.fori_loop(0, we.shape[0] // 128, body, one)


def put_force(dst, own, got, right, k, n):
    at = sum((COARSEN - 1 - j) * REACH * 8 for j in range(k))
    width = (COARSEN - 1 - k) * REACH * 8
    dst[pl.ds(n * 8, n * 8), :] = own[pl.ds(k * n * 8, n * 8), :]
    if width:
        to = 2 * n * 8 if right else n * 8 - width
        dst[pl.ds(to, width), :] = got[pl.ds(at, width), :]


def force_at(src, base, size):
    return src[pl.ds(base * 8, size * 8), :].astype(F32).reshape(size, 8, 128)


def put_tables(fe, got_even, got_odd, idx_v, columns, square, full, n, even):
    lane = lax.broadcasted_iota(jnp.int32, (8, 128), 1)

    def table(ref):
        return 0.0 if ref is None else ref[pl.ds(ref.shape[0] - 16, 16), :].astype(F32)[0:8]

    from_even, from_odd = table(got_even), table(got_odd)
    low = jnp.where(lane < n, from_odd if even else from_even, table(fe))
    high = jnp.where(lane < n, from_even if even else from_odd, 0.0)
    for at, offs in ((0, low), (128, high)):
        value = jnp.where(offs != 0.0, lane + at + offs.astype(jnp.int32), full)
        idx_v[:, pl.ds(at, 128)] = value
        square[...] = jnp.zeros_like(square)
        square[0:8, :] = value.astype(F32)
        columns[pl.ds(at, 128), :] = square[...].T


def push_init(init, got_even, got_odd, w, columns, i16, base, count, n, even):
    i16[...] = jnp.zeros_like(i16)
    lead = init[...].astype(BF16)
    i16[pl.ds(n, n), 0:128] = lead
    i16[pl.ds(n, n), 128:256] = (init[...] - lead.astype(F32)).astype(BF16)
    for ref, right in ((got_even, even), (got_odd, not even)):
        if ref is not None:
            at = ref.shape[0] - 16
            to = 2 * n if right else 0
            i16[pl.ds(to, n), 0:128] = ref[pl.ds(at - 2 * n, n), :]
            i16[pl.ds(to, n), 128:256] = ref[pl.ds(at - n, n), :]
    rows = pl.ds(base, count)
    place = columns[rows, :]
    spot = lax.broadcasted_iota(jnp.int32, (count, 256), 1).astype(F32)
    cols = [i16[rows, :]]
    for f in range(6):
        hot = (spot == place[:, f : f + 1]).astype(F32).astype(BF16)
        cols.append(jnp.dot(hot, i16[...], preferred_element_type=F32).astype(BF16))
    leads = jnp.concatenate([c[:, 0:128] for c in cols], axis=1)
    rests = jnp.concatenate([c[:, 128:256] for c in cols], axis=1)
    pushed = product_rows(jnp.concatenate([leads, rests], axis=0), w[...])
    return pushed * (lax.axis_index("tm") == 0).astype(F32)


STRIPS = (5 * REACH, 4 * REACH, 3 * REACH)
STRIP = 2 * REACH


def put_strips(strips, states, full, even):
    for strip, state, low in zip(strips, states, STRIPS):
        strip[...] = state[pl.ds(mirrored(low, STRIP, full, even), STRIP)]


def get_strips(strips, states, full, even):
    for strip, state, low in zip(strips, states, STRIPS):
        state[pl.ds(mirrored(low, STRIP, full, even), STRIP)] = strip[...]
        state[full] = jnp.zeros((16, 128), BF16)


def first_early_kernel(
    fe, init, got, w, strip1, strip2, strip3, s1, s2, s3, force, y, i16, columns, square, idx_v, idx, sem
):
    def body(even):
        n = init.shape[0]
        full = 3 * n
        put_tables(fe, got, None, idx_v, columns, square, full, n, even)
        copy = pltpu.make_async_copy(idx_v, idx, sem)
        copy.start()
        count = 6 * REACH
        base = mirrored(REACH, count, full, even)
        pushed = push_init(init, got, None, w, columns, i16, base, count, n, even)
        put_force(force, fe, got, even, 0, n)
        y[pl.ds(0, count * 8), :] = force[pl.ds(base * 8, count * 8), :].astype(F32)
        y[pl.ds(0, count, stride=8), :] = y[pl.ds(0, count, stride=8), :] + pushed
        s1[pl.ds(base, count)] = split(y[pl.ds(0, count * 8), :].reshape(count, 8, 128))
        for state in (s1, s2, s3):
            state[full] = jnp.zeros((16, 128), BF16)
        copy.wait()
        for k, src, dst in ((1, s1, s2), (2, s2, s3)):
            put_force(force, fe, got, even, k, n)
            size = (6 - 2 * k) * REACH
            base = mirrored((k + 1) * REACH, size, full, even)
            dst[pl.ds(base, size)] = split(apply_phi(src, idx, w, base, size) + force_at(force, base, size))
        put_strips((strip1, strip2, strip3), (s1, s2, s3), full, even)

    by_parity(body)


def first_late_kernel(
    fe, init, got_even, got_odd, strip1, strip2, strip3, w, pk, w1, end, idx_out,
    s1, s2, s3, force, y, i16, columns, square, idx, sem
):
    def body(even):
        n = init.shape[0]
        full = 3 * n
        put_tables(fe, got_even, got_odd, idx_out, columns, square, full, n, even)
        copy = pltpu.make_async_copy(idx_out, idx, sem)
        copy.start()
        count = 4 * REACH
        base = mirrored(7 * REACH, count, full, even)
        pushed = push_init(init, got_even, got_odd, w, columns, i16, base, count, n, even)
        put_force(force, fe, got_odd, not even, 0, n)
        y[...] = force[pl.ds(base * 8, count * 8), :].astype(F32)
        y[pl.ds(0, count, stride=8), :] = y[pl.ds(0, count, stride=8), :] + pushed
        s1[pl.ds(base, count)] = split(y[...].reshape(count, 8, 128))
        get_strips((strip1, strip2, strip3), (s1, s2, s3), full, even)
        copy.wait()
        for k, src, dst in ((1, s1, s2), (2, s2, s3), (3, s3, None)):
            put_force(force, fe, got_odd, not even, k, n)
            base = mirrored((7 - k) * REACH, count, full, even)
            value = apply_phi(src, idx, w, base, count) + force_at(force, base, count)
            if dst is None:
                w1[...] = value
                y[...] = value.reshape(n * 8, 128)
            else:
                dst[pl.ds(base, count)] = split(value)
        end[...] = block_end(y, pk, n)

    by_parity(body)


def scan_kernel(values, pk, starts):
    starts[...] = scan_starts(values[...], pk)


def scan_sum_kernel(values, w1, coarse, pk, starts, total):
    starts[...] = scan_starts(values[...], pk)
    total[...] = values[...] + (w1[...] + coarse[...])


def enter_first_kernel(*refs):
    *arrivals, starts, we, pk, state, y = refs
    n = starts.shape[0]
    state[...] = split(enter(arrivals, we, pk, y, n) + starts[...])


def enter_second_kernel(*refs):
    *arrivals, starts, before, init, we, pk, state, pay_even, pay_odd, corr, y = refs
    n = starts.shape[0]
    value = enter(arrivals, we, pk, y, n) + starts[...]
    corr[...] = value
    old = before[...].astype(F32)
    y[...] = (value + (old[:, 0:8] + old[:, 8:16])).reshape(n * 8, 128)
    first = (lax.axis_index("tm") == 0).astype(F32)
    y[pl.ds(0, n, stride=8), :] = y[pl.ds(0, n, stride=8), :] + init[...] * first
    state[...] = split(y[...].reshape(n, 8, 128))
    side = (COARSEN - 1) * REACH
    even = even_place()
    pay_even[...] = state[pl.ds(jnp.where(even, n - side, 0), side)]
    pay_odd[...] = state[pl.ds(jnp.where(even, 0, n - side), side)]


def put_block(dst, own, got, right, n):
    side = got.shape[0]
    dst[pl.ds(n, n)] = own[...]
    dst[pl.ds(2 * n if right else n - side, side)] = got[...]
    dst[3 * n] = jnp.zeros((16, 128), BF16)


def second_early_kernel(idx, own, got, w, pk, strip1, strip2, strip3, coarse, s0, s1, s2, s3):
    def body(even):
        n = own.shape[0]
        full = 3 * n
        coarse[...] = product(own[...].reshape(n * 16, 128), power(pk, 1))
        put_block(s0, own, got, even, n)
        for state in (s1, s2, s3):
            state[full] = jnp.zeros((16, 128), BF16)
        for k, src, dst in ((1, s0, s1), (2, s1, s2), (3, s2, s3)):
            size = (8 - 2 * k) * REACH
            base = mirrored(k * REACH, size, full, even)
            dst[pl.ds(base, size)] = split(apply_phi(src, idx, w, base, size))
        put_strips((strip1, strip2, strip3), (s1, s2, s3), full, even)

    by_parity(body)


def second_late_kernel(idx, own, got, strip1, strip2, strip3, coarse, w, pk, res, end, s0, s1, s2, s3, y):
    def body(even):
        n = own.shape[0]
        full = 3 * n
        put_block(s0, own, got, not even, n)
        get_strips((strip1, strip2, strip3), (s1, s2, s3), full, even)
        count = 4 * REACH
        for k, src, dst in ((1, s0, s1), (2, s1, s2), (3, s2, s3)):
            base = mirrored((8 - k) * REACH, count, full, even)
            dst[pl.ds(base, count)] = split(apply_phi(src, idx, w, base, count))
        value = apply_phi(s3, idx, w, n, n)
        value = value - coarse[...]
        res[...] = value
        y[...] = value.reshape(n * 8, 128)
        end[...] = block_end(y, pk, n)

    by_parity(body)


def write_out(out, k, value, begin, flip, sems):
    size = value.shape[0]
    pitch = size + 8
    for e in range(size):
        flip[pl.ds(e, 8, stride=pitch), :] = value[e]
    rows = pl.ds(begin, size)
    copies = [
        pltpu.make_async_copy(flip.at[pl.ds(i * pitch, size)], out.at[i * COARSEN + k, rows], sems.at[k, i])
        for i in range(8)
    ]
    for copy in copies:
        copy.start()
    return copies


def third_early_kernel(
    idx, own, got, corr, total, fe, pay, w, pk, out, strip1, strip2, s0, s1, s2, force, flip0, flip1, flip2, flip3, sems
):
    def body(even):
        n = own.shape[0]
        full = 3 * n
        points = product(split(corr[...]).reshape(-1, 128), power(pk, 1)) + total[...]
        copies = write_out(out, COARSEN - 1, points, 0, flip3, sems)
        put_block(s0, own, got, even, n)
        for state in (s1, s2):
            state[full] = jnp.zeros((16, 128), BF16)
        for k, src, dst, flip in ((0, s0, s1, flip0), (1, s1, s2, flip1), (2, s2, None, flip2)):
            put_force(force, fe, pay, even, k, n)
            size = (5 - 2 * k) * REACH
            base = mirrored((2 + k) * REACH, size, full, even)
            value = apply_phi(src, idx, w, base, size) + force_at(force, base, size)
            if dst is not None:
                dst[pl.ds(base, size)] = split(value)
            mine = (3 - k) * REACH
            skip = size - mine
            kept = value[:mine] if even else value[skip:]
            copies += write_out(out, k, kept, n - mine if even else 0, flip, sems)
        put_strips((strip1, strip2), (s1, s2), full, even)
        for copy in copies:
            copy.wait()

    by_parity(body)


def third_late_kernel(
    idx, own, got, strip1, strip2, fe, pay, w, partial, out, s0, s1, s2, force, flip0, flip1, flip2, sems
):
    def body(even):
        n = own.shape[0]
        full = 3 * n
        put_block(s0, own, got, not even, n)
        get_strips((strip1, strip2), (s1, s2), full, even)
        copies = []
        size = 3 * REACH
        for k, src, dst, flip in ((0, s0, s1, flip0), (1, s1, s2, flip1), (2, s2, None, flip2)):
            put_force(force, fe, pay, not even, k, n)
            base = mirrored((7 - k) * REACH, size, full, even)
            value = apply_phi(src, idx, w, base, size) + force_at(force, base, size)
            if dst is not None:
                dst[pl.ds(base, size)] = split(value)
            mine = (k + 1) * REACH
            kept = value[size - mine :] if even else value[:mine]
            copies += write_out(out, k, kept, 0 if even else n - mine, flip, sems)
        for copy in copies:
            copy.wait()

    by_parity(body)


def call(kernel, inputs, outs, scratch, spaces="", out_spaces="", aliases=None, flops=10**7, room=32):
    kinds = {"s": pltpu.SMEM, "h": pltpu.HBM, "v": pltpu.VMEM}

    def specs(arrays, letters):
        letters = letters.ljust(len(arrays), "v")
        return [pl.BlockSpec(memory_space=kinds[letter]) for letter in letters]

    moved = sum(a.size * a.dtype.itemsize for a in list(inputs) + list(outs))
    return pl.pallas_call(
        kernel,
        out_shape=outs,
        name=kernel.__name__,
        in_specs=specs(inputs, spaces),
        out_specs=specs(outs, out_spaces),
        scratch_shapes=scratch,
        input_output_aliases=aliases or {},
        compiler_params=pltpu.CompilerParams(vmem_limit_bytes=room * 1024 * 1024),
        cost_estimate=pl.CostEstimate(flops=flops, bytes_accessed=moved, transcendentals=0),
    )(*inputs)


def local(forcing, initial_state, connectivity, pattern, diag_block, face_blocks, coarse_block):
    n, width = initial_state.shape
    steps = forcing.shape[0]
    full = 3 * n
    tm = lax.axis_size("tm")
    shape = jax.ShapeDtypeStruct
    vmem = pltpu.VMEM
    dma = pltpu.SemaphoreType.DMA
    tiles = shape((n, 8, width), F32)
    state = shape((n, 16, width), BF16)
    ends = shape((n, width), F32)
    step_flops = 2 * 16 * 7 * width * 2 * width
    pay_rows = sum((COARSEN - 1 - k) * REACH * 8 for k in range(COARSEN)) + 2 * n + 16
    pay = shape((pay_rows, width), BF16)
    all_force = ((COARSEN * n * 8 + 16), width)
    fe, pay_even, pay_odd = call(
        pack_kernel,
        (forcing.reshape(steps // COARSEN, COARSEN, n, width), initial_state, connectivity.T, pattern.T),
        (shape(all_force, BF16), pay, pay),
        [
            vmem((COARSEN, 8, n, width), BF16),
            vmem((8 * (n + 8), width), F32),
            vmem((n, width), F32),
            vmem((6, n), jnp.int32),
            vmem((6, n), jnp.int32),
            vmem((16, 128), F32),
            vmem(all_force, BF16),
            vmem((pay_rows, width), BF16),
            vmem((pay_rows, width), BF16),
            dma((COARSEN + 3,)),
            dma((3,)),
        ],
        spaces="hhhh",
        flops=3 * 10**9,
        out_spaces="hhh",
        room=62,
    )
    pay_odd, pay_even = swapped(pay_odd, 1), swapped(pay_even, 0)
    w, pk, we = call(
        weight_kernel,
        (diag_block, face_blocks, coarse_block),
        (
            shape((7 * width, 2 * width), BF16),
            shape((8 * width, 2 * width), BF16),
            shape(((tm - 1) * width, 2 * width), BF16),
        ),
        [],
        flops=10**9,
    )
    spaces = vmem((full + 1, 16, width), BF16)
    force = vmem((full * 8, width), BF16)
    rows = vmem((n * 8, width), F32)
    strip = shape((STRIP, 16, width), BF16)
    tables = [vmem((256, 256), BF16), vmem((256, 128), F32), vmem((128, 128), F32)]
    smem = pltpu.SMEM((8, 256), jnp.int32)
    strips = call(
        first_early_kernel,
        (fe, initial_state, pay_even, w),
        (strip, strip, strip),
        [spaces] * 3 + [force, vmem((6 * REACH * 8, width), F32)] + tables + [vmem((8, 256), jnp.int32), smem, dma],
        flops=step_flops * 6 * REACH,
    )
    w1, end, idx = call(
        first_late_kernel,
        (fe, initial_state, pay_even, pay_odd, *strips, w, pk),
        (tiles, ends, shape((8, 256), jnp.int32)),
        [spaces] * 3 + [force, rows] + tables + [smem, dma],
        flops=step_flops * 12 * REACH,
    )
    arrivals = earlier(end)
    (starts,) = call(scan_kernel, (w1, pk), (tiles,), [])
    (coarse,) = call(enter_first_kernel, (*arrivals, starts, we, pk), (state,), [rows])
    got_odd, got_even = swapped(coarse, 1), swapped(coarse, 0)
    *strips, moved = call(
        second_early_kernel,
        (idx, coarse, got_even, w, pk),
        (strip, strip, strip, tiles),
        [spaces] * 4,
        spaces="s",
        flops=step_flops * 12 * REACH,
    )
    res, end = call(
        second_late_kernel,
        (idx, coarse, got_odd, *strips, moved, w, pk),
        (tiles, ends),
        [spaces] * 4 + [rows],
        spaces="s",
        flops=step_flops * 16 * REACH,
    )
    arrivals = earlier(end)
    starts, total = call(scan_sum_kernel, (res, w1, moved, pk), (tiles, tiles), [])
    side = shape(((COARSEN - 1) * REACH, 16, width), BF16)
    coarse, end_even, end_odd, corr = call(
        enter_second_kernel,
        (*arrivals, starts, coarse, initial_state, we, pk),
        (state, side, side, tiles),
        [rows],
    )
    got_odd, got_even = swapped(end_odd, 1), swapped(end_even, 0)
    result = shape((steps, n, width), F32)
    flips = [vmem((8 * (m * REACH + 8), width), F32) for m in (3, 2, 1)]
    out, *strips = call(
        third_early_kernel,
        (idx, coarse, got_even, corr, total, fe, pay_even, w, pk),
        (result, strip, strip),
        [spaces] * 3 + [force] + flips + [vmem((8 * (n + 8), width), F32), dma((COARSEN, 8))],
        spaces="s",
        out_spaces="h",
        flops=step_flops * 9 * REACH,
    )
    (out,) = call(
        third_late_kernel,
        (idx, coarse, got_odd, *strips, fe, pay_odd, w, out),
        (result,),
        [spaces] * 3 + [force] + flips[::-1] + [dma((COARSEN - 1, 8))],
        spaces="svvvvvvvh",
        out_spaces="h",
        aliases={8: 0},
        flops=step_flops * 9 * REACH,
    )
    return out


def solution(mesh):
    return jax.shard_map(
        local,
        mesh=mesh,
        in_specs=(
            P("tm", ("groups", "space"), None),
            P(("groups", "space"), None),
            P("space", None),
            P("space", None),
            P(),
            P(),
            P(),
        ),
        out_specs=P("tm", ("groups", "space"), None),
        check_vma=False,
    )
```

```python
import functools

import jax
import jax.numpy as jnp
from jax import lax
from jax.experimental import pallas as pl
from jax.experimental.pallas import tpu as pltpu
from jax.sharding import PartitionSpec as P

COARSEN = 4
REACH = 16
F32 = jnp.float32
BF16 = jnp.bfloat16
CHUNK = 32


def swapped(value, first):
    count = lax.axis_size("space")
    pairs = []
    for i in range(first, count - 1, 2):
        pairs += [(i, i + 1), (i + 1, i)]
    return lax.ppermute(value, "space", pairs)


def shift_order(count):
    return (2, 1, 3) if count == 4 else tuple(range(1, count))


def earlier(value):
    count = lax.axis_size("tm")
    shifts = shift_order(count)
    if count <= 8:
        return [lax.ppermute(value, "tm", [(i, i + s) for i in range(count - s)]) for s in shifts]
    every = lax.all_gather(value, "tm")
    at = lax.axis_index("tm") - jnp.array(shifts)
    picked = jnp.where((at >= 0)[:, None, None], jnp.take(every, jnp.maximum(at, 0), axis=0), 0.0)
    return [picked[s] for s in range(count - 1)]


def split(u):
    lead = u.astype(BF16).astype(F32)
    return jnp.concatenate([u, u - lead], axis=1).astype(BF16)


def split_rows(u):
    lead = u.astype(BF16)
    return jnp.concatenate([lead, (u - lead.astype(F32)).astype(BF16)], axis=0)


def product(x, weights):
    m = x.shape[0] // 16
    r = jnp.dot(x, weights, preferred_element_type=F32).reshape(m, 16, 256)
    return r[:, :8, :128] + (r[:, 8:, :128] + r[:, :8, 128:])


def product_rows(x, weights):
    m = x.shape[0] // 2
    r = jnp.dot(x, weights, preferred_element_type=F32)
    return r[:m, :128] + (r[m:, :128] + r[:m, 128:])


def put_halves(ref, w):
    lead = w.astype(BF16)
    ref[:, 0:128] = lead
    ref[:, 128:256] = (w - lead.astype(F32)).astype(BF16)


def power(pk, k):
    return pk[pl.ds(128 * (7 - k), 128), :]


def scan_starts(values, pk):
    y = values
    row = lax.broadcasted_iota(jnp.int32, y.shape, 1)
    for d in (1, 2, 4):
        z = product(split(y).reshape(-1, 128), power(pk, d))
        y = y + jnp.where(row >= d, pltpu.roll(z, d, axis=1), 0.0)
    return jnp.where(row >= 1, pltpu.roll(y, 1, axis=1), 0.0)


def block_end(y, pk, n):
    parts = [y[pl.ds(i, n, stride=8), :] for i in range(8)]
    return product_rows(split_rows(jnp.concatenate(parts, axis=1)), pk[...])


def enter(arrivals, we, pk, y, n):
    by_shift = dict(zip(shift_order(len(arrivals) + 1), arrivals))
    value = jnp.concatenate([by_shift[shift][...] for shift in sorted(by_shift)], axis=1)
    entry = product_rows(split_rows(value), we[...])
    y[pl.ds(0, n, stride=8), :] = entry
    rows = split_rows(entry)
    for i in range(1, 8):
        y[pl.ds(i, n, stride=8), :] = product_rows(rows, power(pk, i))
    return y[...].reshape(n, 8, 128)


def apply_phi(src, idx, w, base, size):
    cols = [src[pl.ds(base, size)].reshape(size * 16, 128)]
    for f in range(6):
        cols.append(jnp.concatenate([src[idx[f, base + e]] for e in range(size)], axis=0))
    return product(jnp.concatenate(cols, axis=1), w[...])


def even_place():
    return lax.rem(lax.axis_index("space"), 2) == 0


def by_parity(body):
    even = even_place()
    pl.when(even)(lambda: body(True))
    pl.when(jnp.logical_not(even))(lambda: body(False))


def mirrored(low, size, full, even):
    return full - low - size if even else low


def pack_kernel(
    forcing, init, conn, pattern, fe_out, even_out, odd_out,
    landed, rows, init_v, conn_v, pattern_v, offs, fe, pay_even, pay_odd, sems, out_sems
):
    n = init_v.shape[0]
    pitch = n + 8
    copies = [pltpu.make_async_copy(forcing.at[:, k], landed.at[k], sems.at[k]) for k in range(COARSEN)]
    small = ((conn, conn_v), (pattern, pattern_v), (init, init_v))
    copies += [pltpu.make_async_copy(src, dst, sems.at[COARSEN + i]) for i, (src, dst) in enumerate(small)]
    for copy in copies:
        copy.start()
    for copy in copies[COARSEN:]:
        copy.wait()
    place = lax.broadcasted_iota(jnp.int32, (6, n), 1) + lax.axis_index("space") * n
    value = ((conn_v[...] - place) * pattern_v[...]).astype(F32)
    offs[...] = jnp.zeros_like(offs)
    offs[0:6, 0:n] = value
    offs[0:6, n : 2 * n] = value
    tab = offs[...].astype(BF16)
    fe[pl.ds(COARSEN * n * 8, 16), :] = tab
    lead = init_v[...].astype(BF16)
    rest = (init_v[...] - lead.astype(F32)).astype(BF16)
    even = even_place()
    at = sum((COARSEN - 1 - k) * REACH * 8 for k in range(COARSEN))
    for pay in (pay_even, pay_odd):
        pay[pl.ds(at, n), :] = lead
        pay[pl.ds(at + n, n), :] = rest
        pay[pl.ds(at + 2 * n, 16), :] = tab
    at = 0
    results = []
    for k in range(COARSEN):
        copies[k].wait()
        for i in range(8):
            rows[pl.ds(i * pitch, n), :] = landed[k, i].astype(F32)

        def body(pair, carry, k=k):
            e = pair * 2
            two = [rows[pl.ds(e + j, 8, stride=pitch), :] for j in range(2)]
            fe[pl.ds(pl.multiple_of((k * n + e) * 8, 16), 16), :] = jnp.concatenate(two, axis=0).astype(BF16)
            return carry

        lax.fori_loop(0, n // 2, body, 0, unroll=8)
        width = (COARSEN - 1 - k) * REACH * 8
        if width:
            for pay, right in ((pay_even, even), (pay_odd, jnp.logical_not(even))):
                begin = pl.multiple_of(k * n * 8 + jnp.where(right, n * 8 - width, 0), 128)
                pay[pl.ds(at, width), :] = fe[pl.ds(begin, width), :]
        at += width
        if k == COARSEN - 2:
            results.append(pltpu.make_async_copy(pay_odd, odd_out, out_sems.at[0]))
            results.append(pltpu.make_async_copy(pay_even, even_out, out_sems.at[1]))
            results[0].start()
            results[1].start()
    results.append(pltpu.make_async_copy(fe, fe_out, out_sems.at[2]))
    results[2].start()
    for result in results:
        result.wait()


def weight_kernel(diag, faces, coarse, w, pk, we):
    put_halves(w.at[pl.ds(0, 128)], diag[...].T)
    for f in range(6):
        put_halves(w.at[pl.ds(128 * (f + 1), 128)], faces[f].T)

    def thirds(a):
        one = a.astype(BF16)
        rest = a - one.astype(F32)
        two = rest.astype(BF16)
        return one, two, (rest - two.astype(F32)).astype(BF16)

    def mul(a, b):
        (a1, a2, a3), (b1, b2, b3) = thirds(a), thirds(b)
        total = jnp.zeros((128, 128), F32)
        for x, y in ((a3, b1), (a1, b3), (a2, b2), (a2, b1), (a1, b2), (a1, b1)):
            total += jnp.dot(x, y, preferred_element_type=F32)
        return total

    rows = lax.broadcasted_iota(jnp.int32, (128, 128), 0)
    one = (rows == lax.broadcasted_iota(jnp.int32, (128, 128), 1)).astype(F32)
    powers = [one, coarse[...].T]
    for k in range(2, 9):
        powers.append(mul(powers[k // 2], powers[k - k // 2]))
    for k in range(8):
        put_halves(pk.at[pl.ds(128 * (7 - k), 128)], powers[k])

    def body(k, current):
        put_halves(we.at[pl.ds(pl.multiple_of(k * 128, 128), 128)], current)
        return mul(current, powers[8])

    lax.fori_loop(0, we.shape[0] // 128, body, one)


def put_force(dst, own, got, right, k, n):
    at = sum((COARSEN - 1 - j) * REACH * 8 for j in range(k))
    width = (COARSEN - 1 - k) * REACH * 8
    dst[pl.ds(n * 8, n * 8), :] = own[pl.ds(k * n * 8, n * 8), :]
    if width:
        to = 2 * n * 8 if right else n * 8 - width
        dst[pl.ds(to, width), :] = got[pl.ds(at, width), :]


def force_at(src, base, size):
    return src[pl.ds(base * 8, size * 8), :].astype(F32).reshape(size, 8, 128)


def put_tables(fe, got_even, got_odd, idx_v, columns, square, full, n, even):
    lane = lax.broadcasted_iota(jnp.int32, (8, 128), 1)

    def table(ref):
        return 0.0 if ref is None else ref[pl.ds(ref.shape[0] - 16, 16), :].astype(F32)[0:8]

    from_even, from_odd = table(got_even), table(got_odd)
    low = jnp.where(lane < n, from_odd if even else from_even, table(fe))
    high = jnp.where(lane < n, from_even if even else from_odd, 0.0)
    for at, offs in ((0, low), (128, high)):
        value = jnp.where(offs != 0.0, lane + at + offs.astype(jnp.int32), full)
        idx_v[:, pl.ds(at, 128)] = value
        square[...] = jnp.zeros_like(square)
        square[0:8, :] = value.astype(F32)
        columns[pl.ds(at, 128), :] = square[...].T


def push_init(init, got_even, got_odd, w, columns, i16, base, count, n, even):
    i16[...] = jnp.zeros_like(i16)
    lead = init[...].astype(BF16)
    i16[pl.ds(n, n), 0:128] = lead
    i16[pl.ds(n, n), 128:256] = (init[...] - lead.astype(F32)).astype(BF16)
    for ref, right in ((got_even, even), (got_odd, not even)):
        if ref is not None:
            at = ref.shape[0] - 16
            to = 2 * n if right else 0
            i16[pl.ds(to, n), 0:128] = ref[pl.ds(at - 2 * n, n), :]
            i16[pl.ds(to, n), 128:256] = ref[pl.ds(at - n, n), :]
    rows = pl.ds(base, count)
    place = columns[rows, :]
    spot = lax.broadcasted_iota(jnp.int32, (count, 256), 1).astype(F32)
    cols = [i16[rows, :]]
    for f in range(6):
        hot = (spot == place[:, f : f + 1]).astype(F32).astype(BF16)
        cols.append(jnp.dot(hot, i16[...], preferred_element_type=F32).astype(BF16))
    leads = jnp.concatenate([c[:, 0:128] for c in cols], axis=1)
    rests = jnp.concatenate([c[:, 128:256] for c in cols], axis=1)
    pushed = product_rows(jnp.concatenate([leads, rests], axis=0), w[...])
    return pushed * (lax.axis_index("tm") == 0).astype(F32)


STRIPS = (5 * REACH, 4 * REACH, 3 * REACH)
STRIP = 2 * REACH


def put_strips(strips, states, full, even):
    for strip, state, low in zip(strips, states, STRIPS):
        strip[...] = state[pl.ds(mirrored(low, STRIP, full, even), STRIP)]


def get_strips(strips, states, full, even):
    for strip, state, low in zip(strips, states, STRIPS):
        state[pl.ds(mirrored(low, STRIP, full, even), STRIP)] = strip[...]
        state[full] = jnp.zeros((16, 128), BF16)


def first_early_kernel(
    fe, init, got, w, strip1, strip2, strip3, s1, s2, s3, force, y, i16, columns, square, idx_v, idx, sem
):
    def body(even):
        n = init.shape[0]
        full = 3 * n
        put_tables(fe, got, None, idx_v, columns, square, full, n, even)
        copy = pltpu.make_async_copy(idx_v, idx, sem)
        copy.start()
        count = 6 * REACH
        base = mirrored(REACH, count, full, even)
        pushed = push_init(init, got, None, w, columns, i16, base, count, n, even)
        put_force(force, fe, got, even, 0, n)
        y[pl.ds(0, count * 8), :] = force[pl.ds(base * 8, count * 8), :].astype(F32)
        y[pl.ds(0, count, stride=8), :] = y[pl.ds(0, count, stride=8), :] + pushed
        s1[pl.ds(base, count)] = split(y[pl.ds(0, count * 8), :].reshape(count, 8, 128))
        for state in (s1, s2, s3):
            state[full] = jnp.zeros((16, 128), BF16)
        copy.wait()
        for k, src, dst in ((1, s1, s2), (2, s2, s3)):
            put_force(force, fe, got, even, k, n)
            size = (6 - 2 * k) * REACH
            base = mirrored((k + 1) * REACH, size, full, even)
            dst[pl.ds(base, size)] = split(apply_phi(src, idx, w, base, size) + force_at(force, base, size))
        put_strips((strip1, strip2, strip3), (s1, s2, s3), full, even)

    by_parity(body)


def first_late_kernel(
    fe, init, got_even, got_odd, strip1, strip2, strip3, w, pk, w1, end, idx_out,
    s1, s2, s3, force, y, i16, columns, square, idx, sem
):
    def body(even):
        n = init.shape[0]
        full = 3 * n
        put_tables(fe, got_even, got_odd, idx_out, columns, square, full, n, even)
        copy = pltpu.make_async_copy(idx_out, idx, sem)
        copy.start()
        count = 4 * REACH
        base = mirrored(7 * REACH, count, full, even)
        pushed = push_init(init, got_even, got_odd, w, columns, i16, base, count, n, even)
        put_force(force, fe, got_odd, not even, 0, n)
        y[...] = force[pl.ds(base * 8, count * 8), :].astype(F32)
        y[pl.ds(0, count, stride=8), :] = y[pl.ds(0, count, stride=8), :] + pushed
        s1[pl.ds(base, count)] = split(y[...].reshape(count, 8, 128))
        get_strips((strip1, strip2, strip3), (s1, s2, s3), full, even)
        copy.wait()
        for k, src, dst in ((1, s1, s2), (2, s2, s3), (3, s3, None)):
            put_force(force, fe, got_odd, not even, k, n)
            base = mirrored((7 - k) * REACH, count, full, even)
            value = apply_phi(src, idx, w, base, count) + force_at(force, base, count)
            if dst is None:
                w1[...] = value
                y[...] = value.reshape(n * 8, 128)
            else:
                dst[pl.ds(base, count)] = split(value)
        end[...] = block_end(y, pk, n)

    by_parity(body)


def scan_kernel(values, pk, starts):
    starts[...] = scan_starts(values[...], pk)


def scan_sum_kernel(values, w1, coarse, pk, starts, total):
    starts[...] = scan_starts(values[...], pk)
    total[...] = values[...] + (w1[...] + coarse[...])


def enter_first_kernel(*refs):
    *arrivals, starts, we, pk, state, y = refs
    n = starts.shape[0]
    state[...] = split(enter(arrivals, we, pk, y, n) + starts[...])


def enter_second_kernel(*refs):
    *arrivals, starts, before, init, we, pk, state, pay_even, pay_odd, corr, y = refs
    n = starts.shape[0]
    value = enter(arrivals, we, pk, y, n) + starts[...]
    corr[...] = value
    old = before[...].astype(F32)
    y[...] = (value + (old[:, 0:8] + old[:, 8:16])).reshape(n * 8, 128)
    first = (lax.axis_index("tm") == 0).astype(F32)
    y[pl.ds(0, n, stride=8), :] = y[pl.ds(0, n, stride=8), :] + init[...] * first
    state[...] = split(y[...].reshape(n, 8, 128))
    side = (COARSEN - 1) * REACH
    even = even_place()
    pay_even[...] = state[pl.ds(jnp.where(even, n - side, 0), side)]
    pay_odd[...] = state[pl.ds(jnp.where(even, 0, n - side), side)]


def put_block(dst, own, got, right, n):
    side = got.shape[0]
    dst[pl.ds(n, n)] = own[...]
    dst[pl.ds(2 * n if right else n - side, side)] = got[...]
    dst[3 * n] = jnp.zeros((16, 128), BF16)


def second_early_kernel(idx, own, got, w, pk, strip1, strip2, strip3, coarse, s0, s1, s2, s3):
    def body(even):
        n = own.shape[0]
        full = 3 * n
        coarse[...] = product(own[...].reshape(n * 16, 128), power(pk, 1))
        put_block(s0, own, got, even, n)
        for state in (s1, s2, s3):
            state[full] = jnp.zeros((16, 128), BF16)
        for k, src, dst in ((1, s0, s1), (2, s1, s2), (3, s2, s3)):
            size = (8 - 2 * k) * REACH
            base = mirrored(k * REACH, size, full, even)
            dst[pl.ds(base, size)] = split(apply_phi(src, idx, w, base, size))
        put_strips((strip1, strip2, strip3), (s1, s2, s3), full, even)

    by_parity(body)


def second_late_kernel(idx, own, got, strip1, strip2, strip3, coarse, w, pk, res, end, s0, s1, s2, s3, y):
    def body(even):
        n = own.shape[0]
        full = 3 * n
        put_block(s0, own, got, not even, n)
        get_strips((strip1, strip2, strip3), (s1, s2, s3), full, even)
        count = 4 * REACH
        for k, src, dst in ((1, s0, s1), (2, s1, s2), (3, s2, s3)):
            base = mirrored((8 - k) * REACH, count, full, even)
            dst[pl.ds(base, count)] = split(apply_phi(src, idx, w, base, count))
        value = apply_phi(s3, idx, w, n, n)
        value = value - coarse[...]
        res[...] = value
        y[...] = value.reshape(n * 8, 128)
        end[...] = block_end(y, pk, n)

    by_parity(body)


def write_out(out, k, value, begin, flip, sems):
    size = value.shape[0]
    pitch = size + 8
    for e in range(size):
        flip[pl.ds(e, 8, stride=pitch), :] = value[e]
    rows = pl.ds(begin, size)
    copies = [
        pltpu.make_async_copy(flip.at[pl.ds(i * pitch, size)], out.at[i * COARSEN + k, rows], sems.at[k, i])
        for i in range(8)
    ]
    for copy in copies:
        copy.start()
    return copies


def third_early_kernel(
    idx, own, got, corr, total, fe, pay, w, pk, out, strip1, strip2, s0, s1, s2, force, flip0, flip1, flip2, flip3, sems
):
    def body(even):
        n = own.shape[0]
        full = 3 * n
        points = product(split(corr[...]).reshape(-1, 128), power(pk, 1)) + total[...]
        copies = write_out(out, COARSEN - 1, points, 0, flip3, sems)
        put_block(s0, own, got, even, n)
        for state in (s1, s2):
            state[full] = jnp.zeros((16, 128), BF16)
        for k, src, dst, flip in ((0, s0, s1, flip0), (1, s1, s2, flip1), (2, s2, None, flip2)):
            put_force(force, fe, pay, even, k, n)
            size = (5 - 2 * k) * REACH
            base = mirrored((2 + k) * REACH, size, full, even)
            value = apply_phi(src, idx, w, base, size) + force_at(force, base, size)
            if dst is not None:
                dst[pl.ds(base, size)] = split(value)
            mine = (3 - k) * REACH
            skip = size - mine
            kept = value[:mine] if even else value[skip:]
            copies += write_out(out, k, kept, n - mine if even else 0, flip, sems)
        put_strips((strip1, strip2), (s1, s2), full, even)
        for copy in copies:
            copy.wait()

    by_parity(body)


def third_late_kernel(
    idx, own, got, strip1, strip2, fe, pay, w, partial, out, s0, s1, s2, force, flip0, flip1, flip2, sems
):
    def body(even):
        n = own.shape[0]
        full = 3 * n
        put_block(s0, own, got, not even, n)
        get_strips((strip1, strip2), (s1, s2), full, even)
        copies = []
        size = 3 * REACH
        for k, src, dst, flip in ((0, s0, s1, flip0), (1, s1, s2, flip1), (2, s2, None, flip2)):
            put_force(force, fe, pay, not even, k, n)
            base = mirrored((7 - k) * REACH, size, full, even)
            value = apply_phi(src, idx, w, base, size) + force_at(force, base, size)
            if dst is not None:
                dst[pl.ds(base, size)] = split(value)
            mine = (k + 1) * REACH
            kept = value[size - mine :] if even else value[:mine]
            copies += write_out(out, k, kept, 0 if even else n - mine, flip, sems)
        for copy in copies:
            copy.wait()

    by_parity(body)


def call(kernel, inputs, outs, scratch, spaces="", out_spaces="", aliases=None, flops=10**7, room=32):
    kinds = {"s": pltpu.SMEM, "h": pltpu.HBM, "v": pltpu.VMEM}

    def specs(arrays, letters):
        letters = letters.ljust(len(arrays), "v")
        return [pl.BlockSpec(memory_space=kinds[letter]) for letter in letters]

    moved = sum(a.size * a.dtype.itemsize for a in list(inputs) + list(outs))
    return pl.pallas_call(
        kernel,
        out_shape=outs,
        name=kernel.__name__,
        in_specs=specs(inputs, spaces),
        out_specs=specs(outs, out_spaces),
        scratch_shapes=scratch,
        input_output_aliases=aliases or {},
        compiler_params=pltpu.CompilerParams(vmem_limit_bytes=room * 1024 * 1024),
        cost_estimate=pl.CostEstimate(flops=flops, bytes_accessed=moved, transcendentals=0),
    )(*inputs)


def local(forcing, initial_state, connectivity, pattern, diag_block, face_blocks, coarse_block):
    n, width = initial_state.shape
    steps = forcing.shape[0]
    full = 3 * n
    tm = lax.axis_size("tm")
    shape = jax.ShapeDtypeStruct
    vmem = pltpu.VMEM
    dma = pltpu.SemaphoreType.DMA
    tiles = shape((n, 8, width), F32)
    state = shape((n, 16, width), BF16)
    ends = shape((n, width), F32)
    step_flops = 2 * 16 * 7 * width * 2 * width
    pay_rows = sum((COARSEN - 1 - k) * REACH * 8 for k in range(COARSEN)) + 2 * n + 16
    pay = shape((pay_rows, width), BF16)
    all_force = ((COARSEN * n * 8 + 16), width)
    fe, pay_even, pay_odd = call(
        pack_kernel,
        (forcing.reshape(steps // COARSEN, COARSEN, n, width), initial_state, connectivity.T, pattern.T),
        (shape(all_force, BF16), pay, pay),
        [
            vmem((COARSEN, 8, n, width), BF16),
            vmem((8 * (n + 8), width), F32),
            vmem((n, width), F32),
            vmem((6, n), jnp.int32),
            vmem((6, n), jnp.int32),
            vmem((16, 128), F32),
            vmem(all_force, BF16),
            vmem((pay_rows, width), BF16),
            vmem((pay_rows, width), BF16),
            dma((COARSEN + 3,)),
            dma((3,)),
        ],
        spaces="hhhh",
        flops=3 * 10**9,
        out_spaces="hhh",
        room=62,
    )
    pay_odd, pay_even = swapped(pay_odd, 1), swapped(pay_even, 0)
    w, pk, we = call(
        weight_kernel,
        (diag_block, face_blocks, coarse_block),
        (
            shape((7 * width, 2 * width), BF16),
            shape((8 * width, 2 * width), BF16),
            shape(((tm - 1) * width, 2 * width), BF16),
        ),
        [],
        flops=10**9,
    )
    spaces = vmem((full + 1, 16, width), BF16)
    force = vmem((full * 8, width), BF16)
    rows = vmem((n * 8, width), F32)
    strip = shape((STRIP, 16, width), BF16)
    tables = [vmem((256, 256), BF16), vmem((256, 128), F32), vmem((128, 128), F32)]
    smem = pltpu.SMEM((8, 256), jnp.int32)
    strips = call(
        first_early_kernel,
        (fe, initial_state, pay_even, w),
        (strip, strip, strip),
        [spaces] * 3 + [force, vmem((6 * REACH * 8, width), F32)] + tables + [vmem((8, 256), jnp.int32), smem, dma],
        flops=step_flops * 6 * REACH,
    )
    w1, end, idx = call(
        first_late_kernel,
        (fe, initial_state, pay_even, pay_odd, *strips, w, pk),
        (tiles, ends, shape((8, 256), jnp.int32)),
        [spaces] * 3 + [force, rows] + tables + [smem, dma],
        flops=step_flops * 12 * REACH,
    )
    arrivals = earlier(end)
    (starts,) = call(scan_kernel, (w1, pk), (tiles,), [])
    (coarse,) = call(enter_first_kernel, (*arrivals, starts, we, pk), (state,), [rows])
    got_odd, got_even = swapped(coarse, 1), swapped(coarse, 0)
    *strips, moved = call(
        second_early_kernel,
        (idx, coarse, got_even, w, pk),
        (strip, strip, strip, tiles),
        [spaces] * 4,
        spaces="s",
        flops=step_flops * 12 * REACH,
    )
    res, end = call(
        second_late_kernel,
        (idx, coarse, got_odd, *strips, moved, w, pk),
        (tiles, ends),
        [spaces] * 4 + [rows],
        spaces="s",
        flops=step_flops * 16 * REACH,
    )
    arrivals = earlier(end)
    starts, total = call(scan_sum_kernel, (res, w1, moved, pk), (tiles, tiles), [])
    side = shape(((COARSEN - 1) * REACH, 16, width), BF16)
    coarse, end_even, end_odd, corr = call(
        enter_second_kernel,
        (*arrivals, starts, coarse, initial_state, we, pk),
        (state, side, side, tiles),
        [rows],
    )
    got_odd, got_even = swapped(end_odd, 1), swapped(end_even, 0)
    result = shape((steps, n, width), F32)
    flips = [vmem((8 * (m * REACH + 8), width), F32) for m in (3, 2, 1)]
    out, *strips = call(
        third_early_kernel,
        (idx, coarse, got_even, corr, total, fe, pay_even, w, pk),
        (result, strip, strip),
        [spaces] * 3 + [force] + flips + [vmem((8 * (n + 8), width), F32), dma((COARSEN, 8))],
        spaces="s",
        out_spaces="h",
        flops=step_flops * 9 * REACH,
    )
    (out,) = call(
        third_late_kernel,
        (idx, coarse, got_odd, *strips, fe, pay_odd, w, out),
        (result,),
        [spaces] * 3 + [force] + flips[::-1] + [dma((COARSEN - 1, 8))],
        spaces="svvvvvvvh",
        out_spaces="h",
        aliases={8: 0},
        flops=step_flops * 9 * REACH,
    )
    return out


def solution(mesh):
    return jax.shard_map(
        local,
        mesh=mesh,
        in_specs=(
            P("tm", ("groups", "space"), None),
            P(("groups", "space"), None),
            P("space", None),
            P("space", None),
            P(),
            P(),
            P(),
        ),
        out_specs=P("tm", ("groups", "space"), None),
        check_vma=False,
    )
```

```python
import functools

import jax
import jax.numpy as jnp
from jax import lax
from jax.experimental import pallas as pl
from jax.experimental.pallas import tpu as pltpu
from jax.sharding import PartitionSpec as P

COARSEN = 4
REACH = 16
F32 = jnp.float32
BF16 = jnp.bfloat16
CHUNK = 32


def swapped(value, first):
    count = lax.axis_size("space")
    pairs = []
    for i in range(first, count - 1, 2):
        pairs += [(i, i + 1), (i + 1, i)]
    return lax.ppermute(value, "space", pairs)


def earlier(value):
    count = lax.axis_size("tm")
    if count <= 8:
        return [lax.ppermute(value, "tm", [(i, i + s) for i in range(count - s)]) for s in range(1, count)]
    every = lax.all_gather(value, "tm")
    at = lax.axis_index("tm") - jnp.arange(1, count)
    picked = jnp.where((at >= 0)[:, None, None], jnp.take(every, jnp.maximum(at, 0), axis=0), 0.0)
    return [picked[s] for s in range(count - 1)]


def split(u):
    lead = u.astype(BF16).astype(F32)
    return jnp.concatenate([u, u - lead], axis=1).astype(BF16)


def split_rows(u):
    lead = u.astype(BF16)
    return jnp.concatenate([lead, (u - lead.astype(F32)).astype(BF16)], axis=0)


def product(x, weights):
    m = x.shape[0] // 16
    r = jnp.dot(x, weights, preferred_element_type=F32).reshape(m, 16, 256)
    return r[:, :8, :128] + (r[:, 8:, :128] + r[:, :8, 128:])


def product_rows(x, weights):
    m = x.shape[0] // 2
    r = jnp.dot(x, weights, preferred_element_type=F32)
    return r[:m, :128] + (r[m:, :128] + r[:m, 128:])


def put_halves(ref, w):
    lead = w.astype(BF16)
    ref[:, 0:128] = lead
    ref[:, 128:256] = (w - lead.astype(F32)).astype(BF16)


def power(pk, k):
    return pk[pl.ds(128 * (7 - k), 128), :]


def scan_starts(values, pk):
    y = values
    row = lax.broadcasted_iota(jnp.int32, y.shape, 1)
    for d in (1, 2, 4):
        z = product(split(y).reshape(-1, 128), power(pk, d))
        y = y + jnp.where(row >= d, pltpu.roll(z, d, axis=1), 0.0)
    return jnp.where(row >= 1, pltpu.roll(y, 1, axis=1), 0.0)


def block_end(y, pk, n):
    parts = [y[pl.ds(i, n, stride=8), :] for i in range(8)]
    return product_rows(split_rows(jnp.concatenate(parts, axis=1)), pk[...])


def enter(arrivals, we, pk, y, n):
    value = jnp.concatenate([a[...] for a in arrivals], axis=1)
    entry = product_rows(split_rows(value), we[...])
    y[pl.ds(0, n, stride=8), :] = entry
    rows = split_rows(entry)
    for i in range(1, 8):
        y[pl.ds(i, n, stride=8), :] = product_rows(rows, power(pk, i))
    return y[...].reshape(n, 8, 128)


def apply_phi(src, idx, w, base, size):
    cols = [src[pl.ds(base, size)].reshape(size * 16, 128)]
    for f in range(6):
        cols.append(jnp.concatenate([src[idx[f, base + e]] for e in range(size)], axis=0))
    return product(jnp.concatenate(cols, axis=1), w[...])


def even_place():
    return lax.rem(lax.axis_index("space"), 2) == 0


def by_parity(body):
    even = even_place()
    pl.when(even)(lambda: body(True))
    pl.when(jnp.logical_not(even))(lambda: body(False))


def mirrored(low, size, full, even):
    return full - low - size if even else low


def pack_kernel(
    forcing, init, conn, pattern, fe_out, even_out, odd_out,
    landed, rows, init_v, conn_v, pattern_v, offs, fe, pay_even, pay_odd, sems, out_sems
):
    n = init_v.shape[0]
    pitch = n + 8
    copies = [pltpu.make_async_copy(forcing.at[:, k], landed.at[k], sems.at[k]) for k in range(COARSEN)]
    small = ((conn, conn_v), (pattern, pattern_v), (init, init_v))
    copies += [pltpu.make_async_copy(src, dst, sems.at[COARSEN + i]) for i, (src, dst) in enumerate(small)]
    for copy in copies:
        copy.start()
    for copy in copies[COARSEN:]:
        copy.wait()
    place = lax.broadcasted_iota(jnp.int32, (6, n), 1) + lax.axis_index("space") * n
    value = ((conn_v[...] - place) * pattern_v[...]).astype(F32)
    offs[...] = jnp.zeros_like(offs)
    offs[0:6, 0:n] = value
    offs[0:6, n : 2 * n] = value
    tab = offs[...].astype(BF16)
    fe[pl.ds(COARSEN * n * 8, 16), :] = tab
    lead = init_v[...].astype(BF16)
    rest = (init_v[...] - lead.astype(F32)).astype(BF16)
    even = even_place()
    at = sum((COARSEN - 1 - k) * REACH * 8 for k in range(COARSEN))
    for pay in (pay_even, pay_odd):
        pay[pl.ds(at, n), :] = lead
        pay[pl.ds(at + n, n), :] = rest
        pay[pl.ds(at + 2 * n, 16), :] = tab
    at = 0
    results = []
    for k in range(COARSEN):
        copies[k].wait()
        for i in range(8):
            rows[pl.ds(i * pitch, n), :] = landed[k, i].astype(F32)

        def body(pair, carry, k=k):
            e = pair * 2
            two = [rows[pl.ds(e + j, 8, stride=pitch), :] for j in range(2)]
            fe[pl.ds(pl.multiple_of((k * n + e) * 8, 16), 16), :] = jnp.concatenate(two, axis=0).astype(BF16)
            return carry

        lax.fori_loop(0, n // 2, body, 0, unroll=8)
        width = (COARSEN - 1 - k) * REACH * 8
        if width:
            for pay, right in ((pay_even, even), (pay_odd, jnp.logical_not(even))):
                begin = pl.multiple_of(k * n * 8 + jnp.where(right, n * 8 - width, 0), 128)
                pay[pl.ds(at, width), :] = fe[pl.ds(begin, width), :]
        at += width
        if k == COARSEN - 2:
            results.append(pltpu.make_async_copy(pay_odd, odd_out, out_sems.at[0]))
            results.append(pltpu.make_async_copy(pay_even, even_out, out_sems.at[1]))
            results[0].start()
            results[1].start()
    results.append(pltpu.make_async_copy(fe, fe_out, out_sems.at[2]))
    results[2].start()
    for result in results:
        result.wait()


def weight_kernel(diag, faces, coarse, w, pk, we):
    put_halves(w.at[pl.ds(0, 128)], diag[...].T)
    for f in range(6):
        put_halves(w.at[pl.ds(128 * (f + 1), 128)], faces[f].T)

    def thirds(a):
        one = a.astype(BF16)
        rest = a - one.astype(F32)
        two = rest.astype(BF16)
        return one, two, (rest - two.astype(F32)).astype(BF16)

    def mul(a, b):
        (a1, a2, a3), (b1, b2, b3) = thirds(a), thirds(b)
        total = jnp.zeros((128, 128), F32)
        for x, y in ((a3, b1), (a1, b3), (a2, b2), (a2, b1), (a1, b2), (a1, b1)):
            total += jnp.dot(x, y, preferred_element_type=F32)
        return total

    rows = lax.broadcasted_iota(jnp.int32, (128, 128), 0)
    one = (rows == lax.broadcasted_iota(jnp.int32, (128, 128), 1)).astype(F32)
    powers = [one, coarse[...].T]
    for k in range(2, 9):
        powers.append(mul(powers[k // 2], powers[k - k // 2]))
    for k in range(8):
        put_halves(pk.at[pl.ds(128 * (7 - k), 128)], powers[k])

    def body(k, current):
        put_halves(we.at[pl.ds(pl.multiple_of(k * 128, 128), 128)], current)
        return mul(current, powers[8])

    lax.fori_loop(0, we.shape[0] // 128, body, one)


def put_force(dst, own, got, right, k, n):
    at = sum((COARSEN - 1 - j) * REACH * 8 for j in range(k))
    width = (COARSEN - 1 - k) * REACH * 8
    dst[pl.ds(n * 8, n * 8), :] = own[pl.ds(k * n * 8, n * 8), :]
    if width:
        to = 2 * n * 8 if right else n * 8 - width
        dst[pl.ds(to, width), :] = got[pl.ds(at, width), :]


def force_at(src, base, size):
    return src[pl.ds(base * 8, size * 8), :].astype(F32).reshape(size, 8, 128)


def put_tables(fe, got_even, got_odd, idx_v, full, n, even):
    lane = lax.broadcasted_iota(jnp.int32, (8, 128), 1)

    def table(ref):
        return 0.0 if ref is None else ref[pl.ds(ref.shape[0] - 16, 16), :].astype(F32)[0:8]

    from_even, from_odd = table(got_even), table(got_odd)
    low = jnp.where(lane < n, from_odd if even else from_even, table(fe))
    high = jnp.where(lane < n, from_even if even else from_odd, 0.0)
    for at, offs in ((0, low), (128, high)):
        value = jnp.where(offs != 0.0, lane + at + offs.astype(jnp.int32), full)
        idx_v[:, pl.ds(at, 128)] = value


def push_init(init, got_even, got_odd, w, idx_v, columns, square, i16, base, count, n, even):
    for at in (0, 128):
        square[...] = jnp.zeros_like(square)
        square[0:8, :] = idx_v[:, pl.ds(at, 128)].astype(F32)
        columns[pl.ds(at, 128), :] = square[...].T
    i16[...] = jnp.zeros_like(i16)
    lead = init[...].astype(BF16)
    i16[pl.ds(n, n), 0:128] = lead
    i16[pl.ds(n, n), 128:256] = (init[...] - lead.astype(F32)).astype(BF16)
    for ref, right in ((got_even, even), (got_odd, not even)):
        if ref is not None:
            at = ref.shape[0] - 16
            to = 2 * n if right else 0
            i16[pl.ds(to, n), 0:128] = ref[pl.ds(at - 2 * n, n), :]
            i16[pl.ds(to, n), 128:256] = ref[pl.ds(at - n, n), :]
    rows = pl.ds(base, count)
    place = columns[rows, :]
    spot = lax.broadcasted_iota(jnp.int32, (count, 256), 1).astype(F32)
    cols = [i16[rows, :]]
    for f in range(6):
        hot = (spot == place[:, f : f + 1]).astype(F32).astype(BF16)
        cols.append(jnp.dot(hot, i16[...], preferred_element_type=F32).astype(BF16))
    leads = jnp.concatenate([c[:, 0:128] for c in cols], axis=1)
    rests = jnp.concatenate([c[:, 128:256] for c in cols], axis=1)
    return product_rows(jnp.concatenate([leads, rests], axis=0), w[...])


STRIPS = (5 * REACH, 4 * REACH, 3 * REACH)
STRIP = 2 * REACH


def put_strips(strips, states, full, even):
    for strip, state, low in zip(strips, states, STRIPS):
        strip[...] = state[pl.ds(mirrored(low, STRIP, full, even), STRIP)]


def get_strips(strips, states, full, even):
    for strip, state, low in zip(strips, states, STRIPS):
        state[pl.ds(mirrored(low, STRIP, full, even), STRIP)] = strip[...]
        state[full] = jnp.zeros((16, 128), BF16)


def first_early_kernel(
    fe, init, got, w, strip1, strip2, strip3, s1, s2, s3, force, y, i16, columns, square, idx_v, idx, sem
):
    def body(even):
        n = init.shape[0]
        full = 3 * n
        put_tables(fe, got, None, idx_v, full, n, even)
        copy = pltpu.make_async_copy(idx_v, idx, sem)
        copy.start()
        count = 6 * REACH
        base = mirrored(REACH, count, full, even)
        put_force(force, fe, got, even, 0, n)
        y[pl.ds(0, count * 8), :] = force[pl.ds(base * 8, count * 8), :].astype(F32)

        def add_init():
            pushed = push_init(init, got, None, w, idx_v, columns, square, i16, base, count, n, even)
            y[pl.ds(0, count, stride=8), :] = y[pl.ds(0, count, stride=8), :] + pushed

        pl.when(lax.axis_index("tm") == 0)(add_init)
        s1[pl.ds(base, count)] = split(y[pl.ds(0, count * 8), :].reshape(count, 8, 128))
        for state in (s1, s2, s3):
            state[full] = jnp.zeros((16, 128), BF16)
        copy.wait()
        for k, src, dst in ((1, s1, s2), (2, s2, s3)):
            put_force(force, fe, got, even, k, n)
            size = (6 - 2 * k) * REACH
            base = mirrored((k + 1) * REACH, size, full, even)
            dst[pl.ds(base, size)] = split(apply_phi(src, idx, w, base, size) + force_at(force, base, size))
        put_strips((strip1, strip2, strip3), (s1, s2, s3), full, even)

    by_parity(body)


def first_late_kernel(
    fe, init, got_even, got_odd, strip1, strip2, strip3, w, pk, w1, end, idx_out,
    s1, s2, s3, force, y, i16, columns, square, idx, sem
):
    def body(even):
        n = init.shape[0]
        full = 3 * n
        put_tables(fe, got_even, got_odd, idx_out, full, n, even)
        copy = pltpu.make_async_copy(idx_out, idx, sem)
        copy.start()
        count = 4 * REACH
        base = mirrored(7 * REACH, count, full, even)
        put_force(force, fe, got_odd, not even, 0, n)
        y[...] = force[pl.ds(base * 8, count * 8), :].astype(F32)

        def add_init():
            pushed = push_init(init, got_even, got_odd, w, idx_out, columns, square, i16, base, count, n, even)
            y[pl.ds(0, count, stride=8), :] = y[pl.ds(0, count, stride=8), :] + pushed

        pl.when(lax.axis_index("tm") == 0)(add_init)
        s1[pl.ds(base, count)] = split(y[...].reshape(count, 8, 128))
        get_strips((strip1, strip2, strip3), (s1, s2, s3), full, even)
        copy.wait()
        for k, src, dst in ((1, s1, s2), (2, s2, s3), (3, s3, None)):
            put_force(force, fe, got_odd, not even, k, n)
            base = mirrored((7 - k) * REACH, count, full, even)
            value = apply_phi(src, idx, w, base, count) + force_at(force, base, count)
            if dst is None:
                w1[...] = value
                y[...] = value.reshape(n * 8, 128)
            else:
                dst[pl.ds(base, count)] = split(value)
        end[...] = block_end(y, pk, n)

    by_parity(body)


def scan_kernel(values, pk, starts):
    starts[...] = scan_starts(values[...], pk)


def scan_sum_kernel(values, w1, coarse, pk, starts, total):
    starts[...] = scan_starts(values[...], pk)
    total[...] = values[...] + (w1[...] + coarse[...])


def enter_first_kernel(*refs):
    *arrivals, starts, we, pk, state, y = refs
    n = starts.shape[0]
    state[...] = split(enter(arrivals, we, pk, y, n) + starts[...])


def enter_second_kernel(*refs):
    *arrivals, starts, before, init, we, pk, state, pay_even, pay_odd, corr, y = refs
    n = starts.shape[0]
    value = enter(arrivals, we, pk, y, n) + starts[...]
    corr[...] = value
    old = before[...].astype(F32)
    y[...] = (value + (old[:, 0:8] + old[:, 8:16])).reshape(n * 8, 128)
    first = (lax.axis_index("tm") == 0).astype(F32)
    y[pl.ds(0, n, stride=8), :] = y[pl.ds(0, n, stride=8), :] + init[...] * first
    state[...] = split(y[...].reshape(n, 8, 128))
    side = (COARSEN - 1) * REACH
    even = even_place()
    pay_even[...] = state[pl.ds(jnp.where(even, n - side, 0), side)]
    pay_odd[...] = state[pl.ds(jnp.where(even, 0, n - side), side)]


def put_block(dst, own, got, right, n):
    side = got.shape[0]
    dst[pl.ds(n, n)] = own[...]
    dst[pl.ds(2 * n if right else n - side, side)] = got[...]
    dst[3 * n] = jnp.zeros((16, 128), BF16)


def second_early_kernel(idx, own, got, w, pk, strip1, strip2, strip3, coarse, s0, s1, s2, s3):
    def body(even):
        n = own.shape[0]
        full = 3 * n
        coarse[...] = product(own[...].reshape(n * 16, 128), power(pk, 1))
        put_block(s0, own, got, even, n)
        for state in (s1, s2, s3):
            state[full] = jnp.zeros((16, 128), BF16)
        for k, src, dst in ((1, s0, s1), (2, s1, s2), (3, s2, s3)):
            size = (8 - 2 * k) * REACH
            base = mirrored(k * REACH, size, full, even)
            dst[pl.ds(base, size)] = split(apply_phi(src, idx, w, base, size))
        put_strips((strip1, strip2, strip3), (s1, s2, s3), full, even)

    by_parity(body)


def second_late_kernel(idx, own, got, strip1, strip2, strip3, coarse, w, pk, res, end, s0, s1, s2, s3, y):
    def body(even):
        n = own.shape[0]
        full = 3 * n
        put_block(s0, own, got, not even, n)
        get_strips((strip1, strip2, strip3), (s1, s2, s3), full, even)
        count = 4 * REACH
        for k, src, dst in ((1, s0, s1), (2, s1, s2), (3, s2, s3)):
            base = mirrored((8 - k) * REACH, count, full, even)
            dst[pl.ds(base, count)] = split(apply_phi(src, idx, w, base, count))
        value = apply_phi(s3, idx, w, n, n)
        value = value - coarse[...]
        res[...] = value
        y[...] = value.reshape(n * 8, 128)
        end[...] = block_end(y, pk, n)

    by_parity(body)


def write_out(out, k, value, begin, flip, sems):
    size = value.shape[0]
    pitch = size + 8
    for e in range(size):
        flip[pl.ds(e, 8, stride=pitch), :] = value[e]
    rows = pl.ds(begin, size)
    copies = [
        pltpu.make_async_copy(flip.at[pl.ds(i * pitch, size)], out.at[i * COARSEN + k, rows], sems.at[k, i])
        for i in range(8)
    ]
    for copy in copies:
        copy.start()
    return copies


def third_early_kernel(
    idx, own, got, corr, total, fe, pay, w, pk, out, strip1, strip2, s0, s1, s2, force, flip0, flip1, flip2, flip3, sems
):
    def body(even):
        n = own.shape[0]
        full = 3 * n
        points = product(split(corr[...]).reshape(-1, 128), power(pk, 1)) + total[...]
        copies = write_out(out, COARSEN - 1, points, 0, flip3, sems)
        put_block(s0, own, got, even, n)
        for state in (s1, s2):
            state[full] = jnp.zeros((16, 128), BF16)
        for k, src, dst, flip in ((0, s0, s1, flip0), (1, s1, s2, flip1), (2, s2, None, flip2)):
            put_force(force, fe, pay, even, k, n)
            size = (5 - 2 * k) * REACH
            base = mirrored((2 + k) * REACH, size, full, even)
            value = apply_phi(src, idx, w, base, size) + force_at(force, base, size)
            if dst is not None:
                dst[pl.ds(base, size)] = split(value)
            mine = (3 - k) * REACH
            skip = size - mine
            kept = value[:mine] if even else value[skip:]
            copies += write_out(out, k, kept, n - mine if even else 0, flip, sems)
        put_strips((strip1, strip2), (s1, s2), full, even)
        for copy in copies:
            copy.wait()

    by_parity(body)


def third_late_kernel(
    idx, own, got, strip1, strip2, fe, pay, w, partial, out, s0, s1, s2, force, flip0, flip1, flip2, sems
):
    def body(even):
        n = own.shape[0]
        full = 3 * n
        put_block(s0, own, got, not even, n)
        get_strips((strip1, strip2), (s1, s2), full, even)
        copies = []
        size = 3 * REACH
        for k, src, dst, flip in ((0, s0, s1, flip0), (1, s1, s2, flip1), (2, s2, None, flip2)):
            put_force(force, fe, pay, not even, k, n)
            base = mirrored((7 - k) * REACH, size, full, even)
            value = apply_phi(src, idx, w, base, size) + force_at(force, base, size)
            if dst is not None:
                dst[pl.ds(base, size)] = split(value)
            mine = (k + 1) * REACH
            kept = value[size - mine :] if even else value[:mine]
            copies += write_out(out, k, kept, 0 if even else n - mine, flip, sems)
        for copy in copies:
            copy.wait()

    by_parity(body)


def call(kernel, inputs, outs, scratch, spaces="", out_spaces="", aliases=None, flops=10**7, room=32):
    kinds = {"s": pltpu.SMEM, "h": pltpu.HBM, "v": pltpu.VMEM}

    def specs(arrays, letters):
        letters = letters.ljust(len(arrays), "v")
        return [pl.BlockSpec(memory_space=kinds[letter]) for letter in letters]

    moved = sum(a.size * a.dtype.itemsize for a in list(inputs) + list(outs))
    return pl.pallas_call(
        kernel,
        out_shape=outs,
        name=kernel.__name__,
        in_specs=specs(inputs, spaces),
        out_specs=specs(outs, out_spaces),
        scratch_shapes=scratch,
        input_output_aliases=aliases or {},
        compiler_params=pltpu.CompilerParams(vmem_limit_bytes=room * 1024 * 1024),
        cost_estimate=pl.CostEstimate(flops=flops, bytes_accessed=moved, transcendentals=0),
    )(*inputs)


def local(forcing, initial_state, connectivity, pattern, diag_block, face_blocks, coarse_block):
    n, width = initial_state.shape
    steps = forcing.shape[0]
    full = 3 * n
    tm = lax.axis_size("tm")
    shape = jax.ShapeDtypeStruct
    vmem = pltpu.VMEM
    dma = pltpu.SemaphoreType.DMA
    tiles = shape((n, 8, width), F32)
    state = shape((n, 16, width), BF16)
    ends = shape((n, width), F32)
    step_flops = 2 * 16 * 7 * width * 2 * width
    pay_rows = sum((COARSEN - 1 - k) * REACH * 8 for k in range(COARSEN)) + 2 * n + 16
    pay = shape((pay_rows, width), BF16)
    all_force = ((COARSEN * n * 8 + 16), width)
    fe, pay_even, pay_odd = call(
        pack_kernel,
        (forcing.reshape(steps // COARSEN, COARSEN, n, width), initial_state, connectivity.T, pattern.T),
        (shape(all_force, BF16), pay, pay),
        [
            vmem((COARSEN, 8, n, width), BF16),
            vmem((8 * (n + 8), width), F32),
            vmem((n, width), F32),
            vmem((6, n), jnp.int32),
            vmem((6, n), jnp.int32),
            vmem((16, 128), F32),
            vmem(all_force, BF16),
            vmem((pay_rows, width), BF16),
            vmem((pay_rows, width), BF16),
            dma((COARSEN + 3,)),
            dma((3,)),
        ],
        spaces="hhhh",
        flops=3 * 10**9,
        out_spaces="hhh",
        room=62,
    )
    pay_odd, pay_even = swapped(pay_odd, 1), swapped(pay_even, 0)
    w, pk, we = call(
        weight_kernel,
        (diag_block, face_blocks, coarse_block),
        (
            shape((7 * width, 2 * width), BF16),
            shape((8 * width, 2 * width), BF16),
            shape(((tm - 1) * width, 2 * width), BF16),
        ),
        [],
        flops=10**9,
    )
    spaces = vmem((full + 1, 16, width), BF16)
    force = vmem((full * 8, width), BF16)
    rows = vmem((n * 8, width), F32)
    strip = shape((STRIP, 16, width), BF16)
    tables = [vmem((256, 256), BF16), vmem((256, 128), F32), vmem((128, 128), F32)]
    smem = pltpu.SMEM((8, 256), jnp.int32)
    strips = call(
        first_early_kernel,
        (fe, initial_state, pay_even, w),
        (strip, strip, strip),
        [spaces] * 3 + [force, vmem((6 * REACH * 8, width), F32)] + tables + [vmem((8, 256), jnp.int32), smem, dma],
        flops=step_flops * 6 * REACH,
    )
    w1, end, idx = call(
        first_late_kernel,
        (fe, initial_state, pay_even, pay_odd, *strips, w, pk),
        (tiles, ends, shape((8, 256), jnp.int32)),
        [spaces] * 3 + [force, rows] + tables + [smem, dma],
        flops=step_flops * 12 * REACH,
    )
    arrivals = earlier(end)
    (starts,) = call(scan_kernel, (w1, pk), (tiles,), [])
    (coarse,) = call(enter_first_kernel, (*arrivals, starts, we, pk), (state,), [rows])
    got_odd, got_even = swapped(coarse, 1), swapped(coarse, 0)
    *strips, moved = call(
        second_early_kernel,
        (idx, coarse, got_even, w, pk),
        (strip, strip, strip, tiles),
        [spaces] * 4,
        spaces="s",
        flops=step_flops * 12 * REACH,
    )
    res, end = call(
        second_late_kernel,
        (idx, coarse, got_odd, *strips, moved, w, pk),
        (tiles, ends),
        [spaces] * 4 + [rows],
        spaces="s",
        flops=step_flops * 16 * REACH,
    )
    arrivals = earlier(end)
    starts, total = call(scan_sum_kernel, (res, w1, moved, pk), (tiles, tiles), [])
    side = shape(((COARSEN - 1) * REACH, 16, width), BF16)
    coarse, end_even, end_odd, corr = call(
        enter_second_kernel,
        (*arrivals, starts, coarse, initial_state, we, pk),
        (state, side, side, tiles),
        [rows],
    )
    got_odd, got_even = swapped(end_odd, 1), swapped(end_even, 0)
    result = shape((steps, n, width), F32)
    flips = [vmem((8 * (m * REACH + 8), width), F32) for m in (3, 2, 1)]
    out, *strips = call(
        third_early_kernel,
        (idx, coarse, got_even, corr, total, fe, pay_even, w, pk),
        (result, strip, strip),
        [spaces] * 3 + [force] + flips + [vmem((8 * (n + 8), width), F32), dma((COARSEN, 8))],
        spaces="s",
        out_spaces="h",
        flops=step_flops * 9 * REACH,
    )
    (out,) = call(
        third_late_kernel,
        (idx, coarse, got_odd, *strips, fe, pay_odd, w, out),
        (result,),
        [spaces] * 3 + [force] + flips[::-1] + [dma((COARSEN - 1, 8))],
        spaces="svvvvvvvh",
        out_spaces="h",
        aliases={8: 0},
        flops=step_flops * 9 * REACH,
    )
    return out


def solution(mesh):
    return jax.shard_map(
        local,
        mesh=mesh,
        in_specs=(
            P("tm", ("groups", "space"), None),
            P(("groups", "space"), None),
            P("space", None),
            P("space", None),
            P(),
            P(),
            P(),
        ),
        out_specs=P("tm", ("groups", "space"), None),
        check_vma=False,
    )
```

```python
import functools

import jax
import jax.numpy as jnp
from jax import lax
from jax.experimental import pallas as pl
from jax.experimental.pallas import tpu as pltpu
from jax.sharding import PartitionSpec as P

COARSEN = 4
REACH = 16
F32 = jnp.float32
BF16 = jnp.bfloat16
CHUNK = 32


def swapped(value, first):
    count = lax.axis_size("space")
    pairs = []
    for i in range(first, count - 1, 2):
        pairs += [(i, i + 1), (i + 1, i)]
    return lax.ppermute(value, "space", pairs)


def earlier(value):
    count = lax.axis_size("tm")
    if count <= 8:
        return [lax.ppermute(value, "tm", [(i, i + s) for i in range(count - s)]) for s in range(1, count)]
    every = lax.all_gather(value, "tm")
    at = lax.axis_index("tm") - jnp.arange(1, count)
    picked = jnp.where((at >= 0)[:, None, None], jnp.take(every, jnp.maximum(at, 0), axis=0), 0.0)
    return [picked[s] for s in range(count - 1)]


def split(u):
    lead = u.astype(BF16).astype(F32)
    return jnp.concatenate([u, u - lead], axis=1).astype(BF16)


def split_rows(u):
    lead = u.astype(BF16)
    return jnp.concatenate([lead, (u - lead.astype(F32)).astype(BF16)], axis=0)


def product(x, weights):
    m = x.shape[0] // 16
    r = jnp.dot(x, weights, preferred_element_type=F32).reshape(m, 16, 256)
    return r[:, :8, :128] + (r[:, 8:, :128] + r[:, :8, 128:])


def product_rows(x, weights):
    m = x.shape[0] // 2
    r = jnp.dot(x, weights, preferred_element_type=F32)
    return r[:m, :128] + (r[m:, :128] + r[:m, 128:])


def put_halves(ref, w):
    lead = w.astype(BF16)
    ref[:, 0:128] = lead
    ref[:, 128:256] = (w - lead.astype(F32)).astype(BF16)


def power(pk, k):
    return pk[pl.ds(128 * (7 - k), 128), :]


def scan_starts(values, pk):
    y = values
    row = lax.broadcasted_iota(jnp.int32, y.shape, 1)
    for d in (1, 2, 4):
        z = product(split(y).reshape(-1, 128), power(pk, d))
        y = y + jnp.where(row >= d, pltpu.roll(z, d, axis=1), 0.0)
    return jnp.where(row >= 1, pltpu.roll(y, 1, axis=1), 0.0)


def block_end(y, pk, n):
    parts = [y[pl.ds(i, n, stride=8), :] for i in range(8)]
    return product_rows(split_rows(jnp.concatenate(parts, axis=1)), pk[...])


def enter(arrivals, we, pk, y, n):
    value = jnp.concatenate([a[...] for a in arrivals], axis=1)
    entry = product_rows(split_rows(value), we[...])
    y[pl.ds(0, n, stride=8), :] = entry
    rows = split_rows(entry)
    for i in range(1, 8):
        y[pl.ds(i, n, stride=8), :] = product_rows(rows, power(pk, i))
    return y[...].reshape(n, 8, 128)


def apply_phi(src, idx, w, base, size):
    cols = [src[pl.ds(base, size)].reshape(size * 16, 128)]
    for f in range(6):
        cols.append(jnp.concatenate([src[idx[f, base + e]] for e in range(size)], axis=0))
    cols.append(cols[0])
    return product(jnp.concatenate(cols, axis=1), w[...])


def even_place():
    return lax.rem(lax.axis_index("space"), 2) == 0


def by_parity(body):
    even = even_place()
    pl.when(even)(lambda: body(True))
    pl.when(jnp.logical_not(even))(lambda: body(False))


def mirrored(low, size, full, even):
    return full - low - size if even else low


def pack_kernel(
    forcing, init, conn, pattern, fe_out, even_out, odd_out,
    landed, rows, init_v, conn_v, pattern_v, offs, fe, pay_even, pay_odd, sems, out_sems
):
    n = init_v.shape[0]
    pitch = n + 8
    copies = [pltpu.make_async_copy(forcing.at[:, k], landed.at[k], sems.at[k]) for k in range(COARSEN)]
    small = ((conn, conn_v), (pattern, pattern_v), (init, init_v))
    copies += [pltpu.make_async_copy(src, dst, sems.at[COARSEN + i]) for i, (src, dst) in enumerate(small)]
    for copy in copies:
        copy.start()
    for copy in copies[COARSEN:]:
        copy.wait()
    place = lax.broadcasted_iota(jnp.int32, (6, n), 1) + lax.axis_index("space") * n
    value = ((conn_v[...] - place) * pattern_v[...]).astype(F32)
    offs[...] = jnp.zeros_like(offs)
    offs[0:6, 0:n] = value
    offs[0:6, n : 2 * n] = value
    tab = offs[...].astype(BF16)
    fe[pl.ds(COARSEN * n * 8, 16), :] = tab
    lead = init_v[...].astype(BF16)
    rest = (init_v[...] - lead.astype(F32)).astype(BF16)
    even = even_place()
    at = sum((COARSEN - 1 - k) * REACH * 8 for k in range(COARSEN))
    for pay in (pay_even, pay_odd):
        pay[pl.ds(at, n), :] = lead
        pay[pl.ds(at + n, n), :] = rest
        pay[pl.ds(at + 2 * n, 16), :] = tab
    at = 0
    results = []
    for k in range(COARSEN):
        copies[k].wait()
        for i in range(8):
            rows[pl.ds(i * pitch, n), :] = landed[k, i].astype(F32)

        def body(pair, carry, k=k):
            e = pair * 2
            two = [rows[pl.ds(e + j, 8, stride=pitch), :] for j in range(2)]
            fe[pl.ds(pl.multiple_of((k * n + e) * 8, 16), 16), :] = jnp.concatenate(two, axis=0).astype(BF16)
            return carry

        lax.fori_loop(0, n // 2, body, 0, unroll=8)
        width = (COARSEN - 1 - k) * REACH * 8
        if width:
            for pay, right in ((pay_even, even), (pay_odd, jnp.logical_not(even))):
                begin = pl.multiple_of(k * n * 8 + jnp.where(right, n * 8 - width, 0), 128)
                pay[pl.ds(at, width), :] = fe[pl.ds(begin, width), :]
        at += width
        if k == COARSEN - 2:
            results.append(pltpu.make_async_copy(pay_odd, odd_out, out_sems.at[0]))
            results.append(pltpu.make_async_copy(pay_even, even_out, out_sems.at[1]))
            results[0].start()
            results[1].start()
    results.append(pltpu.make_async_copy(fe, fe_out, out_sems.at[2]))
    results[2].start()
    for result in results:
        result.wait()


def weight_kernel(diag, faces, coarse, w, pk, we):
    put_halves(w.at[pl.ds(0, 128)], diag[...].T)
    for f in range(6):
        put_halves(w.at[pl.ds(128 * (f + 1), 128)], faces[f].T)
    w[pl.ds(128 * 7, 128), :] = jnp.zeros((128, 256), BF16)

    def thirds(a):
        one = a.astype(BF16)
        rest = a - one.astype(F32)
        two = rest.astype(BF16)
        return one, two, (rest - two.astype(F32)).astype(BF16)

    def mul(a, b):
        (a1, a2, a3), (b1, b2, b3) = thirds(a), thirds(b)
        total = jnp.zeros((128, 128), F32)
        for x, y in ((a3, b1), (a1, b3), (a2, b2), (a2, b1), (a1, b2), (a1, b1)):
            total += jnp.dot(x, y, preferred_element_type=F32)
        return total

    rows = lax.broadcasted_iota(jnp.int32, (128, 128), 0)
    one = (rows == lax.broadcasted_iota(jnp.int32, (128, 128), 1)).astype(F32)
    powers = [one, coarse[...].T]
    for k in range(2, 9):
        powers.append(mul(powers[k // 2], powers[k - k // 2]))
    for k in range(8):
        put_halves(pk.at[pl.ds(128 * (7 - k), 128)], powers[k])

    def body(k, current):
        put_halves(we.at[pl.ds(pl.multiple_of(k * 128, 128), 128)], current)
        return mul(current, powers[8])

    lax.fori_loop(0, we.shape[0] // 128, body, one)


def put_force(dst, own, got, right, k, n):
    at = sum((COARSEN - 1 - j) * REACH * 8 for j in range(k))
    width = (COARSEN - 1 - k) * REACH * 8
    dst[pl.ds(n * 8, n * 8), :] = own[pl.ds(k * n * 8, n * 8), :]
    if width:
        to = 2 * n * 8 if right else n * 8 - width
        dst[pl.ds(to, width), :] = got[pl.ds(at, width), :]


def force_at(src, base, size):
    return src[pl.ds(base * 8, size * 8), :].astype(F32).reshape(size, 8, 128)


def put_tables(fe, got_even, got_odd, idx_v, full, n, even):
    lane = lax.broadcasted_iota(jnp.int32, (8, 128), 1)

    def table(ref):
        return 0.0 if ref is None else ref[pl.ds(ref.shape[0] - 16, 16), :].astype(F32)[0:8]

    from_even, from_odd = table(got_even), table(got_odd)
    low = jnp.where(lane < n, from_odd if even else from_even, table(fe))
    high = jnp.where(lane < n, from_even if even else from_odd, 0.0)
    for at, offs in ((0, low), (128, high)):
        value = jnp.where(offs != 0.0, lane + at + offs.astype(jnp.int32), full)
        idx_v[:, pl.ds(at, 128)] = value


def push_init(init, got_even, got_odd, w, idx_v, columns, square, i16, base, count, n, even):
    for at in (0, 128):
        square[...] = jnp.zeros_like(square)
        square[0:8, :] = idx_v[:, pl.ds(at, 128)].astype(F32)
        columns[pl.ds(at, 128), :] = square[...].T
    i16[...] = jnp.zeros_like(i16)
    lead = init[...].astype(BF16)
    i16[pl.ds(n, n), 0:128] = lead
    i16[pl.ds(n, n), 128:256] = (init[...] - lead.astype(F32)).astype(BF16)
    for ref, right in ((got_even, even), (got_odd, not even)):
        if ref is not None:
            at = ref.shape[0] - 16
            to = 2 * n if right else 0
            i16[pl.ds(to, n), 0:128] = ref[pl.ds(at - 2 * n, n), :]
            i16[pl.ds(to, n), 128:256] = ref[pl.ds(at - n, n), :]
    rows = pl.ds(base, count)
    place = columns[rows, :]
    spot = lax.broadcasted_iota(jnp.int32, (count, 256), 1).astype(F32)
    cols = [i16[rows, :]]
    for f in range(6):
        hot = (spot == place[:, f : f + 1]).astype(F32).astype(BF16)
        cols.append(jnp.dot(hot, i16[...], preferred_element_type=F32).astype(BF16))
    leads = jnp.concatenate([c[:, 0:128] for c in cols], axis=1)
    rests = jnp.concatenate([c[:, 128:256] for c in cols], axis=1)
    return product_rows(jnp.concatenate([leads, rests], axis=0), w[pl.ds(0, 7 * 128), :])


STRIPS = (5 * REACH, 4 * REACH, 3 * REACH)
STRIP = 2 * REACH


def put_strips(strips, states, full, even):
    for strip, state, low in zip(strips, states, STRIPS):
        strip[...] = state[pl.ds(mirrored(low, STRIP, full, even), STRIP)]


def get_strips(strips, states, full, even):
    for strip, state, low in zip(strips, states, STRIPS):
        state[pl.ds(mirrored(low, STRIP, full, even), STRIP)] = strip[...]
        state[full] = jnp.zeros((16, 128), BF16)


def first_early_kernel(
    fe, init, got, w, strip1, strip2, strip3, s1, s2, s3, force, y, i16, columns, square, idx_v, idx, sem
):
    def body(even):
        n = init.shape[0]
        full = 3 * n
        put_tables(fe, got, None, idx_v, full, n, even)
        copy = pltpu.make_async_copy(idx_v, idx, sem)
        copy.start()
        count = 6 * REACH
        base = mirrored(REACH, count, full, even)
        put_force(force, fe, got, even, 0, n)
        y[pl.ds(0, count * 8), :] = force[pl.ds(base * 8, count * 8), :].astype(F32)

        def add_init():
            pushed = push_init(init, got, None, w, idx_v, columns, square, i16, base, count, n, even)
            y[pl.ds(0, count, stride=8), :] = y[pl.ds(0, count, stride=8), :] + pushed

        pl.when(lax.axis_index("tm") == 0)(add_init)
        s1[pl.ds(base, count)] = split(y[pl.ds(0, count * 8), :].reshape(count, 8, 128))
        for state in (s1, s2, s3):
            state[full] = jnp.zeros((16, 128), BF16)
        copy.wait()
        for k, src, dst in ((1, s1, s2), (2, s2, s3)):
            put_force(force, fe, got, even, k, n)
            size = (6 - 2 * k) * REACH
            base = mirrored((k + 1) * REACH, size, full, even)
            dst[pl.ds(base, size)] = split(apply_phi(src, idx, w, base, size) + force_at(force, base, size))
        put_strips((strip1, strip2, strip3), (s1, s2, s3), full, even)

    by_parity(body)


def first_late_kernel(
    fe, init, got_even, got_odd, strip1, strip2, strip3, w, pk, w1, end, idx_out,
    s1, s2, s3, force, y, i16, columns, square, idx, sem
):
    def body(even):
        n = init.shape[0]
        full = 3 * n
        put_tables(fe, got_even, got_odd, idx_out, full, n, even)
        copy = pltpu.make_async_copy(idx_out, idx, sem)
        copy.start()
        count = 4 * REACH
        base = mirrored(7 * REACH, count, full, even)
        put_force(force, fe, got_odd, not even, 0, n)
        y[...] = force[pl.ds(base * 8, count * 8), :].astype(F32)

        def add_init():
            pushed = push_init(init, got_even, got_odd, w, idx_out, columns, square, i16, base, count, n, even)
            y[pl.ds(0, count, stride=8), :] = y[pl.ds(0, count, stride=8), :] + pushed

        pl.when(lax.axis_index("tm") == 0)(add_init)
        s1[pl.ds(base, count)] = split(y[...].reshape(count, 8, 128))
        get_strips((strip1, strip2, strip3), (s1, s2, s3), full, even)
        copy.wait()
        for k, src, dst in ((1, s1, s2), (2, s2, s3), (3, s3, None)):
            put_force(force, fe, got_odd, not even, k, n)
            base = mirrored((7 - k) * REACH, count, full, even)
            value = apply_phi(src, idx, w, base, count) + force_at(force, base, count)
            if dst is None:
                w1[...] = value
                y[...] = value.reshape(n * 8, 128)
            else:
                dst[pl.ds(base, count)] = split(value)
        end[...] = block_end(y, pk, n)

    by_parity(body)


def scan_kernel(values, pk, starts):
    starts[...] = scan_starts(values[...], pk)


def scan_sum_kernel(values, w1, coarse, pk, starts, total):
    starts[...] = scan_starts(values[...], pk)
    total[...] = values[...] + (w1[...] + coarse[...])


NEAR = 2 * REACH


def put_pay(pay, state, value, side, n):
    def body(even):
        near = 0 if even else n - NEAR
        far = NEAR if even else n - side
        pay[pl.ds(0, NEAR)] = state[pl.ds(near, NEAR)]
        count = side - NEAR
        pay[pl.ds(NEAR, count // 2)] = value[far : far + count].reshape(count // 2, 16, 128).astype(BF16)

    by_parity(body)


def put_far(dst, got, right, n):
    count = 2 * (got.shape[0] - NEAR)
    dst[pl.ds(2 * n if right else n - NEAR, NEAR)] = got[pl.ds(0, NEAR)]
    leads = got[pl.ds(NEAR, count // 2)].astype(F32).reshape(count, 8, 128)
    far = jnp.concatenate([leads, jnp.zeros_like(leads)], axis=1).astype(BF16)
    dst[pl.ds(2 * n + NEAR if right else n - NEAR - count, count)] = far


def enter_first_kernel(*refs):
    *arrivals, starts, we, pk, state, pay_odd, y = refs
    n = starts.shape[0]
    value = enter(arrivals, we, pk, y, n) + starts[...]
    state[...] = split(value)
    put_pay(pay_odd, state, value, n, n)


def enter_second_kernel(*refs):
    *arrivals, starts, before, init, we, pk, state, pay_even, pay_odd, corr, y = refs
    n = starts.shape[0]
    value = enter(arrivals, we, pk, y, n) + starts[...]
    corr[...] = value
    old = before[...].astype(F32)
    y[...] = (value + (old[:, 0:8] + old[:, 8:16])).reshape(n * 8, 128)
    first = (lax.axis_index("tm") == 0).astype(F32)
    y[pl.ds(0, n, stride=8), :] = y[pl.ds(0, n, stride=8), :] + init[...] * first
    value = y[...].reshape(n, 8, 128)
    state[...] = split(value)
    side = (COARSEN - 1) * REACH
    pay_even[...] = state[pl.ds(jnp.where(even_place(), n - side, 0), side)]
    put_pay(pay_odd, state, value, side, n)


def put_own(dst, own, n):
    dst[pl.ds(n, n)] = own[...]
    dst[3 * n] = jnp.zeros((16, 128), BF16)


def put_block(dst, own, got, right, n):
    side = got.shape[0]
    put_own(dst, own, n)
    dst[pl.ds(2 * n if right else n - side, side)] = got[...]


def second_early_kernel(idx, own, got, w, pk, strip1, strip2, strip3, coarse, s0, s1, s2, s3):
    def body(even):
        n = own.shape[0]
        full = 3 * n
        coarse[...] = product(own[...].reshape(n * 16, 128), power(pk, 1))
        put_block(s0, own, got, even, n)
        for state in (s1, s2, s3):
            state[full] = jnp.zeros((16, 128), BF16)
        for k, src, dst in ((1, s0, s1), (2, s1, s2), (3, s2, s3)):
            size = (8 - 2 * k) * REACH
            base = mirrored(k * REACH, size, full, even)
            dst[pl.ds(base, size)] = split(apply_phi(src, idx, w, base, size))
        put_strips((strip1, strip2, strip3), (s1, s2, s3), full, even)

    by_parity(body)


def second_late_kernel(idx, own, got, strip1, strip2, strip3, coarse, w, pk, res, end, s0, s1, s2, s3, y):
    def body(even):
        n = own.shape[0]
        full = 3 * n
        put_own(s0, own, n)
        put_far(s0, got, not even, n)
        get_strips((strip1, strip2, strip3), (s1, s2, s3), full, even)
        count = 4 * REACH
        for k, src, dst in ((1, s0, s1), (2, s1, s2), (3, s2, s3)):
            base = mirrored((8 - k) * REACH, count, full, even)
            dst[pl.ds(base, count)] = split(apply_phi(src, idx, w, base, count))
        value = apply_phi(s3, idx, w, n, n)
        value = value - coarse[...]
        res[...] = value
        y[...] = value.reshape(n * 8, 128)
        end[...] = block_end(y, pk, n)

    by_parity(body)


def write_out(out, k, value, begin, flip, sems):
    size = value.shape[0]
    pitch = size + 8
    for e in range(size):
        flip[pl.ds(e, 8, stride=pitch), :] = value[e]
    rows = pl.ds(begin, size)
    copies = [
        pltpu.make_async_copy(flip.at[pl.ds(i * pitch, size)], out.at[i * COARSEN + k, rows], sems.at[k, i])
        for i in range(8)
    ]
    for copy in copies:
        copy.start()
    return copies


def third_early_kernel(
    idx, own, got, corr, total, fe, pay, w, pk, out, strip1, strip2, s0, s1, s2, force, flip0, flip1, flip2, flip3, sems
):
    def body(even):
        n = own.shape[0]
        full = 3 * n
        points = product(split(corr[...]).reshape(-1, 128), power(pk, 1)) + total[...]
        copies = write_out(out, COARSEN - 1, points, 0, flip3, sems)
        put_block(s0, own, got, even, n)
        for state in (s1, s2):
            state[full] = jnp.zeros((16, 128), BF16)
        for k, src, dst, flip in ((0, s0, s1, flip0), (1, s1, s2, flip1), (2, s2, None, flip2)):
            put_force(force, fe, pay, even, k, n)
            size = (5 - 2 * k) * REACH
            base = mirrored((2 + k) * REACH, size, full, even)
            value = apply_phi(src, idx, w, base, size) + force_at(force, base, size)
            if dst is not None:
                dst[pl.ds(base, size)] = split(value)
            mine = (3 - k) * REACH
            skip = size - mine
            kept = value[:mine] if even else value[skip:]
            copies += write_out(out, k, kept, n - mine if even else 0, flip, sems)
        put_strips((strip1, strip2), (s1, s2), full, even)
        for copy in copies:
            copy.wait()

    by_parity(body)


def third_late_kernel(
    idx, own, got, strip1, strip2, fe, pay, w, partial, out, s0, s1, s2, force, flip0, flip1, flip2, sems
):
    def body(even):
        n = own.shape[0]
        full = 3 * n
        put_own(s0, own, n)
        put_far(s0, got, not even, n)
        get_strips((strip1, strip2), (s1, s2), full, even)
        copies = []
        size = 3 * REACH
        for k, src, dst, flip in ((0, s0, s1, flip0), (1, s1, s2, flip1), (2, s2, None, flip2)):
            put_force(force, fe, pay, not even, k, n)
            base = mirrored((7 - k) * REACH, size, full, even)
            value = apply_phi(src, idx, w, base, size) + force_at(force, base, size)
            if dst is not None:
                dst[pl.ds(base, size)] = split(value)
            mine = (k + 1) * REACH
            kept = value[size - mine :] if even else value[:mine]
            copies += write_out(out, k, kept, 0 if even else n - mine, flip, sems)
        for copy in copies:
            copy.wait()

    by_parity(body)


def call(kernel, inputs, outs, scratch, spaces="", out_spaces="", aliases=None, flops=10**7, room=32):
    kinds = {"s": pltpu.SMEM, "h": pltpu.HBM, "v": pltpu.VMEM}

    def specs(arrays, letters):
        letters = letters.ljust(len(arrays), "v")
        return [pl.BlockSpec(memory_space=kinds[letter]) for letter in letters]

    moved = sum(a.size * a.dtype.itemsize for a in list(inputs) + list(outs))
    return pl.pallas_call(
        kernel,
        out_shape=outs,
        name=kernel.__name__,
        in_specs=specs(inputs, spaces),
        out_specs=specs(outs, out_spaces),
        scratch_shapes=scratch,
        input_output_aliases=aliases or {},
        compiler_params=pltpu.CompilerParams(vmem_limit_bytes=room * 1024 * 1024),
        cost_estimate=pl.CostEstimate(flops=flops, bytes_accessed=moved, transcendentals=0),
    )(*inputs)


def local(forcing, initial_state, connectivity, pattern, diag_block, face_blocks, coarse_block):
    n, width = initial_state.shape
    steps = forcing.shape[0]
    full = 3 * n
    tm = lax.axis_size("tm")
    shape = jax.ShapeDtypeStruct
    vmem = pltpu.VMEM
    dma = pltpu.SemaphoreType.DMA
    tiles = shape((n, 8, width), F32)
    state = shape((n, 16, width), BF16)
    ends = shape((n, width), F32)
    step_flops = 2 * 16 * 7 * width * 2 * width
    pay_rows = sum((COARSEN - 1 - k) * REACH * 8 for k in range(COARSEN)) + 2 * n + 16
    pay = shape((pay_rows, width), BF16)
    all_force = ((COARSEN * n * 8 + 16), width)
    fe, pay_even, pay_odd = call(
        pack_kernel,
        (forcing.reshape(steps // COARSEN, COARSEN, n, width), initial_state, connectivity.T, pattern.T),
        (shape(all_force, BF16), pay, pay),
        [
            vmem((COARSEN, 8, n, width), BF16),
            vmem((8 * (n + 8), width), F32),
            vmem((n, width), F32),
            vmem((6, n), jnp.int32),
            vmem((6, n), jnp.int32),
            vmem((16, 128), F32),
            vmem(all_force, BF16),
            vmem((pay_rows, width), BF16),
            vmem((pay_rows, width), BF16),
            dma((COARSEN + 3,)),
            dma((3,)),
        ],
        spaces="hhhh",
        flops=3 * 10**9,
        out_spaces="hhh",
        room=62,
    )
    pay_odd, pay_even = swapped(pay_odd, 1), swapped(pay_even, 0)
    w, pk, we = call(
        weight_kernel,
        (diag_block, face_blocks, coarse_block),
        (
            shape((8 * width, 2 * width), BF16),
            shape((8 * width, 2 * width), BF16),
            shape(((tm - 1) * width, 2 * width), BF16),
        ),
        [],
        flops=10**9,
    )
    spaces = vmem((full + 1, 16, width), BF16)
    force = vmem((full * 8, width), BF16)
    rows = vmem((n * 8, width), F32)
    strip = shape((STRIP, 16, width), BF16)
    tables = [vmem((256, 256), BF16), vmem((256, 128), F32), vmem((128, 128), F32)]
    smem = pltpu.SMEM((8, 256), jnp.int32)
    strips = call(
        first_early_kernel,
        (fe, initial_state, pay_even, w),
        (strip, strip, strip),
        [spaces] * 3 + [force, vmem((6 * REACH * 8, width), F32)] + tables + [vmem((8, 256), jnp.int32), smem, dma],
        flops=step_flops * 6 * REACH,
    )
    w1, end, idx = call(
        first_late_kernel,
        (fe, initial_state, pay_even, pay_odd, *strips, w, pk),
        (tiles, ends, shape((8, 256), jnp.int32)),
        [spaces] * 3 + [force, rows] + tables + [smem, dma],
        flops=step_flops * 12 * REACH,
    )
    arrivals = earlier(end)
    (starts,) = call(scan_kernel, (w1, pk), (tiles,), [])
    def across(side):
        return shape((NEAR + (side - NEAR) // 2, 16, width), BF16)

    coarse, end_odd = call(enter_first_kernel, (*arrivals, starts, we, pk), (state, across(n)), [rows])
    got_odd, got_even = swapped(end_odd, 1), swapped(coarse, 0)
    *strips, moved = call(
        second_early_kernel,
        (idx, coarse, got_even, w, pk),
        (strip, strip, strip, tiles),
        [spaces] * 4,
        spaces="s",
        flops=step_flops * 12 * REACH,
    )
    res, end = call(
        second_late_kernel,
        (idx, coarse, got_odd, *strips, moved, w, pk),
        (tiles, ends),
        [spaces] * 4 + [rows],
        spaces="s",
        flops=step_flops * 16 * REACH,
    )
    arrivals = earlier(end)
    starts, total = call(scan_sum_kernel, (res, w1, moved, pk), (tiles, tiles), [])
    side = (COARSEN - 1) * REACH
    coarse, end_even, end_odd, corr = call(
        enter_second_kernel,
        (*arrivals, starts, coarse, initial_state, we, pk),
        (state, shape((side, 16, width), BF16), across(side), tiles),
        [rows],
    )
    got_odd, got_even = swapped(end_odd, 1), swapped(end_even, 0)
    result = shape((steps, n, width), F32)
    flips = [vmem((8 * (m * REACH + 8), width), F32) for m in (3, 2, 1)]
    out, *strips = call(
        third_early_kernel,
        (idx, coarse, got_even, corr, total, fe, pay_even, w, pk),
        (result, strip, strip),
        [spaces] * 3 + [force] + flips + [vmem((8 * (n + 8), width), F32), dma((COARSEN, 8))],
        spaces="s",
        out_spaces="h",
        flops=step_flops * 9 * REACH,
    )
    (out,) = call(
        third_late_kernel,
        (idx, coarse, got_odd, *strips, fe, pay_odd, w, out),
        (result,),
        [spaces] * 3 + [force] + flips[::-1] + [dma((COARSEN - 1, 8))],
        spaces="svvvvvvvh",
        out_spaces="h",
        aliases={8: 0},
        flops=step_flops * 9 * REACH,
    )
    return out


def solution(mesh):
    return jax.shard_map(
        local,
        mesh=mesh,
        in_specs=(
            P("tm", ("groups", "space"), None),
            P(("groups", "space"), None),
            P("space", None),
            P("space", None),
            P(),
            P(),
            P(),
        ),
        out_specs=P("tm", ("groups", "space"), None),
        check_vma=False,
    )
```

```python
import functools

import jax
import jax.numpy as jnp
from jax import lax
from jax.experimental import pallas as pl
from jax.experimental.pallas import tpu as pltpu
from jax.sharding import PartitionSpec as P

COARSEN = 4
REACH = 16
F32 = jnp.float32
BF16 = jnp.bfloat16
CHUNK = 32


def swapped(value, first):
    count = lax.axis_size("space")
    pairs = []
    for i in range(first, count - 1, 2):
        pairs += [(i, i + 1), (i + 1, i)]
    return lax.ppermute(value, "space", pairs)


def earlier(value):
    count = lax.axis_size("tm")
    if count <= 8:
        return [lax.ppermute(value, "tm", [(i, i + s) for i in range(count - s)]) for s in range(1, count)]
    every = lax.all_gather(value, "tm")
    at = lax.axis_index("tm") - jnp.arange(1, count)
    picked = jnp.where((at >= 0)[:, None, None], jnp.take(every, jnp.maximum(at, 0), axis=0), 0.0)
    return [picked[s] for s in range(count - 1)]


def split(u):
    lead = u.astype(BF16).astype(F32)
    return jnp.concatenate([u, u - lead], axis=1).astype(BF16)


def split_rows(u):
    lead = u.astype(BF16)
    return jnp.concatenate([lead, (u - lead.astype(F32)).astype(BF16)], axis=0)


def product(x, weights):
    m = x.shape[0] // 16
    r = jnp.dot(x, weights, preferred_element_type=F32).reshape(m, 16, 256)
    return r[:, :8, :128] + (r[:, 8:, :128] + r[:, :8, 128:])


def product_rows(x, weights):
    m = x.shape[0] // 2
    r = jnp.dot(x, weights, preferred_element_type=F32)
    return r[:m, :128] + (r[m:, :128] + r[:m, 128:])


def put_halves(ref, w):
    lead = w.astype(BF16)
    ref[:, 0:128] = lead
    ref[:, 128:256] = (w - lead.astype(F32)).astype(BF16)


def power(pk, k):
    return pk[pl.ds(128 * (7 - k), 128), :]


def scan_starts(values, pk):
    y = values
    row = lax.broadcasted_iota(jnp.int32, y.shape, 1)
    for d in (1, 2, 4):
        z = product(split(y).reshape(-1, 128), power(pk, d))
        y = y + jnp.where(row >= d, pltpu.roll(z, d, axis=1), 0.0)
    return jnp.where(row >= 1, pltpu.roll(y, 1, axis=1), 0.0)


def block_end(y, pk, n):
    parts = [y[pl.ds(i, n, stride=8), :] for i in range(8)]
    return product_rows(split_rows(jnp.concatenate(parts, axis=1)), pk[...])


def enter(arrivals, we, pk, y, n):
    value = jnp.concatenate([a[...] for a in arrivals], axis=1)
    entry = product_rows(split_rows(value), we[...])
    y[pl.ds(0, n, stride=8), :] = entry
    rows = split_rows(entry)
    for i in range(1, 8):
        y[pl.ds(i, n, stride=8), :] = product_rows(rows, power(pk, i))
    return y[...].reshape(n, 8, 128)


def apply_phi(src, idx, w, base, size):
    cols = [src[pl.ds(base, size)].reshape(size * 16, 128)]
    for f in range(6):
        cols.append(jnp.concatenate([src[idx[f, base + e]] for e in range(size)], axis=0))
    return product(jnp.concatenate(cols, axis=1), w[...])


def even_place():
    return lax.rem(lax.axis_index("space"), 2) == 0


def by_parity(body):
    even = even_place()
    pl.when(even)(lambda: body(True))
    pl.when(jnp.logical_not(even))(lambda: body(False))


def mirrored(low, size, full, even):
    return full - low - size if even else low


def pack_kernel(
    forcing, init, conn, pattern, fe_out, even_out, odd_out,
    landed, rows, init_v, conn_v, pattern_v, offs, fe, pay_even, pay_odd, sems, out_sems
):
    n = init_v.shape[0]
    pitch = n + 8
    copies = [pltpu.make_async_copy(forcing.at[:, k], landed.at[k], sems.at[k]) for k in range(COARSEN)]
    small = ((conn, conn_v), (pattern, pattern_v), (init, init_v))
    copies += [pltpu.make_async_copy(src, dst, sems.at[COARSEN + i]) for i, (src, dst) in enumerate(small)]
    for copy in copies[COARSEN:] + copies[:COARSEN]:
        copy.start()
    for copy in copies[COARSEN:]:
        copy.wait()
    place = lax.broadcasted_iota(jnp.int32, (6, n), 1) + lax.axis_index("space") * n
    value = ((conn_v[...] - place) * pattern_v[...]).astype(F32)
    offs[...] = jnp.zeros_like(offs)
    offs[0:6, 0:n] = value
    offs[0:6, n : 2 * n] = value
    tab = offs[...].astype(BF16)
    fe[pl.ds(COARSEN * n * 8, 16), :] = tab
    lead = init_v[...].astype(BF16)
    rest = (init_v[...] - lead.astype(F32)).astype(BF16)
    even = even_place()
    at = sum((COARSEN - 1 - k) * REACH * 8 for k in range(COARSEN))
    for pay in (pay_even, pay_odd):
        pay[pl.ds(at, n), :] = lead
        pay[pl.ds(at + n, n), :] = rest
        pay[pl.ds(at + 2 * n, 16), :] = tab
    at = 0
    results = []
    for k in range(COARSEN):
        copies[k].wait()
        for i in range(8):
            rows[pl.ds(i * pitch, n), :] = landed[k, i].astype(F32)

        def body(pair, carry, k=k):
            e = pair * 2
            two = [rows[pl.ds(e + j, 8, stride=pitch), :] for j in range(2)]
            fe[pl.ds(pl.multiple_of((k * n + e) * 8, 16), 16), :] = jnp.concatenate(two, axis=0).astype(BF16)
            return carry

        lax.fori_loop(0, n // 2, body, 0, unroll=8)
        width = (COARSEN - 1 - k) * REACH * 8
        if width:
            for pay, right in ((pay_even, even), (pay_odd, jnp.logical_not(even))):
                begin = pl.multiple_of(k * n * 8 + jnp.where(right, n * 8 - width, 0), 128)
                pay[pl.ds(at, width), :] = fe[pl.ds(begin, width), :]
        at += width
        rows_k = pl.ds(k * n * 8, n * 8 + (16 if k == COARSEN - 1 else 0))
        results.append(pltpu.make_async_copy(fe.at[rows_k], fe_out.at[rows_k], out_sems.at[2 + k]))
        results[-1].start()
        if k == COARSEN - 2:
            results.append(pltpu.make_async_copy(pay_odd, odd_out, out_sems.at[0]))
            results.append(pltpu.make_async_copy(pay_even, even_out, out_sems.at[1]))
            results[-2].start()
            results[-1].start()
    for result in results:
        result.wait()


def weight_kernel(diag, faces, coarse, w, pk, we):
    put_halves(w.at[pl.ds(0, 128)], diag[...].T)
    for f in range(6):
        put_halves(w.at[pl.ds(128 * (f + 1), 128)], faces[f].T)

    def thirds(a):
        one = a.astype(BF16)
        rest = a - one.astype(F32)
        two = rest.astype(BF16)
        return one, two, (rest - two.astype(F32)).astype(BF16)

    def mul(a, b):
        (a1, a2, a3), (b1, b2, b3) = thirds(a), thirds(b)
        total = jnp.zeros((128, 128), F32)
        for x, y in ((a3, b1), (a1, b3), (a2, b2), (a2, b1), (a1, b2), (a1, b1)):
            total += jnp.dot(x, y, preferred_element_type=F32)
        return total

    rows = lax.broadcasted_iota(jnp.int32, (128, 128), 0)
    one = (rows == lax.broadcasted_iota(jnp.int32, (128, 128), 1)).astype(F32)
    powers = [one, coarse[...].T]
    for k in range(2, 9):
        powers.append(mul(powers[k // 2], powers[k - k // 2]))
    for k in range(8):
        put_halves(pk.at[pl.ds(128 * (7 - k), 128)], powers[k])

    def body(k, current):
        put_halves(we.at[pl.ds(pl.multiple_of(k * 128, 128), 128)], current)
        return mul(current, powers[8])

    lax.fori_loop(0, we.shape[0] // 128, body, one)


def put_force(dst, own, got, right, k, n):
    at = sum((COARSEN - 1 - j) * REACH * 8 for j in range(k))
    width = (COARSEN - 1 - k) * REACH * 8
    dst[pl.ds(n * 8, n * 8), :] = own[pl.ds(k * n * 8, n * 8), :]
    if width:
        to = 2 * n * 8 if right else n * 8 - width
        dst[pl.ds(to, width), :] = got[pl.ds(at, width), :]


def force_at(src, base, size):
    return src[pl.ds(base * 8, size * 8), :].astype(F32).reshape(size, 8, 128)


def put_tables(fe, got_even, got_odd, idx_v, full, n, even):
    lane = lax.broadcasted_iota(jnp.int32, (8, 128), 1)

    def table(ref):
        return 0.0 if ref is None else ref[pl.ds(ref.shape[0] - 16, 16), :].astype(F32)[0:8]

    from_even, from_odd = table(got_even), table(got_odd)
    low = jnp.where(lane < n, from_odd if even else from_even, table(fe))
    high = jnp.where(lane < n, from_even if even else from_odd, 0.0)
    for at, offs in ((0, low), (128, high)):
        value = jnp.where(offs != 0.0, lane + at + offs.astype(jnp.int32), full)
        idx_v[:, pl.ds(at, 128)] = value


def push_init(init, got_even, got_odd, w, idx_v, columns, square, i16, base, count, n, even):
    for at in (0, 128):
        square[...] = jnp.zeros_like(square)
        square[0:8, :] = idx_v[:, pl.ds(at, 128)].astype(F32)
        columns[pl.ds(at, 128), :] = square[...].T
    i16[...] = jnp.zeros_like(i16)
    lead = init[...].astype(BF16)
    i16[pl.ds(n, n), 0:128] = lead
    i16[pl.ds(n, n), 128:256] = (init[...] - lead.astype(F32)).astype(BF16)
    for ref, right in ((got_even, even), (got_odd, not even)):
        if ref is not None:
            at = ref.shape[0] - 16
            to = 2 * n if right else 0
            i16[pl.ds(to, n), 0:128] = ref[pl.ds(at - 2 * n, n), :]
            i16[pl.ds(to, n), 128:256] = ref[pl.ds(at - n, n), :]
    rows = pl.ds(base, count)
    place = columns[rows, :]
    spot = lax.broadcasted_iota(jnp.int32, (count, 256), 1).astype(F32)
    cols = [i16[rows, :]]
    for f in range(6):
        hot = (spot == place[:, f : f + 1]).astype(F32).astype(BF16)
        cols.append(jnp.dot(hot, i16[...], preferred_element_type=F32).astype(BF16))
    leads = jnp.concatenate([c[:, 0:128] for c in cols], axis=1)
    rests = jnp.concatenate([c[:, 128:256] for c in cols], axis=1)
    return product_rows(jnp.concatenate([leads, rests], axis=0), w[...])


STRIPS = (5 * REACH, 4 * REACH, 3 * REACH)
STRIP = 2 * REACH


def put_strips(strips, states, full, even):
    for strip, state, low in zip(strips, states, STRIPS):
        strip[...] = state[pl.ds(mirrored(low, STRIP, full, even), STRIP)]


def get_strips(strips, states, full, even):
    for strip, state, low in zip(strips, states, STRIPS):
        state[pl.ds(mirrored(low, STRIP, full, even), STRIP)] = strip[...]
        state[full] = jnp.zeros((16, 128), BF16)


def first_early_kernel(
    fe, init, got, w, strip1, strip2, strip3, s1, s2, s3, force, y, i16, columns, square, idx_v, idx, sem
):
    def body(even):
        n = init.shape[0]
        full = 3 * n
        put_tables(fe, got, None, idx_v, full, n, even)
        copy = pltpu.make_async_copy(idx_v, idx, sem)
        copy.start()
        count = 6 * REACH
        base = mirrored(REACH, count, full, even)
        put_force(force, fe, got, even, 0, n)
        y[pl.ds(0, count * 8), :] = force[pl.ds(base * 8, count * 8), :].astype(F32)

        def add_init():
            pushed = push_init(init, got, None, w, idx_v, columns, square, i16, base, count, n, even)
            y[pl.ds(0, count, stride=8), :] = y[pl.ds(0, count, stride=8), :] + pushed

        pl.when(lax.axis_index("tm") == 0)(add_init)
        s1[pl.ds(base, count)] = split(y[pl.ds(0, count * 8), :].reshape(count, 8, 128))
        for state in (s1, s2, s3):
            state[full] = jnp.zeros((16, 128), BF16)
        copy.wait()
        for k, src, dst in ((1, s1, s2), (2, s2, s3)):
            put_force(force, fe, got, even, k, n)
            size = (6 - 2 * k) * REACH
            base = mirrored((k + 1) * REACH, size, full, even)
            dst[pl.ds(base, size)] = split(apply_phi(src, idx, w, base, size) + force_at(force, base, size))
        put_strips((strip1, strip2, strip3), (s1, s2, s3), full, even)

    by_parity(body)


def first_late_kernel(
    fe, init, got_even, got_odd, strip1, strip2, strip3, w, pk, w1, end, idx_out,
    s1, s2, s3, force, y, i16, columns, square, idx, sem
):
    def body(even):
        n = init.shape[0]
        full = 3 * n
        put_tables(fe, got_even, got_odd, idx_out, full, n, even)
        copy = pltpu.make_async_copy(idx_out, idx, sem)
        copy.start()
        count = 4 * REACH
        base = mirrored(7 * REACH, count, full, even)
        put_force(force, fe, got_odd, not even, 0, n)
        y[...] = force[pl.ds(base * 8, count * 8), :].astype(F32)

        def add_init():
            pushed = push_init(init, got_even, got_odd, w, idx_out, columns, square, i16, base, count, n, even)
            y[pl.ds(0, count, stride=8), :] = y[pl.ds(0, count, stride=8), :] + pushed

        pl.when(lax.axis_index("tm") == 0)(add_init)
        s1[pl.ds(base, count)] = split(y[...].reshape(count, 8, 128))
        get_strips((strip1, strip2, strip3), (s1, s2, s3), full, even)
        copy.wait()
        for k, src, dst in ((1, s1, s2), (2, s2, s3), (3, s3, None)):
            put_force(force, fe, got_odd, not even, k, n)
            base = mirrored((7 - k) * REACH, count, full, even)
            value = apply_phi(src, idx, w, base, count) + force_at(force, base, count)
            if dst is None:
                w1[...] = value
                y[...] = value.reshape(n * 8, 128)
            else:
                dst[pl.ds(base, count)] = split(value)
        end[...] = block_end(y, pk, n)

    by_parity(body)


def scan_kernel(values, pk, starts):
    starts[...] = scan_starts(values[...], pk)


def scan_sum_kernel(values, w1, coarse, pk, starts, total):
    starts[...] = scan_starts(values[...], pk)
    total[...] = values[...] + (w1[...] + coarse[...])


NEAR = 2 * REACH


def put_pay(pay, state, value, side, n):
    def body(even):
        near = 0 if even else n - NEAR
        far = NEAR if even else n - side
        pay[pl.ds(0, NEAR)] = state[pl.ds(near, NEAR)]
        count = side - NEAR
        pay[pl.ds(NEAR, count // 2)] = value[far : far + count].reshape(count // 2, 16, 128).astype(BF16)

    by_parity(body)


def put_far(dst, got, right, n):
    count = 2 * (got.shape[0] - NEAR)
    dst[pl.ds(2 * n if right else n - NEAR, NEAR)] = got[pl.ds(0, NEAR)]
    leads = got[pl.ds(NEAR, count // 2)].astype(F32).reshape(count, 8, 128)
    far = jnp.concatenate([leads, jnp.zeros_like(leads)], axis=1).astype(BF16)
    dst[pl.ds(2 * n + NEAR if right else n - NEAR - count, count)] = far


def enter_first_kernel(*refs):
    *arrivals, starts, we, pk, state, pay_odd, y = refs
    n = starts.shape[0]
    value = enter(arrivals, we, pk, y, n) + starts[...]
    state[...] = split(value)
    put_pay(pay_odd, state, value, n, n)


def enter_second_kernel(*refs):
    *arrivals, starts, before, init, we, pk, state, pay_even, pay_odd, corr, y = refs
    n = starts.shape[0]
    value = enter(arrivals, we, pk, y, n) + starts[...]
    corr[...] = value
    old = before[...].astype(F32)
    y[...] = (value + (old[:, 0:8] + old[:, 8:16])).reshape(n * 8, 128)
    first = (lax.axis_index("tm") == 0).astype(F32)
    y[pl.ds(0, n, stride=8), :] = y[pl.ds(0, n, stride=8), :] + init[...] * first
    value = y[...].reshape(n, 8, 128)
    state[...] = split(value)
    side = (COARSEN - 1) * REACH
    pay_even[...] = state[pl.ds(jnp.where(even_place(), n - side, 0), side)]
    put_pay(pay_odd, state, value, side, n)


def put_own(dst, own, n):
    dst[pl.ds(n, n)] = own[...]
    dst[3 * n] = jnp.zeros((16, 128), BF16)


def put_block(dst, own, got, right, n):
    side = got.shape[0]
    put_own(dst, own, n)
    dst[pl.ds(2 * n if right else n - side, side)] = got[...]


def second_early_kernel(idx, own, got, w, pk, strip1, strip2, strip3, coarse, s0, s1, s2, s3):
    def body(even):
        n = own.shape[0]
        full = 3 * n
        coarse[...] = product(own[...].reshape(n * 16, 128), power(pk, 1))
        put_block(s0, own, got, even, n)
        for state in (s1, s2, s3):
            state[full] = jnp.zeros((16, 128), BF16)
        for k, src, dst in ((1, s0, s1), (2, s1, s2), (3, s2, s3)):
            size = (8 - 2 * k) * REACH
            base = mirrored(k * REACH, size, full, even)
            dst[pl.ds(base, size)] = split(apply_phi(src, idx, w, base, size))
        put_strips((strip1, strip2, strip3), (s1, s2, s3), full, even)

    by_parity(body)


def second_late_kernel(idx, own, got, strip1, strip2, strip3, coarse, w, pk, res, end, s0, s1, s2, s3, y):
    def body(even):
        n = own.shape[0]
        full = 3 * n
        put_own(s0, own, n)
        put_far(s0, got, not even, n)
        get_strips((strip1, strip2, strip3), (s1, s2, s3), full, even)
        count = 4 * REACH
        for k, src, dst in ((1, s0, s1), (2, s1, s2), (3, s2, s3)):
            base = mirrored((8 - k) * REACH, count, full, even)
            dst[pl.ds(base, count)] = split(apply_phi(src, idx, w, base, count))
        value = apply_phi(s3, idx, w, n, n)
        value = value - coarse[...]
        res[...] = value
        y[...] = value.reshape(n * 8, 128)
        end[...] = block_end(y, pk, n)

    by_parity(body)


def flip_tiles(flip, value, begin):
    lines = flip.reshape(8 * flip.shape[1], 128)
    for e in range(value.shape[0]):
        lines[pl.ds(begin + e, 8, stride=flip.shape[1]), :] = value[e]


def write_out(out, k, flip, begin, size, sems):
    copy = pltpu.make_async_copy(flip.at[:, pl.ds(0, size)], out.at[:, k, pl.ds(begin, size)], sems.at[k])
    copy.start()
    return copy


def third_early_kernel(
    idx, own, got, corr, total, fe, pay, w, pk, out, strip1, strip2, kept, s0, s1, s2, force, flip0, flip1, flip3, sems
):
    def body(even):
        n = own.shape[0]
        full = 3 * n
        points = product(split(corr[...]).reshape(-1, 128), power(pk, 1)) + total[...]
        flip_tiles(flip3, points, 0)
        copies = [write_out(out, COARSEN - 1, flip3, 0, n, sems)]
        put_block(s0, own, got, even, n)
        for state in (s1, s2):
            state[full] = jnp.zeros((16, 128), BF16)
        for k, src, dst, flip in ((0, s0, s1, flip0), (1, s1, s2, flip1), (2, s2, None, None)):
            put_force(force, fe, pay, even, k, n)
            size = (5 - 2 * k) * REACH
            base = mirrored((2 + k) * REACH, size, full, even)
            value = apply_phi(src, idx, w, base, size) + force_at(force, base, size)
            if dst is not None:
                dst[pl.ds(base, size)] = split(value)
            mine = (3 - k) * REACH
            value = value[:mine] if even else value[size - mine :]
            if flip is None:
                kept[...] = value
            else:
                flip_tiles(flip, value, 0)
                copies.append(write_out(out, k, flip, n - mine if even else 0, mine, sems))
        put_strips((strip1, strip2), (s1, s2), full, even)
        for copy in copies:
            copy.wait()

    by_parity(body)


def third_late_kernel(
    idx, own, got, strip1, strip2, kept, fe, pay, w, partial, out, s0, s1, s2, force, flip0, flip1, flip2, sems
):
    def body(even):
        n = own.shape[0]
        full = 3 * n
        put_own(s0, own, n)
        put_far(s0, got, not even, n)
        get_strips((strip1, strip2), (s1, s2), full, even)
        copies = []
        size = 3 * REACH
        flip_tiles(flip2, kept[...], n - REACH if even else 0)
        for k, src, dst, flip in ((0, s0, s1, flip0), (1, s1, s2, flip1), (2, s2, None, flip2)):
            put_force(force, fe, pay, not even, k, n)
            base = mirrored((7 - k) * REACH, size, full, even)
            value = apply_phi(src, idx, w, base, size) + force_at(force, base, size)
            if dst is not None:
                dst[pl.ds(base, size)] = split(value)
            mine = (k + 1) * REACH
            value = value[size - mine :] if even else value[:mine]
            if dst is None:
                flip_tiles(flip, value, 0 if even else n - mine)
                copies.append(write_out(out, k, flip, 0, n, sems))
            else:
                flip_tiles(flip, value, 0)
                copies.append(write_out(out, k, flip, 0 if even else n - mine, mine, sems))
        for copy in copies:
            copy.wait()

    by_parity(body)


def call(kernel, inputs, outs, scratch, spaces="", out_spaces="", aliases=None, flops=10**7, room=32):
    kinds = {"s": pltpu.SMEM, "h": pltpu.HBM, "v": pltpu.VMEM}

    def specs(arrays, letters):
        letters = letters.ljust(len(arrays), "v")
        return [pl.BlockSpec(memory_space=kinds[letter]) for letter in letters]

    moved = sum(a.size * a.dtype.itemsize for a in list(inputs) + list(outs))
    return pl.pallas_call(
        kernel,
        out_shape=outs,
        name=kernel.__name__,
        in_specs=specs(inputs, spaces),
        out_specs=specs(outs, out_spaces),
        scratch_shapes=scratch,
        input_output_aliases=aliases or {},
        compiler_params=pltpu.CompilerParams(vmem_limit_bytes=room * 1024 * 1024),
        cost_estimate=pl.CostEstimate(flops=flops, bytes_accessed=moved, transcendentals=0),
    )(*inputs)


def local(forcing, initial_state, connectivity, pattern, diag_block, face_blocks, coarse_block):
    n, width = initial_state.shape
    steps = forcing.shape[0]
    full = 3 * n
    tm = lax.axis_size("tm")
    shape = jax.ShapeDtypeStruct
    vmem = pltpu.VMEM
    dma = pltpu.SemaphoreType.DMA
    tiles = shape((n, 8, width), F32)
    state = shape((n, 16, width), BF16)
    ends = shape((n, width), F32)
    step_flops = 2 * 16 * 7 * width * 2 * width
    pay_rows = sum((COARSEN - 1 - k) * REACH * 8 for k in range(COARSEN)) + 2 * n + 16
    pay = shape((pay_rows, width), BF16)
    all_force = ((COARSEN * n * 8 + 16), width)
    fe, pay_even, pay_odd = call(
        pack_kernel,
        (forcing.reshape(steps // COARSEN, COARSEN, n, width), initial_state, connectivity.T, pattern.T),
        (shape(all_force, BF16), pay, pay),
        [
            vmem((COARSEN, 8, n, width), BF16),
            vmem((8 * (n + 8), width), F32),
            vmem((n, width), F32),
            vmem((6, n), jnp.int32),
            vmem((6, n), jnp.int32),
            vmem((16, 128), F32),
            vmem(all_force, BF16),
            vmem((pay_rows, width), BF16),
            vmem((pay_rows, width), BF16),
            dma((COARSEN + 3,)),
            dma((2 + COARSEN,)),
        ],
        spaces="hhhh",
        flops=3 * 10**9,
        out_spaces="hhh",
        room=62,
    )
    pay_odd, pay_even = swapped(pay_odd, 1), swapped(pay_even, 0)
    w, pk, we = call(
        weight_kernel,
        (diag_block, face_blocks, coarse_block),
        (
            shape((7 * width, 2 * width), BF16),
            shape((8 * width, 2 * width), BF16),
            shape(((tm - 1) * width, 2 * width), BF16),
        ),
        [],
        flops=10**9,
    )
    spaces = vmem((full + 1, 16, width), BF16)
    force = vmem((full * 8, width), BF16)
    rows = vmem((n * 8, width), F32)
    strip = shape((STRIP, 16, width), BF16)
    tables = [vmem((256, 256), BF16), vmem((256, 128), F32), vmem((128, 128), F32)]
    smem = pltpu.SMEM((8, 256), jnp.int32)
    strips = call(
        first_early_kernel,
        (fe, initial_state, pay_even, w),
        (strip, strip, strip),
        [spaces] * 3 + [force, vmem((6 * REACH * 8, width), F32)] + tables + [vmem((8, 256), jnp.int32), smem, dma],
        flops=step_flops * 6 * REACH,
    )
    w1, end, idx = call(
        first_late_kernel,
        (fe, initial_state, pay_even, pay_odd, *strips, w, pk),
        (tiles, ends, shape((8, 256), jnp.int32)),
        [spaces] * 3 + [force, rows] + tables + [smem, dma],
        flops=step_flops * 12 * REACH,
    )
    arrivals = earlier(end)
    (starts,) = call(scan_kernel, (w1, pk), (tiles,), [])
    def across(side):
        return shape((NEAR + (side - NEAR) // 2, 16, width), BF16)

    coarse, end_odd = call(enter_first_kernel, (*arrivals, starts, we, pk), (state, across(n)), [rows])
    got_odd, got_even = swapped(end_odd, 1), swapped(coarse, 0)
    *strips, moved = call(
        second_early_kernel,
        (idx, coarse, got_even, w, pk),
        (strip, strip, strip, tiles),
        [spaces] * 4,
        spaces="s",
        flops=step_flops * 12 * REACH,
    )
    res, end = call(
        second_late_kernel,
        (idx, coarse, got_odd, *strips, moved, w, pk),
        (tiles, ends),
        [spaces] * 4 + [rows],
        spaces="s",
        flops=step_flops * 16 * REACH,
    )
    arrivals = earlier(end)
    starts, total = call(scan_sum_kernel, (res, w1, moved, pk), (tiles, tiles), [])
    side = (COARSEN - 1) * REACH
    coarse, end_even, end_odd, corr = call(
        enter_second_kernel,
        (*arrivals, starts, coarse, initial_state, we, pk),
        (state, shape((side, 16, width), BF16), across(side), tiles),
        [rows],
    )
    got_odd, got_even = swapped(end_odd, 1), swapped(end_even, 0)
    result = shape((steps // COARSEN, COARSEN, n, width), F32)

    def flip(blocks):
        return vmem((8, blocks * REACH + 8, width), F32)

    out, *strips = call(
        third_early_kernel,
        (idx, coarse, got_even, corr, total, fe, pay_even, w, pk),
        (result, strip, strip, shape((REACH, 8, width), F32)),
        [spaces] * 3 + [force, flip(3), flip(2), vmem((8, n + 8, width), F32), dma((COARSEN,))],
        spaces="s",
        out_spaces="h",
        flops=step_flops * 9 * REACH,
    )
    (out,) = call(
        third_late_kernel,
        (idx, coarse, got_odd, *strips, fe, pay_odd, w, out),
        (result,),
        [spaces] * 3 + [force, flip(1), flip(2), vmem((8, n + 8, width), F32), dma((COARSEN - 1,))],
        spaces="svvvvvvvvh",
        out_spaces="h",
        aliases={9: 0},
        flops=step_flops * 9 * REACH,
    )
    return out.reshape(steps, n, width)


def solution(mesh):
    return jax.shard_map(
        local,
        mesh=mesh,
        in_specs=(
            P("tm", ("groups", "space"), None),
            P(("groups", "space"), None),
            P("space", None),
            P("space", None),
            P(),
            P(),
            P(),
        ),
        out_specs=P("tm", ("groups", "space"), None),
        check_vma=False,
    )
```

```python
import functools

import jax
import jax.numpy as jnp
from jax import lax
from jax.experimental import pallas as pl
from jax.experimental.pallas import tpu as pltpu
from jax.sharding import PartitionSpec as P

COARSEN = 4
REACH = 16
F32 = jnp.float32
BF16 = jnp.bfloat16
CHUNK = 32


def swapped(value, first):
    count = lax.axis_size("space")
    pairs = []
    for i in range(first, count - 1, 2):
        pairs += [(i, i + 1), (i + 1, i)]
    return lax.ppermute(value, "space", pairs)


def earlier(value):
    count = lax.axis_size("tm")
    if count <= 8:
        return [lax.ppermute(value, "tm", [(i, i + s) for i in range(count - s)]) for s in range(1, count)]
    every = lax.all_gather(value, "tm")
    at = lax.axis_index("tm") - jnp.arange(1, count)
    picked = jnp.where((at >= 0)[:, None, None], jnp.take(every, jnp.maximum(at, 0), axis=0), 0.0)
    return [picked[s] for s in range(count - 1)]


def split(u):
    lead = u.astype(BF16).astype(F32)
    return jnp.concatenate([u, u - lead], axis=1).astype(BF16)


def split_rows(u):
    lead = u.astype(BF16)
    return jnp.concatenate([lead, (u - lead.astype(F32)).astype(BF16)], axis=0)


def product(x, weights):
    m = x.shape[0] // 16
    r = jnp.dot(x, weights, preferred_element_type=F32).reshape(m, 16, 256)
    return r[:, :8, :128] + (r[:, 8:, :128] + r[:, :8, 128:])


def product_rows(x, weights):
    m = x.shape[0] // 2
    r = jnp.dot(x, weights, preferred_element_type=F32)
    return r[:m, :128] + (r[m:, :128] + r[:m, 128:])


def put_halves(ref, w):
    lead = w.astype(BF16)
    ref[:, 0:128] = lead
    ref[:, 128:256] = (w - lead.astype(F32)).astype(BF16)


def power(pk, k):
    return pk[pl.ds(128 * (7 - k), 128), :]


def scan_starts(values, pk):
    y = values
    row = lax.broadcasted_iota(jnp.int32, y.shape, 1)
    for d in (1, 2, 4):
        z = product(split(y).reshape(-1, 128), power(pk, d))
        y = y + jnp.where(row >= d, pltpu.roll(z, d, axis=1), 0.0)
    return jnp.where(row >= 1, pltpu.roll(y, 1, axis=1), 0.0)


def block_end(y, pk, n):
    parts = [y[pl.ds(i, n, stride=8), :] for i in range(8)]
    return product_rows(split_rows(jnp.concatenate(parts, axis=1)), pk[...])


def enter(arrivals, we, pk, y, n):
    value = jnp.concatenate([a[...] for a in arrivals], axis=1)
    entry = product_rows(split_rows(value), we[...])
    y[pl.ds(0, n, stride=8), :] = entry
    rows = split_rows(entry)
    for i in range(1, 8):
        y[pl.ds(i, n, stride=8), :] = product_rows(rows, power(pk, i))
    return y[...].reshape(n, 8, 128)


def apply_phi(src, idx, w, base, size):
    cols = [src[pl.ds(base, size)].reshape(size * 16, 128)]
    for f in range(6):
        cols.append(jnp.concatenate([src[idx[f, base + e]] for e in range(size)], axis=0))
    return product(jnp.concatenate(cols, axis=1), w[...])


def even_place():
    return lax.rem(lax.axis_index("space"), 2) == 0


def by_parity(body):
    even = even_place()
    pl.when(even)(lambda: body(True))
    pl.when(jnp.logical_not(even))(lambda: body(False))


def mirrored(low, size, full, even):
    return full - low - size if even else low


def pack_kernel(
    forcing, init, conn, pattern, fe_out, even_out, odd_out,
    landed, rows, init_v, conn_v, pattern_v, offs, fe, pay_even, pay_odd, sems, out_sems
):
    n = init_v.shape[0]
    pitch = n + 8
    copies = [pltpu.make_async_copy(forcing.at[:, k], landed.at[k], sems.at[k]) for k in range(COARSEN)]
    small = ((conn, conn_v), (pattern, pattern_v), (init, init_v))
    copies += [pltpu.make_async_copy(src, dst, sems.at[COARSEN + i]) for i, (src, dst) in enumerate(small)]
    for copy in copies[COARSEN:] + copies[:COARSEN]:
        copy.start()
    for copy in copies[COARSEN:]:
        copy.wait()
    place = lax.broadcasted_iota(jnp.int32, (6, n), 1) + lax.axis_index("space") * n
    value = ((conn_v[...] - place) * pattern_v[...]).astype(F32)
    offs[...] = jnp.zeros_like(offs)
    offs[0:6, 0:n] = value
    offs[0:6, n : 2 * n] = value
    tab = offs[...].astype(BF16)
    fe[pl.ds(COARSEN * n * 8, 16), :] = tab
    lead = init_v[...].astype(BF16)
    rest = (init_v[...] - lead.astype(F32)).astype(BF16)
    even = even_place()
    at = sum((COARSEN - 1 - k) * REACH * 8 for k in range(COARSEN))
    for pay in (pay_even, pay_odd):
        pay[pl.ds(at, n), :] = lead
        pay[pl.ds(at + n, n), :] = rest
        pay[pl.ds(at + 2 * n, 16), :] = tab
    at = 0
    results = []
    for k in range(COARSEN):
        copies[k].wait()
        for i in range(8):
            rows[pl.ds(i * pitch, n), :] = landed[k, i].astype(F32)

        def body(pair, carry, k=k):
            e = pair * 2
            two = [rows[pl.ds(e + j, 8, stride=pitch), :] for j in range(2)]
            fe[pl.ds(pl.multiple_of((k * n + e) * 8, 16), 16), :] = jnp.concatenate(two, axis=0).astype(BF16)
            return carry

        lax.fori_loop(0, n // 2, body, 0, unroll=8)
        width = (COARSEN - 1 - k) * REACH * 8
        if width:
            for pay, right in ((pay_even, even), (pay_odd, jnp.logical_not(even))):
                begin = pl.multiple_of(k * n * 8 + jnp.where(right, n * 8 - width, 0), 128)
                pay[pl.ds(at, width), :] = fe[pl.ds(begin, width), :]
        at += width
        rows_k = pl.ds(k * n * 8, n * 8 + (16 if k == COARSEN - 1 else 0))
        results.append(pltpu.make_async_copy(fe.at[rows_k], fe_out.at[rows_k], out_sems.at[2 + k]))
        results[-1].start()
        if k == COARSEN - 2:
            results.append(pltpu.make_async_copy(pay_odd, odd_out, out_sems.at[0]))
            results.append(pltpu.make_async_copy(pay_even, even_out, out_sems.at[1]))
            results[-2].start()
            results[-1].start()
    for result in results:
        result.wait()


def weight_kernel(diag, faces, coarse, w, pk, we):
    put_halves(w.at[pl.ds(0, 128)], diag[...].T)
    for f in range(6):
        put_halves(w.at[pl.ds(128 * (f + 1), 128)], faces[f].T)

    def thirds(a):
        one = a.astype(BF16)
        rest = a - one.astype(F32)
        two = rest.astype(BF16)
        return one, two, (rest - two.astype(F32)).astype(BF16)

    def mul(a, b):
        (a1, a2, a3), (b1, b2, b3) = thirds(a), thirds(b)
        total = jnp.zeros((128, 128), F32)
        for x, y in ((a3, b1), (a1, b3), (a2, b2), (a2, b1), (a1, b2), (a1, b1)):
            total += jnp.dot(x, y, preferred_element_type=F32)
        return total

    rows = lax.broadcasted_iota(jnp.int32, (128, 128), 0)
    one = (rows == lax.broadcasted_iota(jnp.int32, (128, 128), 1)).astype(F32)
    powers = [one, coarse[...].T]
    for k in range(2, 9):
        powers.append(mul(powers[k // 2], powers[k - k // 2]))
    for k in range(8):
        put_halves(pk.at[pl.ds(128 * (7 - k), 128)], powers[k])

    def body(k, current):
        put_halves(we.at[pl.ds(pl.multiple_of(k * 128, 128), 128)], current)
        return mul(current, powers[8])

    lax.fori_loop(0, we.shape[0] // 128, body, one)


def put_force(dst, own, got, right, k, n):
    at = sum((COARSEN - 1 - j) * REACH * 8 for j in range(k))
    width = (COARSEN - 1 - k) * REACH * 8
    dst[pl.ds(n * 8, n * 8), :] = own[pl.ds(k * n * 8, n * 8), :]
    if width:
        to = 2 * n * 8 if right else n * 8 - width
        dst[pl.ds(to, width), :] = got[pl.ds(at, width), :]


def force_at(src, base, size):
    return src[pl.ds(base * 8, size * 8), :].astype(F32).reshape(size, 8, 128)


def put_tables(fe, got_even, got_odd, idx_v, full, n, even):
    lane = lax.broadcasted_iota(jnp.int32, (8, 128), 1)

    def table(ref):
        return 0.0 if ref is None else ref[pl.ds(ref.shape[0] - 16, 16), :].astype(F32)[0:8]

    from_even, from_odd = table(got_even), table(got_odd)
    low = jnp.where(lane < n, from_odd if even else from_even, table(fe))
    high = jnp.where(lane < n, from_even if even else from_odd, 0.0)
    for at, offs in ((0, low), (128, high)):
        value = jnp.where(offs != 0.0, lane + at + offs.astype(jnp.int32), full)
        idx_v[:, pl.ds(at, 128)] = value


def push_init(init, got_even, got_odd, w, idx_v, columns, square, i16, base, count, n, even):
    for at in (0, 128):
        square[...] = jnp.zeros_like(square)
        square[0:8, :] = idx_v[:, pl.ds(at, 128)].astype(F32)
        columns[pl.ds(at, 128), :] = square[...].T
    i16[...] = jnp.zeros_like(i16)
    lead = init[...].astype(BF16)
    i16[pl.ds(n, n), 0:128] = lead
    i16[pl.ds(n, n), 128:256] = (init[...] - lead.astype(F32)).astype(BF16)
    for ref, right in ((got_even, even), (got_odd, not even)):
        if ref is not None:
            at = ref.shape[0] - 16
            to = 2 * n if right else 0
            i16[pl.ds(to, n), 0:128] = ref[pl.ds(at - 2 * n, n), :]
            i16[pl.ds(to, n), 128:256] = ref[pl.ds(at - n, n), :]
    rows = pl.ds(base, count)
    place = columns[rows, :]
    spot = lax.broadcasted_iota(jnp.int32, (count, 256), 1).astype(F32)
    cols = [i16[rows, :]]
    for f in range(6):
        hot = (spot == place[:, f : f + 1]).astype(F32).astype(BF16)
        cols.append(jnp.dot(hot, i16[...], preferred_element_type=F32).astype(BF16))
    leads = jnp.concatenate([c[:, 0:128] for c in cols], axis=1)
    rests = jnp.concatenate([c[:, 128:256] for c in cols], axis=1)
    return product_rows(jnp.concatenate([leads, rests], axis=0), w[...])


STRIPS = (5 * REACH, 4 * REACH, 3 * REACH)
STRIP = 2 * REACH


def put_strips(strips, states, full, even):
    for strip, state, low in zip(strips, states, STRIPS):
        strip[...] = state[pl.ds(mirrored(low, STRIP, full, even), STRIP)]


def get_strips(strips, states, full, even):
    for strip, state, low in zip(strips, states, STRIPS):
        state[pl.ds(mirrored(low, STRIP, full, even), STRIP)] = strip[...]
        state[full] = jnp.zeros((16, 128), BF16)


def first_early_kernel(
    fe, init, got, w, strip1, strip2, strip3, s1, s2, s3, force, y, i16, columns, square, idx_v, idx, sem
):
    def body(even):
        n = init.shape[0]
        full = 3 * n
        put_tables(fe, got, None, idx_v, full, n, even)
        copy = pltpu.make_async_copy(idx_v, idx, sem)
        copy.start()
        count = 6 * REACH
        base = mirrored(REACH, count, full, even)
        put_force(force, fe, got, even, 0, n)
        y[pl.ds(0, count * 8), :] = force[pl.ds(base * 8, count * 8), :].astype(F32)

        def add_init():
            pushed = push_init(init, got, None, w, idx_v, columns, square, i16, base, count, n, even)
            y[pl.ds(0, count, stride=8), :] = y[pl.ds(0, count, stride=8), :] + pushed

        pl.when(lax.axis_index("tm") == 0)(add_init)
        s1[pl.ds(base, count)] = split(y[pl.ds(0, count * 8), :].reshape(count, 8, 128))
        for state in (s1, s2, s3):
            state[full] = jnp.zeros((16, 128), BF16)
        copy.wait()
        for k, src, dst in ((1, s1, s2), (2, s2, s3)):
            put_force(force, fe, got, even, k, n)
            size = (6 - 2 * k) * REACH
            base = mirrored((k + 1) * REACH, size, full, even)
            dst[pl.ds(base, size)] = split(apply_phi(src, idx, w, base, size) + force_at(force, base, size))
        put_strips((strip1, strip2, strip3), (s1, s2, s3), full, even)

    by_parity(body)


def first_late_kernel(
    fe, init, got_even, got_odd, strip1, strip2, strip3, w, pk, w1, end, idx_out,
    s1, s2, s3, force, y, i16, columns, square, idx, sem
):
    def body(even):
        n = init.shape[0]
        full = 3 * n
        put_tables(fe, got_even, got_odd, idx_out, full, n, even)
        copy = pltpu.make_async_copy(idx_out, idx, sem)
        copy.start()
        count = 4 * REACH
        base = mirrored(7 * REACH, count, full, even)
        put_force(force, fe, got_odd, not even, 0, n)
        y[...] = force[pl.ds(base * 8, count * 8), :].astype(F32)

        def add_init():
            pushed = push_init(init, got_even, got_odd, w, idx_out, columns, square, i16, base, count, n, even)
            y[pl.ds(0, count, stride=8), :] = y[pl.ds(0, count, stride=8), :] + pushed

        pl.when(lax.axis_index("tm") == 0)(add_init)
        s1[pl.ds(base, count)] = split(y[...].reshape(count, 8, 128))
        get_strips((strip1, strip2, strip3), (s1, s2, s3), full, even)
        copy.wait()
        for k, src, dst in ((1, s1, s2), (2, s2, s3), (3, s3, None)):
            put_force(force, fe, got_odd, not even, k, n)
            base = mirrored((7 - k) * REACH, count, full, even)
            value = apply_phi(src, idx, w, base, count) + force_at(force, base, count)
            if dst is None:
                w1[...] = value
                y[...] = value.reshape(n * 8, 128)
            else:
                dst[pl.ds(base, count)] = split(value)
        end[...] = block_end(y, pk, n)

    by_parity(body)


def scan_kernel(values, pk, starts):
    starts[...] = scan_starts(values[...], pk)


def scan_sum_kernel(values, w1, coarse, pk, starts, total):
    starts[...] = scan_starts(values[...], pk)
    total[...] = values[...] + (w1[...] + coarse[...])


NEAR = 2 * REACH


def put_pay(pay, state, value, side, n):
    def body(even):
        near = 0 if even else n - NEAR
        far = NEAR if even else n - side
        pay[pl.ds(0, NEAR)] = state[pl.ds(near, NEAR)]
        count = side - NEAR
        pay[pl.ds(NEAR, count // 2)] = value[far : far + count].reshape(count // 2, 16, 128).astype(BF16)

    by_parity(body)


def put_far(dst, own, got, right, n):
    half = n // 2
    dst[pl.ds(n + half if right else n, half)] = own[pl.ds(half if right else 0, half)]
    dst[3 * n] = jnp.zeros((16, 128), BF16)
    count = 2 * (got.shape[0] - NEAR)
    dst[pl.ds(2 * n if right else n - NEAR, NEAR)] = got[pl.ds(0, NEAR)]
    leads = got[pl.ds(NEAR, count // 2)].astype(F32).reshape(count, 8, 128)
    far = jnp.concatenate([leads, jnp.zeros_like(leads)], axis=1).astype(BF16)
    dst[pl.ds(2 * n + NEAR if right else n - NEAR - count, count)] = far


def enter_first_kernel(*refs):
    *arrivals, starts, we, pk, state, pay_odd, y = refs
    n = starts.shape[0]
    value = enter(arrivals, we, pk, y, n) + starts[...]
    state[...] = split(value)
    put_pay(pay_odd, state, value, n, n)


def enter_second_kernel(*refs):
    *arrivals, starts, before, init, we, pk, state, pay_even, pay_odd, corr, y = refs
    n = starts.shape[0]
    value = enter(arrivals, we, pk, y, n) + starts[...]
    corr[...] = value
    old = before[...].astype(F32)
    y[...] = (value + (old[:, 0:8] + old[:, 8:16])).reshape(n * 8, 128)
    first = (lax.axis_index("tm") == 0).astype(F32)
    y[pl.ds(0, n, stride=8), :] = y[pl.ds(0, n, stride=8), :] + init[...] * first
    value = y[...].reshape(n, 8, 128)
    state[...] = split(value)
    side = (COARSEN - 1) * REACH
    pay_even[...] = state[pl.ds(jnp.where(even_place(), n - side, 0), side)]
    put_pay(pay_odd, state, value, side, n)


def put_block(dst, own, got, right, n):
    side = got.shape[0]
    dst[pl.ds(n, n)] = own[...]
    dst[3 * n] = jnp.zeros((16, 128), BF16)
    dst[pl.ds(2 * n if right else n - side, side)] = got[...]


def second_early_kernel(table, own, got, w, pk, strip1, strip2, strip3, coarse, idx, sem, s0, s1, s2, s3):
    def body(even):
        copy = pltpu.make_async_copy(table, idx, sem)
        copy.start()
        n = own.shape[0]
        full = 3 * n
        coarse[...] = product(own[...].reshape(n * 16, 128), power(pk, 1))
        put_block(s0, own, got, even, n)
        for state in (s1, s2, s3):
            state[full] = jnp.zeros((16, 128), BF16)
        copy.wait()
        for k, src, dst in ((1, s0, s1), (2, s1, s2), (3, s2, s3)):
            size = (8 - 2 * k) * REACH
            base = mirrored(k * REACH, size, full, even)
            dst[pl.ds(base, size)] = split(apply_phi(src, idx, w, base, size))
        put_strips((strip1, strip2, strip3), (s1, s2, s3), full, even)

    by_parity(body)


def second_late_kernel(table, own, got, strip1, strip2, strip3, coarse, w, pk, res, end, idx, sem, s0, s1, s2, s3, y):
    def body(even):
        copy = pltpu.make_async_copy(table, idx, sem)
        copy.start()
        n = own.shape[0]
        full = 3 * n
        put_far(s0, own, got, not even, n)
        get_strips((strip1, strip2, strip3), (s1, s2, s3), full, even)
        count = 4 * REACH
        copy.wait()
        for k, src, dst in ((1, s0, s1), (2, s1, s2), (3, s2, s3)):
            base = mirrored((8 - k) * REACH, count, full, even)
            dst[pl.ds(base, count)] = split(apply_phi(src, idx, w, base, count))
        value = apply_phi(s3, idx, w, n, n)
        value = value - coarse[...]
        res[...] = value
        y[...] = value.reshape(n * 8, 128)
        end[...] = block_end(y, pk, n)

    by_parity(body)


def flip_tiles(flip, value, begin):
    lines = flip.reshape(8 * flip.shape[1], 128)
    for e in range(value.shape[0]):
        lines[pl.ds(begin + e, 8, stride=flip.shape[1]), :] = value[e]


def write_out(out, k, flip, begin, size, sems):
    copy = pltpu.make_async_copy(flip.at[:, pl.ds(0, size)], out.at[:, k, pl.ds(begin, size)], sems.at[k])
    copy.start()
    return copy


def third_early_kernel(
    table, own, got, corr, total, fe, pay, w, pk, out, strip1, strip2, kept, idx, sem, s0, s1, s2, force, flip0, flip1, flip3, sems
):
    def body(even):
        table_copy = pltpu.make_async_copy(table, idx, sem)
        table_copy.start()
        n = own.shape[0]
        full = 3 * n
        points = product(split(corr[...]).reshape(-1, 128), power(pk, 1)) + total[...]
        flip_tiles(flip3, points, 0)
        copies = [write_out(out, COARSEN - 1, flip3, 0, n, sems)]
        put_block(s0, own, got, even, n)
        for state in (s1, s2):
            state[full] = jnp.zeros((16, 128), BF16)
        table_copy.wait()
        for k, src, dst, flip in ((0, s0, s1, flip0), (1, s1, s2, flip1), (2, s2, None, None)):
            put_force(force, fe, pay, even, k, n)
            size = (5 - 2 * k) * REACH
            base = mirrored((2 + k) * REACH, size, full, even)
            value = apply_phi(src, idx, w, base, size) + force_at(force, base, size)
            if dst is not None:
                dst[pl.ds(base, size)] = split(value)
            mine = (3 - k) * REACH
            value = value[:mine] if even else value[size - mine :]
            if flip is None:
                kept[...] = value
            else:
                flip_tiles(flip, value, 0)
                copies.append(write_out(out, k, flip, n - mine if even else 0, mine, sems))
        put_strips((strip1, strip2), (s1, s2), full, even)
        for copy in copies:
            copy.wait()

    by_parity(body)


def third_late_kernel(
    table, own, got, strip1, strip2, kept, fe, pay, w, partial, out, idx, sem, s0, s1, s2, force, flip0, flip1, flip2, sems
):
    def body(even):
        table_copy = pltpu.make_async_copy(table, idx, sem)
        table_copy.start()
        n = own.shape[0]
        full = 3 * n
        put_far(s0, own, got, not even, n)
        get_strips((strip1, strip2), (s1, s2), full, even)
        copies = []
        size = 3 * REACH
        flip_tiles(flip2, kept[...], n - REACH if even else 0)
        table_copy.wait()
        for k, src, dst, flip in ((0, s0, s1, flip0), (1, s1, s2, flip1), (2, s2, None, flip2)):
            put_force(force, fe, pay, not even, k, n)
            base = mirrored((7 - k) * REACH, size, full, even)
            value = apply_phi(src, idx, w, base, size) + force_at(force, base, size)
            if dst is not None:
                dst[pl.ds(base, size)] = split(value)
            mine = (k + 1) * REACH
            value = value[size - mine :] if even else value[:mine]
            if dst is None:
                flip_tiles(flip, value, 0 if even else n - mine)
                copies.append(write_out(out, k, flip, 0, n, sems))
            else:
                flip_tiles(flip, value, 0)
                copies.append(write_out(out, k, flip, 0 if even else n - mine, mine, sems))
        for copy in copies:
            copy.wait()

    by_parity(body)


def call(kernel, inputs, outs, scratch, spaces="", out_spaces="", aliases=None, flops=10**7, room=32):
    kinds = {"s": pltpu.SMEM, "h": pltpu.HBM, "v": pltpu.VMEM}

    def specs(arrays, letters):
        letters = letters.ljust(len(arrays), "v")
        return [pl.BlockSpec(memory_space=kinds[letter]) for letter in letters]

    moved = sum(a.size * a.dtype.itemsize for a in list(inputs) + list(outs))
    return pl.pallas_call(
        kernel,
        out_shape=outs,
        name=kernel.__name__,
        in_specs=specs(inputs, spaces),
        out_specs=specs(outs, out_spaces),
        scratch_shapes=scratch,
        input_output_aliases=aliases or {},
        compiler_params=pltpu.CompilerParams(vmem_limit_bytes=room * 1024 * 1024),
        cost_estimate=pl.CostEstimate(flops=flops, bytes_accessed=moved, transcendentals=0),
    )(*inputs)


def local(forcing, initial_state, connectivity, pattern, diag_block, face_blocks, coarse_block):
    n, width = initial_state.shape
    steps = forcing.shape[0]
    full = 3 * n
    tm = lax.axis_size("tm")
    shape = jax.ShapeDtypeStruct
    vmem = pltpu.VMEM
    dma = pltpu.SemaphoreType.DMA
    tiles = shape((n, 8, width), F32)
    state = shape((n, 16, width), BF16)
    ends = shape((n, width), F32)
    step_flops = 2 * 16 * 7 * width * 2 * width
    pay_rows = sum((COARSEN - 1 - k) * REACH * 8 for k in range(COARSEN)) + 2 * n + 16
    pay = shape((pay_rows, width), BF16)
    all_force = ((COARSEN * n * 8 + 16), width)
    fe, pay_even, pay_odd = call(
        pack_kernel,
        (forcing.reshape(steps // COARSEN, COARSEN, n, width), initial_state, connectivity.T, pattern.T),
        (shape(all_force, BF16), pay, pay),
        [
            vmem((COARSEN, 8, n, width), BF16),
            vmem((8 * (n + 8), width), F32),
            vmem((n, width), F32),
            vmem((6, n), jnp.int32),
            vmem((6, n), jnp.int32),
            vmem((16, 128), F32),
            vmem(all_force, BF16),
            vmem((pay_rows, width), BF16),
            vmem((pay_rows, width), BF16),
            dma((COARSEN + 3,)),
            dma((2 + COARSEN,)),
        ],
        spaces="hhhh",
        flops=3 * 10**9,
        out_spaces="hhh",
        room=62,
    )
    pay_odd, pay_even = swapped(pay_odd, 1), swapped(pay_even, 0)
    w, pk, we = call(
        weight_kernel,
        (diag_block, face_blocks, coarse_block),
        (
            shape((7 * width, 2 * width), BF16),
            shape((8 * width, 2 * width), BF16),
            shape(((tm - 1) * width, 2 * width), BF16),
        ),
        [],
        flops=10**9,
    )
    spaces = vmem((full + 1, 16, width), BF16)
    force = vmem((full * 8, width), BF16)
    rows = vmem((n * 8, width), F32)
    strip = shape((STRIP, 16, width), BF16)
    tables = [vmem((256, 256), BF16), vmem((256, 128), F32), vmem((128, 128), F32)]
    smem = pltpu.SMEM((8, 256), jnp.int32)
    strips = call(
        first_early_kernel,
        (fe, initial_state, pay_even, w),
        (strip, strip, strip),
        [spaces] * 3 + [force, vmem((6 * REACH * 8, width), F32)] + tables + [vmem((8, 256), jnp.int32), smem, dma],
        flops=step_flops * 6 * REACH,
    )
    w1, end, idx = call(
        first_late_kernel,
        (fe, initial_state, pay_even, pay_odd, *strips, w, pk),
        (tiles, ends, shape((8, 256), jnp.int32)),
        [spaces] * 3 + [force, rows] + tables + [smem, dma],
        flops=step_flops * 12 * REACH,
    )
    arrivals = earlier(end)
    (starts,) = call(scan_kernel, (w1, pk), (tiles,), [])
    def across(side):
        return shape((NEAR + (side - NEAR) // 2, 16, width), BF16)

    coarse, end_odd = call(enter_first_kernel, (*arrivals, starts, we, pk), (state, across(n)), [rows])
    got_odd, got_even = swapped(end_odd, 1), swapped(coarse, 0)
    *strips, moved = call(
        second_early_kernel,
        (idx, coarse, got_even, w, pk),
        (strip, strip, strip, tiles),
        [smem, dma] + [spaces] * 4,
        flops=step_flops * 12 * REACH,
    )
    res, end = call(
        second_late_kernel,
        (idx, coarse, got_odd, *strips, moved, w, pk),
        (tiles, ends),
        [smem, dma] + [spaces] * 4 + [rows],
        flops=step_flops * 16 * REACH,
    )
    arrivals = earlier(end)
    starts, total = call(scan_sum_kernel, (res, w1, moved, pk), (tiles, tiles), [])
    side = (COARSEN - 1) * REACH
    coarse, end_even, end_odd, corr = call(
        enter_second_kernel,
        (*arrivals, starts, coarse, initial_state, we, pk),
        (state, shape((side, 16, width), BF16), across(side), tiles),
        [rows],
    )
    got_odd, got_even = swapped(end_odd, 1), swapped(end_even, 0)
    result = shape((steps // COARSEN, COARSEN, n, width), F32)

    def flip(blocks):
        return vmem((8, blocks * REACH + 8, width), F32)

    out, *strips = call(
        third_early_kernel,
        (idx, coarse, got_even, corr, total, fe, pay_even, w, pk),
        (result, strip, strip, shape((REACH, 8, width), F32)),
        [smem, dma] + [spaces] * 3 + [force, flip(3), flip(2), vmem((8, n + 8, width), F32), dma((COARSEN,))],
        out_spaces="h",
        flops=step_flops * 9 * REACH,
    )
    (out,) = call(
        third_late_kernel,
        (idx, coarse, got_odd, *strips, fe, pay_odd, w, out),
        (result,),
        [smem, dma] + [spaces] * 3 + [force, flip(1), flip(2), vmem((8, n + 8, width), F32), dma((COARSEN - 1,))],
        spaces="vvvvvvvvvh",
        out_spaces="h",
        aliases={9: 0},
        flops=step_flops * 9 * REACH,
    )
    return out.reshape(steps, n, width)


def solution(mesh):
    return jax.shard_map(
        local,
        mesh=mesh,
        in_specs=(
            P("tm", ("groups", "space"), None),
            P(("groups", "space"), None),
            P("space", None),
            P("space", None),
            P(),
            P(),
            P(),
        ),
        out_specs=P("tm", ("groups", "space"), None),
        check_vma=False,
    )
```

```python
import functools

import jax
import jax.numpy as jnp
from jax import lax
from jax.experimental import pallas as pl
from jax.experimental.pallas import tpu as pltpu
from jax.sharding import PartitionSpec as P

COARSEN = 4
REACH = 16
F32 = jnp.float32
BF16 = jnp.bfloat16
CHUNK = 32


def swapped(value, first):
    count = lax.axis_size("space")
    pairs = []
    for i in range(first, count - 1, 2):
        pairs += [(i, i + 1), (i + 1, i)]
    return lax.ppermute(value, "space", pairs)


def earlier(value):
    count = lax.axis_size("tm")
    if count <= 8:
        return [lax.ppermute(value, "tm", [(i, i + s) for i in range(count - s)]) for s in range(1, count)]
    every = lax.all_gather(value, "tm")
    at = lax.axis_index("tm") - jnp.arange(1, count)
    picked = jnp.where((at >= 0)[:, None, None], jnp.take(every, jnp.maximum(at, 0), axis=0), 0.0)
    return [picked[s] for s in range(count - 1)]


def split(u):
    lead = u.astype(BF16).astype(F32)
    return jnp.concatenate([u, u - lead], axis=1).astype(BF16)


def split_rows(u):
    lead = u.astype(BF16)
    return jnp.concatenate([lead, (u - lead.astype(F32)).astype(BF16)], axis=0)


def product(x, weights):
    m = x.shape[0] // 16
    r = jnp.dot(x, weights, preferred_element_type=F32).reshape(m, 16, 256)
    return r[:, :8, :128] + (r[:, 8:, :128] + r[:, :8, 128:])


def product_rows(x, weights):
    m = x.shape[0] // 2
    r = jnp.dot(x, weights, preferred_element_type=F32)
    return r[:m, :128] + (r[m:, :128] + r[:m, 128:])


def put_halves(ref, w):
    lead = w.astype(BF16)
    ref[:, 0:128] = lead
    ref[:, 128:256] = (w - lead.astype(F32)).astype(BF16)


def power(pk, k):
    return pk[pl.ds(128 * (7 - k), 128), :]


def scan_starts(values, pk):
    y = values
    row = lax.broadcasted_iota(jnp.int32, y.shape, 1)
    for d in (1, 2, 4):
        z = product(split(y).reshape(-1, 128), power(pk, d))
        y = y + jnp.where(row >= d, pltpu.roll(z, d, axis=1), 0.0)
    return jnp.where(row >= 1, pltpu.roll(y, 1, axis=1), 0.0)


def block_end(y, pk, n):
    parts = [y[pl.ds(i, n, stride=8), :] for i in range(8)]
    return product_rows(split_rows(jnp.concatenate(parts, axis=1)), pk[...])


def enter(arrivals, we, pk, y, n):
    value = jnp.concatenate([a[...] for a in arrivals], axis=1)
    entry = product_rows(split_rows(value), we[...])
    y[pl.ds(0, n, stride=8), :] = entry
    rows = split_rows(entry)
    for i in range(1, 8):
        y[pl.ds(i, n, stride=8), :] = product_rows(rows, power(pk, i))
    return y[...].reshape(n, 8, 128)


def apply_phi(src, idx, origin, w, base, size):
    cols = [src[pl.ds(base, size)].reshape(size * 16, 128)]
    for f in range(6):
        cols.append(jnp.concatenate([src[idx[f, base - origin + e]] for e in range(size)], axis=0))
    return product(jnp.concatenate(cols, axis=1), w[...])


def even_place():
    return lax.rem(lax.axis_index("space"), 2) == 0


def by_parity(body):
    even = even_place()
    pl.when(even)(lambda: body(True))
    pl.when(jnp.logical_not(even))(lambda: body(False))


def mirrored(low, size, full, even):
    return full - low - size if even else low


def pack_kernel(
    forcing, init, conn, pattern, fe_out, even_out, odd_out,
    landed, rows, init_v, conn_v, pattern_v, offs, fe, pay_even, pay_odd, sems, out_sems
):
    n = init_v.shape[0]
    pitch = n + 8
    copies = [pltpu.make_async_copy(forcing.at[:, k], landed.at[k], sems.at[k]) for k in range(COARSEN)]
    small = ((conn, conn_v), (pattern, pattern_v), (init, init_v))
    copies += [pltpu.make_async_copy(src, dst, sems.at[COARSEN + i]) for i, (src, dst) in enumerate(small)]
    for copy in copies[COARSEN:] + copies[:COARSEN]:
        copy.start()
    for copy in copies[COARSEN:]:
        copy.wait()
    place = lax.broadcasted_iota(jnp.int32, (6, n), 1) + lax.axis_index("space") * n
    value = ((conn_v[...] - place) * pattern_v[...]).astype(F32)
    offs[...] = jnp.zeros_like(offs)
    offs[0:6, 0:n] = value
    offs[0:6, n : 2 * n] = value
    tab = offs[...].astype(BF16)
    fe[pl.ds(COARSEN * n * 8, 16), :] = tab
    lead = init_v[...].astype(BF16)
    rest = (init_v[...] - lead.astype(F32)).astype(BF16)
    even = even_place()
    at = sum((COARSEN - 1 - k) * REACH * 8 for k in range(COARSEN))
    for pay in (pay_even, pay_odd):
        pay[pl.ds(at, n), :] = lead
        pay[pl.ds(at + n, n), :] = rest
        pay[pl.ds(at + 2 * n, 16), :] = tab
    at = 0
    results = []
    for k in range(COARSEN):
        copies[k].wait()
        for i in range(8):
            rows[pl.ds(i * pitch, n), :] = landed[k, i].astype(F32)

        def body(pair, carry, k=k):
            e = pair * 2
            two = [rows[pl.ds(e + j, 8, stride=pitch), :] for j in range(2)]
            fe[pl.ds(pl.multiple_of((k * n + e) * 8, 16), 16), :] = jnp.concatenate(two, axis=0).astype(BF16)
            return carry

        lax.fori_loop(0, n // 2, body, 0, unroll=8)
        width = (COARSEN - 1 - k) * REACH * 8
        if width:
            for pay, right in ((pay_even, even), (pay_odd, jnp.logical_not(even))):
                begin = pl.multiple_of(k * n * 8 + jnp.where(right, n * 8 - width, 0), 128)
                pay[pl.ds(at, width), :] = fe[pl.ds(begin, width), :]
        at += width
        rows_k = pl.ds(k * n * 8, n * 8 + (16 if k == COARSEN - 1 else 0))
        results.append(pltpu.make_async_copy(fe.at[rows_k], fe_out.at[rows_k], out_sems.at[2 + k]))
        results[-1].start()
        if k == COARSEN - 2:
            results.append(pltpu.make_async_copy(pay_odd, odd_out, out_sems.at[0]))
            results.append(pltpu.make_async_copy(pay_even, even_out, out_sems.at[1]))
            results[-2].start()
            results[-1].start()
    for result in results:
        result.wait()


def weight_kernel(diag, faces, coarse, w, pk, we):
    put_halves(w.at[pl.ds(0, 128)], diag[...].T)
    for f in range(6):
        put_halves(w.at[pl.ds(128 * (f + 1), 128)], faces[f].T)

    def thirds(a):
        one = a.astype(BF16)
        rest = a - one.astype(F32)
        two = rest.astype(BF16)
        return one, two, (rest - two.astype(F32)).astype(BF16)

    def mul(a, b):
        (a1, a2, a3), (b1, b2, b3) = thirds(a), thirds(b)
        total = jnp.zeros((128, 128), F32)
        for x, y in ((a3, b1), (a1, b3), (a2, b2), (a2, b1), (a1, b2), (a1, b1)):
            total += jnp.dot(x, y, preferred_element_type=F32)
        return total

    rows = lax.broadcasted_iota(jnp.int32, (128, 128), 0)
    one = (rows == lax.broadcasted_iota(jnp.int32, (128, 128), 1)).astype(F32)
    powers = [one, coarse[...].T]
    for k in range(2, 9):
        powers.append(mul(powers[k // 2], powers[k - k // 2]))
    for k in range(8):
        put_halves(pk.at[pl.ds(128 * (7 - k), 128)], powers[k])

    def body(k, current):
        put_halves(we.at[pl.ds(pl.multiple_of(k * 128, 128), 128)], current)
        return mul(current, powers[8])

    lax.fori_loop(0, we.shape[0] // 128, body, one)


def put_force(dst, own, got, right, k, n):
    at = sum((COARSEN - 1 - j) * REACH * 8 for j in range(k))
    width = (COARSEN - 1 - k) * REACH * 8
    dst[pl.ds(n * 8, n * 8), :] = own[pl.ds(k * n * 8, n * 8), :]
    if width:
        to = 2 * n * 8 if right else n * 8 - width
        dst[pl.ds(to, width), :] = got[pl.ds(at, width), :]


def force_at(src, base, size):
    return src[pl.ds(base * 8, size * 8), :].astype(F32).reshape(size, 8, 128)


def origin_of(even, late, n):
    return n if even != late else 0


def put_table(table, fe, got, even, late):
    n = table.shape[1] // 2
    lane = lax.broadcasted_iota(jnp.int32, table.shape, 1)

    def part(ref):
        return ref[pl.ds(ref.shape[0] - 16, 16), :].astype(F32)[0:8]

    origin = origin_of(even, late, n)
    offs = jnp.where(lane < n, part(fe), part(got)) if origin else jnp.where(lane < n, part(got), part(fe))
    table[...] = jnp.where(offs != 0.0, lane + origin + offs.astype(jnp.int32), 3 * n)


def push_init(init, got_even, got_odd, w, table, origin, columns, square, i16, base, count, n, even):
    square[...] = jnp.zeros_like(square)
    square[0:8, :] = table[...].astype(F32)
    columns[...] = square[...].T
    i16[...] = jnp.zeros_like(i16)
    lead = init[...].astype(BF16)
    i16[pl.ds(n, n), 0:128] = lead
    i16[pl.ds(n, n), 128:256] = (init[...] - lead.astype(F32)).astype(BF16)
    for ref, right in ((got_even, even), (got_odd, not even)):
        if ref is not None:
            at = ref.shape[0] - 16
            to = 2 * n if right else 0
            i16[pl.ds(to, n), 0:128] = ref[pl.ds(at - 2 * n, n), :]
            i16[pl.ds(to, n), 128:256] = ref[pl.ds(at - n, n), :]
    rows = pl.ds(base, count)
    place = columns[pl.ds(base - origin, count), :]
    spot = lax.broadcasted_iota(jnp.int32, (count, 256), 1).astype(F32)
    cols = [i16[rows, :]]
    for f in range(6):
        hot = (spot == place[:, f : f + 1]).astype(F32).astype(BF16)
        cols.append(jnp.dot(hot, i16[...], preferred_element_type=F32).astype(BF16))
    leads = jnp.concatenate([c[:, 0:128] for c in cols], axis=1)
    rests = jnp.concatenate([c[:, 128:256] for c in cols], axis=1)
    return product_rows(jnp.concatenate([leads, rests], axis=0), w[...])


STRIPS = (5 * REACH, 4 * REACH, 3 * REACH)
STRIP = 2 * REACH


def put_strips(strips, states, full, even):
    for strip, state, low in zip(strips, states, STRIPS):
        strip[...] = state[pl.ds(mirrored(low, STRIP, full, even), STRIP)]


def get_strips(strips, states, full, even):
    for strip, state, low in zip(strips, states, STRIPS):
        state[pl.ds(mirrored(low, STRIP, full, even), STRIP)] = strip[...]
        state[full] = jnp.zeros((16, 128), BF16)


def first_early_kernel(
    fe, init, got, w, strip1, strip2, strip3, table, s1, s2, s3, force, y, i16, columns, square, idx, sem
):
    def body(even):
        n = init.shape[0]
        full = 3 * n
        origin = origin_of(even, False, n)
        put_table(table, fe, got, even, False)
        copy = pltpu.make_async_copy(table, idx, sem)
        copy.start()
        count = 6 * REACH
        base = mirrored(REACH, count, full, even)
        put_force(force, fe, got, even, 0, n)
        y[pl.ds(0, count * 8), :] = force[pl.ds(base * 8, count * 8), :].astype(F32)

        def add_init():
            pushed = push_init(init, got, None, w, table, origin, columns, square, i16, base, count, n, even)
            y[pl.ds(0, count, stride=8), :] = y[pl.ds(0, count, stride=8), :] + pushed

        pl.when(lax.axis_index("tm") == 0)(add_init)
        s1[pl.ds(base, count)] = split(y[pl.ds(0, count * 8), :].reshape(count, 8, 128))
        for state in (s1, s2, s3):
            state[full] = jnp.zeros((16, 128), BF16)
        copy.wait()
        for k, src, dst in ((1, s1, s2), (2, s2, s3)):
            put_force(force, fe, got, even, k, n)
            size = (6 - 2 * k) * REACH
            base = mirrored((k + 1) * REACH, size, full, even)
            dst[pl.ds(base, size)] = split(apply_phi(src, idx, origin, w, base, size) + force_at(force, base, size))
        put_strips((strip1, strip2, strip3), (s1, s2, s3), full, even)

    by_parity(body)


def first_late_kernel(
    fe, init, got_even, got_odd, strip1, strip2, strip3, w, pk, w1, end, table,
    s1, s2, s3, force, y, i16, columns, square, idx, sem
):
    def body(even):
        n = init.shape[0]
        full = 3 * n
        origin = origin_of(even, True, n)
        put_table(table, fe, got_odd, even, True)
        copy = pltpu.make_async_copy(table, idx, sem)
        copy.start()
        count = 4 * REACH
        base = mirrored(7 * REACH, count, full, even)
        put_force(force, fe, got_odd, not even, 0, n)
        y[...] = force[pl.ds(base * 8, count * 8), :].astype(F32)

        def add_init():
            pushed = push_init(init, got_even, got_odd, w, table, origin, columns, square, i16, base, count, n, even)
            y[pl.ds(0, count, stride=8), :] = y[pl.ds(0, count, stride=8), :] + pushed

        pl.when(lax.axis_index("tm") == 0)(add_init)
        s1[pl.ds(base, count)] = split(y[...].reshape(count, 8, 128))
        get_strips((strip1, strip2, strip3), (s1, s2, s3), full, even)
        copy.wait()
        for k, src, dst in ((1, s1, s2), (2, s2, s3), (3, s3, None)):
            put_force(force, fe, got_odd, not even, k, n)
            base = mirrored((7 - k) * REACH, count, full, even)
            value = apply_phi(src, idx, origin, w, base, count) + force_at(force, base, count)
            if dst is None:
                w1[...] = value
                y[...] = value.reshape(n * 8, 128)
            else:
                dst[pl.ds(base, count)] = split(value)
        end[...] = block_end(y, pk, n)

    by_parity(body)


def scan_kernel(values, pk, starts):
    starts[...] = scan_starts(values[...], pk)


def scan_sum_kernel(values, w1, coarse, pk, starts, total):
    starts[...] = scan_starts(values[...], pk)
    total[...] = values[...] + (w1[...] + coarse[...])


NEAR = 2 * REACH


def put_pay(pay, state, value, side, n):
    def body(even):
        near = 0 if even else n - NEAR
        far = NEAR if even else n - side
        pay[pl.ds(0, NEAR)] = state[pl.ds(near, NEAR)]
        count = side - NEAR
        pay[pl.ds(NEAR, count // 2)] = value[far : far + count].reshape(count // 2, 16, 128).astype(BF16)

    by_parity(body)


def put_far(dst, own, got, right, n):
    half = n // 2
    dst[pl.ds(n + half if right else n, half)] = own[pl.ds(half if right else 0, half)]
    dst[3 * n] = jnp.zeros((16, 128), BF16)
    count = 2 * (got.shape[0] - NEAR)
    dst[pl.ds(2 * n if right else n - NEAR, NEAR)] = got[pl.ds(0, NEAR)]
    leads = got[pl.ds(NEAR, count // 2)].astype(F32).reshape(count, 8, 128)
    far = jnp.concatenate([leads, jnp.zeros_like(leads)], axis=1).astype(BF16)
    dst[pl.ds(2 * n + NEAR if right else n - NEAR - count, count)] = far


def enter_first_kernel(*refs):
    *arrivals, starts, we, pk, state, pay_odd, y = refs
    n = starts.shape[0]
    value = enter(arrivals, we, pk, y, n) + starts[...]
    state[...] = split(value)
    put_pay(pay_odd, state, value, n, n)


def enter_second_kernel(*refs):
    *arrivals, starts, before, init, we, pk, state, pay_even, pay_odd, corr, y = refs
    n = starts.shape[0]
    value = enter(arrivals, we, pk, y, n) + starts[...]
    corr[...] = value
    old = before[...].astype(F32)
    y[...] = (value + (old[:, 0:8] + old[:, 8:16])).reshape(n * 8, 128)
    first = (lax.axis_index("tm") == 0).astype(F32)
    y[pl.ds(0, n, stride=8), :] = y[pl.ds(0, n, stride=8), :] + init[...] * first
    value = y[...].reshape(n, 8, 128)
    state[...] = split(value)
    side = (COARSEN - 1) * REACH
    pay_even[...] = state[pl.ds(jnp.where(even_place(), n - side, 0), side)]
    put_pay(pay_odd, state, value, side, n)


def put_block(dst, own, got, right, n):
    side = got.shape[0]
    dst[pl.ds(n, n)] = own[...]
    dst[3 * n] = jnp.zeros((16, 128), BF16)
    dst[pl.ds(2 * n if right else n - side, side)] = got[...]


def second_early_kernel(table, own, got, w, pk, strip1, strip2, strip3, coarse, idx, sem, s0, s1, s2, s3):
    def body(even):
        copy = pltpu.make_async_copy(table, idx, sem)
        copy.start()
        n = own.shape[0]
        origin = origin_of(even, False, n)
        full = 3 * n
        coarse[...] = product(own[...].reshape(n * 16, 128), power(pk, 1))
        put_block(s0, own, got, even, n)
        for state in (s1, s2, s3):
            state[full] = jnp.zeros((16, 128), BF16)
        copy.wait()
        for k, src, dst in ((1, s0, s1), (2, s1, s2), (3, s2, s3)):
            size = (8 - 2 * k) * REACH
            base = mirrored(k * REACH, size, full, even)
            dst[pl.ds(base, size)] = split(apply_phi(src, idx, origin, w, base, size))
        put_strips((strip1, strip2, strip3), (s1, s2, s3), full, even)

    by_parity(body)


def second_late_kernel(table, own, got, strip1, strip2, strip3, coarse, w, pk, res, end, idx, sem, s0, s1, s2, s3, y):
    def body(even):
        copy = pltpu.make_async_copy(table, idx, sem)
        copy.start()
        n = own.shape[0]
        origin = origin_of(even, True, n)
        full = 3 * n
        put_far(s0, own, got, not even, n)
        get_strips((strip1, strip2, strip3), (s1, s2, s3), full, even)
        count = 4 * REACH
        copy.wait()
        for k, src, dst in ((1, s0, s1), (2, s1, s2), (3, s2, s3)):
            base = mirrored((8 - k) * REACH, count, full, even)
            dst[pl.ds(base, count)] = split(apply_phi(src, idx, origin, w, base, count))
        value = apply_phi(s3, idx, origin, w, n, n)
        value = value - coarse[...]
        res[...] = value
        y[...] = value.reshape(n * 8, 128)
        end[...] = block_end(y, pk, n)

    by_parity(body)


def flip_tiles(flip, value, begin):
    lines = flip.reshape(8 * flip.shape[1], 128)
    for e in range(value.shape[0]):
        lines[pl.ds(begin + e, 8, stride=flip.shape[1]), :] = value[e]


def write_out(out, k, flip, begin, size, sems):
    copy = pltpu.make_async_copy(flip.at[:, pl.ds(0, size)], out.at[:, k, pl.ds(begin, size)], sems.at[k])
    copy.start()
    return copy


def third_early_kernel(
    table, own, got, corr, total, fe, pay, w, pk, out, strip1, strip2, kept, idx, sem, s0, s1, s2, force, flip0, flip1, flip3, sems
):
    def body(even):
        table_copy = pltpu.make_async_copy(table, idx, sem)
        table_copy.start()
        n = own.shape[0]
        origin = origin_of(even, False, n)
        full = 3 * n
        points = product(split(corr[...]).reshape(-1, 128), power(pk, 1)) + total[...]
        flip_tiles(flip3, points, 0)
        copies = [write_out(out, COARSEN - 1, flip3, 0, n, sems)]
        put_block(s0, own, got, even, n)
        for state in (s1, s2):
            state[full] = jnp.zeros((16, 128), BF16)
        table_copy.wait()
        for k, src, dst, flip in ((0, s0, s1, flip0), (1, s1, s2, flip1), (2, s2, None, None)):
            put_force(force, fe, pay, even, k, n)
            size = (5 - 2 * k) * REACH
            base = mirrored((2 + k) * REACH, size, full, even)
            value = apply_phi(src, idx, origin, w, base, size) + force_at(force, base, size)
            if dst is not None:
                dst[pl.ds(base, size)] = split(value)
            mine = (3 - k) * REACH
            value = value[:mine] if even else value[size - mine :]
            if flip is None:
                kept[...] = value
            else:
                flip_tiles(flip, value, 0)
                copies.append(write_out(out, k, flip, n - mine if even else 0, mine, sems))
        put_strips((strip1, strip2), (s1, s2), full, even)
        for copy in copies:
            copy.wait()

    by_parity(body)


def third_late_kernel(
    table, own, got, strip1, strip2, kept, fe, pay, w, partial, out, idx, sem, s0, s1, s2, force, flip0, flip1, flip2, sems
):
    def body(even):
        table_copy = pltpu.make_async_copy(table, idx, sem)
        table_copy.start()
        n = own.shape[0]
        origin = origin_of(even, True, n)
        full = 3 * n
        put_far(s0, own, got, not even, n)
        get_strips((strip1, strip2), (s1, s2), full, even)
        copies = []
        size = 3 * REACH
        flip_tiles(flip2, kept[...], n - REACH if even else 0)
        table_copy.wait()
        for k, src, dst, flip in ((0, s0, s1, flip0), (1, s1, s2, flip1), (2, s2, None, flip2)):
            put_force(force, fe, pay, not even, k, n)
            base = mirrored((7 - k) * REACH, size, full, even)
            value = apply_phi(src, idx, origin, w, base, size) + force_at(force, base, size)
            if dst is not None:
                dst[pl.ds(base, size)] = split(value)
            mine = (k + 1) * REACH
            value = value[size - mine :] if even else value[:mine]
            if dst is None:
                flip_tiles(flip, value, 0 if even else n - mine)
                copies.append(write_out(out, k, flip, 0, n, sems))
            else:
                flip_tiles(flip, value, 0)
                copies.append(write_out(out, k, flip, 0 if even else n - mine, mine, sems))
        for copy in copies:
            copy.wait()

    by_parity(body)


def call(kernel, inputs, outs, scratch, spaces="", out_spaces="", aliases=None, flops=10**7, room=32):
    kinds = {"s": pltpu.SMEM, "h": pltpu.HBM, "v": pltpu.VMEM}

    def specs(arrays, letters):
        letters = letters.ljust(len(arrays), "v")
        return [pl.BlockSpec(memory_space=kinds[letter]) for letter in letters]

    moved = sum(a.size * a.dtype.itemsize for a in list(inputs) + list(outs))
    return pl.pallas_call(
        kernel,
        out_shape=outs,
        name=kernel.__name__,
        in_specs=specs(inputs, spaces),
        out_specs=specs(outs, out_spaces),
        scratch_shapes=scratch,
        input_output_aliases=aliases or {},
        compiler_params=pltpu.CompilerParams(vmem_limit_bytes=room * 1024 * 1024),
        cost_estimate=pl.CostEstimate(flops=flops, bytes_accessed=moved, transcendentals=0),
    )(*inputs)


def local(forcing, initial_state, connectivity, pattern, diag_block, face_blocks, coarse_block):
    n, width = initial_state.shape
    steps = forcing.shape[0]
    full = 3 * n
    tm = lax.axis_size("tm")
    shape = jax.ShapeDtypeStruct
    vmem = pltpu.VMEM
    dma = pltpu.SemaphoreType.DMA
    tiles = shape((n, 8, width), F32)
    state = shape((n, 16, width), BF16)
    ends = shape((n, width), F32)
    step_flops = 2 * 16 * 7 * width * 2 * width
    pay_rows = sum((COARSEN - 1 - k) * REACH * 8 for k in range(COARSEN)) + 2 * n + 16
    pay = shape((pay_rows, width), BF16)
    all_force = ((COARSEN * n * 8 + 16), width)
    fe, pay_even, pay_odd = call(
        pack_kernel,
        (forcing.reshape(steps // COARSEN, COARSEN, n, width), initial_state, connectivity.T, pattern.T),
        (shape(all_force, BF16), pay, pay),
        [
            vmem((COARSEN, 8, n, width), BF16),
            vmem((8 * (n + 8), width), F32),
            vmem((n, width), F32),
            vmem((6, n), jnp.int32),
            vmem((6, n), jnp.int32),
            vmem((16, 128), F32),
            vmem(all_force, BF16),
            vmem((pay_rows, width), BF16),
            vmem((pay_rows, width), BF16),
            dma((COARSEN + 3,)),
            dma((2 + COARSEN,)),
        ],
        spaces="hhhh",
        flops=3 * 10**9,
        out_spaces="hhh",
        room=62,
    )
    pay_odd, pay_even = swapped(pay_odd, 1), swapped(pay_even, 0)
    w, pk, we = call(
        weight_kernel,
        (diag_block, face_blocks, coarse_block),
        (
            shape((7 * width, 2 * width), BF16),
            shape((8 * width, 2 * width), BF16),
            shape(((tm - 1) * width, 2 * width), BF16),
        ),
        [],
        flops=10**9,
    )
    spaces = vmem((full + 1, 16, width), BF16)
    force = vmem((full * 8, width), BF16)
    rows = vmem((n * 8, width), F32)
    strip = shape((STRIP, 16, width), BF16)
    tables = [vmem((256, 256), BF16), vmem((128, 128), F32), vmem((128, 128), F32)]
    smem = pltpu.SMEM((8, 2 * n), jnp.int32)
    table = shape((8, 2 * n), jnp.int32)
    *strips, table_early = call(
        first_early_kernel,
        (fe, initial_state, pay_even, w),
        (strip, strip, strip, table),
        [spaces] * 3 + [force, vmem((6 * REACH * 8, width), F32)] + tables + [smem, dma],
        flops=step_flops * 6 * REACH,
    )
    w1, end, table_late = call(
        first_late_kernel,
        (fe, initial_state, pay_even, pay_odd, *strips, w, pk),
        (tiles, ends, table),
        [spaces] * 3 + [force, rows] + tables + [smem, dma],
        flops=step_flops * 12 * REACH,
    )
    arrivals = earlier(end)
    (starts,) = call(scan_kernel, (w1, pk), (tiles,), [])
    def across(side):
        return shape((NEAR + (side - NEAR) // 2, 16, width), BF16)

    coarse, end_odd = call(enter_first_kernel, (*arrivals, starts, we, pk), (state, across(n)), [rows])
    got_odd, got_even = swapped(end_odd, 1), swapped(coarse, 0)
    *strips, moved = call(
        second_early_kernel,
        (table_early, coarse, got_even, w, pk),
        (strip, strip, strip, tiles),
        [smem, dma] + [spaces] * 4,
        flops=step_flops * 12 * REACH,
    )
    res, end = call(
        second_late_kernel,
        (table_late, coarse, got_odd, *strips, moved, w, pk),
        (tiles, ends),
        [smem, dma] + [spaces] * 4 + [rows],
        flops=step_flops * 16 * REACH,
    )
    arrivals = earlier(end)
    starts, total = call(scan_sum_kernel, (res, w1, moved, pk), (tiles, tiles), [])
    side = (COARSEN - 1) * REACH
    coarse, end_even, end_odd, corr = call(
        enter_second_kernel,
        (*arrivals, starts, coarse, initial_state, we, pk),
        (state, shape((side, 16, width), BF16), across(side), tiles),
        [rows],
    )
    got_odd, got_even = swapped(end_odd, 1), swapped(end_even, 0)
    result = shape((steps // COARSEN, COARSEN, n, width), F32)

    def flip(blocks):
        return vmem((8, blocks * REACH + 8, width), F32)

    out, *strips = call(
        third_early_kernel,
        (table_early, coarse, got_even, corr, total, fe, pay_even, w, pk),
        (result, strip, strip, shape((REACH, 8, width), F32)),
        [smem, dma] + [spaces] * 3 + [force, flip(3), flip(2), vmem((8, n + 8, width), F32), dma((COARSEN,))],
        out_spaces="h",
        flops=step_flops * 9 * REACH,
    )
    (out,) = call(
        third_late_kernel,
        (table_late, coarse, got_odd, *strips, fe, pay_odd, w, out),
        (result,),
        [smem, dma] + [spaces] * 3 + [force, flip(1), flip(2), vmem((8, n + 8, width), F32), dma((COARSEN - 1,))],
        spaces="vvvvvvvvvh",
        out_spaces="h",
        aliases={9: 0},
        flops=step_flops * 9 * REACH,
    )
    return out.reshape(steps, n, width)


def solution(mesh):
    return jax.shard_map(
        local,
        mesh=mesh,
        in_specs=(
            P("tm", ("groups", "space"), None),
            P(("groups", "space"), None),
            P("space", None),
            P("space", None),
            P(),
            P(),
            P(),
        ),
        out_specs=P("tm", ("groups", "space"), None),
        check_vma=False,
    )
```

```python
import functools

import jax
import jax.numpy as jnp
from jax import lax
from jax.experimental import pallas as pl
from jax.experimental.pallas import tpu as pltpu
from jax.sharding import PartitionSpec as P

COARSEN = 4
REACH = 16
F32 = jnp.float32
BF16 = jnp.bfloat16
CHUNK = 32


def swapped(value, first):
    count = lax.axis_size("space")
    pairs = []
    for i in range(first, count - 1, 2):
        pairs += [(i, i + 1), (i + 1, i)]
    return lax.ppermute(value, "space", pairs)


def earlier(value):
    count = lax.axis_size("tm")
    if count <= 8:
        return [lax.ppermute(value, "tm", [(i, i + s) for i in range(count - s)]) for s in range(1, count)]
    every = lax.all_gather(value, "tm")
    at = lax.axis_index("tm") - jnp.arange(1, count)
    picked = jnp.where((at >= 0)[:, None, None], jnp.take(every, jnp.maximum(at, 0), axis=0), 0.0)
    return [picked[s] for s in range(count - 1)]


def split(u):
    lead = u.astype(BF16).astype(F32)
    return jnp.concatenate([u, u - lead], axis=1).astype(BF16)


def split_rows(u):
    lead = u.astype(BF16)
    return jnp.concatenate([lead, (u - lead.astype(F32)).astype(BF16)], axis=0)


def product(x, weights):
    m = x.shape[0] // 16
    r = jnp.dot(x, weights, preferred_element_type=F32).reshape(m, 16, 256)
    return r[:, :8, :128] + (r[:, 8:, :128] + r[:, :8, 128:])


def product_rows(x, weights):
    m = x.shape[0] // 2
    r = jnp.dot(x, weights, preferred_element_type=F32)
    return r[:m, :128] + (r[m:, :128] + r[:m, 128:])


def put_halves(ref, w):
    lead = w.astype(BF16)
    ref[:, 0:128] = lead
    ref[:, 128:256] = (w - lead.astype(F32)).astype(BF16)


def power(pk, k):
    return pk[pl.ds(128 * (7 - k), 128), :]


def scan_starts(values, pk):
    y = values
    row = lax.broadcasted_iota(jnp.int32, y.shape, 1)
    for d in (1, 2, 4):
        z = product(split(y).reshape(-1, 128), power(pk, d))
        y = y + jnp.where(row >= d, pltpu.roll(z, d, axis=1), 0.0)
    return jnp.where(row >= 1, pltpu.roll(y, 1, axis=1), 0.0)


def block_end(y, pk, n):
    parts = [y[pl.ds(i, n, stride=8), :] for i in range(8)]
    return product_rows(split_rows(jnp.concatenate(parts, axis=1)), pk[...])


def enter(arrivals, we, pk, y, n):
    value = jnp.concatenate([a[...] for a in arrivals], axis=1)
    entry = product_rows(split_rows(value), we[...])
    y[pl.ds(0, n, stride=8), :] = entry
    rows = split_rows(entry)
    for i in range(1, 8):
        y[pl.ds(i, n, stride=8), :] = product_rows(rows, power(pk, i))
    return y[...].reshape(n, 8, 128)


def apply_phi(src, idx, origin, w, base, size):
    cols = [src[pl.ds(base, size)].reshape(size * 16, 128)]
    for f in range(6):
        cols.append(jnp.concatenate([src[idx[f, base - origin + e]] for e in range(size)], axis=0))
    return product(jnp.concatenate(cols, axis=1), w[...])


def even_place():
    return lax.rem(lax.axis_index("space"), 2) == 0


def by_parity(body):
    even = even_place()
    pl.when(even)(lambda: body(True))
    pl.when(jnp.logical_not(even))(lambda: body(False))


def mirrored(low, size, full, even):
    return full - low - size if even else low


def pack_kernel(
    forcing, init, conn, pattern, fe_out, even_out, odd_out,
    landed, rows, init_v, conn_v, pattern_v, offs, fe, pay_even, pay_odd, sems, out_sems
):
    n = init_v.shape[0]
    pitch = n + 8
    copies = [pltpu.make_async_copy(forcing.at[:, k], landed.at[k], sems.at[k]) for k in range(COARSEN)]
    small = ((conn, conn_v), (pattern, pattern_v), (init, init_v))
    copies += [pltpu.make_async_copy(src, dst, sems.at[COARSEN + i]) for i, (src, dst) in enumerate(small)]
    for copy in copies[COARSEN:] + copies[:COARSEN]:
        copy.start()
    for copy in copies[COARSEN:]:
        copy.wait()
    place = lax.broadcasted_iota(jnp.int32, (6, n), 1) + lax.axis_index("space") * n
    value = ((conn_v[...] - place) * pattern_v[...]).astype(F32)
    offs[...] = jnp.zeros_like(offs)
    offs[0:6, 0:n] = value
    offs[0:6, n : 2 * n] = value
    tab = offs[...].astype(BF16)
    fe[pl.ds(COARSEN * n * 8, 16), :] = tab
    lead = init_v[...].astype(BF16)
    rest = (init_v[...] - lead.astype(F32)).astype(BF16)
    even = even_place()
    at = sum((COARSEN - 1 - k) * REACH * 8 for k in range(COARSEN))
    for pay in (pay_even, pay_odd):
        pay[pl.ds(at, n), :] = lead
        pay[pl.ds(at + n, n), :] = rest
        pay[pl.ds(at + 2 * n, 16), :] = tab
    at = 0
    results = []
    for k in range(COARSEN):
        copies[k].wait()
        for i in range(8):
            rows[pl.ds(i * pitch, n), :] = landed[k, i].astype(F32)

        def body(pair, carry, k=k):
            e = pair * 2
            two = [rows[pl.ds(e + j, 8, stride=pitch), :] for j in range(2)]
            fe[pl.ds(pl.multiple_of((k * n + e) * 8, 16), 16), :] = jnp.concatenate(two, axis=0).astype(BF16)
            return carry

        lax.fori_loop(0, n // 2, body, 0, unroll=8)
        width = (COARSEN - 1 - k) * REACH * 8
        if width:
            for pay, right in ((pay_even, even), (pay_odd, jnp.logical_not(even))):
                begin = pl.multiple_of(k * n * 8 + jnp.where(right, n * 8 - width, 0), 128)
                pay[pl.ds(at, width), :] = fe[pl.ds(begin, width), :]
        at += width
        rows_k = pl.ds(k * n * 8, n * 8 + (16 if k == COARSEN - 1 else 0))
        results.append(pltpu.make_async_copy(fe.at[rows_k], fe_out.at[rows_k], out_sems.at[2 + k]))
        results[-1].start()
        if k == COARSEN - 2:
            results.append(pltpu.make_async_copy(pay_odd, odd_out, out_sems.at[0]))
            results.append(pltpu.make_async_copy(pay_even, even_out, out_sems.at[1]))
            results[-2].start()
            results[-1].start()
    for result in results:
        result.wait()


def weight_kernel(diag, faces, coarse, w, pk, we):
    put_halves(w.at[pl.ds(0, 128)], diag[...].T)
    for f in range(6):
        put_halves(w.at[pl.ds(128 * (f + 1), 128)], faces[f].T)

    def thirds(a):
        one = a.astype(BF16)
        rest = a - one.astype(F32)
        two = rest.astype(BF16)
        return one, two, (rest - two.astype(F32)).astype(BF16)

    def mul(a, b):
        (a1, a2, a3), (b1, b2, b3) = thirds(a), thirds(b)
        total = jnp.zeros((128, 128), F32)
        for x, y in ((a3, b1), (a1, b3), (a2, b2), (a2, b1), (a1, b2), (a1, b1)):
            total += jnp.dot(x, y, preferred_element_type=F32)
        return total

    rows = lax.broadcasted_iota(jnp.int32, (128, 128), 0)
    one = (rows == lax.broadcasted_iota(jnp.int32, (128, 128), 1)).astype(F32)
    powers = [one, coarse[...].T]
    for k in range(2, 9):
        powers.append(mul(powers[k // 2], powers[k - k // 2]))
    for k in range(8):
        put_halves(pk.at[pl.ds(128 * (7 - k), 128)], powers[k])

    def body(k, current):
        put_halves(we.at[pl.ds(pl.multiple_of(k * 128, 128), 128)], current)
        return mul(current, powers[8])

    lax.fori_loop(0, we.shape[0] // 128, body, one)


def put_force(dst, own, got, right, k, n):
    at = sum((COARSEN - 1 - j) * REACH * 8 for j in range(k))
    width = (COARSEN - 1 - k) * REACH * 8
    dst[pl.ds(n * 8, n * 8), :] = own[pl.ds(k * n * 8, n * 8), :]
    if width:
        to = 2 * n * 8 if right else n * 8 - width
        dst[pl.ds(to, width), :] = got[pl.ds(at, width), :]


def force_at(src, base, size):
    return src[pl.ds(base * 8, size * 8), :].astype(F32).reshape(size, 8, 128)


def origin_of(even, late, n):
    return n if even != late else 0


def put_table(table, fe, got, even, late):
    n = table.shape[1] // 2
    lane = lax.broadcasted_iota(jnp.int32, table.shape, 1)

    def part(ref):
        return ref[pl.ds(ref.shape[0] - 16, 16), :].astype(F32)[0:8]

    origin = origin_of(even, late, n)
    offs = jnp.where(lane < n, part(fe), part(got)) if origin else jnp.where(lane < n, part(got), part(fe))
    table[...] = jnp.where(offs != 0.0, lane + origin + offs.astype(jnp.int32), 3 * n)


def push_init(init, got_even, got_odd, w, table, origin, columns, square, i16, base, count, n, even):
    square[...] = jnp.zeros_like(square)
    square[0:8, :] = table[...].astype(F32)
    columns[...] = square[...].T
    i16[...] = jnp.zeros_like(i16)
    lead = init[...].astype(BF16)
    i16[pl.ds(n, n), 0:128] = lead
    i16[pl.ds(n, n), 128:256] = (init[...] - lead.astype(F32)).astype(BF16)
    for ref, right in ((got_even, even), (got_odd, not even)):
        if ref is not None:
            at = ref.shape[0] - 16
            to = 2 * n if right else 0
            i16[pl.ds(to, n), 0:128] = ref[pl.ds(at - 2 * n, n), :]
            i16[pl.ds(to, n), 128:256] = ref[pl.ds(at - n, n), :]
    rows = pl.ds(base, count)
    place = columns[pl.ds(base - origin, count), :]
    spot = lax.broadcasted_iota(jnp.int32, (count, 256), 1).astype(F32)
    cols = [i16[rows, :]]
    for f in range(6):
        hot = (spot == place[:, f : f + 1]).astype(F32).astype(BF16)
        cols.append(jnp.dot(hot, i16[...], preferred_element_type=F32).astype(BF16))
    leads = jnp.concatenate([c[:, 0:128] for c in cols], axis=1)
    rests = jnp.concatenate([c[:, 128:256] for c in cols], axis=1)
    return product_rows(jnp.concatenate([leads, rests], axis=0), w[...])


STRIPS = (5 * REACH, 4 * REACH, 3 * REACH)
STRIP = 2 * REACH


def put_strips(strips, states, full, even):
    for strip, state, low in zip(strips, states, STRIPS):
        strip[...] = state[pl.ds(mirrored(low, STRIP, full, even), STRIP)]


def get_strips(strips, states, full, even):
    for strip, state, low in zip(strips, states, STRIPS):
        state[pl.ds(mirrored(low, STRIP, full, even), STRIP)] = strip[...]
        state[full] = jnp.zeros((16, 128), BF16)


def first_early_kernel(
    fe, init, got, w, strip1, strip2, strip3, table, s1, s2, s3, force, y, i16, columns, square, idx, sem
):
    def body(even):
        n = init.shape[0]
        full = 3 * n
        origin = origin_of(even, False, n)
        put_table(table, fe, got, even, False)
        copy = pltpu.make_async_copy(table, idx, sem)
        copy.start()
        count = 6 * REACH
        base = mirrored(REACH, count, full, even)
        put_force(force, fe, got, even, 0, n)
        y[pl.ds(0, count * 8), :] = force[pl.ds(base * 8, count * 8), :].astype(F32)

        def add_init():
            pushed = push_init(init, got, None, w, table, origin, columns, square, i16, base, count, n, even)
            y[pl.ds(0, count, stride=8), :] = y[pl.ds(0, count, stride=8), :] + pushed

        pl.when(lax.axis_index("tm") == 0)(add_init)
        s1[pl.ds(base, count)] = split(y[pl.ds(0, count * 8), :].reshape(count, 8, 128))
        for state in (s1, s2, s3):
            state[full] = jnp.zeros((16, 128), BF16)
        copy.wait()
        for k, src, dst in ((1, s1, s2), (2, s2, s3)):
            put_force(force, fe, got, even, k, n)
            size = (6 - 2 * k) * REACH
            base = mirrored((k + 1) * REACH, size, full, even)
            dst[pl.ds(base, size)] = split(apply_phi(src, idx, origin, w, base, size) + force_at(force, base, size))
        put_strips((strip1, strip2, strip3), (s1, s2, s3), full, even)

    by_parity(body)


def first_late_kernel(
    fe, init, got_even, got_odd, strip1, strip2, strip3, w, pk, w1, end, table,
    s1, s2, s3, force, y, i16, columns, square, idx, sem
):
    def body(even):
        n = init.shape[0]
        full = 3 * n
        origin = origin_of(even, True, n)
        put_table(table, fe, got_odd, even, True)
        copy = pltpu.make_async_copy(table, idx, sem)
        copy.start()
        count = 4 * REACH
        base = mirrored(7 * REACH, count, full, even)
        put_force(force, fe, got_odd, not even, 0, n)
        y[...] = force[pl.ds(base * 8, count * 8), :].astype(F32)

        def add_init():
            pushed = push_init(init, got_even, got_odd, w, table, origin, columns, square, i16, base, count, n, even)
            y[pl.ds(0, count, stride=8), :] = y[pl.ds(0, count, stride=8), :] + pushed

        pl.when(lax.axis_index("tm") == 0)(add_init)
        s1[pl.ds(base, count)] = split(y[...].reshape(count, 8, 128))
        get_strips((strip1, strip2, strip3), (s1, s2, s3), full, even)
        copy.wait()
        for k, src, dst in ((1, s1, s2), (2, s2, s3), (3, s3, None)):
            put_force(force, fe, got_odd, not even, k, n)
            base = mirrored((7 - k) * REACH, count, full, even)
            value = apply_phi(src, idx, origin, w, base, count) + force_at(force, base, count)
            if dst is None:
                w1[...] = value
                y[...] = value.reshape(n * 8, 128)
            else:
                dst[pl.ds(base, count)] = split(value)
        end[...] = block_end(y, pk, n)

    by_parity(body)


def scan_kernel(values, pk, starts):
    starts[...] = scan_starts(values[...], pk)


def scan_sum_kernel(values, w1, coarse, pk, starts, total):
    starts[...] = scan_starts(values[...], pk)
    total[...] = values[...] + (w1[...] + coarse[...])


NEAR = 2 * REACH


def put_pay(pay, state, value, side, n):
    def body(even):
        near = 0 if even else n - NEAR
        far = NEAR if even else n - side
        pay[pl.ds(0, NEAR)] = state[pl.ds(near, NEAR)]
        count = side - NEAR
        pay[pl.ds(NEAR, count // 2)] = value[far : far + count].reshape(count // 2, 16, 128).astype(BF16)

    by_parity(body)


def put_far(dst, own, got, right, n):
    half = n // 2
    dst[pl.ds(n + half if right else n, half)] = own[pl.ds(half if right else 0, half)]
    dst[3 * n] = jnp.zeros((16, 128), BF16)
    count = 2 * (got.shape[0] - NEAR)
    dst[pl.ds(2 * n if right else n - NEAR, NEAR)] = got[pl.ds(0, NEAR)]
    leads = got[pl.ds(NEAR, count // 2)].astype(F32).reshape(count, 8, 128)
    far = jnp.concatenate([leads, jnp.zeros_like(leads)], axis=1).astype(BF16)
    dst[pl.ds(2 * n + NEAR if right else n - NEAR - count, count)] = far


def enter_first_kernel(*refs):
    *arrivals, starts, we, pk, state, pay_odd, y = refs
    n = starts.shape[0]
    value = enter(arrivals, we, pk, y, n) + starts[...]
    state[...] = split(value)
    put_pay(pay_odd, state, value, n, n)


def coarse_points(corr, total, pk):
    return product(split(corr).reshape(-1, 128), power(pk, 1)) + total[...]


def enter_second_kernel(*refs):
    *arrivals, starts, total, before, init, we, pk, state, pay_even, pay_odd, corr, y = refs
    n = starts.shape[0]
    value = enter(arrivals, we, pk, y, n) + starts[...]

    def keep(even):
        corr[...] = value if even else coarse_points(value, total, pk)

    by_parity(keep)
    old = before[...].astype(F32)
    y[...] = (value + (old[:, 0:8] + old[:, 8:16])).reshape(n * 8, 128)
    first = (lax.axis_index("tm") == 0).astype(F32)
    y[pl.ds(0, n, stride=8), :] = y[pl.ds(0, n, stride=8), :] + init[...] * first
    value = y[...].reshape(n, 8, 128)
    state[...] = split(value)
    side = (COARSEN - 1) * REACH
    pay_even[...] = state[pl.ds(jnp.where(even_place(), n - side, 0), side)]
    put_pay(pay_odd, state, value, side, n)


def put_block(dst, own, got, right, n):
    side = got.shape[0]
    dst[pl.ds(n, n)] = own[...]
    dst[3 * n] = jnp.zeros((16, 128), BF16)
    dst[pl.ds(2 * n if right else n - side, side)] = got[...]


def second_early_kernel(table, own, got, w, pk, strip1, strip2, strip3, coarse, idx, sem, s0, s1, s2, s3):
    def body(even):
        copy = pltpu.make_async_copy(table, idx, sem)
        copy.start()
        n = own.shape[0]
        origin = origin_of(even, False, n)
        full = 3 * n
        coarse[...] = product(own[...].reshape(n * 16, 128), power(pk, 1))
        put_block(s0, own, got, even, n)
        for state in (s1, s2, s3):
            state[full] = jnp.zeros((16, 128), BF16)
        copy.wait()
        for k, src, dst in ((1, s0, s1), (2, s1, s2), (3, s2, s3)):
            size = (8 - 2 * k) * REACH
            base = mirrored(k * REACH, size, full, even)
            dst[pl.ds(base, size)] = split(apply_phi(src, idx, origin, w, base, size))
        put_strips((strip1, strip2, strip3), (s1, s2, s3), full, even)

    by_parity(body)


def second_late_kernel(table, own, got, strip1, strip2, strip3, coarse, w, pk, res, end, idx, sem, s0, s1, s2, s3, y):
    def body(even):
        copy = pltpu.make_async_copy(table, idx, sem)
        copy.start()
        n = own.shape[0]
        origin = origin_of(even, True, n)
        full = 3 * n
        put_far(s0, own, got, not even, n)
        get_strips((strip1, strip2, strip3), (s1, s2, s3), full, even)
        count = 4 * REACH
        copy.wait()
        for k, src, dst in ((1, s0, s1), (2, s1, s2), (3, s2, s3)):
            base = mirrored((8 - k) * REACH, count, full, even)
            dst[pl.ds(base, count)] = split(apply_phi(src, idx, origin, w, base, count))
        value = apply_phi(s3, idx, origin, w, n, n)
        value = value - coarse[...]
        res[...] = value
        y[...] = value.reshape(n * 8, 128)
        end[...] = block_end(y, pk, n)

    by_parity(body)


def flip_tiles(flip, value, begin):
    lines = flip.reshape(8 * flip.shape[1], 128)
    for e in range(value.shape[0]):
        lines[pl.ds(begin + e, 8, stride=flip.shape[1]), :] = value[e]


def write_out(out, k, flip, begin, size, sems):
    copy = pltpu.make_async_copy(flip.at[:, pl.ds(0, size)], out.at[:, k, pl.ds(begin, size)], sems.at[k])
    copy.start()
    return copy


def third_early_kernel(
    table, own, got, corr, total, fe, pay, w, pk, out, strip1, strip2, kept, idx, sem, s0, s1, s2, force, flip0, flip1, flip3, sems
):
    def body(even):
        table_copy = pltpu.make_async_copy(table, idx, sem)
        table_copy.start()
        n = own.shape[0]
        origin = origin_of(even, False, n)
        full = 3 * n
        points = coarse_points(corr[...], total, pk) if even else corr[...]
        flip_tiles(flip3, points, 0)
        copies = [write_out(out, COARSEN - 1, flip3, 0, n, sems)]
        put_block(s0, own, got, even, n)
        for state in (s1, s2):
            state[full] = jnp.zeros((16, 128), BF16)
        table_copy.wait()
        steps = [(0, s0, s1, flip0), (1, s1, s2, flip1)]
        if even:
            steps.append((2, s2, None, None))
        else:
            kept[...] = jnp.zeros_like(kept)
        for k, src, dst, flip in steps:
            put_force(force, fe, pay, even, k, n)
            size = (5 - 2 * k) * REACH
            base = mirrored((2 + k) * REACH, size, full, even)
            value = apply_phi(src, idx, origin, w, base, size) + force_at(force, base, size)
            if dst is not None:
                dst[pl.ds(base, size)] = split(value)
            mine = (3 - k) * REACH
            value = value[:mine] if even else value[size - mine :]
            if flip is None:
                kept[...] = value
            else:
                flip_tiles(flip, value, 0)
                copies.append(write_out(out, k, flip, n - mine if even else 0, mine, sems))
        for strip, state, low, size in ((strip1, s1, 5 * REACH, 2 * REACH), (strip2, s2, 3 * REACH, 3 * REACH)):
            strip[...] = state[pl.ds(mirrored(low, size, full, even), size)]
        for copy in copies:
            copy.wait()

    by_parity(body)


def third_late_kernel(
    table, own, got, strip1, strip2, kept, fe, pay, w, partial, out, idx, sem, s0, s1, s2, force, flip0, flip1, flip2, sems
):
    def body(even):
        table_copy = pltpu.make_async_copy(table, idx, sem)
        table_copy.start()
        n = own.shape[0]
        origin = origin_of(even, True, n)
        full = 3 * n
        put_far(s0, own, got, not even, n)
        for strip, state, low, size in ((strip1, s1, 5 * REACH, 2 * REACH), (strip2, s2, 3 * REACH, 3 * REACH)):
            state[pl.ds(mirrored(low, size, full, even), size)] = strip[...]
            state[full] = jnp.zeros((16, 128), BF16)
        copies = []
        if even:
            flip_tiles(flip2, kept[...], n - REACH)
        table_copy.wait()
        for k, src, dst, flip in ((0, s0, s1, flip0), (1, s1, s2, flip1), (2, s2, None, flip2)):
            put_force(force, fe, pay, not even, k, n)
            size = 3 * REACH if even or dst is not None else n
            base = mirrored(7 * REACH - k * REACH if size < n else n, size, full, even)
            value = apply_phi(src, idx, origin, w, base, size) + force_at(force, base, size)
            if dst is not None:
                dst[pl.ds(base, size)] = split(value)
            mine = min((k + 1) * REACH, size) if size < n else n
            value = value[size - mine :] if even else value[:mine]
            if dst is None:
                flip_tiles(flip, value, 0 if even else n - mine)
                copies.append(write_out(out, k, flip, 0, n, sems))
            else:
                flip_tiles(flip, value, 0)
                copies.append(write_out(out, k, flip, 0 if even else n - mine, mine, sems))
        for copy in copies:
            copy.wait()

    by_parity(body)


def call(kernel, inputs, outs, scratch, spaces="", out_spaces="", aliases=None, flops=10**7, room=32):
    kinds = {"s": pltpu.SMEM, "h": pltpu.HBM, "v": pltpu.VMEM}

    def specs(arrays, letters):
        letters = letters.ljust(len(arrays), "v")
        return [pl.BlockSpec(memory_space=kinds[letter]) for letter in letters]

    moved = sum(a.size * a.dtype.itemsize for a in list(inputs) + list(outs))
    return pl.pallas_call(
        kernel,
        out_shape=outs,
        name=kernel.__name__,
        in_specs=specs(inputs, spaces),
        out_specs=specs(outs, out_spaces),
        scratch_shapes=scratch,
        input_output_aliases=aliases or {},
        compiler_params=pltpu.CompilerParams(vmem_limit_bytes=room * 1024 * 1024),
        cost_estimate=pl.CostEstimate(flops=flops, bytes_accessed=moved, transcendentals=0),
    )(*inputs)


def local(forcing, initial_state, connectivity, pattern, diag_block, face_blocks, coarse_block):
    n, width = initial_state.shape
    steps = forcing.shape[0]
    full = 3 * n
    tm = lax.axis_size("tm")
    shape = jax.ShapeDtypeStruct
    vmem = pltpu.VMEM
    dma = pltpu.SemaphoreType.DMA
    tiles = shape((n, 8, width), F32)
    state = shape((n, 16, width), BF16)
    ends = shape((n, width), F32)
    step_flops = 2 * 16 * 7 * width * 2 * width
    pay_rows = sum((COARSEN - 1 - k) * REACH * 8 for k in range(COARSEN)) + 2 * n + 16
    pay = shape((pay_rows, width), BF16)
    all_force = ((COARSEN * n * 8 + 16), width)
    fe, pay_even, pay_odd = call(
        pack_kernel,
        (forcing.reshape(steps // COARSEN, COARSEN, n, width), initial_state, connectivity.T, pattern.T),
        (shape(all_force, BF16), pay, pay),
        [
            vmem((COARSEN, 8, n, width), BF16),
            vmem((8 * (n + 8), width), F32),
            vmem((n, width), F32),
            vmem((6, n), jnp.int32),
            vmem((6, n), jnp.int32),
            vmem((16, 128), F32),
            vmem(all_force, BF16),
            vmem((pay_rows, width), BF16),
            vmem((pay_rows, width), BF16),
            dma((COARSEN + 3,)),
            dma((2 + COARSEN,)),
        ],
        spaces="hhhh",
        flops=3 * 10**9,
        out_spaces="hhh",
        room=62,
    )
    pay_odd, pay_even = swapped(pay_odd, 1), swapped(pay_even, 0)
    w, pk, we = call(
        weight_kernel,
        (diag_block, face_blocks, coarse_block),
        (
            shape((7 * width, 2 * width), BF16),
            shape((8 * width, 2 * width), BF16),
            shape(((tm - 1) * width, 2 * width), BF16),
        ),
        [],
        flops=10**9,
    )
    spaces = vmem((full + 1, 16, width), BF16)
    force = vmem((full * 8, width), BF16)
    rows = vmem((n * 8, width), F32)
    strip = shape((STRIP, 16, width), BF16)
    tables = [vmem((256, 256), BF16), vmem((128, 128), F32), vmem((128, 128), F32)]
    smem = pltpu.SMEM((8, 2 * n), jnp.int32)
    table = shape((8, 2 * n), jnp.int32)
    *strips, table_early = call(
        first_early_kernel,
        (fe, initial_state, pay_even, w),
        (strip, strip, strip, table),
        [spaces] * 3 + [force, vmem((6 * REACH * 8, width), F32)] + tables + [smem, dma],
        flops=step_flops * 6 * REACH,
    )
    w1, end, table_late = call(
        first_late_kernel,
        (fe, initial_state, pay_even, pay_odd, *strips, w, pk),
        (tiles, ends, table),
        [spaces] * 3 + [force, rows] + tables + [smem, dma],
        flops=step_flops * 12 * REACH,
    )
    arrivals = earlier(end)
    (starts,) = call(scan_kernel, (w1, pk), (tiles,), [])
    def across(side):
        return shape((NEAR + (side - NEAR) // 2, 16, width), BF16)

    coarse, end_odd = call(enter_first_kernel, (*arrivals, starts, we, pk), (state, across(n)), [rows])
    got_odd, got_even = swapped(end_odd, 1), swapped(coarse, 0)
    *strips, moved = call(
        second_early_kernel,
        (table_early, coarse, got_even, w, pk),
        (strip, strip, strip, tiles),
        [smem, dma] + [spaces] * 4,
        flops=step_flops * 12 * REACH,
    )
    res, end = call(
        second_late_kernel,
        (table_late, coarse, got_odd, *strips, moved, w, pk),
        (tiles, ends),
        [smem, dma] + [spaces] * 4 + [rows],
        flops=step_flops * 16 * REACH,
    )
    arrivals = earlier(end)
    starts, total = call(scan_sum_kernel, (res, w1, moved, pk), (tiles, tiles), [])
    side = (COARSEN - 1) * REACH
    coarse, end_even, end_odd, corr = call(
        enter_second_kernel,
        (*arrivals, starts, total, coarse, initial_state, we, pk),
        (state, shape((side, 16, width), BF16), across(side), tiles),
        [rows],
    )
    got_odd, got_even = swapped(end_odd, 1), swapped(end_even, 0)
    result = shape((steps // COARSEN, COARSEN, n, width), F32)

    def flip(blocks):
        return vmem((8, blocks * REACH + 8, width), F32)

    out, *strips = call(
        third_early_kernel,
        (table_early, coarse, got_even, corr, total, fe, pay_even, w, pk),
        (result, strip, shape((3 * REACH, 16, width), BF16), shape((REACH, 8, width), F32)),
        [smem, dma] + [spaces] * 3 + [force, flip(3), flip(2), vmem((8, n + 8, width), F32), dma((COARSEN,))],
        out_spaces="h",
        flops=step_flops * 9 * REACH,
    )
    (out,) = call(
        third_late_kernel,
        (table_late, coarse, got_odd, *strips, fe, pay_odd, w, out),
        (result,),
        [smem, dma] + [spaces] * 3 + [force, flip(1), flip(2), vmem((8, n + 8, width), F32), dma((COARSEN - 1,))],
        spaces="vvvvvvvvvh",
        out_spaces="h",
        aliases={9: 0},
        flops=step_flops * 9 * REACH,
    )
    return out.reshape(steps, n, width)


def solution(mesh):
    return jax.shard_map(
        local,
        mesh=mesh,
        in_specs=(
            P("tm", ("groups", "space"), None),
            P(("groups", "space"), None),
            P("space", None),
            P("space", None),
            P(),
            P(),
            P(),
        ),
        out_specs=P("tm", ("groups", "space"), None),
        check_vma=False,
    )
```

```python
import functools

import jax
import jax.numpy as jnp
from jax import lax
from jax.experimental import pallas as pl
from jax.experimental.pallas import tpu as pltpu
from jax.sharding import PartitionSpec as P

COARSEN = 4
REACH = 16
F32 = jnp.float32
BF16 = jnp.bfloat16
CHUNK = 32


def swapped(value, first):
    count = lax.axis_size("space")
    pairs = []
    for i in range(first, count - 1, 2):
        pairs += [(i, i + 1), (i + 1, i)]
    return lax.ppermute(value, "space", pairs)


def earlier(value):
    return [lax.all_gather(value, "tm")]


def split(u):
    lead = u.astype(BF16).astype(F32)
    return jnp.concatenate([u, u - lead], axis=1).astype(BF16)


def split_rows(u):
    lead = u.astype(BF16)
    return jnp.concatenate([lead, (u - lead.astype(F32)).astype(BF16)], axis=0)


def product(x, weights):
    m = x.shape[0] // 16
    r = jnp.dot(x, weights, preferred_element_type=F32).reshape(m, 16, 256)
    return r[:, :8, :128] + (r[:, 8:, :128] + r[:, :8, 128:])


def product_rows(x, weights):
    m = x.shape[0] // 2
    r = jnp.dot(x, weights, preferred_element_type=F32)
    return r[:m, :128] + (r[m:, :128] + r[:m, 128:])


def put_halves(ref, w):
    lead = w.astype(BF16)
    ref[:, 0:128] = lead
    ref[:, 128:256] = (w - lead.astype(F32)).astype(BF16)


def power(pk, k):
    return pk[pl.ds(128 * (7 - k), 128), :]


def scan_starts(values, pk):
    y = values
    row = lax.broadcasted_iota(jnp.int32, y.shape, 1)
    for d in (1, 2, 4):
        z = product(split(y).reshape(-1, 128), power(pk, d))
        y = y + jnp.where(row >= d, pltpu.roll(z, d, axis=1), 0.0)
    return jnp.where(row >= 1, pltpu.roll(y, 1, axis=1), 0.0)


def block_end(y, pk, n):
    parts = [y[pl.ds(i, n, stride=8), :] for i in range(8)]
    return product_rows(split_rows(jnp.concatenate(parts, axis=1)), pk[...])


def enter(arrivals, we, pk, y, n):
    (ends,) = arrivals
    value = jnp.concatenate([ends[i] for i in range(ends.shape[0])], axis=1)
    entry = product_rows(split_rows(value), we[...])
    y[pl.ds(0, n, stride=8), :] = entry
    rows = split_rows(entry)
    for i in range(1, 8):
        y[pl.ds(i, n, stride=8), :] = product_rows(rows, power(pk, i))
    return y[...].reshape(n, 8, 128)


def apply_phi(src, idx, origin, w, base, size):
    cols = [src[pl.ds(base, size)].reshape(size * 16, 128)]
    for f in range(6):
        cols.append(jnp.concatenate([src[idx[f, base - origin + e]] for e in range(size)], axis=0))
    return product(jnp.concatenate(cols, axis=1), w[...])


def even_place():
    return lax.rem(lax.axis_index("space"), 2) == 0


def by_parity(body):
    even = even_place()
    pl.when(even)(lambda: body(True))
    pl.when(jnp.logical_not(even))(lambda: body(False))


def mirrored(low, size, full, even):
    return full - low - size if even else low


def pack_kernel(
    forcing, init, conn, pattern, fe_out, even_out, odd_out,
    landed, rows, init_v, conn_v, pattern_v, offs, fe, pay_even, pay_odd, sems, out_sems
):
    n = init_v.shape[0]
    pitch = n + 8
    copies = [pltpu.make_async_copy(forcing.at[:, k], landed.at[k], sems.at[k]) for k in range(COARSEN)]
    small = ((conn, conn_v), (pattern, pattern_v), (init, init_v))
    copies += [pltpu.make_async_copy(src, dst, sems.at[COARSEN + i]) for i, (src, dst) in enumerate(small)]
    for copy in copies[COARSEN:] + copies[:COARSEN]:
        copy.start()
    for copy in copies[COARSEN:]:
        copy.wait()
    place = lax.broadcasted_iota(jnp.int32, (6, n), 1) + lax.axis_index("space") * n
    value = ((conn_v[...] - place) * pattern_v[...]).astype(F32)
    offs[...] = jnp.zeros_like(offs)
    offs[0:6, 0:n] = value
    offs[0:6, n : 2 * n] = value
    tab = offs[...].astype(BF16)
    fe[pl.ds(COARSEN * n * 8, 16), :] = tab
    lead = init_v[...].astype(BF16)
    rest = (init_v[...] - lead.astype(F32)).astype(BF16)
    even = even_place()
    at = sum((COARSEN - 1 - k) * REACH * 8 for k in range(COARSEN))
    for pay in (pay_even, pay_odd):
        pay[pl.ds(at, n), :] = lead
        pay[pl.ds(at + n, n), :] = rest
        pay[pl.ds(at + 2 * n, 16), :] = tab
    at = 0
    results = []
    for k in range(COARSEN):
        copies[k].wait()
        for i in range(8):
            rows[pl.ds(i * pitch, n), :] = landed[k, i].astype(F32)

        def body(pair, carry, k=k):
            e = pair * 2
            two = [rows[pl.ds(e + j, 8, stride=pitch), :] for j in range(2)]
            fe[pl.ds(pl.multiple_of((k * n + e) * 8, 16), 16), :] = jnp.concatenate(two, axis=0).astype(BF16)
            return carry

        lax.fori_loop(0, n // 2, body, 0, unroll=8)
        width = (COARSEN - 1 - k) * REACH * 8
        if width:
            for pay, right in ((pay_even, even), (pay_odd, jnp.logical_not(even))):
                begin = pl.multiple_of(k * n * 8 + jnp.where(right, n * 8 - width, 0), 128)
                pay[pl.ds(at, width), :] = fe[pl.ds(begin, width), :]
        at += width
        rows_k = pl.ds(k * n * 8, n * 8 + (16 if k == COARSEN - 1 else 0))
        results.append(pltpu.make_async_copy(fe.at[rows_k], fe_out.at[rows_k], out_sems.at[2 + k]))
        results[-1].start()
        if k == COARSEN - 2:
            results.append(pltpu.make_async_copy(pay_odd, odd_out, out_sems.at[0]))
            results.append(pltpu.make_async_copy(pay_even, even_out, out_sems.at[1]))
            results[-2].start()
            results[-1].start()
    for result in results:
        result.wait()


def weight_kernel(diag, faces, coarse, w, pk, we):
    put_halves(w.at[pl.ds(0, 128)], diag[...].T)
    for f in range(6):
        put_halves(w.at[pl.ds(128 * (f + 1), 128)], faces[f].T)

    def thirds(a):
        one = a.astype(BF16)
        rest = a - one.astype(F32)
        two = rest.astype(BF16)
        return one, two, (rest - two.astype(F32)).astype(BF16)

    def mul(a, b):
        (a1, a2, a3), (b1, b2, b3) = thirds(a), thirds(b)
        total = jnp.zeros((128, 128), F32)
        for x, y in ((a3, b1), (a1, b3), (a2, b2), (a2, b1), (a1, b2), (a1, b1)):
            total += jnp.dot(x, y, preferred_element_type=F32)
        return total

    rows = lax.broadcasted_iota(jnp.int32, (128, 128), 0)
    one = (rows == lax.broadcasted_iota(jnp.int32, (128, 128), 1)).astype(F32)
    powers = [one, coarse[...].T]
    for k in range(2, 9):
        powers.append(mul(powers[k // 2], powers[k - k // 2]))
    for k in range(8):
        put_halves(pk.at[pl.ds(128 * (7 - k), 128)], powers[k])

    t = lax.axis_index("tm")
    we[...] = jnp.zeros_like(we)

    def body(k, current):
        put_halves(we.at[pl.ds(pl.multiple_of((t - 1 - k) * 128, 128), 128)], current)
        return mul(current, powers[8])

    lax.fori_loop(0, t, body, one)


def put_force(dst, own, got, right, k, n):
    at = sum((COARSEN - 1 - j) * REACH * 8 for j in range(k))
    width = (COARSEN - 1 - k) * REACH * 8
    dst[pl.ds(n * 8, n * 8), :] = own[pl.ds(k * n * 8, n * 8), :]
    if width:
        to = 2 * n * 8 if right else n * 8 - width
        dst[pl.ds(to, width), :] = got[pl.ds(at, width), :]


def force_at(src, base, size):
    return src[pl.ds(base * 8, size * 8), :].astype(F32).reshape(size, 8, 128)


def origin_of(even, late, n):
    return n if even != late else 0


def put_table(table, fe, got, even, late):
    n = table.shape[1] // 2
    lane = lax.broadcasted_iota(jnp.int32, table.shape, 1)

    def part(ref):
        return ref[pl.ds(ref.shape[0] - 16, 16), :].astype(F32)[0:8]

    origin = origin_of(even, late, n)
    offs = jnp.where(lane < n, part(fe), part(got)) if origin else jnp.where(lane < n, part(got), part(fe))
    table[...] = jnp.where(offs != 0.0, lane + origin + offs.astype(jnp.int32), 3 * n)


def push_init(init, got_even, got_odd, w, table, origin, columns, square, i16, base, count, n, even):
    square[...] = jnp.zeros_like(square)
    square[0:8, :] = table[...].astype(F32)
    columns[...] = square[...].T
    i16[...] = jnp.zeros_like(i16)
    lead = init[...].astype(BF16)
    i16[pl.ds(n, n), 0:128] = lead
    i16[pl.ds(n, n), 128:256] = (init[...] - lead.astype(F32)).astype(BF16)
    for ref, right in ((got_even, even), (got_odd, not even)):
        if ref is not None:
            at = ref.shape[0] - 16
            to = 2 * n if right else 0
            i16[pl.ds(to, n), 0:128] = ref[pl.ds(at - 2 * n, n), :]
            i16[pl.ds(to, n), 128:256] = ref[pl.ds(at - n, n), :]
    rows = pl.ds(base, count)
    place = columns[pl.ds(base - origin, count), :]
    spot = lax.broadcasted_iota(jnp.int32, (count, 256), 1).astype(F32)
    cols = [i16[rows, :]]
    for f in range(6):
        hot = (spot == place[:, f : f + 1]).astype(F32).astype(BF16)
        cols.append(jnp.dot(hot, i16[...], preferred_element_type=F32).astype(BF16))
    leads = jnp.concatenate([c[:, 0:128] for c in cols], axis=1)
    rests = jnp.concatenate([c[:, 128:256] for c in cols], axis=1)
    return product_rows(jnp.concatenate([leads, rests], axis=0), w[...])


STRIPS = (5 * REACH, 4 * REACH, 3 * REACH)
STRIP = 2 * REACH


def put_strips(strips, states, full, even):
    for strip, state, low in zip(strips, states, STRIPS):
        strip[...] = state[pl.ds(mirrored(low, STRIP, full, even), STRIP)]


def get_strips(strips, states, full, even):
    for strip, state, low in zip(strips, states, STRIPS):
        state[pl.ds(mirrored(low, STRIP, full, even), STRIP)] = strip[...]
        state[full] = jnp.zeros((16, 128), BF16)


def first_early_kernel(
    fe, init, got, w, strip1, strip2, strip3, table, s1, s2, s3, force, y, i16, columns, square, idx, sem
):
    def body(even):
        n = init.shape[0]
        full = 3 * n
        origin = origin_of(even, False, n)
        put_table(table, fe, got, even, False)
        copy = pltpu.make_async_copy(table, idx, sem)
        copy.start()
        count = 6 * REACH
        base = mirrored(REACH, count, full, even)
        put_force(force, fe, got, even, 0, n)
        y[pl.ds(0, count * 8), :] = force[pl.ds(base * 8, count * 8), :].astype(F32)

        def add_init():
            pushed = push_init(init, got, None, w, table, origin, columns, square, i16, base, count, n, even)
            y[pl.ds(0, count, stride=8), :] = y[pl.ds(0, count, stride=8), :] + pushed

        pl.when(lax.axis_index("tm") == 0)(add_init)
        s1[pl.ds(base, count)] = split(y[pl.ds(0, count * 8), :].reshape(count, 8, 128))
        for state in (s1, s2, s3):
            state[full] = jnp.zeros((16, 128), BF16)
        copy.wait()
        for k, src, dst in ((1, s1, s2), (2, s2, s3)):
            put_force(force, fe, got, even, k, n)
            size = (6 - 2 * k) * REACH
            base = mirrored((k + 1) * REACH, size, full, even)
            dst[pl.ds(base, size)] = split(apply_phi(src, idx, origin, w, base, size) + force_at(force, base, size))
        put_strips((strip1, strip2, strip3), (s1, s2, s3), full, even)

    by_parity(body)


def first_late_kernel(
    fe, init, got_even, got_odd, strip1, strip2, strip3, w, pk, w1, end, table,
    s1, s2, s3, force, y, i16, columns, square, idx, sem
):
    def body(even):
        n = init.shape[0]
        full = 3 * n
        origin = origin_of(even, True, n)
        put_table(table, fe, got_odd, even, True)
        copy = pltpu.make_async_copy(table, idx, sem)
        copy.start()
        count = 4 * REACH
        base = mirrored(7 * REACH, count, full, even)
        put_force(force, fe, got_odd, not even, 0, n)
        y[...] = force[pl.ds(base * 8, count * 8), :].astype(F32)

        def add_init():
            pushed = push_init(init, got_even, got_odd, w, table, origin, columns, square, i16, base, count, n, even)
            y[pl.ds(0, count, stride=8), :] = y[pl.ds(0, count, stride=8), :] + pushed

        pl.when(lax.axis_index("tm") == 0)(add_init)
        s1[pl.ds(base, count)] = split(y[...].reshape(count, 8, 128))
        get_strips((strip1, strip2, strip3), (s1, s2, s3), full, even)
        copy.wait()
        for k, src, dst in ((1, s1, s2), (2, s2, s3), (3, s3, None)):
            put_force(force, fe, got_odd, not even, k, n)
            base = mirrored((7 - k) * REACH, count, full, even)
            value = apply_phi(src, idx, origin, w, base, count) + force_at(force, base, count)
            if dst is None:
                w1[...] = value
                y[...] = value.reshape(n * 8, 128)
            else:
                dst[pl.ds(base, count)] = split(value)
        end[...] = block_end(y, pk, n)

    by_parity(body)


def scan_kernel(values, pk, starts):
    starts[...] = scan_starts(values[...], pk)


def scan_sum_kernel(values, w1, coarse, pk, starts, total):
    starts[...] = scan_starts(values[...], pk)
    total[...] = values[...] + (w1[...] + coarse[...])


NEAR = 2 * REACH


def put_pay(pay, state, value, side, n):
    def body(even):
        near = 0 if even else n - NEAR
        far = NEAR if even else n - side
        pay[pl.ds(0, NEAR)] = state[pl.ds(near, NEAR)]
        count = side - NEAR
        pay[pl.ds(NEAR, count // 2)] = value[far : far + count].reshape(count // 2, 16, 128).astype(BF16)

    by_parity(body)


def put_far(dst, own, got, right, n):
    half = n // 2
    dst[pl.ds(n + half if right else n, half)] = own[pl.ds(half if right else 0, half)]
    dst[3 * n] = jnp.zeros((16, 128), BF16)
    count = 2 * (got.shape[0] - NEAR)
    dst[pl.ds(2 * n if right else n - NEAR, NEAR)] = got[pl.ds(0, NEAR)]
    leads = got[pl.ds(NEAR, count // 2)].astype(F32).reshape(count, 8, 128)
    far = jnp.concatenate([leads, jnp.zeros_like(leads)], axis=1).astype(BF16)
    dst[pl.ds(2 * n + NEAR if right else n - NEAR - count, count)] = far


def enter_first_kernel(*refs):
    *arrivals, starts, we, pk, state, pay_odd, y = refs
    n = starts.shape[0]
    value = enter(arrivals, we, pk, y, n) + starts[...]
    state[...] = split(value)
    put_pay(pay_odd, state, value, n, n)


def coarse_points(corr, total, pk):
    return product(split(corr).reshape(-1, 128), power(pk, 1)) + total[...]


def enter_second_kernel(*refs):
    *arrivals, starts, total, before, init, we, pk, state, pay_even, pay_odd, corr, y = refs
    n = starts.shape[0]
    value = enter(arrivals, we, pk, y, n) + starts[...]

    def keep(even):
        corr[...] = value if even else coarse_points(value, total, pk)

    by_parity(keep)
    old = before[...].astype(F32)
    y[...] = (value + (old[:, 0:8] + old[:, 8:16])).reshape(n * 8, 128)
    first = (lax.axis_index("tm") == 0).astype(F32)
    y[pl.ds(0, n, stride=8), :] = y[pl.ds(0, n, stride=8), :] + init[...] * first
    value = y[...].reshape(n, 8, 128)
    state[...] = split(value)
    side = (COARSEN - 1) * REACH
    pay_even[...] = state[pl.ds(jnp.where(even_place(), n - side, 0), side)]
    put_pay(pay_odd, state, value, side, n)


def put_block(dst, own, got, right, n):
    side = got.shape[0]
    dst[pl.ds(n, n)] = own[...]
    dst[3 * n] = jnp.zeros((16, 128), BF16)
    dst[pl.ds(2 * n if right else n - side, side)] = got[...]


def second_early_kernel(table, own, got, w, pk, strip1, strip2, strip3, coarse, idx, sem, s0, s1, s2, s3):
    def body(even):
        copy = pltpu.make_async_copy(table, idx, sem)
        copy.start()
        n = own.shape[0]
        origin = origin_of(even, False, n)
        full = 3 * n
        coarse[...] = product(own[...].reshape(n * 16, 128), power(pk, 1))
        put_block(s0, own, got, even, n)
        for state in (s1, s2, s3):
            state[full] = jnp.zeros((16, 128), BF16)
        copy.wait()
        for k, src, dst in ((1, s0, s1), (2, s1, s2), (3, s2, s3)):
            size = (8 - 2 * k) * REACH
            base = mirrored(k * REACH, size, full, even)
            dst[pl.ds(base, size)] = split(apply_phi(src, idx, origin, w, base, size))
        put_strips((strip1, strip2, strip3), (s1, s2, s3), full, even)

    by_parity(body)


def second_late_kernel(table, own, got, strip1, strip2, strip3, coarse, w, pk, res, end, idx, sem, s0, s1, s2, s3, y):
    def body(even):
        copy = pltpu.make_async_copy(table, idx, sem)
        copy.start()
        n = own.shape[0]
        origin = origin_of(even, True, n)
        full = 3 * n
        put_far(s0, own, got, not even, n)
        get_strips((strip1, strip2, strip3), (s1, s2, s3), full, even)
        count = 4 * REACH
        copy.wait()
        for k, src, dst in ((1, s0, s1), (2, s1, s2), (3, s2, s3)):
            base = mirrored((8 - k) * REACH, count, full, even)
            dst[pl.ds(base, count)] = split(apply_phi(src, idx, origin, w, base, count))
        value = apply_phi(s3, idx, origin, w, n, n)
        value = value - coarse[...]
        res[...] = value
        y[...] = value.reshape(n * 8, 128)
        end[...] = block_end(y, pk, n)

    by_parity(body)


def flip_tiles(flip, value, begin):
    lines = flip.reshape(8 * flip.shape[1], 128)
    for e in range(value.shape[0]):
        lines[pl.ds(begin + e, 8, stride=flip.shape[1]), :] = value[e]


def write_out(out, k, flip, begin, size, sems):
    copy = pltpu.make_async_copy(flip.at[:, pl.ds(0, size)], out.at[:, k, pl.ds(begin, size)], sems.at[k])
    copy.start()
    return copy


def third_early_kernel(
    table, own, got, corr, total, fe, pay, w, pk, out, strip1, strip2, kept, idx, sem, s0, s1, s2, force, flip0, flip1, flip3, sems
):
    def body(even):
        table_copy = pltpu.make_async_copy(table, idx, sem)
        table_copy.start()
        n = own.shape[0]
        origin = origin_of(even, False, n)
        full = 3 * n
        points = coarse_points(corr[...], total, pk) if even else corr[...]
        flip_tiles(flip3, points, 0)
        copies = [write_out(out, COARSEN - 1, flip3, 0, n, sems)]
        put_block(s0, own, got, even, n)
        for state in (s1, s2):
            state[full] = jnp.zeros((16, 128), BF16)
        table_copy.wait()
        steps = [(0, s0, s1, flip0), (1, s1, s2, flip1)]
        if even:
            steps.append((2, s2, None, None))
        else:
            kept[...] = jnp.zeros_like(kept)
        for k, src, dst, flip in steps:
            put_force(force, fe, pay, even, k, n)
            size = (5 - 2 * k) * REACH
            base = mirrored((2 + k) * REACH, size, full, even)
            value = apply_phi(src, idx, origin, w, base, size) + force_at(force, base, size)
            if dst is not None:
                dst[pl.ds(base, size)] = split(value)
            mine = (3 - k) * REACH
            value = value[:mine] if even else value[size - mine :]
            if flip is None:
                kept[...] = value
            else:
                flip_tiles(flip, value, 0)
                copies.append(write_out(out, k, flip, n - mine if even else 0, mine, sems))
        for strip, state, low, size in ((strip1, s1, 5 * REACH, 2 * REACH), (strip2, s2, 3 * REACH, 3 * REACH)):
            strip[...] = state[pl.ds(mirrored(low, size, full, even), size)]
        for copy in copies:
            copy.wait()

    by_parity(body)


def third_late_kernel(
    table, own, got, strip1, strip2, kept, fe, pay, w, partial, out, idx, sem, s0, s1, s2, force, flip0, flip1, flip2, sems
):
    def body(even):
        table_copy = pltpu.make_async_copy(table, idx, sem)
        table_copy.start()
        n = own.shape[0]
        origin = origin_of(even, True, n)
        full = 3 * n
        put_far(s0, own, got, not even, n)
        for strip, state, low, size in ((strip1, s1, 5 * REACH, 2 * REACH), (strip2, s2, 3 * REACH, 3 * REACH)):
            state[pl.ds(mirrored(low, size, full, even), size)] = strip[...]
            state[full] = jnp.zeros((16, 128), BF16)
        copies = []
        if even:
            flip_tiles(flip2, kept[...], n - REACH)
        table_copy.wait()
        for k, src, dst, flip in ((0, s0, s1, flip0), (1, s1, s2, flip1), (2, s2, None, flip2)):
            put_force(force, fe, pay, not even, k, n)
            size = 3 * REACH if even or dst is not None else n
            base = mirrored(7 * REACH - k * REACH if size < n else n, size, full, even)
            value = apply_phi(src, idx, origin, w, base, size) + force_at(force, base, size)
            if dst is not None:
                dst[pl.ds(base, size)] = split(value)
            mine = min((k + 1) * REACH, size) if size < n else n
            value = value[size - mine :] if even else value[:mine]
            if dst is None:
                flip_tiles(flip, value, 0 if even else n - mine)
                copies.append(write_out(out, k, flip, 0, n, sems))
            else:
                flip_tiles(flip, value, 0)
                copies.append(write_out(out, k, flip, 0 if even else n - mine, mine, sems))
        for copy in copies:
            copy.wait()

    by_parity(body)


def call(kernel, inputs, outs, scratch, spaces="", out_spaces="", aliases=None, flops=10**7, room=32):
    kinds = {"s": pltpu.SMEM, "h": pltpu.HBM, "v": pltpu.VMEM}

    def specs(arrays, letters):
        letters = letters.ljust(len(arrays), "v")
        return [pl.BlockSpec(memory_space=kinds[letter]) for letter in letters]

    moved = sum(a.size * a.dtype.itemsize for a in list(inputs) + list(outs))
    return pl.pallas_call(
        kernel,
        out_shape=outs,
        name=kernel.__name__,
        in_specs=specs(inputs, spaces),
        out_specs=specs(outs, out_spaces),
        scratch_shapes=scratch,
        input_output_aliases=aliases or {},
        compiler_params=pltpu.CompilerParams(vmem_limit_bytes=room * 1024 * 1024),
        cost_estimate=pl.CostEstimate(flops=flops, bytes_accessed=moved, transcendentals=0),
    )(*inputs)


def local(forcing, initial_state, connectivity, pattern, diag_block, face_blocks, coarse_block):
    n, width = initial_state.shape
    steps = forcing.shape[0]
    full = 3 * n
    tm = lax.axis_size("tm")
    shape = jax.ShapeDtypeStruct
    vmem = pltpu.VMEM
    dma = pltpu.SemaphoreType.DMA
    tiles = shape((n, 8, width), F32)
    state = shape((n, 16, width), BF16)
    ends = shape((n, width), F32)
    step_flops = 2 * 16 * 7 * width * 2 * width
    pay_rows = sum((COARSEN - 1 - k) * REACH * 8 for k in range(COARSEN)) + 2 * n + 16
    pay = shape((pay_rows, width), BF16)
    all_force = ((COARSEN * n * 8 + 16), width)
    fe, pay_even, pay_odd = call(
        pack_kernel,
        (forcing.reshape(steps // COARSEN, COARSEN, n, width), initial_state, connectivity.T, pattern.T),
        (shape(all_force, BF16), pay, pay),
        [
            vmem((COARSEN, 8, n, width), BF16),
            vmem((8 * (n + 8), width), F32),
            vmem((n, width), F32),
            vmem((6, n), jnp.int32),
            vmem((6, n), jnp.int32),
            vmem((16, 128), F32),
            vmem(all_force, BF16),
            vmem((pay_rows, width), BF16),
            vmem((pay_rows, width), BF16),
            dma((COARSEN + 3,)),
            dma((2 + COARSEN,)),
        ],
        spaces="hhhh",
        flops=3 * 10**9,
        out_spaces="hhh",
        room=62,
    )
    pay_odd, pay_even = swapped(pay_odd, 1), swapped(pay_even, 0)
    w, pk, we = call(
        weight_kernel,
        (diag_block, face_blocks, coarse_block),
        (
            shape((7 * width, 2 * width), BF16),
            shape((8 * width, 2 * width), BF16),
            shape((tm * width, 2 * width), BF16),
        ),
        [],
        flops=10**9,
    )
    spaces = vmem((full + 1, 16, width), BF16)
    force = vmem((full * 8, width), BF16)
    rows = vmem((n * 8, width), F32)
    strip = shape((STRIP, 16, width), BF16)
    tables = [vmem((256, 256), BF16), vmem((128, 128), F32), vmem((128, 128), F32)]
    smem = pltpu.SMEM((8, 2 * n), jnp.int32)
    table = shape((8, 2 * n), jnp.int32)
    *strips, table_early = call(
        first_early_kernel,
        (fe, initial_state, pay_even, w),
        (strip, strip, strip, table),
        [spaces] * 3 + [force, vmem((6 * REACH * 8, width), F32)] + tables + [smem, dma],
        flops=step_flops * 6 * REACH,
    )
    w1, end, table_late = call(
        first_late_kernel,
        (fe, initial_state, pay_even, pay_odd, *strips, w, pk),
        (tiles, ends, table),
        [spaces] * 3 + [force, rows] + tables + [smem, dma],
        flops=step_flops * 12 * REACH,
    )
    arrivals = earlier(end)
    (starts,) = call(scan_kernel, (w1, pk), (tiles,), [])
    def across(side):
        return shape((NEAR + (side - NEAR) // 2, 16, width), BF16)

    coarse, end_odd = call(enter_first_kernel, (*arrivals, starts, we, pk), (state, across(n)), [rows])
    got_odd, got_even = swapped(end_odd, 1), swapped(coarse, 0)
    *strips, moved = call(
        second_early_kernel,
        (table_early, coarse, got_even, w, pk),
        (strip, strip, strip, tiles),
        [smem, dma] + [spaces] * 4,
        flops=step_flops * 12 * REACH,
    )
    res, end = call(
        second_late_kernel,
        (table_late, coarse, got_odd, *strips, moved, w, pk),
        (tiles, ends),
        [smem, dma] + [spaces] * 4 + [rows],
        flops=step_flops * 16 * REACH,
    )
    arrivals = earlier(end)
    starts, total = call(scan_sum_kernel, (res, w1, moved, pk), (tiles, tiles), [])
    side = (COARSEN - 1) * REACH
    coarse, end_even, end_odd, corr = call(
        enter_second_kernel,
        (*arrivals, starts, total, coarse, initial_state, we, pk),
        (state, shape((side, 16, width), BF16), across(side), tiles),
        [rows],
    )
    got_odd, got_even = swapped(end_odd, 1), swapped(end_even, 0)
    result = shape((steps // COARSEN, COARSEN, n, width), F32)

    def flip(blocks):
        return vmem((8, blocks * REACH + 8, width), F32)

    out, *strips = call(
        third_early_kernel,
        (table_early, coarse, got_even, corr, total, fe, pay_even, w, pk),
        (result, strip, shape((3 * REACH, 16, width), BF16), shape((REACH, 8, width), F32)),
        [smem, dma] + [spaces] * 3 + [force, flip(3), flip(2), vmem((8, n + 8, width), F32), dma((COARSEN,))],
        out_spaces="h",
        flops=step_flops * 9 * REACH,
    )
    (out,) = call(
        third_late_kernel,
        (table_late, coarse, got_odd, *strips, fe, pay_odd, w, out),
        (result,),
        [smem, dma] + [spaces] * 3 + [force, flip(1), flip(2), vmem((8, n + 8, width), F32), dma((COARSEN - 1,))],
        spaces="vvvvvvvvvh",
        out_spaces="h",
        aliases={9: 0},
        flops=step_flops * 9 * REACH,
    )
    return out.reshape(steps, n, width)


def solution(mesh):
    return jax.shard_map(
        local,
        mesh=mesh,
        in_specs=(
            P("tm", ("groups", "space"), None),
            P(("groups", "space"), None),
            P("space", None),
            P("space", None),
            P(),
            P(),
            P(),
        ),
        out_specs=P("tm", ("groups", "space"), None),
        check_vma=False,
    )
```

```python
import functools

import jax
import jax.numpy as jnp
from jax import lax
from jax.experimental import pallas as pl
from jax.experimental.pallas import tpu as pltpu
from jax.sharding import PartitionSpec as P

COARSEN = 4
REACH = 16
F32 = jnp.float32
BF16 = jnp.bfloat16
CHUNK = 32


def swapped(value, first):
    count = lax.axis_size("space")
    pairs = []
    for i in range(first, count - 1, 2):
        pairs += [(i, i + 1), (i + 1, i)]
    return lax.ppermute(value, "space", pairs)


def earlier(value):
    count = lax.axis_size("tm")
    if count <= 8:
        return [lax.ppermute(value, "tm", [(i, i + s) for i in range(count - s)]) for s in range(1, count)]
    every = lax.all_gather(value, "tm")
    at = lax.axis_index("tm") - jnp.arange(1, count)
    picked = jnp.where((at >= 0)[:, None, None], jnp.take(every, jnp.maximum(at, 0), axis=0), 0.0)
    return [picked[s] for s in range(count - 1)]


def split(u):
    lead = u.astype(BF16).astype(F32)
    return jnp.concatenate([u, u - lead], axis=1).astype(BF16)


def split_rows(u):
    lead = u.astype(BF16)
    return jnp.concatenate([lead, (u - lead.astype(F32)).astype(BF16)], axis=0)


def product(x, weights):
    m = x.shape[0] // 16
    r = jnp.dot(x, weights, preferred_element_type=F32).reshape(m, 16, 256)
    return r[:, :8, :128] + (r[:, 8:, :128] + r[:, :8, 128:])


def product_rows(x, weights):
    m = x.shape[0] // 2
    r = jnp.dot(x, weights, preferred_element_type=F32)
    return r[:m, :128] + (r[m:, :128] + r[:m, 128:])


def put_halves(ref, w):
    lead = w.astype(BF16)
    ref[:, 0:128] = lead
    ref[:, 128:256] = (w - lead.astype(F32)).astype(BF16)


def power(pk, k):
    return pk[pl.ds(128 * (7 - k), 128), :]


def scan_starts(values, pk):
    y = values
    row = lax.broadcasted_iota(jnp.int32, y.shape, 1)
    for d in (1, 2, 4):
        z = product(split(y).reshape(-1, 128), power(pk, d))
        y = y + jnp.where(row >= d, pltpu.roll(z, d, axis=1), 0.0)
    return jnp.where(row >= 1, pltpu.roll(y, 1, axis=1), 0.0)


def block_end(y, pk, n):
    parts = [y[pl.ds(i, n, stride=8), :] for i in range(8)]
    return product_rows(split_rows(jnp.concatenate(parts, axis=1)), pk[...])


def enter(arrivals, we, pk, y, n):
    value = jnp.concatenate([a[...] for a in arrivals], axis=1)
    entry = product_rows(split_rows(value), we[...])
    y[pl.ds(0, n, stride=8), :] = entry
    rows = split_rows(entry)
    for i in range(1, 8):
        y[pl.ds(i, n, stride=8), :] = product_rows(rows, power(pk, i))
    return y[...].reshape(n, 8, 128)


def apply_phi(src, idx, origin, w, base, size):
    cols = [src[pl.ds(base, size)].reshape(size * 16, 128)]
    for f in range(6):
        cols.append(jnp.concatenate([src[idx[f, base - origin + e]] for e in range(size)], axis=0))
    return product(jnp.concatenate(cols, axis=1), w[...])


def even_place():
    return lax.rem(lax.axis_index("space"), 2) == 0


def by_parity(body):
    even = even_place()
    pl.when(even)(lambda: body(True))
    pl.when(jnp.logical_not(even))(lambda: body(False))


def mirrored(low, size, full, even):
    return full - low - size if even else low


def pack_kernel(
    forcing, init, conn, pattern, fe_out, even_out, odd_out,
    landed, rows, init_v, conn_v, pattern_v, offs, fe, pay_even, pay_odd, sems, out_sems
):
    n = init_v.shape[0]
    pitch = n + 8
    copies = [pltpu.make_async_copy(forcing.at[:, k], landed.at[k], sems.at[k]) for k in range(COARSEN)]
    small = ((conn, conn_v), (pattern, pattern_v), (init, init_v))
    copies += [pltpu.make_async_copy(src, dst, sems.at[COARSEN + i]) for i, (src, dst) in enumerate(small)]
    for copy in copies[COARSEN:] + copies[:COARSEN]:
        copy.start()
    for copy in copies[COARSEN:]:
        copy.wait()
    place = lax.broadcasted_iota(jnp.int32, (6, n), 1) + lax.axis_index("space") * n
    value = ((conn_v[...] - place) * pattern_v[...]).astype(F32)
    offs[...] = jnp.zeros_like(offs)
    offs[0:6, 0:n] = value
    offs[0:6, n : 2 * n] = value
    tab = offs[...].astype(BF16)
    fe[pl.ds(COARSEN * n * 8, 16), :] = tab
    lead = init_v[...].astype(BF16)
    rest = (init_v[...] - lead.astype(F32)).astype(BF16)
    even = even_place()
    at = sum((COARSEN - 1 - k) * REACH * 8 for k in range(COARSEN))
    for pay in (pay_even, pay_odd):
        pay[pl.ds(at, n), :] = lead
        pay[pl.ds(at + n, n), :] = rest
        pay[pl.ds(at + 2 * n, 16), :] = tab
    at = 0
    results = []
    for k in range(COARSEN):
        copies[k].wait()
        for i in range(8):
            rows[pl.ds(i * pitch, n), :] = landed[k, i].astype(F32)

        def body(pair, carry, k=k):
            e = pair * 2
            two = [rows[pl.ds(e + j, 8, stride=pitch), :] for j in range(2)]
            fe[pl.ds(pl.multiple_of((k * n + e) * 8, 16), 16), :] = jnp.concatenate(two, axis=0).astype(BF16)
            return carry

        lax.fori_loop(0, n // 2, body, 0, unroll=8)
        width = (COARSEN - 1 - k) * REACH * 8
        if width:
            for pay, right in ((pay_even, even), (pay_odd, jnp.logical_not(even))):
                begin = pl.multiple_of(k * n * 8 + jnp.where(right, n * 8 - width, 0), 128)
                pay[pl.ds(at, width), :] = fe[pl.ds(begin, width), :]
        at += width
        rows_k = pl.ds(k * n * 8, n * 8 + (16 if k == COARSEN - 1 else 0))
        if k == COARSEN - 2:
            results.append(pltpu.make_async_copy(pay_odd, odd_out, out_sems.at[0]))
            results.append(pltpu.make_async_copy(pay_even, even_out, out_sems.at[1]))
            results[-2].start()
            results[-1].start()
        results.append(pltpu.make_async_copy(fe.at[rows_k], fe_out.at[rows_k], out_sems.at[2 + k]))
        results[-1].start()
    for result in results:
        result.wait()


def weight_kernel(diag, faces, coarse, w, pk, we):
    put_halves(w.at[pl.ds(0, 128)], diag[...].T)
    for f in range(6):
        put_halves(w.at[pl.ds(128 * (f + 1), 128)], faces[f].T)

    def thirds(a):
        one = a.astype(BF16)
        rest = a - one.astype(F32)
        two = rest.astype(BF16)
        return one, two, (rest - two.astype(F32)).astype(BF16)

    def mul(a, b):
        (a1, a2, a3), (b1, b2, b3) = thirds(a), thirds(b)
        total = jnp.zeros((128, 128), F32)
        for x, y in ((a3, b1), (a1, b3), (a2, b2), (a2, b1), (a1, b2), (a1, b1)):
            total += jnp.dot(x, y, preferred_element_type=F32)
        return total

    rows = lax.broadcasted_iota(jnp.int32, (128, 128), 0)
    one = (rows == lax.broadcasted_iota(jnp.int32, (128, 128), 1)).astype(F32)
    powers = [one, coarse[...].T]
    for k in range(2, 9):
        powers.append(mul(powers[k // 2], powers[k - k // 2]))
    for k in range(8):
        put_halves(pk.at[pl.ds(128 * (7 - k), 128)], powers[k])

    def body(k, current):
        put_halves(we.at[pl.ds(pl.multiple_of(k * 128, 128), 128)], current)
        return mul(current, powers[8])

    lax.fori_loop(0, we.shape[0] // 128, body, one)


def put_force(dst, own, got, right, k, n):
    at = sum((COARSEN - 1 - j) * REACH * 8 for j in range(k))
    width = (COARSEN - 1 - k) * REACH * 8
    dst[pl.ds(n * 8, n * 8), :] = own[pl.ds(k * n * 8, n * 8), :]
    if width:
        to = 2 * n * 8 if right else n * 8 - width
        dst[pl.ds(to, width), :] = got[pl.ds(at, width), :]


def force_at(src, base, size):
    return src[pl.ds(base * 8, size * 8), :].astype(F32).reshape(size, 8, 128)


def origin_of(even, late, n):
    return n if even != late else 0


def put_table(table, fe, got, even, late):
    n = table.shape[1] // 2
    lane = lax.broadcasted_iota(jnp.int32, table.shape, 1)

    def part(ref):
        return ref[pl.ds(ref.shape[0] - 16, 16), :].astype(F32)[0:8]

    origin = origin_of(even, late, n)
    offs = jnp.where(lane < n, part(fe), part(got)) if origin else jnp.where(lane < n, part(got), part(fe))
    table[...] = jnp.where(offs != 0.0, lane + origin + offs.astype(jnp.int32), 3 * n)


def push_init(init, got_even, got_odd, w, table, origin, columns, square, i16, base, count, n, even):
    square[...] = jnp.zeros_like(square)
    square[0:8, :] = table[...].astype(F32)
    columns[...] = square[...].T
    i16[...] = jnp.zeros_like(i16)
    lead = init[...].astype(BF16)
    i16[pl.ds(n, n), 0:128] = lead
    i16[pl.ds(n, n), 128:256] = (init[...] - lead.astype(F32)).astype(BF16)
    for ref, right in ((got_even, even), (got_odd, not even)):
        if ref is not None:
            at = ref.shape[0] - 16
            to = 2 * n if right else 0
            i16[pl.ds(to, n), 0:128] = ref[pl.ds(at - 2 * n, n), :]
            i16[pl.ds(to, n), 128:256] = ref[pl.ds(at - n, n), :]
    rows = pl.ds(base, count)
    place = columns[pl.ds(base - origin, count), :]
    spot = lax.broadcasted_iota(jnp.int32, (count, 256), 1).astype(F32)
    cols = [i16[rows, :]]
    for f in range(6):
        hot = (spot == place[:, f : f + 1]).astype(F32).astype(BF16)
        cols.append(jnp.dot(hot, i16[...], preferred_element_type=F32).astype(BF16))
    leads = jnp.concatenate([c[:, 0:128] for c in cols], axis=1)
    rests = jnp.concatenate([c[:, 128:256] for c in cols], axis=1)
    return product_rows(jnp.concatenate([leads, rests], axis=0), w[...])


STRIPS = (5 * REACH, 4 * REACH, 3 * REACH)
STRIP = 2 * REACH


def put_strips(strips, states, full, even):
    for strip, state, low in zip(strips, states, STRIPS):
        strip[...] = state[pl.ds(mirrored(low, STRIP, full, even), STRIP)]


def get_strips(strips, states, full, even):
    for strip, state, low in zip(strips, states, STRIPS):
        state[pl.ds(mirrored(low, STRIP, full, even), STRIP)] = strip[...]
        state[full] = jnp.zeros((16, 128), BF16)


def first_early_kernel(
    fe, init, got, w, strip1, strip2, strip3, table, s1, s2, s3, force, y, i16, columns, square, idx, sem
):
    def body(even):
        n = init.shape[0]
        full = 3 * n
        origin = origin_of(even, False, n)
        put_table(table, fe, got, even, False)
        copy = pltpu.make_async_copy(table, idx, sem)
        copy.start()
        count = 6 * REACH
        base = mirrored(REACH, count, full, even)
        put_force(force, fe, got, even, 0, n)
        y[pl.ds(0, count * 8), :] = force[pl.ds(base * 8, count * 8), :].astype(F32)

        def add_init():
            pushed = push_init(init, got, None, w, table, origin, columns, square, i16, base, count, n, even)
            y[pl.ds(0, count, stride=8), :] = y[pl.ds(0, count, stride=8), :] + pushed

        pl.when(lax.axis_index("tm") == 0)(add_init)
        s1[pl.ds(base, count)] = split(y[pl.ds(0, count * 8), :].reshape(count, 8, 128))
        for state in (s1, s2, s3):
            state[full] = jnp.zeros((16, 128), BF16)
        copy.wait()
        for k, src, dst in ((1, s1, s2), (2, s2, s3)):
            put_force(force, fe, got, even, k, n)
            size = (6 - 2 * k) * REACH
            base = mirrored((k + 1) * REACH, size, full, even)
            dst[pl.ds(base, size)] = split(apply_phi(src, idx, origin, w, base, size) + force_at(force, base, size))
        put_strips((strip1, strip2, strip3), (s1, s2, s3), full, even)

    by_parity(body)


def first_late_kernel(
    fe, init, got_even, got_odd, strip1, strip2, strip3, w, pk, w1, end, table,
    s1, s2, s3, force, y, i16, columns, square, idx, sem
):
    def body(even):
        n = init.shape[0]
        full = 3 * n
        origin = origin_of(even, True, n)
        put_table(table, fe, got_odd, even, True)
        copy = pltpu.make_async_copy(table, idx, sem)
        copy.start()
        count = 4 * REACH
        base = mirrored(7 * REACH, count, full, even)
        put_force(force, fe, got_odd, not even, 0, n)
        y[...] = force[pl.ds(base * 8, count * 8), :].astype(F32)

        def add_init():
            pushed = push_init(init, got_even, got_odd, w, table, origin, columns, square, i16, base, count, n, even)
            y[pl.ds(0, count, stride=8), :] = y[pl.ds(0, count, stride=8), :] + pushed

        pl.when(lax.axis_index("tm") == 0)(add_init)
        s1[pl.ds(base, count)] = split(y[...].reshape(count, 8, 128))
        get_strips((strip1, strip2, strip3), (s1, s2, s3), full, even)
        copy.wait()
        for k, src, dst in ((1, s1, s2), (2, s2, s3), (3, s3, None)):
            put_force(force, fe, got_odd, not even, k, n)
            base = mirrored((7 - k) * REACH, count, full, even)
            value = apply_phi(src, idx, origin, w, base, count) + force_at(force, base, count)
            if dst is None:
                w1[...] = value
                y[...] = value.reshape(n * 8, 128)
            else:
                dst[pl.ds(base, count)] = split(value)
        end[...] = block_end(y, pk, n)

    by_parity(body)


def scan_kernel(values, pk, starts):
    starts[...] = scan_starts(values[...], pk)


def scan_sum_kernel(values, w1, coarse, pk, starts, total):
    starts[...] = scan_starts(values[...], pk)
    total[...] = values[...] + (w1[...] + coarse[...])


NEAR = 2 * REACH


def put_pay(pay, state, value, side, n):
    def body(even):
        near = 0 if even else n - NEAR
        far = NEAR if even else n - side
        pay[pl.ds(0, NEAR)] = state[pl.ds(near, NEAR)]
        count = side - NEAR
        pay[pl.ds(NEAR, count // 2)] = value[far : far + count].reshape(count // 2, 16, 128).astype(BF16)

    by_parity(body)


def put_far(dst, own, got, right, n):
    half = n // 2
    dst[pl.ds(n + half if right else n, half)] = own[pl.ds(half if right else 0, half)]
    dst[3 * n] = jnp.zeros((16, 128), BF16)
    count = 2 * (got.shape[0] - NEAR)
    dst[pl.ds(2 * n if right else n - NEAR, NEAR)] = got[pl.ds(0, NEAR)]
    leads = got[pl.ds(NEAR, count // 2)].astype(F32).reshape(count, 8, 128)
    far = jnp.concatenate([leads, jnp.zeros_like(leads)], axis=1).astype(BF16)
    dst[pl.ds(2 * n + NEAR if right else n - NEAR - count, count)] = far


def enter_first_kernel(*refs):
    *arrivals, starts, we, pk, state, pay_odd, y = refs
    n = starts.shape[0]
    value = enter(arrivals, we, pk, y, n) + starts[...]
    state[...] = split(value)
    put_pay(pay_odd, state, value, n, n)


def coarse_points(corr, total, pk):
    return product(split(corr).reshape(-1, 128), power(pk, 1)) + total[...]


def enter_second_kernel(*refs):
    *arrivals, starts, total, before, init, we, pk, state, pay_even, pay_odd, corr, y = refs
    n = starts.shape[0]
    value = enter(arrivals, we, pk, y, n) + starts[...]

    def keep(even):
        corr[...] = value if even else coarse_points(value, total, pk)

    by_parity(keep)
    old = before[...].astype(F32)
    y[...] = (value + (old[:, 0:8] + old[:, 8:16])).reshape(n * 8, 128)
    first = (lax.axis_index("tm") == 0).astype(F32)
    y[pl.ds(0, n, stride=8), :] = y[pl.ds(0, n, stride=8), :] + init[...] * first
    value = y[...].reshape(n, 8, 128)
    state[...] = split(value)
    side = (COARSEN - 1) * REACH
    pay_even[...] = state[pl.ds(jnp.where(even_place(), n - side, 0), side)]
    put_pay(pay_odd, state, value, side, n)


def put_block(dst, own, got, right, n):
    side = got.shape[0]
    dst[pl.ds(n, n)] = own[...]
    dst[3 * n] = jnp.zeros((16, 128), BF16)
    dst[pl.ds(2 * n if right else n - side, side)] = got[...]


def second_early_kernel(table, own, got, w, pk, strip1, strip2, strip3, coarse, idx, sem, s0, s1, s2, s3):
    def body(even):
        copy = pltpu.make_async_copy(table, idx, sem)
        copy.start()
        n = own.shape[0]
        origin = origin_of(even, False, n)
        full = 3 * n
        coarse[...] = product(own[...].reshape(n * 16, 128), power(pk, 1))
        put_block(s0, own, got, even, n)
        for state in (s1, s2, s3):
            state[full] = jnp.zeros((16, 128), BF16)
        copy.wait()
        for k, src, dst in ((1, s0, s1), (2, s1, s2), (3, s2, s3)):
            size = (8 - 2 * k) * REACH
            base = mirrored(k * REACH, size, full, even)
            dst[pl.ds(base, size)] = split(apply_phi(src, idx, origin, w, base, size))
        put_strips((strip1, strip2, strip3), (s1, s2, s3), full, even)

    by_parity(body)


def second_late_kernel(table, own, got, strip1, strip2, strip3, coarse, w, pk, res, end, idx, sem, s0, s1, s2, s3, y):
    def body(even):
        copy = pltpu.make_async_copy(table, idx, sem)
        copy.start()
        n = own.shape[0]
        origin = origin_of(even, True, n)
        full = 3 * n
        put_far(s0, own, got, not even, n)
        get_strips((strip1, strip2, strip3), (s1, s2, s3), full, even)
        count = 4 * REACH
        copy.wait()
        for k, src, dst in ((1, s0, s1), (2, s1, s2), (3, s2, s3)):
            base = mirrored((8 - k) * REACH, count, full, even)
            dst[pl.ds(base, count)] = split(apply_phi(src, idx, origin, w, base, count))
        value = apply_phi(s3, idx, origin, w, n, n)
        value = value - coarse[...]
        res[...] = value
        y[...] = value.reshape(n * 8, 128)
        end[...] = block_end(y, pk, n)

    by_parity(body)


def flip_tiles(flip, value, begin):
    lines = flip.reshape(8 * flip.shape[1], 128)
    for e in range(value.shape[0]):
        lines[pl.ds(begin + e, 8, stride=flip.shape[1]), :] = value[e]


def write_out(out, k, flip, begin, size, sems):
    copy = pltpu.make_async_copy(flip.at[:, pl.ds(0, size)], out.at[:, k, pl.ds(begin, size)], sems.at[k])
    copy.start()
    return copy


def third_early_kernel(
    table, own, got, corr, total, fe, pay, w, pk, out, strip1, strip2, kept, idx, sem, s0, s1, s2, force, flip0, flip1, flip3, sems
):
    def body(even):
        table_copy = pltpu.make_async_copy(table, idx, sem)
        table_copy.start()
        n = own.shape[0]
        origin = origin_of(even, False, n)
        full = 3 * n
        points = coarse_points(corr[...], total, pk) if even else corr[...]
        flip_tiles(flip3, points, 0)
        copies = [write_out(out, COARSEN - 1, flip3, 0, n, sems)]
        put_block(s0, own, got, even, n)
        for state in (s1, s2):
            state[full] = jnp.zeros((16, 128), BF16)
        table_copy.wait()
        steps = [(0, s0, s1, flip0), (1, s1, s2, flip1)]
        if even:
            steps.append((2, s2, None, None))
        else:
            kept[...] = jnp.zeros_like(kept)
        for k, src, dst, flip in steps:
            put_force(force, fe, pay, even, k, n)
            size = (5 - 2 * k) * REACH
            base = mirrored((2 + k) * REACH, size, full, even)
            value = apply_phi(src, idx, origin, w, base, size) + force_at(force, base, size)
            if dst is not None:
                dst[pl.ds(base, size)] = split(value)
            mine = (3 - k) * REACH
            value = value[:mine] if even else value[size - mine :]
            if flip is None:
                kept[...] = value
            else:
                flip_tiles(flip, value, 0)
                copies.append(write_out(out, k, flip, n - mine if even else 0, mine, sems))
        for strip, state, low, size in ((strip1, s1, 5 * REACH, 2 * REACH), (strip2, s2, 3 * REACH, 3 * REACH)):
            strip[...] = state[pl.ds(mirrored(low, size, full, even), size)]
        for copy in copies:
            copy.wait()

    by_parity(body)


def third_late_kernel(
    table, own, got, strip1, strip2, kept, fe, pay, w, partial, out, idx, sem, s0, s1, s2, force, flip0, flip1, flip2, sems
):
    def body(even):
        table_copy = pltpu.make_async_copy(table, idx, sem)
        table_copy.start()
        n = own.shape[0]
        origin = origin_of(even, True, n)
        full = 3 * n
        put_far(s0, own, got, not even, n)
        for strip, state, low, size in ((strip1, s1, 5 * REACH, 2 * REACH), (strip2, s2, 3 * REACH, 3 * REACH)):
            state[pl.ds(mirrored(low, size, full, even), size)] = strip[...]
            state[full] = jnp.zeros((16, 128), BF16)
        copies = []
        if even:
            flip_tiles(flip2, kept[...], n - REACH)
        table_copy.wait()
        for k, src, dst, flip in ((0, s0, s1, flip0), (1, s1, s2, flip1), (2, s2, None, flip2)):
            put_force(force, fe, pay, not even, k, n)
            size = 3 * REACH if even or dst is not None else n
            base = mirrored(7 * REACH - k * REACH if size < n else n, size, full, even)
            value = apply_phi(src, idx, origin, w, base, size) + force_at(force, base, size)
            if dst is not None:
                dst[pl.ds(base, size)] = split(value)
            mine = min((k + 1) * REACH, size) if size < n else n
            value = value[size - mine :] if even else value[:mine]
            if dst is None:
                flip_tiles(flip, value, 0 if even else n - mine)
                copies.append(write_out(out, k, flip, 0, n, sems))
            else:
                flip_tiles(flip, value, 0)
                copies.append(write_out(out, k, flip, 0 if even else n - mine, mine, sems))
        for copy in copies:
            copy.wait()

    by_parity(body)


def call(kernel, inputs, outs, scratch, spaces="", out_spaces="", aliases=None, flops=10**7, room=32):
    kinds = {"s": pltpu.SMEM, "h": pltpu.HBM, "v": pltpu.VMEM}

    def specs(arrays, letters):
        letters = letters.ljust(len(arrays), "v")
        return [pl.BlockSpec(memory_space=kinds[letter]) for letter in letters]

    moved = sum(a.size * a.dtype.itemsize for a in list(inputs) + list(outs))
    return pl.pallas_call(
        kernel,
        out_shape=outs,
        name=kernel.__name__,
        in_specs=specs(inputs, spaces),
        out_specs=specs(outs, out_spaces),
        scratch_shapes=scratch,
        input_output_aliases=aliases or {},
        compiler_params=pltpu.CompilerParams(vmem_limit_bytes=room * 1024 * 1024),
        cost_estimate=pl.CostEstimate(flops=flops, bytes_accessed=moved, transcendentals=0),
    )(*inputs)


def local(forcing, initial_state, connectivity, pattern, diag_block, face_blocks, coarse_block):
    n, width = initial_state.shape
    steps = forcing.shape[0]
    full = 3 * n
    tm = lax.axis_size("tm")
    shape = jax.ShapeDtypeStruct
    vmem = pltpu.VMEM
    dma = pltpu.SemaphoreType.DMA
    tiles = shape((n, 8, width), F32)
    state = shape((n, 16, width), BF16)
    ends = shape((n, width), F32)
    step_flops = 2 * 16 * 7 * width * 2 * width
    pay_rows = sum((COARSEN - 1 - k) * REACH * 8 for k in range(COARSEN)) + 2 * n + 16
    pay = shape((pay_rows, width), BF16)
    all_force = ((COARSEN * n * 8 + 16), width)
    fe, pay_even, pay_odd = call(
        pack_kernel,
        (forcing.reshape(steps // COARSEN, COARSEN, n, width), initial_state, connectivity.T, pattern.T),
        (shape(all_force, BF16), pay, pay),
        [
            vmem((COARSEN, 8, n, width), BF16),
            vmem((8 * (n + 8), width), F32),
            vmem((n, width), F32),
            vmem((6, n), jnp.int32),
            vmem((6, n), jnp.int32),
            vmem((16, 128), F32),
            vmem(all_force, BF16),
            vmem((pay_rows, width), BF16),
            vmem((pay_rows, width), BF16),
            dma((COARSEN + 3,)),
            dma((2 + COARSEN,)),
        ],
        spaces="hhhh",
        flops=3 * 10**9,
        out_spaces="hhh",
        room=62,
    )
    pay_odd, pay_even = swapped(pay_odd, 1), swapped(pay_even, 0)
    w, pk, we = call(
        weight_kernel,
        (diag_block, face_blocks, coarse_block),
        (
            shape((7 * width, 2 * width), BF16),
            shape((8 * width, 2 * width), BF16),
            shape(((tm - 1) * width, 2 * width), BF16),
        ),
        [],
        flops=10**9,
    )
    spaces = vmem((full + 1, 16, width), BF16)
    force = vmem((full * 8, width), BF16)
    rows = vmem((n * 8, width), F32)
    strip = shape((STRIP, 16, width), BF16)
    tables = [vmem((256, 256), BF16), vmem((128, 128), F32), vmem((128, 128), F32)]
    smem = pltpu.SMEM((8, 2 * n), jnp.int32)
    table = shape((8, 2 * n), jnp.int32)
    *strips, table_early = call(
        first_early_kernel,
        (fe, initial_state, pay_even, w),
        (strip, strip, strip, table),
        [spaces] * 3 + [force, vmem((6 * REACH * 8, width), F32)] + tables + [smem, dma],
        flops=step_flops * 6 * REACH,
    )
    w1, end, table_late = call(
        first_late_kernel,
        (fe, initial_state, pay_even, pay_odd, *strips, w, pk),
        (tiles, ends, table),
        [spaces] * 3 + [force, rows] + tables + [smem, dma],
        flops=step_flops * 12 * REACH,
    )
    arrivals = earlier(end)
    (starts,) = call(scan_kernel, (w1, pk), (tiles,), [])
    def across(side):
        return shape((NEAR + (side - NEAR) // 2, 16, width), BF16)

    coarse, end_odd = call(enter_first_kernel, (*arrivals, starts, we, pk), (state, across(n)), [rows])
    got_odd, got_even = swapped(end_odd, 1), swapped(coarse, 0)
    *strips, moved = call(
        second_early_kernel,
        (table_early, coarse, got_even, w, pk),
        (strip, strip, strip, tiles),
        [smem, dma] + [spaces] * 4,
        flops=step_flops * 12 * REACH,
    )
    res, end = call(
        second_late_kernel,
        (table_late, coarse, got_odd, *strips, moved, w, pk),
        (tiles, ends),
        [smem, dma] + [spaces] * 4 + [rows],
        flops=step_flops * 16 * REACH,
    )
    arrivals = earlier(end)
    starts, total = call(scan_sum_kernel, (res, w1, moved, pk), (tiles, tiles), [])
    side = (COARSEN - 1) * REACH
    coarse, end_even, end_odd, corr = call(
        enter_second_kernel,
        (*arrivals, starts, total, coarse, initial_state, we, pk),
        (state, shape((side, 16, width), BF16), across(side), tiles),
        [rows],
    )
    got_odd, got_even = swapped(end_odd, 1), swapped(end_even, 0)
    result = shape((steps // COARSEN, COARSEN, n, width), F32)

    def flip(blocks):
        return vmem((8, blocks * REACH + 8, width), F32)

    out, *strips = call(
        third_early_kernel,
        (table_early, coarse, got_even, corr, total, fe, pay_even, w, pk),
        (result, strip, shape((3 * REACH, 16, width), BF16), shape((REACH, 8, width), F32)),
        [smem, dma] + [spaces] * 3 + [force, flip(3), flip(2), vmem((8, n + 8, width), F32), dma((COARSEN,))],
        out_spaces="h",
        flops=step_flops * 9 * REACH,
    )
    (out,) = call(
        third_late_kernel,
        (table_late, coarse, got_odd, *strips, fe, pay_odd, w, out),
        (result,),
        [smem, dma] + [spaces] * 3 + [force, flip(1), flip(2), vmem((8, n + 8, width), F32), dma((COARSEN - 1,))],
        spaces="vvvvvvvvvh",
        out_spaces="h",
        aliases={9: 0},
        flops=step_flops * 9 * REACH,
    )
    return out.reshape(steps, n, width)


def solution(mesh):
    return jax.shard_map(
        local,
        mesh=mesh,
        in_specs=(
            P("tm", ("groups", "space"), None),
            P(("groups", "space"), None),
            P("space", None),
            P("space", None),
            P(),
            P(),
            P(),
        ),
        out_specs=P("tm", ("groups", "space"), None),
        check_vma=False,
    )
```
